32 devices in a mesh: seq: 16 (over z, x, core), batch: 2 (over y).
Axes of the slice: x: 2, y: 2, z: 4, core: 2. Of those that a mesh axis runs over, the one named last changes fastest.
Arguments:
- enc_in: bfloat16 [2, 1024, 512], P('batch', 'seq'), may hold values from -6 to 6
- series: bfloat16 [2, 1024, 862], P('batch', 'seq'), may hold values from -6 to 6
- channel_mask: int32 [16, 862], replicated, may hold values 0 or 1
- item_group: int32 [2], P('batch'), may hold values from 0 to 15
- tau_scale: float32 [2], P('batch'), may hold values from 0.6 to 1.8
- delta_shift: bfloat16 [2, 1024], P('batch', 'seq'), may hold values from -16 to 16
- dec_in: bfloat16 [2, 1024, 512], P('batch', 'seq'), may hold values from -6 to 6
- value_embed: bfloat16 [862, 512], replicated, may hold values from -0.21875 to 0.21875
- enc_qkv: bfloat16 [3, 512, 512], replicated, may hold values from -0.25 to 0.25
- enc_out: bfloat16 [512, 512], replicated, may hold values from -6 to 6
- enc_ff_in: bfloat16 [512, 2048], replicated, may hold values from -0.25 to 0.25
- enc_ff_out: bfloat16 [2048, 512], replicated, may hold values from -0.125 to 0.125
- enc_query_bias: float32 [512], replicated, may hold values from -0.6 to 0.6
- enc_bias: float32 [5, 512], replicated, may hold values from -0.3 to 0.3
- enc_gain: float32 [2, 512], replicated, may hold values from 0.5 to 1.5
- dec_qkv: bfloat16 [3, 512, 512], replicated, may hold values from -0.25 to 0.25
- dec_out: bfloat16 [512, 512], replicated, may hold values from -3 to 3
- cross_qkv: bfloat16 [3, 512, 512], replicated, may hold values from -0.25 to 0.25
- cross_out: bfloat16 [512, 512], replicated, may hold values from -6 to 6
- dec_ff_in: bfloat16 [512, 2048], replicated, may hold values from -0.25 to 0.25
- dec_ff_out: bfloat16 [2048, 512], replicated, may hold values from -0.125 to 0.125
- dec_bias: float32 [10, 512], replicated, may hold values from -0.3 to 0.3
- dec_gain: float32 [3, 512], replicated, may hold values from 0.5 to 1.5
- ff_bias: float32 [2, 2048], replicated, may hold values from -1.5 to 1.5
- cotangent: bfloat16 [2, 1024, 512], P('batch', 'seq'), may hold values from -6 to 6
Outputs:
- dec_result: bfloat16 [2, 1024, 512], P('batch', 'seq')
- grad_enc_in: float32 [2, 1024, 512], P('batch', 'seq')
- grad_dec_in: float32 [2, 1024, 512], P('batch', 'seq')
- grad_value_embed: float32 [862, 512], P(None, 'seq')
- grad_enc_qkv: float32 [3, 512, 512], P(None, None, 'seq')
- grad_enc_out: float32 [512, 512], P(None, 'seq')
- grad_enc_ff_in: float32 [512, 2048], P(None, 'seq')
- grad_enc_ff_out: float32 [2048, 512], P(None, 'seq')
- grad_enc_query_bias: float32 [512], P('seq')
- grad_enc_bias: float32 [5, 512], P(None, 'seq')
- grad_enc_gain: float32 [2, 512], P(None, 'seq')
- grad_dec_qkv: float32 [3, 512, 512], P(None, None, 'seq')
- grad_dec_out: float32 [512, 512], P(None, 'seq')
- grad_cross_qkv: float32 [3, 512, 512], P(None, None, 'seq')
- grad_cross_out: float32 [512, 512], P(None, 'seq')
- grad_dec_ff_in: float32 [512, 2048], P(None, 'seq')
- grad_dec_ff_out: float32 [2048, 512], P(None, 'seq')
- grad_dec_bias: float32 [10, 512], P(None, 'seq')
- grad_dec_gain: float32 [3, 512], P(None, 'seq')
- grad_ff_bias: float32 [2, 2048], P(None, 'seq')
The draws below stay inside these ranges and needn't reach their ends.
All inputs are finite; a program needn't handle non-finite values.
Results may differ from the reference program's by a relative error of at most 0.035.
Values may be sent and summed in bfloat16 or wider, within the bound.
A program may use at most 192 MiB of HBM per device.

```python
import math
import jax
import jax.numpy as jnp
from jax import lax

D = 512
HEADS = 8
FF = 2048
CMAX = 862
GROUPS = 16
ITEMS = 2
LENC = 1024
LDEC = 1024


def touch_ends(values, stream_key, smallest, top_value):
    shape = values.shape
    index_at = [jax.random.randint(jax.random.fold_in(stream_key, axis), (), 0, shape[axis]) for axis in range(len(shape))]
    values = values.at[tuple(index_at)].set(smallest)
    longest = shape.index(max(shape))
    index_at[longest] = (index_at[longest] + 1) % shape[longest]
    return values.at[tuple(index_at)].set(top_value)


def with_spikes(array, stream_key, source, target, shards_of, factor):
    owner, partner = [(jnp.arange(array.shape[axis_at]) // (array.shape[axis_at] // shards_of)).reshape([-1 if axis == axis_at else 1 for axis in range(array.ndim)]) for axis_at in (source, target)]
    chosen = jax.random.permutation(stream_key, shards_of)[partner]
    strong = (owner == chosen) | (owner == (partner + shards_of // 2) % shards_of)
    return jnp.where(strong, factor * array, array)


def steps_of(rng, extent, cuts, smallest, top_value):
    def one(dim, blocks):
        draws = jax.random.uniform(jax.random.fold_in(jax.random.fold_in(rng, 6), dim), (blocks,), jnp.float32, smallest / len(cuts), top_value / len(cuts))
        return jnp.repeat(jnp.exp(draws), extent[dim] // blocks).reshape((-1,) + (1,) * (len(extent) - dim - 1))

    level = one(*cuts[0])
    for cut in cuts[1:]:
        level = level * one(*cut)
    return level


def normal_values(own_key, dims, scale, reach, split=(), kind=jnp.bfloat16):
    array = jax.random.normal(own_key, dims, jnp.float32) * scale
    if len(split) > 0:
        array = steps_of(own_key, dims, split, -0.22, 0.18) * array
    return jnp.clip(array, min=-reach, max=reach).astype(kind)


def heavy_noise(rng, extent, deviation, limit, cuts, heavy, kind=jnp.bfloat16):
    drawn = deviation * jax.random.normal(rng, extent, jnp.float32)
    if cuts:
        drawn = drawn * steps_of(rng, extent, cuts, -0.22, 0.18)
    return jnp.clip(with_spikes(drawn, jax.random.fold_in(rng, 3), *heavy), -limit, limit).astype(kind)


def setup_inputs(seed: int = 0) -> dict:
    keys = jax.random.split(jax.random.key(seed), 26)
    return {
        "enc_in": normal_values(keys[0], (ITEMS, LENC, D), 1.0, 6.0, ((0, 2), (1, 16))),
        "series": normal_values(keys[1], (ITEMS, LENC, CMAX), 1.0, 6.0, ((0, 2), (1, 16))),
        "channel_mask": touch_ends((jax.random.randint(keys[2], (GROUPS, CMAX), 0, 2) < 1).astype(jnp.int32), jax.random.fold_in(keys[2], 1), 0, 1),
        "item_group": jax.random.randint(keys[3], (ITEMS,), 0, GROUPS).astype(jnp.int32),
        "tau_scale": jnp.clip(jnp.exp(math.log(1.8) - 1.0986122 * jax.random.uniform(keys[4], (ITEMS,), jnp.float32) ** steps_of(keys[4], (ITEMS,), ((0, 2),), -0.2, 0.2)), 0.6, 1.8),
        "delta_shift": normal_values(keys[5], (ITEMS, LENC), 4.0, 16.0, ((0, 2), (1, 16))),
        "dec_in": normal_values(keys[6], (ITEMS, LDEC, D), 1.0, 6.0, ((0, 2), (1, 16))),
        "value_embed": normal_values(keys[7], (CMAX, D), CMAX ** -0.5, 0.21875),
        "enc_qkv": normal_values(keys[8], (3, D, D), D ** -0.5, 0.25),
        "enc_out": normal_values(keys[9], (D, D), 1 ** -0.5, 6.0),
        "enc_ff_in": normal_values(keys[10], (D, FF), D ** -0.5, 0.25),
        "enc_ff_out": normal_values(keys[11], (FF, D), FF ** -0.5, 0.125),
        "enc_query_bias": normal_values(keys[12], (D,), 0.1, 0.6, (), jnp.float32),
        "enc_bias": normal_values(keys[13], (5, D), 0.05, 0.3, (), jnp.float32),
        "enc_gain": jnp.clip(1.0 + 0.1 * jax.random.normal(keys[14], (2, D), jnp.float32), 0.5, 1.5),
        "dec_qkv": normal_values(keys[15], (3, D, D), D ** -0.5, 0.25),
        "dec_out": normal_values(keys[16], (D, D), 4 ** -0.5, 3.0),
        "cross_qkv": normal_values(keys[17], (3, D, D), D ** -0.5, 0.25),
        "cross_out": normal_values(keys[18], (D, D), 1 ** -0.5, 6.0),
        "dec_ff_in": normal_values(keys[19], (D, FF), D ** -0.5, 0.25),
        "dec_ff_out": normal_values(keys[20], (FF, D), FF ** -0.5, 0.125),
        "dec_bias": normal_values(keys[21], (10, D), 0.05, 0.3, (), jnp.float32),
        "dec_gain": jnp.clip(1.0 + 0.1 * jax.random.normal(keys[22], (3, D), jnp.float32), 0.5, 1.5),
        "ff_bias": normal_values(keys[23], (2, FF), 0.25, 1.5, (), jnp.float32),
        "cotangent": heavy_noise(keys[24], (ITEMS, LDEC, D), 1.0, 6.0, ((0, 2), (1, 16)), (1, 2, 16, 2.0)),
    }


@jax.custom_vjp
def low(v):
    return lax.optimization_barrier(v.astype(jnp.bfloat16)).astype(jnp.float32)

@jax.custom_vjp
def low_back(v):
    return v

def low_keep(v):
    return (low(v), None)

def low_pass(kept, grad):
    return (grad,)

def back_keep(v):
    return (v, None)

def back_low(kept, grad):
    return (low(grad),)
low.defvjp(low_keep, low_pass)
low_back.defvjp(back_keep, back_low)

def matmul_high(left, right):
    return jnp.matmul(left, right, precision=lax.Precision.HIGHEST)

def rounded_both(value):
    return low_back(low(value))

def layer_norm(inputs, gain_vector, shift_vector):
    average = lax.optimization_barrier(jnp.mean(inputs, axis=-1, keepdims=True))
    centred = inputs - average
    variance = lax.optimization_barrier(jnp.mean(centred * centred, axis=-1, keepdims=True))
    return centred * lax.rsqrt(variance + 1e-05) * gain_vector + shift_vector

def attention(queries, key_rows, value_rows, tau_value, key_shift, causal):
    query_len = queries.shape[0]
    key_len = key_rows.shape[0]
    width = queries.shape[1]
    head_size = width // HEADS
    key_heads = key_rows.reshape(key_len, HEADS, head_size)
    value_heads = value_rows.reshape(key_len, HEADS, head_size)
    block_rows = math.gcd(query_len, 512)
    block_count = query_len // block_rows
    query_blocks = queries.reshape(block_count, block_rows, HEADS, head_size)
    starts = jnp.arange(block_count, dtype=jnp.int32) * block_rows
    key_pos = jnp.arange(key_len, dtype=jnp.int32)

    def one_block(inputs):
        query_block, first_row = inputs
        raw_scores = jnp.einsum('qhd,khd->hqk', query_block, key_heads, precision=lax.Precision.HIGHEST)
        scores = low_back((tau_value * raw_scores + key_shift[None, None, :]) * 0.125)
        if causal:
            query_pos = first_row + jnp.arange(block_rows, dtype=jnp.int32)
            scores = jnp.where((query_pos[:, None] >= key_pos[None, :])[None], scores, -1e+30)
        row_max = lax.optimization_barrier(jnp.max(scores, axis=-1, keepdims=True))
        weights = jnp.exp(scores - row_max)
        probabilities = weights / lax.optimization_barrier(jnp.sum(weights, axis=-1, keepdims=True))
        mixed_values = jnp.einsum('hqk,khd->qhd', probabilities, value_heads, precision=lax.Precision.HIGHEST)
        return mixed_values.reshape(block_rows, width)
    outputs = lax.map(jax.checkpoint(one_block), (query_blocks, starts))
    return outputs.reshape(query_len, width)

def attention_branch(query_side, key_side, qkv_weights, out_weight, query_bias, value_bias, out_bias, tau_value, key_shift, causal):
    queries = rounded_both(matmul_high(query_side, qkv_weights[0]) + query_bias)
    key_rows = rounded_both(matmul_high(key_side, qkv_weights[1]))
    value_rows = rounded_both(matmul_high(key_side, qkv_weights[2]) + value_bias)
    attended = rounded_both(attention(queries, key_rows, value_rows, tau_value, key_shift, causal))
    return low_back(matmul_high(attended, out_weight) + out_bias)

def feed_forward(inputs, weight_in, bias_in, weight_out, bias_out):
    pre_act = low_back(matmul_high(low(inputs), weight_in) + bias_in)
    activated = low(jax.nn.gelu(pre_act, approximate=False))
    return low_back(matmul_high(activated, weight_out) + bias_out)

def item_forward(params, enc_row, series_row, dec_row, tau_value, key_shift):
    value_embed, enc_qkv, enc_out, enc_ff_in, enc_ff_out, enc_query_bias, enc_bias, enc_gain, dec_qkv, dec_out, cross_qkv, cross_out, dec_ff_in, dec_ff_out, dec_bias, dec_gain, ff_bias = params
    embedded = enc_row + low_back(matmul_high(series_row, value_embed))
    enc_hidden = low(embedded)
    enc_branch = attention_branch(enc_hidden, enc_hidden, enc_qkv, enc_out, enc_query_bias, enc_bias[0], enc_bias[1], tau_value, key_shift, False)
    first_enc = layer_norm(embedded + enc_branch, enc_gain[0], enc_bias[3])
    encoded = layer_norm(first_enc + feed_forward(first_enc, enc_ff_in, ff_bias[0], enc_ff_out, enc_bias[2]), enc_gain[1], enc_bias[4])
    memory = low(encoded)
    dec_hidden = low(dec_row)
    no_shift = jnp.zeros_like(dec_row[:, 0])
    self_branch = attention_branch(dec_hidden, dec_hidden, dec_qkv, dec_out, dec_bias[0], dec_bias[1], dec_bias[2], tau_value, no_shift, True)
    first_dec = layer_norm(dec_row + self_branch, dec_gain[0], dec_bias[7])
    cross_branch = attention_branch(low(first_dec), memory, cross_qkv, cross_out, dec_bias[3], dec_bias[4], dec_bias[5], tau_value, key_shift, False)
    second_dec = layer_norm(first_dec + cross_branch, dec_gain[1], dec_bias[8])
    third_in = second_dec + feed_forward(second_dec, dec_ff_in, ff_bias[1], dec_ff_out, dec_bias[6])
    return layer_norm(third_in, dec_gain[2], dec_bias[9])

def reference(enc_in, series, channel_mask, item_group, tau_scale, delta_shift, dec_in, value_embed, enc_qkv, enc_out, enc_ff_in, enc_ff_out, enc_query_bias, enc_bias, enc_gain, dec_qkv, dec_out, cross_qkv, cross_out, dec_ff_in, dec_ff_out, dec_bias, dec_gain, ff_bias, cotangent):
    chosen = (item_group[:, None] == jnp.arange(GROUPS, dtype=jnp.int32)[None, :]).astype(jnp.float32)
    channels = matmul_high(chosen, channel_mask.astype(jnp.float32))
    masked_series = series.astype(jnp.float32) * channels[:, None, :]
    shifts = delta_shift.astype(jnp.float32)
    weights_in = (value_embed.astype(jnp.float32), enc_qkv.astype(jnp.float32), enc_out.astype(jnp.float32), enc_ff_in.astype(jnp.float32), enc_ff_out.astype(jnp.float32), enc_query_bias.astype(jnp.float32), enc_bias.astype(jnp.float32), enc_gain.astype(jnp.float32), dec_qkv.astype(jnp.float32), dec_out.astype(jnp.float32), cross_qkv.astype(jnp.float32), cross_out.astype(jnp.float32), dec_ff_in.astype(jnp.float32), dec_ff_out.astype(jnp.float32), dec_bias.astype(jnp.float32), dec_gain.astype(jnp.float32), ff_bias.astype(jnp.float32))

    def forward(enc_values, dec_values, *params):

        def per_item(inputs):
            return item_forward(params, inputs[0], inputs[1], inputs[2], inputs[3], inputs[4])
        return lax.map(per_item, (enc_values, masked_series, dec_values, tau_scale, shifts))
    result, pullback = jax.vjp(forward, enc_in.astype(jnp.float32), dec_in.astype(jnp.float32), *weights_in)
    gradients = pullback(cotangent.astype(jnp.float32))
    return (result.astype(jnp.bfloat16), gradients[0], gradients[1], gradients[2], gradients[3], gradients[4], gradients[5], gradients[6], gradients[7], gradients[8], gradients[9], gradients[10], gradients[11], gradients[12], gradients[13], gradients[14], gradients[15], gradients[16], gradients[17], gradients[18])
```

```python
from functools import partial
import math

import jax
import jax.numpy as jnp
from jax import lax
from jax.experimental import pallas as pl
from jax.experimental.pallas import tpu as pltpu
from jax.sharding import PartitionSpec as P

HEADS = 8
GROUPS = 16
SEQ = "seq"
BATCH = "batch"


epsilon = 1e-05
masked_score = -1e30


def layer_norm(inputs, gain_vector, shift_vector):
    average = jnp.mean(inputs, axis=-1, keepdims=True)
    centred = inputs - average
    variance = jnp.mean(centred * centred, axis=-1, keepdims=True)
    return centred * lax.rsqrt(variance + epsilon) * gain_vector + shift_vector


def norm_backward(inputs, gain_vector, shift_vector, upstream):
    ignored, pullback = jax.vjp(layer_norm, inputs, gain_vector, shift_vector)
    return pullback(upstream)


def project(inputs, weight_matrix):
    return jnp.dot(inputs, weight_matrix, preferred_element_type=jnp.float32)


def project_back(gradient, weight_matrix):
    return jnp.einsum("ilf,kf->ilk", gradient, weight_matrix, preferred_element_type=jnp.float32)


def weight_grad(inputs, gradient):
    return jnp.einsum("ilk,ilf->kf", inputs, gradient, preferred_element_type=jnp.float32)


def row_total(gradient):
    return jnp.sum(gradient.astype(jnp.float32), axis=(0, 1))


def split_heads(values):
    return values.reshape(values.shape[:2] + (HEADS, values.shape[2] // HEADS))


def merge_heads(head_values):
    return jnp.transpose(head_values, (0, 2, 1, 3)).reshape(
        head_values.shape[0], head_values.shape[2], -1
    )


def over_blocks(update, totals, arrays, shard_rows):
    length = arrays[0].shape[1]
    block_rows = shard_rows * math.gcd(length // shard_rows, 8)
    block_count = length // block_rows
    stacked = tuple(
        (
            jnp.moveaxis(
                member.reshape((member.shape[0], block_count, block_rows) + member.shape[2:]), 1, 0
            )
            for member in arrays
        )
    )
    offsets = jnp.arange(block_count, dtype=jnp.int32) * block_rows

    def advance(running, inputs):
        return (update(running, inputs[0], inputs[1]), None)

    totals, ignored = lax.scan(advance, totals, (stacked, offsets))
    return totals


def head_scores(query_heads, key_heads, tau_value, key_shift):
    raw_scores = jnp.einsum(
        "iqhd,ikhd->ihqk", query_heads, key_heads, preferred_element_type=jnp.float32
    )
    return (tau_value[:, None, None, None] * raw_scores + key_shift[:, None, None, :]) * 0.125


def causal_mask(scores, query_pos, key_pos):
    allowed = query_pos[:, None] >= key_pos[None, :]
    return jnp.where(allowed[None, None], scores, masked_score)


def fresh_totals(item_count, row_count, head_size):
    return (
        jnp.full((item_count, HEADS, row_count), masked_score, jnp.float32),
        jnp.zeros((item_count, HEADS, row_count), jnp.float32),
        jnp.zeros((item_count, HEADS, row_count, head_size), jnp.float32),
    )


def finish_forward(totals):
    running_max, running_sum, weighted = totals
    output = merge_heads(weighted / running_sum[..., None])
    log_total = jnp.transpose(running_max + jnp.log(running_sum), (0, 2, 1))
    return (output, log_total)


def row_products(grad_rows, mixed_rows):
    return jnp.sum(split_heads(grad_rows).astype(jnp.float32) * split_heads(mixed_rows), axis=-1)


def scaled_grad(head_totals, tau_value):
    return merge_heads(head_totals * (tau_value * 0.125)[:, None, None, None]).astype(jnp.bfloat16)


def plain_unpack(fetched):
    return (fetched[0], fetched[1], fetched[2].astype(jnp.float32))


def self_unpack(fetched):
    return (fetched[0], fetched[1], jnp.zeros(fetched[0].shape[:2], jnp.float32))


def forward_update(query_heads, tau_value, query_pos, causal, unpack, shard_rows):

    def update(totals, fetched, offset):

        def block_update(running, piece_parts, inner_offset):
            running_max, running_sum, weighted = running
            key_rows, value_rows, key_shift = unpack(piece_parts)
            scores = head_scores(query_heads, split_heads(key_rows), tau_value, key_shift)
            if causal:
                key_pos = inner_offset + jnp.arange(key_rows.shape[1], dtype=jnp.int32)
                scores = causal_mask(scores, query_pos, key_pos)
            new_max = jnp.maximum(running_max, jnp.max(scores, axis=-1))
            factor = jnp.exp(running_max - new_max)
            weights = jnp.exp(scores - new_max[..., None])
            new_sum = running_sum * factor + jnp.sum(weights, axis=-1)
            mixed_values = jnp.einsum(
                "ihqk,ikhd->ihqd",
                weights,
                split_heads(value_rows).astype(jnp.float32),
                preferred_element_type=jnp.float32,
            )
            return (new_max, new_sum, weighted * factor[..., None] + mixed_values)

        return over_blocks(block_update, totals, fetched, shard_rows)

    return update


def query_grad_update(
    query_heads, grad_heads, log_total, row_dot, tau_value, query_pos, causal, unpack, shard_rows
):

    def update(totals, fetched, offset):

        def block_update(running, piece_parts, inner_offset):
            key_rows, value_rows, key_shift = unpack(piece_parts)
            key_heads = split_heads(key_rows)
            scores = head_scores(query_heads, key_heads, tau_value, key_shift)
            if causal:
                key_pos = inner_offset + jnp.arange(key_rows.shape[1], dtype=jnp.int32)
                scores = causal_mask(scores, query_pos, key_pos)
            probabilities = jnp.exp(scores - log_total[..., None])
            prob_grads = jnp.einsum(
                "iqhd,ikhd->ihqk",
                grad_heads,
                split_heads(value_rows),
                preferred_element_type=jnp.float32,
            )
            score_grads = (probabilities * (prob_grads - row_dot[..., None])).astype(jnp.bfloat16)
            return running + jnp.einsum(
                "ihqk,ikhd->ihqd", score_grads, key_heads, preferred_element_type=jnp.float32
            )

        return over_blocks(block_update, totals, fetched, shard_rows)

    return update


def key_grad_update(key_heads, value_heads, key_shift, tau_value, key_pos, causal, shard_rows):

    def update(totals, fetched, offset):

        def block_update(running, piece_parts, inner_offset):
            key_total, value_total = running
            query_heads = split_heads(piece_parts[0].astype(jnp.bfloat16))
            grad_heads = split_heads(piece_parts[1].astype(jnp.bfloat16))
            log_rows = jnp.transpose(piece_parts[2], (0, 2, 1))
            dot_rows = jnp.transpose(piece_parts[3], (0, 2, 1))
            scores = head_scores(query_heads, key_heads, tau_value, key_shift)
            if causal:
                query_pos = inner_offset + jnp.arange(piece_parts[0].shape[1], dtype=jnp.int32)
                scores = causal_mask(scores, query_pos, key_pos)
            probabilities = jnp.exp(scores - log_rows[..., None])
            value_total = value_total + jnp.einsum(
                "ihqk,iqhd->ihkd",
                probabilities,
                grad_heads.astype(jnp.float32),
                preferred_element_type=jnp.float32,
            )
            prob_grads = jnp.einsum(
                "iqhd,ikhd->ihqk", grad_heads, value_heads, preferred_element_type=jnp.float32
            )
            score_grads = (probabilities * (prob_grads - dot_rows[..., None])).astype(jnp.bfloat16)
            key_total = key_total + jnp.einsum(
                "ihqk,iqhd->ihkd", score_grads, query_heads, preferred_element_type=jnp.float32
            )
            return (key_total, value_total)

        return over_blocks(block_update, totals, fetched, shard_rows)

    return update


def feed_forward_back(upstream, hidden, pre_act, activated, weight_in, weight_out):
    out_grad = upstream.astype(jnp.bfloat16)
    out_weight_grad = weight_grad(activated, out_grad)
    out_bias_grad = row_total(out_grad)
    act_grad = project_back(out_grad, weight_out)
    ignored, gelu_back = jax.vjp(partial(jax.nn.gelu, approximate=False), pre_act)
    pre_grad = gelu_back(act_grad)[0].astype(jnp.bfloat16)
    return (
        project_back(pre_grad, weight_in),
        weight_grad(hidden, pre_grad),
        row_total(pre_grad),
        out_weight_grad,
        out_bias_grad,
    )


def local(
    enc_in,
    series,
    channel_mask,
    item_group,
    tau_scale,
    delta_shift,
    dec_in,
    value_embed,
    enc_qkv,
    enc_out,
    enc_ff_in,
    enc_ff_out,
    enc_query_bias,
    enc_bias,
    enc_gain,
    dec_qkv,
    dec_out,
    cross_qkv,
    cross_out,
    dec_ff_in,
    dec_ff_out,
    dec_bias,
    dec_gain,
    ff_bias,
    cotangent,
):
    item_count, enc_rows, width = enc_in.shape
    dec_rows = dec_in.shape[1]
    head_size = width // HEADS
    seq_index = lax.axis_index(SEQ)
    enc_pos = seq_index * enc_rows + jnp.arange(enc_rows, dtype=jnp.int32)
    dec_pos = seq_index * dec_rows + jnp.arange(dec_rows, dtype=jnp.int32)
    enc_shift = delta_shift.astype(jnp.float32)
    chosen = (item_group[:, None] == jnp.arange(GROUPS, dtype=jnp.int32)[None, :]).astype(
        jnp.float32
    )
    channels = jnp.dot(chosen, channel_mask.astype(jnp.float32), precision=lax.Precision.HIGHEST)
    masked_series = (series.astype(jnp.float32) * channels[:, None, :]).astype(jnp.bfloat16)
    embedded = enc_in.astype(jnp.float32) + project(masked_series, value_embed)
    enc_hidden = embedded.astype(jnp.bfloat16)
    enc_query = (project(enc_hidden, enc_qkv[0]) + enc_query_bias).astype(jnp.bfloat16)
    enc_key = project(enc_hidden, enc_qkv[1]).astype(jnp.bfloat16)
    enc_value = (project(enc_hidden, enc_qkv[2]) + enc_bias[0]).astype(jnp.bfloat16)
    enc_update = forward_update(
        split_heads(enc_query), tau_scale, enc_pos, False, plain_unpack, enc_rows
    )
    enc_mixed, enc_log = finish_forward(
        enc_update(
            fresh_totals(item_count, enc_rows, head_size),
            (
                lax.all_gather(enc_key, SEQ, axis=1, tiled=True),
                lax.all_gather(enc_value, SEQ, axis=1, tiled=True),
                lax.all_gather(delta_shift, SEQ, axis=1, tiled=True),
            ),
            jnp.int32(0),
        )
    )
    enc_attended = enc_mixed.astype(jnp.bfloat16)
    enc_first_in = embedded + project(enc_attended, enc_out) + enc_bias[1]
    enc_first = layer_norm(enc_first_in, enc_gain[0], enc_bias[3])
    enc_ff_hidden = enc_first.astype(jnp.bfloat16)
    enc_ff_pre = project(enc_ff_hidden, enc_ff_in) + ff_bias[0]
    enc_ff_act = jax.nn.gelu(enc_ff_pre, approximate=False).astype(jnp.bfloat16)
    enc_second_in = enc_first + project(enc_ff_act, enc_ff_out) + enc_bias[2]
    encoded = layer_norm(enc_second_in, enc_gain[1], enc_bias[4])
    memory = encoded.astype(jnp.bfloat16)
    self_query = (project(dec_in, dec_qkv[0]) + dec_bias[0]).astype(jnp.bfloat16)
    self_key = project(dec_in, dec_qkv[1]).astype(jnp.bfloat16)
    self_value = (project(dec_in, dec_qkv[2]) + dec_bias[1]).astype(jnp.bfloat16)
    self_update = forward_update(
        split_heads(self_query), tau_scale, dec_pos, True, self_unpack, dec_rows
    )
    self_mixed, self_log = finish_forward(
        self_update(
            fresh_totals(item_count, dec_rows, head_size),
            (
                lax.all_gather(self_key, SEQ, axis=1, tiled=True),
                lax.all_gather(self_value, SEQ, axis=1, tiled=True),
            ),
            jnp.int32(0),
        )
    )
    self_attended = self_mixed.astype(jnp.bfloat16)
    dec_first_in = dec_in.astype(jnp.float32) + project(self_attended, dec_out) + dec_bias[2]
    dec_first = layer_norm(dec_first_in, dec_gain[0], dec_bias[7])
    cross_hidden = dec_first.astype(jnp.bfloat16)
    cross_query = (project(cross_hidden, cross_qkv[0]) + dec_bias[3]).astype(jnp.bfloat16)
    cross_key = project(memory, cross_qkv[1]).astype(jnp.bfloat16)
    cross_value = (project(memory, cross_qkv[2]) + dec_bias[4]).astype(jnp.bfloat16)
    cross_start = fresh_totals(item_count, dec_rows, head_size)
    cross_update = forward_update(
        split_heads(cross_query), tau_scale, dec_pos, False, plain_unpack, enc_rows
    )
    cross_totals = cross_update(
        cross_start,
        (
            lax.all_gather(cross_key, SEQ, axis=1, tiled=True),
            lax.all_gather(cross_value, SEQ, axis=1, tiled=True),
            lax.all_gather(delta_shift, SEQ, axis=1, tiled=True),
        ),
        jnp.int32(0),
    )
    cross_mixed, cross_log = finish_forward(cross_totals)
    cross_attended = cross_mixed.astype(jnp.bfloat16)
    dec_second_in = dec_first + project(cross_attended, cross_out) + dec_bias[5]
    dec_second = layer_norm(dec_second_in, dec_gain[1], dec_bias[8])
    dec_ff_hidden = dec_second.astype(jnp.bfloat16)
    dec_ff_pre = project(dec_ff_hidden, dec_ff_in) + ff_bias[1]
    dec_ff_act = jax.nn.gelu(dec_ff_pre, approximate=False).astype(jnp.bfloat16)
    dec_third_in = dec_second + project(dec_ff_act, dec_ff_out) + dec_bias[6]
    decoded = layer_norm(dec_third_in, dec_gain[2], dec_bias[9])
    third_grad, dec_gain_three, dec_bias_three = norm_backward(
        dec_third_in, dec_gain[2], dec_bias[9], cotangent.astype(jnp.float32)
    )
    from_dec_ff, dec_ff_in_grad, dec_ff_bias_grad, dec_ff_out_grad, dec_ff_out_bias = (
        feed_forward_back(third_grad, dec_ff_hidden, dec_ff_pre, dec_ff_act, dec_ff_in, dec_ff_out)
    )
    second_grad, dec_gain_two, dec_bias_two = norm_backward(
        dec_second_in, dec_gain[1], dec_bias[8], third_grad + from_dec_ff
    )
    cross_branch_grad = second_grad.astype(jnp.bfloat16)
    cross_out_grad = weight_grad(cross_attended, cross_branch_grad)
    cross_out_bias = row_total(cross_branch_grad)
    cross_mixed_grad = project_back(cross_branch_grad, cross_out).astype(jnp.bfloat16)
    cross_dot = row_products(cross_mixed_grad, cross_mixed)
    cross_query_start = jnp.zeros((item_count, HEADS, dec_rows, head_size), jnp.float32)
    cross_back = query_grad_update(
        split_heads(cross_query),
        split_heads(cross_mixed_grad),
        jnp.transpose(cross_log, (0, 2, 1)),
        jnp.transpose(cross_dot, (0, 2, 1)),
        tau_scale,
        dec_pos,
        False,
        plain_unpack,
        enc_rows,
    )
    cross_query_total = cross_back(
        cross_query_start,
        (
            lax.all_gather(cross_key, SEQ, axis=1, tiled=True),
            lax.all_gather(cross_value, SEQ, axis=1, tiled=True),
            lax.all_gather(delta_shift, SEQ, axis=1, tiled=True),
        ),
        jnp.int32(0),
    )
    cross_query_grad = scaled_grad(cross_query_total, tau_scale)
    cross_key_update = key_grad_update(
        split_heads(cross_key),
        split_heads(cross_value),
        enc_shift,
        tau_scale,
        enc_pos,
        False,
        dec_rows,
    )
    cross_key_start = (
        jnp.zeros((item_count, HEADS, enc_rows, head_size), jnp.float32),
        jnp.zeros((item_count, HEADS, enc_rows, head_size), jnp.float32),
    )
    cross_key_total, cross_value_total = cross_key_update(
        cross_key_start,
        (
            lax.all_gather(cross_query.astype(jnp.float32), SEQ, axis=1, tiled=True),
            lax.all_gather(cross_mixed_grad.astype(jnp.float32), SEQ, axis=1, tiled=True),
            lax.all_gather(cross_log, SEQ, axis=1, tiled=True),
            lax.all_gather(cross_dot, SEQ, axis=1, tiled=True),
        ),
        jnp.int32(0),
    )
    cross_key_grad = scaled_grad(cross_key_total, tau_scale)
    cross_value_grad = merge_heads(cross_value_total).astype(jnp.bfloat16)
    cross_qkv_grad = jnp.stack(
        [
            weight_grad(cross_hidden, cross_query_grad),
            weight_grad(memory, cross_key_grad),
            weight_grad(memory, cross_value_grad),
        ]
    )
    memory_grad = project_back(cross_key_grad, cross_qkv[1]) + project_back(
        cross_value_grad, cross_qkv[2]
    )
    first_grad, dec_gain_one, dec_bias_one = norm_backward(
        dec_first_in,
        dec_gain[0],
        dec_bias[7],
        second_grad + project_back(cross_query_grad, cross_qkv[0]),
    )
    self_branch_grad = first_grad.astype(jnp.bfloat16)
    dec_out_grad = weight_grad(self_attended, self_branch_grad)
    self_out_bias = row_total(self_branch_grad)
    self_mixed_grad = project_back(self_branch_grad, dec_out).astype(jnp.bfloat16)
    self_dot = row_products(self_mixed_grad, self_mixed)
    self_back = query_grad_update(
        split_heads(self_query),
        split_heads(self_mixed_grad),
        jnp.transpose(self_log, (0, 2, 1)),
        jnp.transpose(self_dot, (0, 2, 1)),
        tau_scale,
        dec_pos,
        True,
        self_unpack,
        dec_rows,
    )
    self_query_total = self_back(
        jnp.zeros((item_count, HEADS, dec_rows, head_size), jnp.float32),
        (
            lax.all_gather(self_key, SEQ, axis=1, tiled=True),
            lax.all_gather(self_value, SEQ, axis=1, tiled=True),
        ),
        jnp.int32(0),
    )
    self_query_grad = scaled_grad(self_query_total, tau_scale)
    self_key_update = key_grad_update(
        split_heads(self_key),
        split_heads(self_value),
        jnp.zeros((item_count, dec_rows), jnp.float32),
        tau_scale,
        dec_pos,
        True,
        dec_rows,
    )
    self_key_start = (
        jnp.zeros((item_count, HEADS, dec_rows, head_size), jnp.float32),
        jnp.zeros((item_count, HEADS, dec_rows, head_size), jnp.float32),
    )
    self_key_total, self_value_total = self_key_update(
        self_key_start,
        (
            lax.all_gather(self_query.astype(jnp.float32), SEQ, axis=1, tiled=True),
            lax.all_gather(self_mixed_grad.astype(jnp.float32), SEQ, axis=1, tiled=True),
            lax.all_gather(self_log, SEQ, axis=1, tiled=True),
            lax.all_gather(self_dot, SEQ, axis=1, tiled=True),
        ),
        jnp.int32(0),
    )
    self_key_grad = scaled_grad(self_key_total, tau_scale)
    self_value_grad = merge_heads(self_value_total).astype(jnp.bfloat16)
    dec_qkv_grad = jnp.stack(
        [
            weight_grad(dec_in, self_query_grad),
            weight_grad(dec_in, self_key_grad),
            weight_grad(dec_in, self_value_grad),
        ]
    )
    dec_in_grad = (
        first_grad
        + project_back(self_query_grad, dec_qkv[0])
        + project_back(self_key_grad, dec_qkv[1])
        + project_back(self_value_grad, dec_qkv[2])
    )
    enc_second_grad, enc_gain_two, enc_bias_two = norm_backward(
        enc_second_in, enc_gain[1], enc_bias[4], memory_grad
    )
    from_enc_ff, enc_ff_in_grad, enc_ff_bias_grad, enc_ff_out_grad, enc_ff_out_bias = (
        feed_forward_back(
            enc_second_grad, enc_ff_hidden, enc_ff_pre, enc_ff_act, enc_ff_in, enc_ff_out
        )
    )
    enc_first_grad, enc_gain_one, enc_bias_one = norm_backward(
        enc_first_in, enc_gain[0], enc_bias[3], enc_second_grad + from_enc_ff
    )
    enc_branch_grad = enc_first_grad.astype(jnp.bfloat16)
    enc_out_grad = weight_grad(enc_attended, enc_branch_grad)
    enc_out_bias = row_total(enc_branch_grad)
    enc_mixed_grad = project_back(enc_branch_grad, enc_out).astype(jnp.bfloat16)
    enc_dot = row_products(enc_mixed_grad, enc_mixed)
    enc_back = query_grad_update(
        split_heads(enc_query),
        split_heads(enc_mixed_grad),
        jnp.transpose(enc_log, (0, 2, 1)),
        jnp.transpose(enc_dot, (0, 2, 1)),
        tau_scale,
        enc_pos,
        False,
        plain_unpack,
        enc_rows,
    )
    enc_query_total = enc_back(
        jnp.zeros((item_count, HEADS, enc_rows, head_size), jnp.float32),
        (
            lax.all_gather(enc_key, SEQ, axis=1, tiled=True),
            lax.all_gather(enc_value, SEQ, axis=1, tiled=True),
            lax.all_gather(delta_shift, SEQ, axis=1, tiled=True),
        ),
        jnp.int32(0),
    )
    enc_query_grad = scaled_grad(enc_query_total, tau_scale)
    enc_key_update = key_grad_update(
        split_heads(enc_key), split_heads(enc_value), enc_shift, tau_scale, enc_pos, False, enc_rows
    )
    enc_key_start = (
        jnp.zeros((item_count, HEADS, enc_rows, head_size), jnp.float32),
        jnp.zeros((item_count, HEADS, enc_rows, head_size), jnp.float32),
    )
    enc_key_total, enc_value_total = enc_key_update(
        enc_key_start,
        (
            lax.all_gather(enc_query.astype(jnp.float32), SEQ, axis=1, tiled=True),
            lax.all_gather(enc_mixed_grad.astype(jnp.float32), SEQ, axis=1, tiled=True),
            lax.all_gather(enc_log, SEQ, axis=1, tiled=True),
            lax.all_gather(enc_dot, SEQ, axis=1, tiled=True),
        ),
        jnp.int32(0),
    )
    enc_key_grad = scaled_grad(enc_key_total, tau_scale)
    enc_value_grad = merge_heads(enc_value_total).astype(jnp.bfloat16)
    enc_qkv_grad = jnp.stack(
        [
            weight_grad(enc_hidden, enc_query_grad),
            weight_grad(enc_hidden, enc_key_grad),
            weight_grad(enc_hidden, enc_value_grad),
        ]
    )
    enc_in_grad = (
        enc_first_grad
        + project_back(enc_query_grad, enc_qkv[0])
        + project_back(enc_key_grad, enc_qkv[1])
        + project_back(enc_value_grad, enc_qkv[2])
    )
    embed_grad = weight_grad(masked_series, enc_in_grad.astype(jnp.bfloat16))
    enc_query_bias_grad = row_total(enc_query_grad)
    enc_bias_grad = jnp.stack(
        [row_total(enc_value_grad), enc_out_bias, enc_ff_out_bias, enc_bias_one, enc_bias_two]
    )
    enc_gain_grad = jnp.stack([enc_gain_one, enc_gain_two])
    dec_bias_grad = jnp.stack(
        [
            row_total(self_query_grad),
            row_total(self_value_grad),
            self_out_bias,
            row_total(cross_query_grad),
            row_total(cross_value_grad),
            cross_out_bias,
            dec_ff_out_bias,
            dec_bias_one,
            dec_bias_two,
            dec_bias_three,
        ]
    )
    dec_gain_grad = jnp.stack([dec_gain_one, dec_gain_two, dec_gain_three])
    ff_bias_grad = jnp.stack([enc_ff_bias_grad, dec_ff_bias_grad])
    shares = (
        lax.psum_scatter(embed_grad, SEQ, scatter_dimension=1, tiled=True),
        lax.psum_scatter(enc_qkv_grad, SEQ, scatter_dimension=2, tiled=True),
        lax.psum_scatter(enc_out_grad, SEQ, scatter_dimension=1, tiled=True),
        lax.psum_scatter(enc_ff_in_grad, SEQ, scatter_dimension=1, tiled=True),
        lax.psum_scatter(enc_ff_out_grad, SEQ, scatter_dimension=1, tiled=True),
        lax.psum_scatter(enc_query_bias_grad, SEQ, scatter_dimension=0, tiled=True),
        lax.psum_scatter(enc_bias_grad, SEQ, scatter_dimension=1, tiled=True),
        lax.psum_scatter(enc_gain_grad, SEQ, scatter_dimension=1, tiled=True),
        lax.psum_scatter(dec_qkv_grad, SEQ, scatter_dimension=2, tiled=True),
        lax.psum_scatter(dec_out_grad, SEQ, scatter_dimension=1, tiled=True),
        lax.psum_scatter(cross_qkv_grad, SEQ, scatter_dimension=2, tiled=True),
        lax.psum_scatter(cross_out_grad, SEQ, scatter_dimension=1, tiled=True),
        lax.psum_scatter(dec_ff_in_grad, SEQ, scatter_dimension=1, tiled=True),
        lax.psum_scatter(dec_ff_out_grad, SEQ, scatter_dimension=1, tiled=True),
        lax.psum_scatter(dec_bias_grad, SEQ, scatter_dimension=1, tiled=True),
        lax.psum_scatter(dec_gain_grad, SEQ, scatter_dimension=1, tiled=True),
        lax.psum_scatter(ff_bias_grad, SEQ, scatter_dimension=1, tiled=True),
    )
    summed = lax.psum(
        (
            shares[0],
            shares[1],
            shares[2],
            shares[3],
            shares[4],
            shares[5],
            shares[6],
            shares[7],
            shares[8],
            shares[9],
            shares[10],
            shares[11],
            shares[12],
            shares[13],
            shares[14],
            shares[15],
            shares[16],
        ),
        BATCH,
    )
    return (
        decoded.astype(jnp.bfloat16),
        enc_in_grad,
        dec_in_grad,
        summed[0],
        summed[1],
        summed[2],
        summed[3],
        summed[4],
        summed[5],
        summed[6],
        summed[7],
        summed[8],
        summed[9],
        summed[10],
        summed[11],
        summed[12],
        summed[13],
        summed[14],
        summed[15],
        summed[16],
    )


F32 = jnp.float32
BF16 = jnp.bfloat16
MESH = pl.DeviceIdType.MESH
QUAD = 4
HALVES = 2
CORES = 2
LANES = 128
LINK_COUNT = 320
VMEM_BYTES = 60 << 20
LOAD_ORDER = (
    "value_embed",
    "enc_qkv",
    "dec_qkv",
    "enc_out",
    "enc_ff_in",
    "enc_ff_out",
    "dec_out",
    "cross_qkv",
    "cross_out",
    "dec_ff_in",
    "dec_ff_out",
)


def mm(left, right):
    return jnp.dot(left, right, preferred_element_type=F32)


def mm_right_t(left, right):
    return lax.dot_general(left, right, (((1,), (1,)), ((), ())), preferred_element_type=F32)


def mm_left_t(left, right):
    return lax.dot_general(left, right, (((0,), (0,)), ((), ())), preferred_element_type=F32)


def lane_index(shape):
    return lax.broadcasted_iota(jnp.int32, shape, len(shape) - 1)


def swap_halves(values):
    return pltpu.roll(values, LANES // 2, axis=1)


def low_lanes(first, second):
    return jnp.where(lane_index(first.shape) < LANES // 2, first, second)


def pack_rows(values):
    half = values.shape[0] // 2
    packed = []
    for pair in range(values.shape[1] // LANES):
        group = values[:, pair * LANES : (pair + 1) * LANES]
        top, bottom = group[:half], group[half:]
        packed.append(low_lanes(top, swap_halves(bottom)))
        packed.append(low_lanes(swap_halves(top), bottom))
    return packed


def unpack_rows(packed):
    groups = []
    for pair in range(len(packed) // 2):
        first, second = packed[2 * pair], packed[2 * pair + 1]
        top = low_lanes(first, swap_halves(second))
        bottom = low_lanes(swap_halves(first), second)
        groups.append(jnp.concatenate([top, bottom], axis=0))
    return jnp.concatenate(groups, axis=1)


def pack_pairs(keys, values):
    packed = []
    for pair in range(keys.shape[1] // LANES):
        key_group = keys[:, pair * LANES : (pair + 1) * LANES]
        value_group = values[:, pair * LANES : (pair + 1) * LANES]
        packed.append(low_lanes(key_group, swap_halves(value_group)))
        packed.append(low_lanes(swap_halves(key_group), value_group))
    return packed


def unpack_pairs(packed):
    keys, values = [], []
    for pair in range(len(packed) // 2):
        first, second = packed[2 * pair], packed[2 * pair + 1]
        keys.append(low_lanes(first, swap_halves(second)))
        values.append(low_lanes(swap_halves(first), second))
    return jnp.concatenate(keys, axis=1), jnp.concatenate(values, axis=1)


def norm_forward(values, gain, shift):
    centred = values - jnp.mean(values, axis=-1, keepdims=True)
    scale = lax.rsqrt(jnp.mean(centred * centred, axis=-1, keepdims=True) + epsilon)
    unit = centred * scale
    return unit * gain + shift, unit, scale


def norm_back(upstream, unit, scale, gain):
    inner = upstream * gain
    result = scale * (
        inner
        - jnp.mean(inner, axis=-1, keepdims=True)
        - unit * jnp.mean(inner * unit, axis=-1, keepdims=True)
    )
    return (
        result,
        jnp.sum(upstream * unit, axis=0, keepdims=True),
        jnp.sum(upstream, axis=0, keepdims=True),
    )


def rounded(values):
    return values.astype(BF16).astype(F32)


class View:
    def __init__(self, entries):
        for name, entry in entries.items():
            if isinstance(entry, dict):
                entry = View(entry)
            elif isinstance(entry, (list, tuple)):
                entry = [View(part) if isinstance(part, dict) else part for part in entry]
            setattr(self, name, entry)


class Weight:
    def __init__(self, copy, held):
        self.copy, self.held, self.here = copy, held, False
        copy.start()

    def __call__(self):
        if not self.here:
            self.copy.wait()
            self.here = True
        return self.held


def fused_body(structures, *refs):
    entries = {}
    for structure in structures:
        count = structure.num_leaves
        entries.update(jax.tree.unflatten(structure, refs[:count]))
        refs = refs[count:]
    ref = View(entries)
    rows, width = ref.enc_in.shape
    hidden, channels, chips = ref.ff_bias.shape[1], ref.series.shape[1], HEADS
    packed_rows = rows // 2
    keys_total = chips * CORES * rows
    block_queries = chips * packed_rows
    column = width // (chips * CORES)
    depth = chips * CORES // QUAD

    place = lax.axis_index(SEQ)
    item = lax.axis_index(BATCH)
    core = lax.rem(place, 2)
    chip = place // 2
    x_place = lax.rem(chip, 2)
    z_place = chip // 2
    quad = lax.rem(place, QUAD)
    core_dev = (chip * 2 + (1 - core), item)
    x_dev = (z_place * QUAD + (1 - x_place) * 2 + core, item)
    diagonal_dev = (z_place * QUAD + (1 - x_place) * 2 + (1 - core), item)
    item_dev = (place, 1 - item)
    x_quad = (1 - x_place) * 2 + core

    def same_core(step):
        peer = lax.rem(chip + step, chips)
        return peer, (peer * 2 + core, item)

    def z_peer(step):
        peer = lax.rem(z_place + step, depth)
        return peer, (peer * QUAD + quad, item)

    barrier = pltpu.get_barrier_semaphore()
    greeted = [core_dev, diagonal_dev, item_dev] + [same_core(step)[1] for step in range(1, chips)]
    for device in greeted:
        pl.semaphore_signal(barrier, inc=1, device_id=device, device_id_type=MESH)

    loaded = {}
    for index, name in enumerate(LOAD_ORDER):
        source, target = getattr(ref.weight, name), getattr(ref.held, name)
        copy = pltpu.make_async_copy(source, target, ref.load_sem.at[index])
        loaded[name] = Weight(copy, target)
    weight = View(loaded)

    sends = []

    def send(source, target, device):
        index = len(sends)
        copy = pltpu.make_async_remote_copy(
            src_ref=source,
            dst_ref=target,
            send_sem=ref.send_sem.at[index],
            recv_sem=ref.recv_sem.at[index],
            device_id=device,
            device_id_type=MESH,
        )
        copy.start()
        sends.append(copy)
        return copy

    def arrive(copies):
        for copy in copies:
            copy.wait_recv()

    def spread(source, target_at):
        copies = []
        for step in range(1, chips):
            peer, device = same_core(step)
            copies.append(send(source.at[peer], target_at(chip), device))
        return copies

    def share(block):
        return [
            block,
            send(block.at[quad], block.at[quad], core_dev),
            send(block.at[quad], block.at[quad], x_dev),
        ]

    def relay(shared):
        block = shared[0]
        shared[2].wait_recv()
        shared.append(send(block.at[x_quad], block.at[x_quad], core_dev))

    def settle(shared):
        shared[1].wait_recv()
        shared[3].wait_recv()

    def gathered(block):
        value = block[...]
        return value.reshape(value.shape[0] * value.shape[1], value.shape[2])

    def cut_columns(values, group, start):
        part = lane_index((rows, LANES)) // column
        for member in range(QUAD):
            total = None
            for level in range(depth):
                cut = values[:, level * LANES : (level + 1) * LANES]
                shift = (column * (level - member)) % LANES
                moved = pltpu.roll(cut, shift, axis=1) if shift else cut
                total = moved if total is None else jnp.where(part == level, moved, total)
            group.cut[member, :, start : start + LANES] = total.astype(BF16)

    def share_columns(group, start, stop):
        source, target = group.cut, group.met
        target[quad, :, start:stop] = source[quad, :, start:stop]
        copies = []
        for device, member in (
            (core_dev, x_place * 2 + 1 - core),
            (x_dev, x_quad),
            (diagonal_dev, (1 - x_place) * 2 + 1 - core),
        ):
            copies.append(
                send(
                    source.at[member, :, pl.ds(start, stop - start)],
                    target.at[quad, :, pl.ds(start, stop - start)],
                    device,
                )
            )
        return copies

    def columns_of(group, start, stop):
        value = group.met[:, :, start:stop]
        return value.reshape(QUAD * rows, stop - start)

    def put_rows(target, level, start, values):
        half = target.shape[2]
        count = values.shape[0]
        done = 0
        while done < count:
            which, offset = divmod(start + done, half)
            take = min(count - done, half - offset)
            target[which, level, offset : offset + take, :] = values[done : done + take, :]
            done += take

    def put_gradient(target, start, gradient):
        count = gradient.shape[0] // depth
        gradient = gradient.astype(BF16)
        short = -gradient.shape[1] % width
        pieces = gradient.shape[1] // width
        for level in range(depth):
            block = gradient[level * count : (level + 1) * count]
            for piece in range(pieces):
                put_rows(
                    target,
                    level,
                    start + piece * count,
                    block[:, piece * width : (piece + 1) * width],
                )
            if short:
                tail = jnp.concatenate(
                    [block[:, pieces * width :], jnp.zeros((count, short), BF16)], axis=1
                )
                put_rows(target, level, start + pieces * count, tail)

    def reduce_item(group):
        part, arrived = group.part, group.item
        return [send(part.at[1 - item], arrived, item_dev)]

    def reduce_depth(group):
        part, arrived = group.part, group.item
        total, landing = group.half, group.depth
        total[...] = (part[item].astype(F32) + arrived[...].astype(F32)).astype(BF16)
        copies = []
        for step in range(1, depth):
            peer, device = z_peer(step)
            copies.append(send(total.at[peer], landing.at[step - 1], device))
        return copies

    def reduce_last(group):
        total, landing = group.half, group.depth
        result = group.sum
        value = total[z_place].astype(F32)
        for step in range(1, depth):
            value = value + landing[step - 1].astype(F32)
        result[item] = value.astype(BF16)
        return [send(result.at[item], result.at[item], item_dev)]

    def set_vector(row, value):
        ref.vec[row : row + 1, :] = value

    att_enc, att_self, att_cross = ref.attention
    one, two, three = ref.group
    for group, result in zip(ref.group, ref.sums):
        group.sum = result
    enc_ff = (weight.enc_ff_in, weight.enc_ff_out)
    dec_ff = (weight.dec_ff_in, weight.dec_ff_out)

    tau = ref.tau_scale[0]
    group_row = lax.broadcasted_iota(jnp.int32, ref.channel_mask.shape, 0)
    chosen = jnp.where(
        group_row == ref.item_group[0], ref.channel_mask[...].astype(F32), 0.0
    )
    channel_row = jnp.sum(chosen, axis=0, keepdims=True)
    masked = (ref.series[...].astype(F32) * channel_row).astype(BF16)
    ref.x_series[quad] = jnp.zeros(ref.x_series.shape[1:], BF16)
    ref.x_series[quad, :, 0:channels] = masked

    shift_row = ref.delta_shift[...].astype(F32)
    ref.t_shift[...] = jnp.broadcast_to(
        jnp.concatenate([shift_row, shift_row], axis=1), ref.t_shift.shape
    )

    embedded = ref.enc_in[...].astype(F32) + mm(masked, weight.value_embed()[...])
    ref.embedded[...] = embedded
    enc_hidden = embedded.astype(BF16)
    ref.x_enc_hidden[quad] = enc_hidden

    def send_queries(own, query):
        for head, packed in enumerate(pack_rows(query)):
            own.t_query[head] = packed.astype(BF16)
        own.query[chip] = own.t_query[chip]
        return spread(own.t_query, lambda at: own.query.at[at])

    def send_pairs(own, keys, values):
        for head, packed in enumerate(pack_pairs(keys, values)):
            own.t_pair[head] = packed.astype(BF16)
        own.pair[chip, core] = own.t_pair[chip]
        return spread(own.t_pair, lambda at: own.pair.at[at, core])

    def pass_on(own):
        block = own.pair
        return [send(block.at[:, core], block.at[:, core], core_dev)]

    qkv = weight.enc_qkv()
    enc_query = mm(enc_hidden, qkv[0]) + ref.enc_query_bias[...]
    enc_key = mm(enc_hidden, qkv[1])
    enc_value = mm(enc_hidden, qkv[2]) + ref.enc_bias[0:1, :]
    pl.semaphore_wait(barrier, len(greeted))
    go_enc_pair = send_pairs(att_enc, enc_key, enc_value)
    go_enc_query = send_queries(att_enc, enc_query)
    ref.shift[chip, core] = ref.t_shift[...]
    go_shift = []
    for step in range(1, chips):
        go_shift.append(
            send(ref.t_shift, ref.shift.at[chip, core], same_core(step)[1])
        )

    dec_hidden = ref.dec_in[...]
    ref.x_dec_in[quad] = dec_hidden
    qkv = weight.dec_qkv()
    self_query = mm(dec_hidden, qkv[0]) + ref.dec_bias[0:1, :]
    self_key = mm(dec_hidden, qkv[1])
    self_value = mm(dec_hidden, qkv[2]) + ref.dec_bias[1:2, :]
    go_self_pair = send_pairs(att_self, self_key, self_value)
    go_self_query = send_queries(att_self, self_query)

    def attention(own, shifted, causal):
        pairs = own.pair[...].reshape(keys_total, LANES)
        pairs_t = pairs.T
        own.pair_t[...] = pairs_t
        query_t = own.query[...].reshape(block_queries, LANES).astype(F32).T
        zeros = jnp.zeros((LANES // 2, block_queries), F32)
        for half in range(HALVES):
            part = query_t[half * LANES // 2 : (half + 1) * LANES // 2]
            side = jnp.concatenate([part, zeros], axis=0).astype(BF16)
            scores = mm(pairs, side) * (tau * 0.125)
            if shifted:
                moved = ref.shift_columns[...]
                scores = scores + jnp.concatenate([moved] * (block_queries // LANES), axis=1)
            if causal:
                key_at = lax.broadcasted_iota(jnp.int32, scores.shape, 0)
                lane = lane_index(scores.shape)
                query_at = (
                    (lane // packed_rows * 2 + core) * rows
                    + half * packed_rows
                    + lane % packed_rows
                )
                scores = jnp.where(key_at > query_at, masked_score, scores)
            weights = jnp.exp(scores - jnp.max(scores, axis=0, keepdims=True))
            inverse = 1.0 / jnp.sum(weights, axis=0, keepdims=True)
            low_weights = weights.astype(BF16)
            own.weights[half] = low_weights
            own.inverse[half] = jnp.broadcast_to(inverse, (8, block_queries))
            mixed_t = mm(pairs_t, low_weights)[LANES // 2 :] * inverse
            own.mixed_t[half * LANES // 2 : (half + 1) * LANES // 2, :] = mixed_t
        mixed = own.mixed_t[...].T.astype(BF16)
        own.t_mixed[...] = mixed.reshape(chips, packed_rows, LANES)
        own.mixed[chip] = own.t_mixed[chip]
        return spread(own.t_mixed, lambda at: own.mixed.at[at])

    def mixed_rows(own):
        return unpack_rows(
            [own.mixed[head].astype(F32) for head in range(chips)]
        ).astype(BF16)

    arrive(go_enc_pair)
    on_enc = pass_on(att_enc)
    arrive(go_shift)
    on_shift = [send(ref.shift.at[:, core], ref.shift.at[:, core], core_dev)]
    arrive(go_enc_query)
    arrive(go_self_pair)
    on_self = pass_on(att_self)
    arrive(on_shift)
    for block in range(chips):
        line = low_lanes(ref.shift[block, 0], ref.shift[block, 1])[0:1, :] * 0.125
        ref.shift_columns[block * LANES : (block + 1) * LANES, :] = jnp.broadcast_to(
            line, (LANES, LANES)
        ).T
    arrive(on_enc)
    back_enc = attention(att_enc, True, False)
    arrive(on_self)
    arrive(go_self_query)
    back_self = attention(att_self, False, True)
    shares = [share(ref.x_series), share(ref.x_enc_hidden), share(ref.x_dec_in)]

    def feed_forward(values, weights, bias_row, out_bias, side):
        low = values.astype(BF16)
        side.hidden[quad] = low
        weight_in, weight_out = weights[0](), weights[1]()
        total = out_bias
        for piece in range(hidden // width):
            cut = slice(piece * width, (piece + 1) * width)
            pre = mm(low, weight_in[:, cut]) + ref.ff_bias[bias_row : bias_row + 1, cut]
            normal = 0.5 * (1.0 + lax.erf(pre * 0.7071067811865476))
            act = (pre * normal).astype(BF16)
            side.slope[:, cut] = normal + pre * (
                jnp.exp(pre * pre * -0.5) * 0.3989422804014327
            )
            side.act[quad, :, cut] = act
            total = total + mm(act, weight_out[cut, :])
        return total

    def feed_forward_back(upstream, weights, side, vector_row, group):
        low = upstream.astype(BF16)
        weight_in, weight_out = weights[0](), weights[1]()
        total = None
        for piece in range(hidden // width):
            cut = slice(piece * width, (piece + 1) * width)
            act_grad = mm_right_t(low, weight_out[cut, :])
            pre_grad = (act_grad * side.slope[:, cut]).astype(BF16)
            set_vector(
                vector_row + piece, jnp.sum(pre_grad.astype(F32), axis=0, keepdims=True)
            )
            for member in range(QUAD):
                at = piece * LANES
                group.cut[member, :, at : at + LANES] = pre_grad[
                    :, member * LANES : (member + 1) * LANES
                ]
            more = mm_right_t(pre_grad, weight_in[:, cut])
            total = more if total is None else total + more
        return total

    def save_norm(index, unit, scale):
        ref.unit[index] = unit
        ref.scale[index] = jnp.broadcast_to(scale, (rows, LANES))

    def saved_norm(index):
        return ref.unit[index], ref.scale[index, :, 0:1]

    arrive(back_enc)
    attended = mixed_rows(att_enc)
    ref.x_enc_mixed[quad] = attended
    first, unit, scale = norm_forward(
        embedded + mm(attended, weight.enc_out()[...]) + ref.enc_bias[1:2, :],
        ref.enc_gain[0:1, :],
        ref.enc_bias[3:4, :],
    )
    save_norm(0, unit, scale)
    second, unit, scale = norm_forward(
        first + feed_forward(first, enc_ff, 0, ref.enc_bias[2:3, :], ref.enc_ff),
        ref.enc_gain[1:2, :],
        ref.enc_bias[4:5, :],
    )
    save_norm(1, unit, scale)
    memory = second.astype(BF16)
    ref.x_memory[quad] = memory
    qkv = weight.cross_qkv()
    cross_key = mm(memory, qkv[1])
    cross_value = mm(memory, qkv[2]) + ref.dec_bias[4:5, :]
    go_cross_pair = send_pairs(att_cross, cross_key, cross_value)

    arrive(back_self)
    attended = mixed_rows(att_self)
    ref.x_self_mixed[quad] = attended
    first, unit, scale = norm_forward(
        ref.dec_in[...].astype(F32)
        + mm(attended, weight.dec_out()[...])
        + ref.dec_bias[2:3, :],
        ref.dec_gain[0:1, :],
        ref.dec_bias[7:8, :],
    )
    save_norm(2, unit, scale)
    ref.first_dec[...] = first
    low = first.astype(BF16)
    ref.x_cross_hidden[quad] = low
    go_cross_query = send_queries(att_cross, mm(low, qkv[0]) + ref.dec_bias[3:4, :])
    for shared in shares:
        relay(shared)
    shares_two = [
        share(block)
        for block in (
            ref.x_enc_mixed,
            ref.enc_ff.hidden,
            ref.x_memory,
            ref.x_self_mixed,
            ref.x_cross_hidden,
        )
    ]

    arrive(go_cross_pair)
    on_cross = pass_on(att_cross)
    arrive(go_cross_query)
    arrive(on_cross)
    back_cross = attention(att_cross, True, False)
    for shared in shares_two:
        relay(shared)
    shares_three = [share(ref.enc_ff.act)]
    arrive(back_cross)
    attended = mixed_rows(att_cross)
    ref.x_cross_mixed[quad] = attended
    second, unit, scale = norm_forward(
        ref.first_dec[...]
        + mm(attended, weight.cross_out()[...])
        + ref.dec_bias[5:6, :],
        ref.dec_gain[1:2, :],
        ref.dec_bias[8:9, :],
    )
    save_norm(3, unit, scale)

    third, unit, scale = norm_forward(
        second + feed_forward(second, dec_ff, 1, ref.dec_bias[6:7, :], ref.dec_ff),
        ref.dec_gain[2:3, :],
        ref.dec_bias[9:10, :],
    )
    ref.dec_result[...] = third.astype(BF16)

    def norm_step(index, upstream, gain, gain_row, gain_vector, shift_vector):
        unit, scale = saved_norm(index)
        result, gain_grad, shift_grad = norm_back(
            upstream, unit, scale, gain[gain_row : gain_row + 1, :]
        )
        set_vector(gain_vector, gain_grad)
        set_vector(shift_vector, shift_grad)
        return result

    def column_sum(values):
        return jnp.sum(rounded(values), axis=0, keepdims=True)

    third_grad, gain_grad, shift_grad = norm_back(
        ref.cotangent[...].astype(F32), unit, scale, ref.dec_gain[2:3, :]
    )
    set_vector(20, gain_grad)
    set_vector(17, shift_grad)
    from_ff = feed_forward_back(third_grad, dec_ff, ref.dec_ff, 25, one)
    second_grad = norm_step(3, third_grad + from_ff, ref.dec_gain, 1, 19, 16)
    ref.second_grad[...] = second_grad

    def send_mixed_grad(own, branch_grad, out_weight):
        mixed_grad = mm_right_t(branch_grad.astype(BF16), out_weight[...])
        for head, packed in enumerate(pack_rows(mixed_grad)):
            own.t_grad[head] = packed.astype(BF16)
        own.grad[chip] = own.t_grad[chip]
        return spread(own.t_grad, lambda at: own.grad.at[at])

    go_cross_grad = send_mixed_grad(att_cross, second_grad, weight.cross_out())
    cut_columns(third_grad, one, hidden // QUAD)
    cut_columns(second_grad, one, hidden // QUAD + LANES)
    set_vector(14, column_sum(third_grad))
    set_vector(13, column_sum(second_grad))
    columns_one = share_columns(one, 0, hidden // QUAD + 2 * LANES)
    for shared in shares_three:
        relay(shared)
    shares_four = [share(block) for block in (ref.x_cross_mixed, ref.dec_ff.hidden, ref.dec_ff.act)]

    def attention_back(own):
        pairs = own.pair[...].reshape(keys_total, LANES)
        pairs_t = own.pair_t[...]
        queries = own.query[...].reshape(block_queries, LANES).astype(F32)
        grads = own.grad[...].reshape(block_queries, LANES).astype(F32)
        grads_t = grads.T
        zeros = jnp.zeros((LANES // 2, block_queries), F32)
        blank = jnp.zeros_like(queries)
        query_grads = []
        key_total = value_total = None
        for half in range(HALVES):
            cut = slice(half * LANES // 2, (half + 1) * LANES // 2)
            grad_t = grads_t[cut]
            row_dot = jnp.sum(grad_t * own.mixed_t[cut, :], axis=0, keepdims=True)
            side = jnp.concatenate([zeros, grad_t], axis=0).astype(BF16)
            prob_grads = mm(pairs, side)
            probabilities = own.weights[half].astype(F32) * own.inverse[half, 0:1, :]
            score_grads = (probabilities * (prob_grads - row_dot)).astype(BF16)
            query_grads.append(mm(pairs_t, score_grads)[: LANES // 2])
            if half == 0:
                query_side = low_lanes(queries, blank)
                grad_side = low_lanes(blank, swap_halves(grads))
            else:
                query_side = low_lanes(swap_halves(queries), blank)
                grad_side = low_lanes(blank, grads)
            key_part = mm(score_grads, query_side.astype(BF16))
            value_part = mm(probabilities.astype(BF16), grad_side.astype(BF16))
            key_total = key_part if key_total is None else key_total + key_part
            value_total = value_part if value_total is None else value_total + value_part
        factor = tau * 0.125
        query_grad = (jnp.concatenate(query_grads, axis=0) * factor).T.astype(BF16)
        own.t_query_grad[...] = query_grad.reshape(chips, packed_rows, LANES)
        own.query_grad[chip] = own.t_query_grad[chip]
        go_query = spread(
            own.t_query_grad, lambda at: own.query_grad.at[at]
        )
        pair_grad = (key_total * factor + value_total).reshape(chips, CORES, rows, LANES)
        for which in range(CORES):
            ref.pair_sum[which] = pair_grad[:, which]
            own.t_part[which] = pair_grad[:, which].astype(BF16)
        exchange = send(own.t_part.at[1 - core], own.part, core_dev)
        return go_query, exchange

    def attention_back_pairs(own, exchange):
        exchange.wait_recv()
        total = ref.pair_sum[core] + own.part[...].astype(F32)
        own.t_pair_grad[...] = total.astype(BF16)
        own.pair_grad[chip] = own.t_pair_grad[chip]
        return spread(own.t_pair_grad, lambda at: own.pair_grad.at[at])

    def query_grad_rows(own):
        return unpack_rows(
            [own.query_grad[head].astype(F32) for head in range(chips)]
        )

    def pair_grad_rows(own):
        return unpack_pairs([own.pair_grad[head].astype(F32) for head in range(chips)])

    arrive(go_cross_grad)
    go_query, exchange = attention_back(att_cross)
    for shared in shares_four:
        relay(shared)
    go_pair = attention_back_pairs(att_cross, exchange)

    ff_width = hidden // QUAD
    for shared in shares_four:
        settle(shared)
    arrive(columns_one)
    put_gradient(
        one.part, 0, mm_left_t(columns_of(one, 0, ff_width), gathered(ref.dec_ff.hidden))
    )
    put_gradient(
        one.part,
        LANES,
        mm_left_t(columns_of(one, ff_width, ff_width + LANES), gathered(ref.dec_ff.act)),
    )
    put_gradient(
        one.part,
        2 * LANES,
        mm_left_t(
            columns_of(one, ff_width + LANES, ff_width + 2 * LANES), gathered(ref.x_cross_mixed)
        ),
    )
    item_one = reduce_item(one)

    qkv = weight.cross_qkv()
    arrive(go_query)
    cross_query_grad = query_grad_rows(att_cross)
    first_grad = norm_step(
        2,
        ref.second_grad[...] + mm_right_t(cross_query_grad.astype(BF16), qkv[0]),
        ref.dec_gain,
        0,
        18,
        15,
    )
    ref.first_grad[...] = first_grad
    go_self_grad = send_mixed_grad(att_self, first_grad, weight.dec_out())
    set_vector(10, column_sum(first_grad))

    arrive(go_pair)
    cross_key_grad, cross_value_grad = pair_grad_rows(att_cross)
    memory_grad = mm_right_t(cross_key_grad.astype(BF16), qkv[1]) + mm_right_t(
        cross_value_grad.astype(BF16), qkv[2]
    )
    enc_second_grad = norm_step(1, memory_grad, ref.enc_gain, 1, 7, 5)
    from_ff = feed_forward_back(enc_second_grad, enc_ff, ref.enc_ff, 21, two)
    enc_first_grad = norm_step(0, enc_second_grad + from_ff, ref.enc_gain, 0, 6, 4)
    ref.enc_first_grad[...] = enc_first_grad
    go_enc_grad = send_mixed_grad(att_enc, enc_first_grad, weight.enc_out())
    set_vector(3, column_sum(enc_second_grad))
    set_vector(2, column_sum(enc_first_grad))
    set_vector(11, column_sum(cross_query_grad))
    set_vector(12, column_sum(cross_value_grad))
    for row in (0, 1, 8, 9, 29, 30, 31):
        set_vector(row, jnp.zeros((1, width), F32))
    vec_item = send(ref.vec, ref.vec_item, item_dev)
    for index, values in enumerate(
        (enc_second_grad, enc_first_grad, first_grad)
        + (cross_query_grad, cross_key_grad, cross_value_grad)
    ):
        cut_columns(values, two, ff_width + index * LANES)
    columns_two = share_columns(two, 0, ff_width + 6 * LANES)

    arrive(go_self_grad)
    go_self_query_grad, exchange = attention_back(att_self)
    arrive(item_one)
    depth_one = reduce_depth(one)
    go_self_pair_grad = attention_back_pairs(att_self, exchange)
    vec_item.wait_recv()
    ref.vec_a[...] = ref.vec[...] + ref.vec_item[...]
    vec_core = send(ref.vec_a, ref.vec_core, core_dev)
    arrive(go_enc_grad)
    go_enc_query_grad, exchange = attention_back(att_enc)
    vec_core.wait_recv()
    ref.vec_b[...] = ref.vec_a[...] + ref.vec_core[...]
    vec_x = send(ref.vec_b, ref.vec_x, x_dev)
    go_enc_pair_grad = attention_back_pairs(att_enc, exchange)

    for shared in shares + shares_two + shares_three:
        settle(shared)
    arrive(columns_two)
    put_gradient(
        two.part, 0, mm_left_t(columns_of(two, 0, ff_width), gathered(ref.enc_ff.hidden))
    )
    put_gradient(
        two.part,
        LANES,
        mm_left_t(columns_of(two, ff_width, ff_width + LANES), gathered(ref.enc_ff.act)),
    )
    for index, (block, count) in enumerate(
        ((ref.x_enc_mixed, 1), (ref.x_self_mixed, 1), (ref.x_cross_hidden, 1), (ref.x_memory, 2))
    ):
        start = ff_width + (index + 1) * LANES
        gradient = mm_left_t(columns_of(two, start, start + count * LANES), gathered(block))
        for which in range(count):
            put_gradient(
                two.part,
                2 * LANES + (index + which) * column,
                gradient[which * LANES : (which + 1) * LANES],
            )
    item_two = reduce_item(two)
    vec_x.wait_recv()
    ref.vec_c[...] = ref.vec_b[...] + ref.vec_x[...]
    vec_depth = [
        send(ref.vec_c, ref.vec_depth.at[step - 1], z_peer(step)[1])
        for step in range(1, depth)
    ]
    arrive(depth_one)
    last_one = reduce_last(one)

    def input_grad(own, weights, first):
        query_grad = query_grad_rows(own)
        key_grad, value_grad = pair_grad_rows(own)
        total = (
            first[...]
            + mm_right_t(query_grad.astype(BF16), weights[0])
            + mm_right_t(key_grad.astype(BF16), weights[1])
            + mm_right_t(value_grad.astype(BF16), weights[2])
        )
        return total, query_grad, key_grad, value_grad

    arrive(go_self_query_grad)
    arrive(go_self_pair_grad)
    total, query_grad, key_grad, value_grad = input_grad(att_self, weight.dec_qkv(), ref.first_grad)
    ref.dec_grad[...] = total
    for index, values in enumerate((query_grad, key_grad, value_grad)):
        cut_columns(values, three, index * LANES)
    columns_self = share_columns(three, 0, 3 * LANES)
    arrive(item_two)
    depth_two = reduce_depth(two)
    arrive(go_enc_query_grad)
    arrive(go_enc_pair_grad)
    total, query_grad, key_grad, value_grad = input_grad(att_enc, weight.enc_qkv(), ref.enc_first_grad)
    ref.enc_grad[...] = total
    for index, values in enumerate((query_grad, key_grad, value_grad, total)):
        cut_columns(values, three, (3 + index) * LANES)
    columns_enc = share_columns(three, 3 * LANES, 7 * LANES)
    arrive(columns_self)

    def gradient_three(start, count, block, row):
        gradient = mm_left_t(
            columns_of(three, start * LANES, (start + count) * LANES), gathered(block)
        )
        for which in range(count):
            put_gradient(
                three.part, row + which * column, gradient[which * LANES : (which + 1) * LANES]
            )

    gradient_three(0, 3, ref.x_dec_in, 0)
    arrive(columns_enc)
    gradient_three(3, 3, ref.x_enc_hidden, 3 * column)
    gradient_three(6, 1, ref.x_series, 6 * column)
    totals = [
        jnp.sum(
            columns_of(three, index * LANES, (index + 1) * LANES).astype(F32),
            axis=0,
            keepdims=True,
        )
        for index in (0, 2, 3, 5)
    ]
    totals = jnp.concatenate(totals + [jnp.zeros((column - 4, LANES), F32)], axis=0)
    totals = jnp.concatenate([totals, jnp.zeros((column, width - LANES), F32)], axis=1)
    for level in range(depth):
        put_rows(three.part, level, 8 * column, totals.astype(BF16))
    item_three = reduce_item(three)
    arrive(vec_depth)
    total = ref.vec_c[...]
    for step in range(1, depth):
        total = total + ref.vec_depth[step - 1]
    ref.vectors[...] = total
    arrive(depth_two)
    last_two = reduce_last(two)
    arrive(item_three)
    depth_three = reduce_depth(three)
    arrive(last_one)
    arrive(last_two)
    arrive(depth_three)
    last_three = reduce_last(three)
    arrive(last_three)
    for copy in sends:
        copy.wait_send()


def finish_body(*refs):
    (
        dec_in,
        enc_grad_in,
        dec_grad_in,
        one,
        two,
        three,
        vectors,
        dec_out,
        enc_grad,
        dec_grad,
        g_embed,
        g_enc_qkv,
        g_enc_out,
        g_enc_ff_in,
        g_enc_ff_out,
        g_enc_query_bias,
        g_enc_bias,
        g_enc_gain,
        g_dec_qkv,
        g_dec_out,
        g_cross_qkv,
        g_cross_out,
        g_dec_ff_in,
        g_dec_ff_out,
        g_dec_bias,
        g_dec_gain,
        g_ff_bias,
    ) = refs
    place = lax.axis_index(SEQ)
    column, width = g_enc_out.shape
    channels = g_embed.shape[1]
    level, member = place // QUAD, lax.rem(place, QUAD)
    dec_out[...] = dec_in[...]
    enc_grad[...] = enc_grad_in[...]
    dec_grad[...] = dec_grad_in[...]

    def whole(block):
        value = block[...]
        return value.reshape(value.shape[0] * value.shape[1], value.shape[2]).astype(F32)

    def narrow(target, block, start):
        for piece in range(target.shape[1] // width):
            target[:, piece * width : (piece + 1) * width] = block[
                start + piece * column : start + (piece + 1) * column
            ]

    first = whole(one)
    g_dec_ff_in[...] = first[0:LANES].T
    narrow(g_dec_ff_out, first, LANES)
    narrow(g_cross_out, first, 2 * LANES)
    second = whole(two)
    g_enc_ff_in[...] = second[0:LANES].T
    narrow(g_enc_ff_out, second, LANES)
    narrow(g_enc_out, second, 2 * LANES)
    narrow(g_dec_out, second, 2 * LANES + column)
    for index in range(3):
        start = 2 * LANES + (2 + index) * column
        g_cross_qkv[index] = second[start : start + column]
    third = whole(three)
    for index in range(3):
        g_dec_qkv[index] = third[index * column : (index + 1) * column]
        g_enc_qkv[index] = third[(3 + index) * column : (4 + index) * column]
    g_embed[:, 0:width] = third[6 * column : 7 * column]
    g_embed[:, width:channels] = third[7 * column : 8 * column, 0 : channels - width]

    group = vectors[:, pl.ds(pl.multiple_of(level * LANES, LANES), LANES)]
    moved = pltpu.roll(group, lax.rem(LANES - member * column, LANES), axis=1)
    rows = moved[:, 0:column]
    late = third[2 * LANES : 2 * LANES + 8, 0:LANES]
    late = pltpu.roll(late, lax.rem(LANES - level * column, LANES), axis=1)[:, 0:column]
    g_enc_query_bias[...] = late[2:3]
    g_enc_bias[...] = jnp.concatenate([late[3:4], rows[2:6]], axis=0)
    g_enc_gain[...] = rows[6:8]
    g_dec_bias[...] = jnp.concatenate([late[0:2], rows[10:18]], axis=0)
    g_dec_gain[...] = rows[18:21]
    lanes = pl.ds(pl.multiple_of(member * LANES, LANES), LANES)
    hidden_rows = vectors[:, lanes]
    row_index = lax.broadcasted_iota(jnp.int32, hidden_rows.shape, 0)
    for index in range(2):
        chosen = jnp.where(row_index == 21 + 4 * index + level, hidden_rows, 0.0)
        g_ff_bias[index : index + 1, :] = jnp.sum(chosen, axis=0, keepdims=True)


def fused_local(
    enc_in,
    series,
    channel_mask,
    item_group,
    tau_scale,
    delta_shift,
    dec_in,
    value_embed,
    enc_qkv,
    enc_out,
    enc_ff_in,
    enc_ff_out,
    enc_query_bias,
    enc_bias,
    enc_gain,
    dec_qkv,
    dec_out,
    cross_qkv,
    cross_out,
    dec_ff_in,
    dec_ff_out,
    dec_bias,
    dec_gain,
    ff_bias,
    cotangent,
):
    rows, width = enc_in.shape[1:]
    hidden = enc_ff_in.shape[1]
    channels = value_embed.shape[0]
    chips = HEADS
    column = width // (chips * CORES)
    depth = chips * CORES // QUAD
    padded = -(-channels // LANES) * LANES
    keys_total = chips * CORES * rows
    queries = chips * rows // 2
    in_smem = pl.BlockSpec(memory_space=pltpu.SMEM)
    in_vmem = pl.BlockSpec(memory_space=pltpu.VMEM)
    anywhere = pl.BlockSpec(memory_space=pl.ANY)

    weights = dict(
        value_embed=value_embed,
        enc_qkv=enc_qkv,
        enc_out=enc_out,
        enc_ff_in=enc_ff_in,
        enc_ff_out=enc_ff_out,
        dec_qkv=dec_qkv,
        dec_out=dec_out,
        cross_qkv=cross_qkv,
        cross_out=cross_out,
        dec_ff_in=dec_ff_in,
        dec_ff_out=dec_ff_out,
    )
    scalars = dict(item_group=item_group, tau_scale=tau_scale)
    blocks = dict(
        enc_in=enc_in[0],
        series=series[0],
        channel_mask=channel_mask,
        delta_shift=delta_shift,
        dec_in=dec_in[0],
        cotangent=cotangent[0],
        enc_query_bias=enc_query_bias[None],
        enc_bias=enc_bias,
        enc_gain=enc_gain,
        dec_bias=dec_bias,
        dec_gain=dec_gain,
        ff_bias=ff_bias,
    )
    inputs = (scalars, blocks, dict(weight=weights))
    in_specs = (
        [in_smem] * len(scalars) + [in_vmem] * len(blocks) + [anywhere] * len(weights)
    )

    def low(*shape):
        return pltpu.VMEM(shape, BF16)

    def full(*shape):
        return pltpu.VMEM(shape, F32)

    def exchanged(features):
        return low(QUAD, rows, features)

    def attention_space():
        packed = low(chips, rows // 2, LANES)
        paired = low(chips, rows, LANES)
        both = low(chips, CORES, rows, LANES)
        return dict(
            query=packed,
            t_query=packed,
            mixed=packed,
            t_mixed=packed,
            grad=packed,
            t_grad=packed,
            query_grad=packed,
            t_query_grad=packed,
            t_pair=paired,
            pair=both,
            t_pair_grad=paired,
            pair_grad=paired,
            t_part=low(CORES, chips, rows, LANES),
            part=paired,
            pair_t=low(LANES, keys_total),
            weights=low(HALVES, keys_total, queries),
            inverse=full(HALVES, 8, queries),
            mixed_t=full(LANES, queries),
        )

    def feed_forward_space():
        return dict(
            hidden=exchanged(width), act=exchanged(hidden), slope=full(rows, hidden)
        )

    def group_space(count, features):
        half = count // 2
        return dict(
            cut=exchanged(features),
            met=exchanged(features),
            part=low(2, depth, half, width),
            item=low(depth, half, width),
            half=low(depth, half, width),
            depth=low(depth - 1, half, width),
        )

    group_rows = (2 * LANES + column, 3 * LANES + column, 2 * LANES + column)
    group_features = (hidden // QUAD + 2 * LANES, hidden // QUAD + 6 * LANES, 7 * LANES)
    scratch = dict(
        held={name: low(*value.shape) for name, value in weights.items()},
        x_series=exchanged(padded),
        x_enc_hidden=exchanged(width),
        x_dec_in=exchanged(width),
        x_enc_mixed=exchanged(width),
        x_memory=exchanged(width),
        x_self_mixed=exchanged(width),
        x_cross_hidden=exchanged(width),
        x_cross_mixed=exchanged(width),
        enc_ff=feed_forward_space(),
        dec_ff=feed_forward_space(),
        attention=[attention_space() for index in range(3)],
        group=[group_space(*sizes) for sizes in zip(group_rows, group_features)],
        pair_sum=full(CORES, chips, rows, LANES),
        t_shift=full(8, LANES),
        shift=full(chips, CORES, 8, LANES),
        shift_columns=full(keys_total, LANES),
        embedded=full(rows, width),
        first_dec=full(rows, width),
        second_grad=full(rows, width),
        first_grad=full(rows, width),
        enc_first_grad=full(rows, width),
        unit=full(4, rows, width),
        scale=full(4, rows, LANES),
        vec=full(32, width),
        vec_item=full(32, width),
        vec_a=full(32, width),
        vec_core=full(32, width),
        vec_b=full(32, width),
        vec_x=full(32, width),
        vec_c=full(32, width),
        vec_depth=full(depth - 1, 32, width),
        load_sem=pltpu.SemaphoreType.DMA((len(weights),)),
        send_sem=pltpu.SemaphoreType.DMA((LINK_COUNT,)),
        recv_sem=pltpu.SemaphoreType.DMA((LINK_COUNT,)),
    )
    outputs = dict(
        dec_result=jax.ShapeDtypeStruct((rows, width), BF16),
        enc_grad=jax.ShapeDtypeStruct((rows, width), F32),
        dec_grad=jax.ShapeDtypeStruct((rows, width), F32),
        sums=[jax.ShapeDtypeStruct((2, count // 2, width), BF16) for count in group_rows],
        vectors=jax.ShapeDtypeStruct((32, width), F32),
    )
    out_shapes, out_structure = jax.tree.flatten(outputs)
    scratch_shapes, scratch_structure = jax.tree.flatten(scratch)
    operands = jax.tree.leaves(inputs)
    structures = [jax.tree.structure(part) for part in inputs]
    results = pl.pallas_call(
        partial(fused_body, structures + [out_structure, scratch_structure]),
        out_shape=out_shapes,
        in_specs=in_specs,
        out_specs=[in_vmem] * len(out_shapes),
        scratch_shapes=scratch_shapes,
        compiler_params=pltpu.CompilerParams(
            collective_id=1, has_side_effects=True, vmem_limit_bytes=VMEM_BYTES
        ),
        name="layers",
    )(*operands)
    results = jax.tree.unflatten(out_structure, results)
    results = [
        results[key] for key in ("dec_result", "enc_grad", "dec_grad")
    ] + results["sums"] + [results["vectors"]]

    final = [
        (rows, width),
        (rows, width),
        (rows, width),
        (column, channels),
        (3, column, width),
        (column, width),
        (width, hidden // (chips * CORES)),
        (column, hidden),
        (1, column),
        (5, column),
        (2, column),
        (3, column, width),
        (column, width),
        (3, column, width),
        (column, width),
        (width, hidden // (chips * CORES)),
        (column, hidden),
        (10, column),
        (3, column),
        (2, hidden // (chips * CORES)),
    ]
    outputs = pl.pallas_call(
        finish_body,
        out_shape=[
            jax.ShapeDtypeStruct(shape, BF16 if index == 0 else F32)
            for index, shape in enumerate(final)
        ],
        in_specs=[in_vmem] * len(results),
        out_specs=[in_vmem] * len(final),
        compiler_params=pltpu.CompilerParams(vmem_limit_bytes=VMEM_BYTES),
        name="columns",
    )(*results)
    outputs = list(outputs)
    for index in range(3):
        outputs[index] = outputs[index][None]
    outputs[8] = outputs[8][0]
    for index in (3, 4, 5, 7, 11, 12, 13, 14, 16):
        outputs[index] = jnp.swapaxes(outputs[index], -1, -2)
    return tuple(outputs)


def solution(mesh):
    in_specs = (
        P(BATCH, SEQ, None),
        P(BATCH, SEQ, None),
        P(),
        P(BATCH),
        P(BATCH),
        P(BATCH, SEQ),
        P(BATCH, SEQ, None),
        P(),
        P(),
        P(),
        P(),
        P(),
        P(),
        P(),
        P(),
        P(),
        P(),
        P(),
        P(),
        P(),
        P(),
        P(),
        P(),
        P(),
        P(BATCH, SEQ, None),
    )
    out_specs = (
        P(BATCH, SEQ, None),
        P(BATCH, SEQ, None),
        P(BATCH, SEQ, None),
        P(None, SEQ),
        P(None, None, SEQ),
        P(None, SEQ),
        P(None, SEQ),
        P(None, SEQ),
        P(SEQ),
        P(None, SEQ),
        P(None, SEQ),
        P(None, None, SEQ),
        P(None, SEQ),
        P(None, None, SEQ),
        P(None, SEQ),
        P(None, SEQ),
        P(None, SEQ),
        P(None, SEQ),
        P(None, SEQ),
        P(None, SEQ),
    )
    fits = mesh.shape[SEQ] == HEADS * CORES and mesh.shape[BATCH] == 2
    return jax.shard_map(
        fused_local if fits else local, mesh=mesh, in_specs=in_specs, out_specs=out_specs, check_vma=False)
```

```python
from functools import partial
import math

import jax
import jax.numpy as jnp
from jax import lax
from jax.experimental import pallas as pl
from jax.experimental.pallas import tpu as pltpu
from jax.sharding import PartitionSpec as P

HEADS = 8
GROUPS = 16
SEQ = "seq"
BATCH = "batch"


epsilon = 1e-05
masked_score = -1e30


def layer_norm(inputs, gain_vector, shift_vector):
    average = jnp.mean(inputs, axis=-1, keepdims=True)
    centred = inputs - average
    variance = jnp.mean(centred * centred, axis=-1, keepdims=True)
    return centred * lax.rsqrt(variance + epsilon) * gain_vector + shift_vector


def norm_backward(inputs, gain_vector, shift_vector, upstream):
    ignored, pullback = jax.vjp(layer_norm, inputs, gain_vector, shift_vector)
    return pullback(upstream)


def project(inputs, weight_matrix):
    return jnp.dot(inputs, weight_matrix, preferred_element_type=jnp.float32)


def project_back(gradient, weight_matrix):
    return jnp.einsum("ilf,kf->ilk", gradient, weight_matrix, preferred_element_type=jnp.float32)


def weight_grad(inputs, gradient):
    return jnp.einsum("ilk,ilf->kf", inputs, gradient, preferred_element_type=jnp.float32)


def row_total(gradient):
    return jnp.sum(gradient.astype(jnp.float32), axis=(0, 1))


def split_heads(values):
    return values.reshape(values.shape[:2] + (HEADS, values.shape[2] // HEADS))


def merge_heads(head_values):
    return jnp.transpose(head_values, (0, 2, 1, 3)).reshape(
        head_values.shape[0], head_values.shape[2], -1
    )


def over_blocks(update, totals, arrays, shard_rows):
    length = arrays[0].shape[1]
    block_rows = shard_rows * math.gcd(length // shard_rows, 8)
    block_count = length // block_rows
    stacked = tuple(
        (
            jnp.moveaxis(
                member.reshape((member.shape[0], block_count, block_rows) + member.shape[2:]), 1, 0
            )
            for member in arrays
        )
    )
    offsets = jnp.arange(block_count, dtype=jnp.int32) * block_rows

    def advance(running, inputs):
        return (update(running, inputs[0], inputs[1]), None)

    totals, ignored = lax.scan(advance, totals, (stacked, offsets))
    return totals


def head_scores(query_heads, key_heads, tau_value, key_shift):
    raw_scores = jnp.einsum(
        "iqhd,ikhd->ihqk", query_heads, key_heads, preferred_element_type=jnp.float32
    )
    return (tau_value[:, None, None, None] * raw_scores + key_shift[:, None, None, :]) * 0.125


def causal_mask(scores, query_pos, key_pos):
    allowed = query_pos[:, None] >= key_pos[None, :]
    return jnp.where(allowed[None, None], scores, masked_score)


def fresh_totals(item_count, row_count, head_size):
    return (
        jnp.full((item_count, HEADS, row_count), masked_score, jnp.float32),
        jnp.zeros((item_count, HEADS, row_count), jnp.float32),
        jnp.zeros((item_count, HEADS, row_count, head_size), jnp.float32),
    )


def finish_forward(totals):
    running_max, running_sum, weighted = totals
    output = merge_heads(weighted / running_sum[..., None])
    log_total = jnp.transpose(running_max + jnp.log(running_sum), (0, 2, 1))
    return (output, log_total)


def row_products(grad_rows, mixed_rows):
    return jnp.sum(split_heads(grad_rows).astype(jnp.float32) * split_heads(mixed_rows), axis=-1)


def scaled_grad(head_totals, tau_value):
    return merge_heads(head_totals * (tau_value * 0.125)[:, None, None, None]).astype(jnp.bfloat16)


def plain_unpack(fetched):
    return (fetched[0], fetched[1], fetched[2].astype(jnp.float32))


def self_unpack(fetched):
    return (fetched[0], fetched[1], jnp.zeros(fetched[0].shape[:2], jnp.float32))


def forward_update(query_heads, tau_value, query_pos, causal, unpack, shard_rows):

    def update(totals, fetched, offset):

        def block_update(running, piece_parts, inner_offset):
            running_max, running_sum, weighted = running
            key_rows, value_rows, key_shift = unpack(piece_parts)
            scores = head_scores(query_heads, split_heads(key_rows), tau_value, key_shift)
            if causal:
                key_pos = inner_offset + jnp.arange(key_rows.shape[1], dtype=jnp.int32)
                scores = causal_mask(scores, query_pos, key_pos)
            new_max = jnp.maximum(running_max, jnp.max(scores, axis=-1))
            factor = jnp.exp(running_max - new_max)
            weights = jnp.exp(scores - new_max[..., None])
            new_sum = running_sum * factor + jnp.sum(weights, axis=-1)
            mixed_values = jnp.einsum(
                "ihqk,ikhd->ihqd",
                weights,
                split_heads(value_rows).astype(jnp.float32),
                preferred_element_type=jnp.float32,
            )
            return (new_max, new_sum, weighted * factor[..., None] + mixed_values)

        return over_blocks(block_update, totals, fetched, shard_rows)

    return update


def query_grad_update(
    query_heads, grad_heads, log_total, row_dot, tau_value, query_pos, causal, unpack, shard_rows
):

    def update(totals, fetched, offset):

        def block_update(running, piece_parts, inner_offset):
            key_rows, value_rows, key_shift = unpack(piece_parts)
            key_heads = split_heads(key_rows)
            scores = head_scores(query_heads, key_heads, tau_value, key_shift)
            if causal:
                key_pos = inner_offset + jnp.arange(key_rows.shape[1], dtype=jnp.int32)
                scores = causal_mask(scores, query_pos, key_pos)
            probabilities = jnp.exp(scores - log_total[..., None])
            prob_grads = jnp.einsum(
                "iqhd,ikhd->ihqk",
                grad_heads,
                split_heads(value_rows),
                preferred_element_type=jnp.float32,
            )
            score_grads = (probabilities * (prob_grads - row_dot[..., None])).astype(jnp.bfloat16)
            return running + jnp.einsum(
                "ihqk,ikhd->ihqd", score_grads, key_heads, preferred_element_type=jnp.float32
            )

        return over_blocks(block_update, totals, fetched, shard_rows)

    return update


def key_grad_update(key_heads, value_heads, key_shift, tau_value, key_pos, causal, shard_rows):

    def update(totals, fetched, offset):

        def block_update(running, piece_parts, inner_offset):
            key_total, value_total = running
            query_heads = split_heads(piece_parts[0].astype(jnp.bfloat16))
            grad_heads = split_heads(piece_parts[1].astype(jnp.bfloat16))
            log_rows = jnp.transpose(piece_parts[2], (0, 2, 1))
            dot_rows = jnp.transpose(piece_parts[3], (0, 2, 1))
            scores = head_scores(query_heads, key_heads, tau_value, key_shift)
            if causal:
                query_pos = inner_offset + jnp.arange(piece_parts[0].shape[1], dtype=jnp.int32)
                scores = causal_mask(scores, query_pos, key_pos)
            probabilities = jnp.exp(scores - log_rows[..., None])
            value_total = value_total + jnp.einsum(
                "ihqk,iqhd->ihkd",
                probabilities,
                grad_heads.astype(jnp.float32),
                preferred_element_type=jnp.float32,
            )
            prob_grads = jnp.einsum(
                "iqhd,ikhd->ihqk", grad_heads, value_heads, preferred_element_type=jnp.float32
            )
            score_grads = (probabilities * (prob_grads - dot_rows[..., None])).astype(jnp.bfloat16)
            key_total = key_total + jnp.einsum(
                "ihqk,iqhd->ihkd", score_grads, query_heads, preferred_element_type=jnp.float32
            )
            return (key_total, value_total)

        return over_blocks(block_update, totals, fetched, shard_rows)

    return update


def feed_forward_back(upstream, hidden, pre_act, activated, weight_in, weight_out):
    out_grad = upstream.astype(jnp.bfloat16)
    out_weight_grad = weight_grad(activated, out_grad)
    out_bias_grad = row_total(out_grad)
    act_grad = project_back(out_grad, weight_out)
    ignored, gelu_back = jax.vjp(partial(jax.nn.gelu, approximate=False), pre_act)
    pre_grad = gelu_back(act_grad)[0].astype(jnp.bfloat16)
    return (
        project_back(pre_grad, weight_in),
        weight_grad(hidden, pre_grad),
        row_total(pre_grad),
        out_weight_grad,
        out_bias_grad,
    )


def local(
    enc_in,
    series,
    channel_mask,
    item_group,
    tau_scale,
    delta_shift,
    dec_in,
    value_embed,
    enc_qkv,
    enc_out,
    enc_ff_in,
    enc_ff_out,
    enc_query_bias,
    enc_bias,
    enc_gain,
    dec_qkv,
    dec_out,
    cross_qkv,
    cross_out,
    dec_ff_in,
    dec_ff_out,
    dec_bias,
    dec_gain,
    ff_bias,
    cotangent,
):
    item_count, enc_rows, width = enc_in.shape
    dec_rows = dec_in.shape[1]
    head_size = width // HEADS
    seq_index = lax.axis_index(SEQ)
    enc_pos = seq_index * enc_rows + jnp.arange(enc_rows, dtype=jnp.int32)
    dec_pos = seq_index * dec_rows + jnp.arange(dec_rows, dtype=jnp.int32)
    enc_shift = delta_shift.astype(jnp.float32)
    chosen = (item_group[:, None] == jnp.arange(GROUPS, dtype=jnp.int32)[None, :]).astype(
        jnp.float32
    )
    channels = jnp.dot(chosen, channel_mask.astype(jnp.float32), precision=lax.Precision.HIGHEST)
    masked_series = (series.astype(jnp.float32) * channels[:, None, :]).astype(jnp.bfloat16)
    embedded = enc_in.astype(jnp.float32) + project(masked_series, value_embed)
    enc_hidden = embedded.astype(jnp.bfloat16)
    enc_query = (project(enc_hidden, enc_qkv[0]) + enc_query_bias).astype(jnp.bfloat16)
    enc_key = project(enc_hidden, enc_qkv[1]).astype(jnp.bfloat16)
    enc_value = (project(enc_hidden, enc_qkv[2]) + enc_bias[0]).astype(jnp.bfloat16)
    enc_update = forward_update(
        split_heads(enc_query), tau_scale, enc_pos, False, plain_unpack, enc_rows
    )
    enc_mixed, enc_log = finish_forward(
        enc_update(
            fresh_totals(item_count, enc_rows, head_size),
            (
                lax.all_gather(enc_key, SEQ, axis=1, tiled=True),
                lax.all_gather(enc_value, SEQ, axis=1, tiled=True),
                lax.all_gather(delta_shift, SEQ, axis=1, tiled=True),
            ),
            jnp.int32(0),
        )
    )
    enc_attended = enc_mixed.astype(jnp.bfloat16)
    enc_first_in = embedded + project(enc_attended, enc_out) + enc_bias[1]
    enc_first = layer_norm(enc_first_in, enc_gain[0], enc_bias[3])
    enc_ff_hidden = enc_first.astype(jnp.bfloat16)
    enc_ff_pre = project(enc_ff_hidden, enc_ff_in) + ff_bias[0]
    enc_ff_act = jax.nn.gelu(enc_ff_pre, approximate=False).astype(jnp.bfloat16)
    enc_second_in = enc_first + project(enc_ff_act, enc_ff_out) + enc_bias[2]
    encoded = layer_norm(enc_second_in, enc_gain[1], enc_bias[4])
    memory = encoded.astype(jnp.bfloat16)
    self_query = (project(dec_in, dec_qkv[0]) + dec_bias[0]).astype(jnp.bfloat16)
    self_key = project(dec_in, dec_qkv[1]).astype(jnp.bfloat16)
    self_value = (project(dec_in, dec_qkv[2]) + dec_bias[1]).astype(jnp.bfloat16)
    self_update = forward_update(
        split_heads(self_query), tau_scale, dec_pos, True, self_unpack, dec_rows
    )
    self_mixed, self_log = finish_forward(
        self_update(
            fresh_totals(item_count, dec_rows, head_size),
            (
                lax.all_gather(self_key, SEQ, axis=1, tiled=True),
                lax.all_gather(self_value, SEQ, axis=1, tiled=True),
            ),
            jnp.int32(0),
        )
    )
    self_attended = self_mixed.astype(jnp.bfloat16)
    dec_first_in = dec_in.astype(jnp.float32) + project(self_attended, dec_out) + dec_bias[2]
    dec_first = layer_norm(dec_first_in, dec_gain[0], dec_bias[7])
    cross_hidden = dec_first.astype(jnp.bfloat16)
    cross_query = (project(cross_hidden, cross_qkv[0]) + dec_bias[3]).astype(jnp.bfloat16)
    cross_key = project(memory, cross_qkv[1]).astype(jnp.bfloat16)
    cross_value = (project(memory, cross_qkv[2]) + dec_bias[4]).astype(jnp.bfloat16)
    cross_start = fresh_totals(item_count, dec_rows, head_size)
    cross_update = forward_update(
        split_heads(cross_query), tau_scale, dec_pos, False, plain_unpack, enc_rows
    )
    cross_totals = cross_update(
        cross_start,
        (
            lax.all_gather(cross_key, SEQ, axis=1, tiled=True),
            lax.all_gather(cross_value, SEQ, axis=1, tiled=True),
            lax.all_gather(delta_shift, SEQ, axis=1, tiled=True),
        ),
        jnp.int32(0),
    )
    cross_mixed, cross_log = finish_forward(cross_totals)
    cross_attended = cross_mixed.astype(jnp.bfloat16)
    dec_second_in = dec_first + project(cross_attended, cross_out) + dec_bias[5]
    dec_second = layer_norm(dec_second_in, dec_gain[1], dec_bias[8])
    dec_ff_hidden = dec_second.astype(jnp.bfloat16)
    dec_ff_pre = project(dec_ff_hidden, dec_ff_in) + ff_bias[1]
    dec_ff_act = jax.nn.gelu(dec_ff_pre, approximate=False).astype(jnp.bfloat16)
    dec_third_in = dec_second + project(dec_ff_act, dec_ff_out) + dec_bias[6]
    decoded = layer_norm(dec_third_in, dec_gain[2], dec_bias[9])
    third_grad, dec_gain_three, dec_bias_three = norm_backward(
        dec_third_in, dec_gain[2], dec_bias[9], cotangent.astype(jnp.float32)
    )
    from_dec_ff, dec_ff_in_grad, dec_ff_bias_grad, dec_ff_out_grad, dec_ff_out_bias = (
        feed_forward_back(third_grad, dec_ff_hidden, dec_ff_pre, dec_ff_act, dec_ff_in, dec_ff_out)
    )
    second_grad, dec_gain_two, dec_bias_two = norm_backward(
        dec_second_in, dec_gain[1], dec_bias[8], third_grad + from_dec_ff
    )
    cross_branch_grad = second_grad.astype(jnp.bfloat16)
    cross_out_grad = weight_grad(cross_attended, cross_branch_grad)
    cross_out_bias = row_total(cross_branch_grad)
    cross_mixed_grad = project_back(cross_branch_grad, cross_out).astype(jnp.bfloat16)
    cross_dot = row_products(cross_mixed_grad, cross_mixed)
    cross_query_start = jnp.zeros((item_count, HEADS, dec_rows, head_size), jnp.float32)
    cross_back = query_grad_update(
        split_heads(cross_query),
        split_heads(cross_mixed_grad),
        jnp.transpose(cross_log, (0, 2, 1)),
        jnp.transpose(cross_dot, (0, 2, 1)),
        tau_scale,
        dec_pos,
        False,
        plain_unpack,
        enc_rows,
    )
    cross_query_total = cross_back(
        cross_query_start,
        (
            lax.all_gather(cross_key, SEQ, axis=1, tiled=True),
            lax.all_gather(cross_value, SEQ, axis=1, tiled=True),
            lax.all_gather(delta_shift, SEQ, axis=1, tiled=True),
        ),
        jnp.int32(0),
    )
    cross_query_grad = scaled_grad(cross_query_total, tau_scale)
    cross_key_update = key_grad_update(
        split_heads(cross_key),
        split_heads(cross_value),
        enc_shift,
        tau_scale,
        enc_pos,
        False,
        dec_rows,
    )
    cross_key_start = (
        jnp.zeros((item_count, HEADS, enc_rows, head_size), jnp.float32),
        jnp.zeros((item_count, HEADS, enc_rows, head_size), jnp.float32),
    )
    cross_key_total, cross_value_total = cross_key_update(
        cross_key_start,
        (
            lax.all_gather(cross_query.astype(jnp.float32), SEQ, axis=1, tiled=True),
            lax.all_gather(cross_mixed_grad.astype(jnp.float32), SEQ, axis=1, tiled=True),
            lax.all_gather(cross_log, SEQ, axis=1, tiled=True),
            lax.all_gather(cross_dot, SEQ, axis=1, tiled=True),
        ),
        jnp.int32(0),
    )
    cross_key_grad = scaled_grad(cross_key_total, tau_scale)
    cross_value_grad = merge_heads(cross_value_total).astype(jnp.bfloat16)
    cross_qkv_grad = jnp.stack(
        [
            weight_grad(cross_hidden, cross_query_grad),
            weight_grad(memory, cross_key_grad),
            weight_grad(memory, cross_value_grad),
        ]
    )
    memory_grad = project_back(cross_key_grad, cross_qkv[1]) + project_back(
        cross_value_grad, cross_qkv[2]
    )
    first_grad, dec_gain_one, dec_bias_one = norm_backward(
        dec_first_in,
        dec_gain[0],
        dec_bias[7],
        second_grad + project_back(cross_query_grad, cross_qkv[0]),
    )
    self_branch_grad = first_grad.astype(jnp.bfloat16)
    dec_out_grad = weight_grad(self_attended, self_branch_grad)
    self_out_bias = row_total(self_branch_grad)
    self_mixed_grad = project_back(self_branch_grad, dec_out).astype(jnp.bfloat16)
    self_dot = row_products(self_mixed_grad, self_mixed)
    self_back = query_grad_update(
        split_heads(self_query),
        split_heads(self_mixed_grad),
        jnp.transpose(self_log, (0, 2, 1)),
        jnp.transpose(self_dot, (0, 2, 1)),
        tau_scale,
        dec_pos,
        True,
        self_unpack,
        dec_rows,
    )
    self_query_total = self_back(
        jnp.zeros((item_count, HEADS, dec_rows, head_size), jnp.float32),
        (
            lax.all_gather(self_key, SEQ, axis=1, tiled=True),
            lax.all_gather(self_value, SEQ, axis=1, tiled=True),
        ),
        jnp.int32(0),
    )
    self_query_grad = scaled_grad(self_query_total, tau_scale)
    self_key_update = key_grad_update(
        split_heads(self_key),
        split_heads(self_value),
        jnp.zeros((item_count, dec_rows), jnp.float32),
        tau_scale,
        dec_pos,
        True,
        dec_rows,
    )
    self_key_start = (
        jnp.zeros((item_count, HEADS, dec_rows, head_size), jnp.float32),
        jnp.zeros((item_count, HEADS, dec_rows, head_size), jnp.float32),
    )
    self_key_total, self_value_total = self_key_update(
        self_key_start,
        (
            lax.all_gather(self_query.astype(jnp.float32), SEQ, axis=1, tiled=True),
            lax.all_gather(self_mixed_grad.astype(jnp.float32), SEQ, axis=1, tiled=True),
            lax.all_gather(self_log, SEQ, axis=1, tiled=True),
            lax.all_gather(self_dot, SEQ, axis=1, tiled=True),
        ),
        jnp.int32(0),
    )
    self_key_grad = scaled_grad(self_key_total, tau_scale)
    self_value_grad = merge_heads(self_value_total).astype(jnp.bfloat16)
    dec_qkv_grad = jnp.stack(
        [
            weight_grad(dec_in, self_query_grad),
            weight_grad(dec_in, self_key_grad),
            weight_grad(dec_in, self_value_grad),
        ]
    )
    dec_in_grad = (
        first_grad
        + project_back(self_query_grad, dec_qkv[0])
        + project_back(self_key_grad, dec_qkv[1])
        + project_back(self_value_grad, dec_qkv[2])
    )
    enc_second_grad, enc_gain_two, enc_bias_two = norm_backward(
        enc_second_in, enc_gain[1], enc_bias[4], memory_grad
    )
    from_enc_ff, enc_ff_in_grad, enc_ff_bias_grad, enc_ff_out_grad, enc_ff_out_bias = (
        feed_forward_back(
            enc_second_grad, enc_ff_hidden, enc_ff_pre, enc_ff_act, enc_ff_in, enc_ff_out
        )
    )
    enc_first_grad, enc_gain_one, enc_bias_one = norm_backward(
        enc_first_in, enc_gain[0], enc_bias[3], enc_second_grad + from_enc_ff
    )
    enc_branch_grad = enc_first_grad.astype(jnp.bfloat16)
    enc_out_grad = weight_grad(enc_attended, enc_branch_grad)
    enc_out_bias = row_total(enc_branch_grad)
    enc_mixed_grad = project_back(enc_branch_grad, enc_out).astype(jnp.bfloat16)
    enc_dot = row_products(enc_mixed_grad, enc_mixed)
    enc_back = query_grad_update(
        split_heads(enc_query),
        split_heads(enc_mixed_grad),
        jnp.transpose(enc_log, (0, 2, 1)),
        jnp.transpose(enc_dot, (0, 2, 1)),
        tau_scale,
        enc_pos,
        False,
        plain_unpack,
        enc_rows,
    )
    enc_query_total = enc_back(
        jnp.zeros((item_count, HEADS, enc_rows, head_size), jnp.float32),
        (
            lax.all_gather(enc_key, SEQ, axis=1, tiled=True),
            lax.all_gather(enc_value, SEQ, axis=1, tiled=True),
            lax.all_gather(delta_shift, SEQ, axis=1, tiled=True),
        ),
        jnp.int32(0),
    )
    enc_query_grad = scaled_grad(enc_query_total, tau_scale)
    enc_key_update = key_grad_update(
        split_heads(enc_key), split_heads(enc_value), enc_shift, tau_scale, enc_pos, False, enc_rows
    )
    enc_key_start = (
        jnp.zeros((item_count, HEADS, enc_rows, head_size), jnp.float32),
        jnp.zeros((item_count, HEADS, enc_rows, head_size), jnp.float32),
    )
    enc_key_total, enc_value_total = enc_key_update(
        enc_key_start,
        (
            lax.all_gather(enc_query.astype(jnp.float32), SEQ, axis=1, tiled=True),
            lax.all_gather(enc_mixed_grad.astype(jnp.float32), SEQ, axis=1, tiled=True),
            lax.all_gather(enc_log, SEQ, axis=1, tiled=True),
            lax.all_gather(enc_dot, SEQ, axis=1, tiled=True),
        ),
        jnp.int32(0),
    )
    enc_key_grad = scaled_grad(enc_key_total, tau_scale)
    enc_value_grad = merge_heads(enc_value_total).astype(jnp.bfloat16)
    enc_qkv_grad = jnp.stack(
        [
            weight_grad(enc_hidden, enc_query_grad),
            weight_grad(enc_hidden, enc_key_grad),
            weight_grad(enc_hidden, enc_value_grad),
        ]
    )
    enc_in_grad = (
        enc_first_grad
        + project_back(enc_query_grad, enc_qkv[0])
        + project_back(enc_key_grad, enc_qkv[1])
        + project_back(enc_value_grad, enc_qkv[2])
    )
    embed_grad = weight_grad(masked_series, enc_in_grad.astype(jnp.bfloat16))
    enc_query_bias_grad = row_total(enc_query_grad)
    enc_bias_grad = jnp.stack(
        [row_total(enc_value_grad), enc_out_bias, enc_ff_out_bias, enc_bias_one, enc_bias_two]
    )
    enc_gain_grad = jnp.stack([enc_gain_one, enc_gain_two])
    dec_bias_grad = jnp.stack(
        [
            row_total(self_query_grad),
            row_total(self_value_grad),
            self_out_bias,
            row_total(cross_query_grad),
            row_total(cross_value_grad),
            cross_out_bias,
            dec_ff_out_bias,
            dec_bias_one,
            dec_bias_two,
            dec_bias_three,
        ]
    )
    dec_gain_grad = jnp.stack([dec_gain_one, dec_gain_two, dec_gain_three])
    ff_bias_grad = jnp.stack([enc_ff_bias_grad, dec_ff_bias_grad])
    shares = (
        lax.psum_scatter(embed_grad, SEQ, scatter_dimension=1, tiled=True),
        lax.psum_scatter(enc_qkv_grad, SEQ, scatter_dimension=2, tiled=True),
        lax.psum_scatter(enc_out_grad, SEQ, scatter_dimension=1, tiled=True),
        lax.psum_scatter(enc_ff_in_grad, SEQ, scatter_dimension=1, tiled=True),
        lax.psum_scatter(enc_ff_out_grad, SEQ, scatter_dimension=1, tiled=True),
        lax.psum_scatter(enc_query_bias_grad, SEQ, scatter_dimension=0, tiled=True),
        lax.psum_scatter(enc_bias_grad, SEQ, scatter_dimension=1, tiled=True),
        lax.psum_scatter(enc_gain_grad, SEQ, scatter_dimension=1, tiled=True),
        lax.psum_scatter(dec_qkv_grad, SEQ, scatter_dimension=2, tiled=True),
        lax.psum_scatter(dec_out_grad, SEQ, scatter_dimension=1, tiled=True),
        lax.psum_scatter(cross_qkv_grad, SEQ, scatter_dimension=2, tiled=True),
        lax.psum_scatter(cross_out_grad, SEQ, scatter_dimension=1, tiled=True),
        lax.psum_scatter(dec_ff_in_grad, SEQ, scatter_dimension=1, tiled=True),
        lax.psum_scatter(dec_ff_out_grad, SEQ, scatter_dimension=1, tiled=True),
        lax.psum_scatter(dec_bias_grad, SEQ, scatter_dimension=1, tiled=True),
        lax.psum_scatter(dec_gain_grad, SEQ, scatter_dimension=1, tiled=True),
        lax.psum_scatter(ff_bias_grad, SEQ, scatter_dimension=1, tiled=True),
    )
    summed = lax.psum(
        (
            shares[0],
            shares[1],
            shares[2],
            shares[3],
            shares[4],
            shares[5],
            shares[6],
            shares[7],
            shares[8],
            shares[9],
            shares[10],
            shares[11],
            shares[12],
            shares[13],
            shares[14],
            shares[15],
            shares[16],
        ),
        BATCH,
    )
    return (
        decoded.astype(jnp.bfloat16),
        enc_in_grad,
        dec_in_grad,
        summed[0],
        summed[1],
        summed[2],
        summed[3],
        summed[4],
        summed[5],
        summed[6],
        summed[7],
        summed[8],
        summed[9],
        summed[10],
        summed[11],
        summed[12],
        summed[13],
        summed[14],
        summed[15],
        summed[16],
    )


F32 = jnp.float32
BF16 = jnp.bfloat16
MESH = pl.DeviceIdType.MESH
QUAD = 4
HALVES = 2
CORES = 2
LANES = 128
LINK_COUNT = 320
VMEM_BYTES = 60 << 20
LOAD_FIRST = 3
LOAD_ORDER = (
    "value_embed",
    "enc_qkv",
    "dec_qkv",
    "enc_out",
    "enc_ff_in",
    "enc_ff_out",
    "dec_out",
    "cross_qkv",
    "cross_out",
    "dec_ff_in",
    "dec_ff_out",
)


def mm(left, right):
    return jnp.dot(left, right, preferred_element_type=F32)


def mm_right_t(left, right):
    return lax.dot_general(left, right, (((1,), (1,)), ((), ())), preferred_element_type=F32)


def mm_left_t(left, right):
    return lax.dot_general(left, right, (((0,), (0,)), ((), ())), preferred_element_type=F32)


def lane_index(shape):
    return lax.broadcasted_iota(jnp.int32, shape, len(shape) - 1)


def swap_halves(values):
    return pltpu.roll(values, LANES // 2, axis=1)


def low_lanes(first, second):
    return jnp.where(lane_index(first.shape) < LANES // 2, first, second)


def pack_rows(values):
    half = values.shape[0] // 2
    packed = []
    for pair in range(values.shape[1] // LANES):
        group = values[:, pair * LANES : (pair + 1) * LANES]
        top, bottom = group[:half], group[half:]
        packed.append(low_lanes(top, swap_halves(bottom)))
        packed.append(low_lanes(swap_halves(top), bottom))
    return packed


def unpack_rows(packed):
    groups = []
    for pair in range(len(packed) // 2):
        first, second = packed[2 * pair], packed[2 * pair + 1]
        top = low_lanes(first, swap_halves(second))
        bottom = low_lanes(swap_halves(first), second)
        groups.append(jnp.concatenate([top, bottom], axis=0))
    return jnp.concatenate(groups, axis=1)


def pack_pairs(keys, values):
    packed = []
    for pair in range(keys.shape[1] // LANES):
        key_group = keys[:, pair * LANES : (pair + 1) * LANES]
        value_group = values[:, pair * LANES : (pair + 1) * LANES]
        packed.append(low_lanes(key_group, swap_halves(value_group)))
        packed.append(low_lanes(swap_halves(key_group), value_group))
    return packed


def unpack_pairs(packed):
    keys, values = [], []
    for pair in range(len(packed) // 2):
        first, second = packed[2 * pair], packed[2 * pair + 1]
        keys.append(low_lanes(first, swap_halves(second)))
        values.append(low_lanes(swap_halves(first), second))
    return jnp.concatenate(keys, axis=1), jnp.concatenate(values, axis=1)


def norm_forward(values, gain, shift):
    centred = values - jnp.mean(values, axis=-1, keepdims=True)
    scale = lax.rsqrt(jnp.mean(centred * centred, axis=-1, keepdims=True) + epsilon)
    unit = centred * scale
    return unit * gain + shift, unit, scale


def norm_back(upstream, unit, scale, gain):
    inner = upstream * gain
    result = scale * (
        inner
        - jnp.mean(inner, axis=-1, keepdims=True)
        - unit * jnp.mean(inner * unit, axis=-1, keepdims=True)
    )
    return (
        result,
        jnp.sum(upstream * unit, axis=0, keepdims=True),
        jnp.sum(upstream, axis=0, keepdims=True),
    )


def rounded(values):
    return values.astype(BF16).astype(F32)


class View:
    def __init__(self, entries):
        for name, entry in entries.items():
            if isinstance(entry, dict):
                entry = View(entry)
            elif isinstance(entry, (list, tuple)):
                entry = [View(part) if isinstance(part, dict) else part for part in entry]
            setattr(self, name, entry)


class Weight:
    def __init__(self, copy, held):
        self.copy, self.held, self.here = copy, held, False

    def start(self):
        self.copy.start()

    def __call__(self):
        if not self.here:
            self.copy.wait()
            self.here = True
        return self.held


def fused_body(structures, *refs):
    entries = {}
    for structure in structures:
        count = structure.num_leaves
        entries.update(jax.tree.unflatten(structure, refs[:count]))
        refs = refs[count:]
    ref = View(entries)
    small = View(entries["held_blocks"])
    rows, width = ref.enc_in.shape
    hidden, channels, chips = ref.ff_bias.shape[1], ref.series.shape[1], HEADS
    packed_rows = rows // 2
    keys_total = chips * CORES * rows
    block_queries = chips * packed_rows
    column = width // (chips * CORES)
    depth = chips * CORES // QUAD

    place = lax.axis_index(SEQ)
    item = lax.axis_index(BATCH)
    core = lax.rem(place, 2)
    chip = place // 2
    x_place = lax.rem(chip, 2)
    z_place = chip // 2
    quad = lax.rem(place, QUAD)
    core_dev = (chip * 2 + (1 - core), item)
    x_dev = (z_place * QUAD + (1 - x_place) * 2 + core, item)
    diagonal_dev = (z_place * QUAD + (1 - x_place) * 2 + (1 - core), item)
    item_dev = (place, 1 - item)
    x_quad = (1 - x_place) * 2 + core

    def same_core(step):
        peer = lax.rem(chip + step, chips)
        return peer, (peer * 2 + core, item)

    def z_peer(step):
        peer = lax.rem(z_place + step, depth)
        return peer, (peer * QUAD + quad, item)

    barrier = pltpu.get_barrier_semaphore()
    greeted = [core_dev, diagonal_dev, item_dev] + [same_core(step)[1] for step in range(1, chips)]
    for device in greeted:
        pl.semaphore_signal(barrier, inc=1, device_id=device, device_id_type=MESH)

    blocks = []
    for index, (name, target) in enumerate(entries["held_blocks"].items()):
        blocks.append(pltpu.make_async_copy(entries[name], target, ref.block_sem.at[index]))
        blocks[-1].start()
    loaded = {}
    for index, name in enumerate(LOAD_ORDER):
        source, target = getattr(ref.weight, name), getattr(ref.held, name)
        copy = pltpu.make_async_copy(source, target, ref.load_sem.at[index])
        loaded[name] = Weight(copy, target)
    weight = View(loaded)
    for name in LOAD_ORDER[:LOAD_FIRST]:
        loaded[name].start()
    for copy in blocks:
        copy.wait()

    stores = []

    def store(source, target):
        index = len(stores)
        stores.append(pltpu.make_async_copy(source, target, ref.store_sem.at[index]))
        stores[-1].start()

    sends = []

    def send(source, target, device):
        index = len(sends)
        copy = pltpu.make_async_remote_copy(
            src_ref=source,
            dst_ref=target,
            send_sem=ref.send_sem.at[index],
            recv_sem=ref.recv_sem.at[index],
            device_id=device,
            device_id_type=MESH,
        )
        copy.start()
        sends.append(copy)
        return copy

    def arrive(copies):
        for copy in copies:
            copy.wait_recv()

    def spread(source, target_at):
        copies = []
        for step in range(1, chips):
            peer, device = same_core(step)
            copies.append(send(source.at[peer], target_at(chip), device))
        return copies

    def share(block):
        return [
            block,
            send(block.at[quad], block.at[quad], core_dev),
            send(block.at[quad], block.at[quad], x_dev),
        ]

    def relay(shared):
        block = shared[0]
        shared[2].wait_recv()
        shared.append(send(block.at[x_quad], block.at[x_quad], core_dev))

    def settle(shared):
        shared[1].wait_recv()
        shared[3].wait_recv()

    def gathered(block):
        value = block[...]
        return value.reshape(value.shape[0] * value.shape[1], value.shape[2])

    def cut_columns(values, group, start):
        part = lane_index((rows, LANES)) // column
        for member in range(QUAD):
            total = None
            for level in range(depth):
                cut = values[:, level * LANES : (level + 1) * LANES]
                shift = (column * (level - member)) % LANES
                moved = pltpu.roll(cut, shift, axis=1) if shift else cut
                total = moved if total is None else jnp.where(part == level, moved, total)
            group.cut[member, :, start : start + LANES] = total.astype(BF16)

    def share_columns(group, start, stop):
        source, target = group.cut, group.met
        target[quad, :, start:stop] = source[quad, :, start:stop]
        copies = []
        for device, member in (
            (core_dev, x_place * 2 + 1 - core),
            (x_dev, x_quad),
            (diagonal_dev, (1 - x_place) * 2 + 1 - core),
        ):
            copies.append(
                send(
                    source.at[member, :, pl.ds(start, stop - start)],
                    target.at[quad, :, pl.ds(start, stop - start)],
                    device,
                )
            )
        return copies

    def columns_of(group, start, stop):
        value = group.met[:, :, start:stop]
        return value.reshape(QUAD * rows, stop - start)

    def put_rows(target, level, start, values):
        half = target.shape[2]
        count = values.shape[0]
        done = 0
        while done < count:
            which, offset = divmod(start + done, half)
            take = min(count - done, half - offset)
            target[which, level, offset : offset + take, :] = values[done : done + take, :]
            done += take

    def put_gradient(target, start, gradient):
        count = gradient.shape[0] // depth
        gradient = gradient.astype(BF16)
        short = -gradient.shape[1] % width
        pieces = gradient.shape[1] // width
        for level in range(depth):
            block = gradient[level * count : (level + 1) * count]
            for piece in range(pieces):
                put_rows(
                    target,
                    level,
                    start + piece * count,
                    block[:, piece * width : (piece + 1) * width],
                )
            if short:
                tail = jnp.concatenate(
                    [block[:, pieces * width :], jnp.zeros((count, short), BF16)], axis=1
                )
                put_rows(target, level, start + pieces * count, tail)

    def reduce_item(group):
        part, arrived = group.part, group.item
        return [send(part.at[1 - item], arrived, item_dev)]

    def reduce_depth(group):
        part, arrived = group.part, group.item
        total, landing = group.half, group.depth
        total[...] = (part[item].astype(F32) + arrived[...].astype(F32)).astype(BF16)
        copies = []
        for step in range(1, depth):
            peer, device = z_peer(step)
            copies.append(send(total.at[peer], landing.at[step - 1], device))
        return copies

    def reduce_last(group):
        total, landing = group.half, group.depth
        result = group.sum
        value = total[z_place].astype(F32)
        for step in range(1, depth):
            value = value + landing[step - 1].astype(F32)
        result[item] = value.astype(BF16)
        return [send(result.at[item], result.at[item], item_dev)]

    def finish(group, index, copies):
        arrive(copies)
        store(group.sum, ref.sums[index])

    def set_vector(row, value):
        ref.vec[row : row + 1, :] = value

    att_enc, att_self, att_cross = ref.attention
    dec_in_part, dec_out_part, cross_part, enc_in_part, enc_out_part, self_part, last_part = (
        ref.group
    )
    enc_ff = (weight.enc_ff_in, weight.enc_ff_out)
    dec_ff = (weight.dec_ff_in, weight.dec_ff_out)

    def build(group, row, start, features, block, wide=False):
        gradient = mm_left_t(columns_of(group, start, start + features), gathered(block))
        if wide:
            put_gradient(group.part, row, gradient)
            return
        for which in range(features // LANES):
            put_gradient(
                group.part,
                row + which * column,
                gradient[which * LANES : (which + 1) * LANES],
            )

    tau = ref.tau_scale[0]
    group_row = lax.broadcasted_iota(jnp.int32, small.channel_mask.shape, 0)
    chosen = jnp.where(
        group_row == ref.item_group[0], small.channel_mask[...].astype(F32), 0.0
    )
    channel_row = jnp.sum(chosen, axis=0, keepdims=True)
    masked = (small.series[...].astype(F32) * channel_row).astype(BF16)
    ref.x_series[quad] = jnp.zeros(ref.x_series.shape[1:], BF16)
    ref.x_series[quad, :, 0:channels] = masked

    shift_row = small.delta_shift[...].astype(F32)
    ref.t_shift[...] = jnp.broadcast_to(
        jnp.concatenate([shift_row, shift_row], axis=1), ref.t_shift.shape
    )

    embedded = small.enc_in[...].astype(F32) + mm(masked, weight.value_embed()[...])
    ref.embedded[...] = embedded
    enc_hidden = embedded.astype(BF16)
    ref.x_enc_hidden[quad] = enc_hidden
    for name in LOAD_ORDER[LOAD_FIRST:]:
        loaded[name].start()

    def send_queries(own, query):
        for head, packed in enumerate(pack_rows(query)):
            own.t_query[head] = packed.astype(BF16)
        own.query[chip] = own.t_query[chip]
        return spread(own.t_query, lambda at: own.query.at[at])

    def send_pairs(own, keys, values):
        for head, packed in enumerate(pack_pairs(keys, values)):
            own.t_pair[head] = packed.astype(BF16)
        own.pair[chip, core] = own.t_pair[chip]
        return spread(own.t_pair, lambda at: own.pair.at[at, core])

    def pass_on(own):
        block = own.pair
        return [send(block.at[:, core], block.at[:, core], core_dev)]

    qkv = weight.enc_qkv()
    enc_query = mm(enc_hidden, qkv[0]) + small.enc_query_bias[...]
    enc_key = mm(enc_hidden, qkv[1])
    enc_value = mm(enc_hidden, qkv[2]) + small.enc_bias[0:1, :]
    pl.semaphore_wait(barrier, len(greeted))
    go_enc_pair = send_pairs(att_enc, enc_key, enc_value)
    go_enc_query = send_queries(att_enc, enc_query)
    ref.shift[chip, core] = ref.t_shift[...]
    go_shift = []
    for step in range(1, chips):
        go_shift.append(
            send(ref.t_shift, ref.shift.at[chip, core], same_core(step)[1])
        )

    dec_hidden = small.dec_in[...]
    ref.x_dec_in[quad] = dec_hidden
    qkv = weight.dec_qkv()
    self_query = mm(dec_hidden, qkv[0]) + small.dec_bias[0:1, :]
    self_key = mm(dec_hidden, qkv[1])
    self_value = mm(dec_hidden, qkv[2]) + small.dec_bias[1:2, :]
    go_self_pair = send_pairs(att_self, self_key, self_value)
    go_self_query = send_queries(att_self, self_query)

    def attention(own, shifted, causal):
        pairs = own.pair[...].reshape(keys_total, LANES)
        pairs_t = pairs.T
        own.pair_t[...] = pairs_t
        query_t = own.query[...].reshape(block_queries, LANES).astype(F32).T
        zeros = jnp.zeros((LANES // 2, block_queries), F32)
        for half in range(HALVES):
            part = query_t[half * LANES // 2 : (half + 1) * LANES // 2]
            side = jnp.concatenate([part, zeros], axis=0).astype(BF16)
            scores = mm(pairs, side) * (tau * 0.125)
            if shifted:
                moved = ref.shift_columns[...]
                scores = scores + jnp.concatenate([moved] * (block_queries // LANES), axis=1)
            if causal:
                key_at = lax.broadcasted_iota(jnp.int32, scores.shape, 0)
                lane = lane_index(scores.shape)
                query_at = (
                    (lane // packed_rows * 2 + core) * rows
                    + half * packed_rows
                    + lane % packed_rows
                )
                scores = jnp.where(key_at > query_at, masked_score, scores)
            weights = jnp.exp(scores - jnp.max(scores, axis=0, keepdims=True))
            inverse = 1.0 / jnp.sum(weights, axis=0, keepdims=True)
            low_weights = weights.astype(BF16)
            own.weights[half] = low_weights
            own.inverse[half] = jnp.broadcast_to(inverse, (8, block_queries))
            mixed_t = mm(pairs_t, low_weights)[LANES // 2 :] * inverse
            own.mixed_t[half * LANES // 2 : (half + 1) * LANES // 2, :] = mixed_t
        mixed = own.mixed_t[...].T.astype(BF16)
        own.t_mixed[...] = mixed.reshape(chips, packed_rows, LANES)
        own.mixed[chip] = own.t_mixed[chip]
        return spread(own.t_mixed, lambda at: own.mixed.at[at])

    def mixed_rows(own):
        return unpack_rows(
            [own.mixed[head].astype(F32) for head in range(chips)]
        ).astype(BF16)

    arrive(go_enc_pair)
    on_enc = pass_on(att_enc)
    arrive(go_shift)
    on_shift = [send(ref.shift.at[:, core], ref.shift.at[:, core], core_dev)]
    arrive(go_enc_query)
    arrive(go_self_pair)
    on_self = pass_on(att_self)
    arrive(on_shift)
    for block in range(chips):
        line = low_lanes(ref.shift[block, 0], ref.shift[block, 1])[0:1, :] * 0.125
        ref.shift_columns[block * LANES : (block + 1) * LANES, :] = jnp.broadcast_to(
            line, (LANES, LANES)
        ).T
    arrive(on_enc)
    back_enc = attention(att_enc, True, False)
    arrive(on_self)
    arrive(go_self_query)
    back_self = attention(att_self, False, True)
    shares = [share(ref.x_series), share(ref.x_enc_hidden), share(ref.x_dec_in)]

    def feed_forward(values, weights, bias_row, out_bias, side):
        low = values.astype(BF16)
        side.hidden[quad] = low
        weight_in, weight_out = weights[0](), weights[1]()
        total = out_bias
        for piece in range(hidden // width):
            cut = slice(piece * width, (piece + 1) * width)
            pre = mm(low, weight_in[:, cut]) + small.ff_bias[bias_row : bias_row + 1, cut]
            normal = 0.5 * (1.0 + lax.erf(pre * 0.7071067811865476))
            act = (pre * normal).astype(BF16)
            side.slope[:, cut] = normal + pre * (
                jnp.exp(pre * pre * -0.5) * 0.3989422804014327
            )
            side.act[quad, :, cut] = act
            total = total + mm(act, weight_out[cut, :])
        return total

    def feed_forward_back(upstream, weights, side, vector_row, group):
        low = upstream.astype(BF16)
        weight_in, weight_out = weights[0](), weights[1]()
        total = None
        for piece in range(hidden // width):
            cut = slice(piece * width, (piece + 1) * width)
            act_grad = mm_right_t(low, weight_out[cut, :])
            pre_grad = (act_grad * side.slope[:, cut]).astype(BF16)
            set_vector(
                vector_row + piece, jnp.sum(pre_grad.astype(F32), axis=0, keepdims=True)
            )
            for member in range(QUAD):
                at = piece * LANES
                group.cut[member, :, at : at + LANES] = pre_grad[
                    :, member * LANES : (member + 1) * LANES
                ]
            more = mm_right_t(pre_grad, weight_in[:, cut])
            total = more if total is None else total + more
        return total

    def save_norm(index, unit, scale):
        ref.unit[index] = unit
        ref.scale[index] = jnp.broadcast_to(scale, (rows, LANES))

    def saved_norm(index):
        return ref.unit[index], ref.scale[index, :, 0:1]

    arrive(back_enc)
    attended = mixed_rows(att_enc)
    ref.x_enc_mixed[quad] = attended
    first, unit, scale = norm_forward(
        embedded + mm(attended, weight.enc_out()[...]) + small.enc_bias[1:2, :],
        small.enc_gain[0:1, :],
        small.enc_bias[3:4, :],
    )
    save_norm(0, unit, scale)
    second, unit, scale = norm_forward(
        first + feed_forward(first, enc_ff, 0, small.enc_bias[2:3, :], ref.enc_ff),
        small.enc_gain[1:2, :],
        small.enc_bias[4:5, :],
    )
    save_norm(1, unit, scale)
    memory = second.astype(BF16)
    ref.x_memory[quad] = memory
    qkv = weight.cross_qkv()
    cross_key = mm(memory, qkv[1])
    cross_value = mm(memory, qkv[2]) + small.dec_bias[4:5, :]
    go_cross_pair = send_pairs(att_cross, cross_key, cross_value)

    arrive(back_self)
    attended = mixed_rows(att_self)
    ref.x_self_mixed[quad] = attended
    first, unit, scale = norm_forward(
        small.dec_in[...].astype(F32)
        + mm(attended, weight.dec_out()[...])
        + small.dec_bias[2:3, :],
        small.dec_gain[0:1, :],
        small.dec_bias[7:8, :],
    )
    save_norm(2, unit, scale)
    ref.first_dec[...] = first
    low = first.astype(BF16)
    ref.x_cross_hidden[quad] = low
    go_cross_query = send_queries(att_cross, mm(low, qkv[0]) + small.dec_bias[3:4, :])
    for shared in shares:
        relay(shared)
    shares_two = [
        share(block)
        for block in (
            ref.x_enc_mixed,
            ref.enc_ff.hidden,
            ref.x_memory,
            ref.x_self_mixed,
            ref.x_cross_hidden,
        )
    ]

    arrive(go_cross_pair)
    on_cross = pass_on(att_cross)
    arrive(go_cross_query)
    arrive(on_cross)
    back_cross = attention(att_cross, True, False)
    for shared in shares_two:
        relay(shared)
    shares_three = [share(ref.enc_ff.act)]
    arrive(back_cross)
    attended = mixed_rows(att_cross)
    ref.x_cross_mixed[quad] = attended
    second, unit, scale = norm_forward(
        ref.first_dec[...]
        + mm(attended, weight.cross_out()[...])
        + small.dec_bias[5:6, :],
        small.dec_gain[1:2, :],
        small.dec_bias[8:9, :],
    )
    save_norm(3, unit, scale)
    shares_four = [share(ref.x_cross_mixed)]

    forward = feed_forward(second, dec_ff, 1, small.dec_bias[6:7, :], ref.dec_ff)
    shares_four += [share(ref.dec_ff.hidden), share(ref.dec_ff.act)]
    third, unit, scale = norm_forward(
        second + forward,
        small.dec_gain[2:3, :],
        small.dec_bias[9:10, :],
    )
    ref.o_dec_result[...] = third.astype(BF16)
    store(ref.o_dec_result, ref.dec_result)

    def norm_step(index, upstream, gain, gain_row, gain_vector, shift_vector):
        unit, scale = saved_norm(index)
        result, gain_grad, shift_grad = norm_back(
            upstream, unit, scale, gain[gain_row : gain_row + 1, :]
        )
        set_vector(gain_vector, gain_grad)
        set_vector(shift_vector, shift_grad)
        return result

    def column_sum(values):
        return jnp.sum(rounded(values), axis=0, keepdims=True)

    third_grad, gain_grad, shift_grad = norm_back(
        small.cotangent[...].astype(F32), unit, scale, small.dec_gain[2:3, :]
    )
    set_vector(20, gain_grad)
    set_vector(17, shift_grad)
    from_ff = feed_forward_back(third_grad, dec_ff, ref.dec_ff, 25, dec_in_part)
    second_grad = norm_step(3, third_grad + from_ff, small.dec_gain, 1, 19, 16)
    ref.second_grad[...] = second_grad

    def send_mixed_grad(own, branch_grad, out_weight):
        mixed_grad = mm_right_t(branch_grad.astype(BF16), out_weight[...])
        for head, packed in enumerate(pack_rows(mixed_grad)):
            own.t_grad[head] = packed.astype(BF16)
        own.grad[chip] = own.t_grad[chip]
        return spread(own.t_grad, lambda at: own.grad.at[at])

    go_cross_grad = send_mixed_grad(att_cross, second_grad, weight.cross_out())
    ff_width = hidden // QUAD
    columns_dec_in = share_columns(dec_in_part, 0, ff_width)
    cut_columns(third_grad, dec_out_part, 0)
    cut_columns(second_grad, dec_out_part, LANES)
    columns_dec_out = share_columns(dec_out_part, 0, 2 * LANES)
    set_vector(14, column_sum(third_grad))
    set_vector(13, column_sum(second_grad))
    for shared in shares_three + shares_four:
        relay(shared)

    def attention_back(own):
        pairs = own.pair[...].reshape(keys_total, LANES)
        pairs_t = own.pair_t[...]
        queries = own.query[...].reshape(block_queries, LANES).astype(F32)
        grads = own.grad[...].reshape(block_queries, LANES).astype(F32)
        grads_t = grads.T
        zeros = jnp.zeros((LANES // 2, block_queries), F32)
        blank = jnp.zeros_like(queries)
        query_grads = []
        key_total = value_total = None
        for half in range(HALVES):
            cut = slice(half * LANES // 2, (half + 1) * LANES // 2)
            grad_t = grads_t[cut]
            row_dot = jnp.sum(grad_t * own.mixed_t[cut, :], axis=0, keepdims=True)
            side = jnp.concatenate([zeros, grad_t], axis=0).astype(BF16)
            prob_grads = mm(pairs, side)
            probabilities = own.weights[half].astype(F32) * own.inverse[half, 0:1, :]
            score_grads = (probabilities * (prob_grads - row_dot)).astype(BF16)
            query_grads.append(mm(pairs_t, score_grads)[: LANES // 2])
            if half == 0:
                query_side = low_lanes(queries, blank)
                grad_side = low_lanes(blank, swap_halves(grads))
            else:
                query_side = low_lanes(swap_halves(queries), blank)
                grad_side = low_lanes(blank, grads)
            key_part = mm(score_grads, query_side.astype(BF16))
            value_part = mm(probabilities.astype(BF16), grad_side.astype(BF16))
            key_total = key_part if key_total is None else key_total + key_part
            value_total = value_part if value_total is None else value_total + value_part
        factor = tau * 0.125
        query_grad = (jnp.concatenate(query_grads, axis=0) * factor).T.astype(BF16)
        own.t_query_grad[...] = query_grad.reshape(chips, packed_rows, LANES)
        own.query_grad[chip] = own.t_query_grad[chip]
        go_query = spread(
            own.t_query_grad, lambda at: own.query_grad.at[at]
        )
        pair_grad = (key_total * factor + value_total).reshape(chips, CORES, rows, LANES)
        for which in range(CORES):
            ref.pair_sum[which] = pair_grad[:, which]
            own.t_part[which] = pair_grad[:, which].astype(BF16)
        exchange = send(own.t_part.at[1 - core], own.part, core_dev)
        return go_query, exchange

    def attention_back_pairs(own, exchange):
        exchange.wait_recv()
        total = ref.pair_sum[core] + own.part[...].astype(F32)
        own.t_pair_grad[...] = total.astype(BF16)
        own.pair_grad[chip] = own.t_pair_grad[chip]
        return spread(own.t_pair_grad, lambda at: own.pair_grad.at[at])

    def query_grad_rows(own):
        return unpack_rows(
            [own.query_grad[head].astype(F32) for head in range(chips)]
        )

    def pair_grad_rows(own):
        return unpack_pairs([own.pair_grad[head].astype(F32) for head in range(chips)])

    arrive(go_cross_grad)
    go_query, exchange = attention_back(att_cross)
    go_pair = attention_back_pairs(att_cross, exchange)

    for shared in shares_four:
        settle(shared)
    arrive(columns_dec_in)
    build(dec_in_part, 0, 0, ff_width, ref.dec_ff.hidden, wide=True)
    item_dec_in = reduce_item(dec_in_part)
    arrive(columns_dec_out)
    build(dec_out_part, 0, 0, LANES, ref.dec_ff.act)
    build(dec_out_part, LANES, LANES, LANES, ref.x_cross_mixed)
    item_dec_out = reduce_item(dec_out_part)

    qkv = weight.cross_qkv()
    arrive(go_query)
    cross_query_grad = query_grad_rows(att_cross)
    first_grad = norm_step(
        2,
        ref.second_grad[...] + mm_right_t(cross_query_grad.astype(BF16), qkv[0]),
        small.dec_gain,
        0,
        18,
        15,
    )
    ref.first_grad[...] = first_grad
    go_self_grad = send_mixed_grad(att_self, first_grad, weight.dec_out())
    set_vector(10, column_sum(first_grad))

    arrive(go_pair)
    cross_key_grad, cross_value_grad = pair_grad_rows(att_cross)
    memory_grad = mm_right_t(cross_key_grad.astype(BF16), qkv[1]) + mm_right_t(
        cross_value_grad.astype(BF16), qkv[2]
    )
    enc_second_grad = norm_step(1, memory_grad, small.enc_gain, 1, 7, 5)
    from_ff = feed_forward_back(enc_second_grad, enc_ff, ref.enc_ff, 21, enc_in_part)
    enc_first_grad = norm_step(0, enc_second_grad + from_ff, small.enc_gain, 0, 6, 4)
    ref.enc_first_grad[...] = enc_first_grad
    go_enc_grad = send_mixed_grad(att_enc, enc_first_grad, weight.enc_out())
    set_vector(3, column_sum(enc_second_grad))
    set_vector(2, column_sum(enc_first_grad))
    set_vector(11, column_sum(cross_query_grad))
    set_vector(12, column_sum(cross_value_grad))
    for row in (0, 1, 8, 9, 29, 30, 31):
        set_vector(row, jnp.zeros((1, width), F32))
    vec_item = send(ref.vec, ref.vec_item, item_dev)
    for index, values in enumerate(
        (cross_query_grad, cross_key_grad, cross_value_grad, first_grad)
    ):
        cut_columns(values, cross_part, index * LANES)
    columns_cross = share_columns(cross_part, 0, 4 * LANES)
    columns_enc_in = share_columns(enc_in_part, 0, ff_width)
    cut_columns(enc_second_grad, enc_out_part, 0)
    cut_columns(enc_first_grad, enc_out_part, LANES)
    columns_enc_out = share_columns(enc_out_part, 0, 2 * LANES)

    arrive(go_self_grad)
    go_self_query_grad, exchange = attention_back(att_self)
    arrive(item_dec_in)
    depth_dec_in = reduce_depth(dec_in_part)
    go_self_pair_grad = attention_back_pairs(att_self, exchange)
    for shared in shares + shares_two + shares_three:
        settle(shared)
    arrive(columns_cross)
    build(cross_part, 0, 0, LANES, ref.x_cross_hidden)
    build(cross_part, column, LANES, 2 * LANES, ref.x_memory)
    build(cross_part, 3 * column, 3 * LANES, LANES, ref.x_self_mixed)
    item_cross = reduce_item(cross_part)
    vec_item.wait_recv()
    ref.vec_a[...] = ref.vec[...] + ref.vec_item[...]
    vec_core = send(ref.vec_a, ref.vec_core, core_dev)
    arrive(go_enc_grad)
    go_enc_query_grad, exchange = attention_back(att_enc)
    go_enc_pair_grad = attention_back_pairs(att_enc, exchange)
    vec_core.wait_recv()
    ref.vec_b[...] = ref.vec_a[...] + ref.vec_core[...]
    vec_x = send(ref.vec_b, ref.vec_x, x_dev)
    arrive(item_dec_out)
    depth_dec_out = reduce_depth(dec_out_part)

    arrive(columns_enc_in)
    build(enc_in_part, 0, 0, ff_width, ref.enc_ff.hidden, wide=True)
    item_enc_in = reduce_item(enc_in_part)
    arrive(columns_enc_out)
    build(enc_out_part, 0, 0, LANES, ref.enc_ff.act)
    build(enc_out_part, LANES, LANES, LANES, ref.x_enc_mixed)
    item_enc_out = reduce_item(enc_out_part)
    vec_x.wait_recv()
    ref.vec_c[...] = ref.vec_b[...] + ref.vec_x[...]
    vec_depth = [
        send(ref.vec_c, ref.vec_depth.at[step - 1], z_peer(step)[1])
        for step in range(1, depth)
    ]

    def input_grad(own, weights, first):
        query_grad = query_grad_rows(own)
        key_grad, value_grad = pair_grad_rows(own)
        total = (
            first[...]
            + mm_right_t(query_grad.astype(BF16), weights[0])
            + mm_right_t(key_grad.astype(BF16), weights[1])
            + mm_right_t(value_grad.astype(BF16), weights[2])
        )
        return total, query_grad, key_grad, value_grad

    arrive(go_self_query_grad)
    arrive(go_self_pair_grad)
    total, query_grad, key_grad, value_grad = input_grad(att_self, weight.dec_qkv(), ref.first_grad)
    ref.o_dec_grad[...] = total
    store(ref.o_dec_grad, ref.dec_grad)
    for index, values in enumerate((query_grad, key_grad, value_grad)):
        cut_columns(values, self_part, index * LANES)
    columns_self = share_columns(self_part, 0, 3 * LANES)
    arrive(depth_dec_in)
    last_dec_in = reduce_last(dec_in_part)
    arrive(item_cross)
    depth_cross = reduce_depth(cross_part)
    arrive(go_enc_query_grad)
    arrive(go_enc_pair_grad)
    total, query_grad, key_grad, value_grad = input_grad(att_enc, weight.enc_qkv(), ref.enc_first_grad)
    ref.o_enc_grad[...] = total
    store(ref.o_enc_grad, ref.enc_grad)
    for index, values in enumerate((query_grad, key_grad, value_grad, total)):
        cut_columns(values, last_part, index * LANES)
    columns_enc = share_columns(last_part, 0, 4 * LANES)
    arrive(columns_self)
    build(self_part, 0, 0, 3 * LANES, ref.x_dec_in)
    item_self = reduce_item(self_part)
    arrive(depth_dec_out)
    last_dec_out = reduce_last(dec_out_part)
    arrive(item_enc_in)
    depth_enc_in = reduce_depth(enc_in_part)
    arrive(columns_enc)
    build(last_part, 0, 0, 3 * LANES, ref.x_enc_hidden)
    build(last_part, 3 * column, 3 * LANES, LANES, ref.x_series)
    totals = [
        jnp.sum(
            columns_of(group, index * LANES, (index + 1) * LANES).astype(F32),
            axis=0,
            keepdims=True,
        )
        for group, index in ((self_part, 0), (self_part, 2), (last_part, 0), (last_part, 2))
    ]
    totals = jnp.concatenate(totals + [jnp.zeros((column - 4, LANES), F32)], axis=0)
    totals = jnp.concatenate([totals, jnp.zeros((column, width - LANES), F32)], axis=1)
    for level in range(depth):
        put_rows(last_part.part, level, 5 * column, totals.astype(BF16))
    item_last = reduce_item(last_part)
    arrive(vec_depth)
    total = ref.vec_c[...]
    for step in range(1, depth):
        total = total + ref.vec_depth[step - 1]
    ref.o_vectors[...] = total
    store(ref.o_vectors, ref.vectors)
    arrive(item_enc_out)
    depth_enc_out = reduce_depth(enc_out_part)
    arrive(depth_cross)
    last_cross = reduce_last(cross_part)
    arrive(item_self)
    depth_self = reduce_depth(self_part)
    arrive(depth_enc_in)
    last_enc_in = reduce_last(enc_in_part)
    arrive(item_last)
    depth_last = reduce_depth(last_part)
    arrive(depth_enc_out)
    last_enc_out = reduce_last(enc_out_part)
    finish(dec_in_part, 0, last_dec_in)
    finish(dec_out_part, 1, last_dec_out)
    finish(cross_part, 2, last_cross)
    arrive(depth_self)
    last_self = reduce_last(self_part)
    arrive(depth_last)
    last_last = reduce_last(last_part)
    finish(enc_in_part, 3, last_enc_in)
    finish(enc_out_part, 4, last_enc_out)
    finish(self_part, 5, last_self)
    finish(last_part, 6, last_last)
    for copy in stores:
        copy.wait()
    for copy in sends:
        copy.wait_send()


def finish_body(*refs):
    (
        dec_in,
        enc_grad_in,
        dec_grad_in,
        ff_in_two,
        ff_out_two,
        cross,
        ff_in_one,
        ff_out_one,
        self_part,
        last,
        vectors,
        dec_out,
        enc_grad,
        dec_grad,
        g_embed,
        g_enc_qkv,
        g_enc_out,
        g_enc_ff_in,
        g_enc_ff_out,
        g_enc_query_bias,
        g_enc_bias,
        g_enc_gain,
        g_dec_qkv,
        g_dec_out,
        g_cross_qkv,
        g_cross_out,
        g_dec_ff_in,
        g_dec_ff_out,
        g_dec_bias,
        g_dec_gain,
        g_ff_bias,
    ) = refs
    place = lax.axis_index(SEQ)
    column, width = g_enc_out.shape
    channels = g_embed.shape[1]
    level, member = place // QUAD, lax.rem(place, QUAD)
    dec_out[...] = dec_in[...]
    enc_grad[...] = enc_grad_in[...]
    dec_grad[...] = dec_grad_in[...]

    def whole(block):
        value = block[...]
        return value.reshape(value.shape[0] * value.shape[1], value.shape[2]).astype(F32)

    def narrow(target, block, start):
        for piece in range(target.shape[1] // width):
            target[:, piece * width : (piece + 1) * width] = block[
                start + piece * column : start + (piece + 1) * column
            ]

    g_dec_ff_in[...] = whole(ff_in_two).T
    block = whole(ff_out_two)
    narrow(g_dec_ff_out, block, 0)
    narrow(g_cross_out, block, LANES)
    block = whole(cross)
    for index in range(3):
        g_cross_qkv[index] = block[index * column : (index + 1) * column]
    narrow(g_dec_out, block, 3 * column)
    g_enc_ff_in[...] = whole(ff_in_one).T
    block = whole(ff_out_one)
    narrow(g_enc_ff_out, block, 0)
    narrow(g_enc_out, block, LANES)
    block = whole(self_part)
    for index in range(3):
        g_dec_qkv[index] = block[index * column : (index + 1) * column]
    block = whole(last)
    for index in range(3):
        g_enc_qkv[index] = block[index * column : (index + 1) * column]
    g_embed[:, 0:width] = block[3 * column : 4 * column]
    g_embed[:, width:channels] = block[4 * column : 5 * column, 0 : channels - width]

    group = vectors[:, pl.ds(pl.multiple_of(level * LANES, LANES), LANES)]
    moved = pltpu.roll(group, lax.rem(LANES - member * column, LANES), axis=1)
    rows = moved[:, 0:column]
    late = block[5 * column : 5 * column + 8, 0:LANES]
    late = pltpu.roll(late, lax.rem(LANES - level * column, LANES), axis=1)[:, 0:column]
    g_enc_query_bias[...] = late[2:3]
    g_enc_bias[...] = jnp.concatenate([late[3:4], rows[2:6]], axis=0)
    g_enc_gain[...] = rows[6:8]
    g_dec_bias[...] = jnp.concatenate([late[0:2], rows[10:18]], axis=0)
    g_dec_gain[...] = rows[18:21]
    lanes = pl.ds(pl.multiple_of(member * LANES, LANES), LANES)
    hidden_rows = vectors[:, lanes]
    row_index = lax.broadcasted_iota(jnp.int32, hidden_rows.shape, 0)
    for index in range(2):
        chosen = jnp.where(row_index == 21 + 4 * index + level, hidden_rows, 0.0)
        g_ff_bias[index : index + 1, :] = jnp.sum(chosen, axis=0, keepdims=True)


def fused_local(
    enc_in,
    series,
    channel_mask,
    item_group,
    tau_scale,
    delta_shift,
    dec_in,
    value_embed,
    enc_qkv,
    enc_out,
    enc_ff_in,
    enc_ff_out,
    enc_query_bias,
    enc_bias,
    enc_gain,
    dec_qkv,
    dec_out,
    cross_qkv,
    cross_out,
    dec_ff_in,
    dec_ff_out,
    dec_bias,
    dec_gain,
    ff_bias,
    cotangent,
):
    rows, width = enc_in.shape[1:]
    hidden = enc_ff_in.shape[1]
    channels = value_embed.shape[0]
    chips = HEADS
    column = width // (chips * CORES)
    depth = chips * CORES // QUAD
    padded = -(-channels // LANES) * LANES
    keys_total = chips * CORES * rows
    queries = chips * rows // 2
    in_smem = pl.BlockSpec(memory_space=pltpu.SMEM)
    in_vmem = pl.BlockSpec(memory_space=pltpu.VMEM)
    anywhere = pl.BlockSpec(memory_space=pl.ANY)

    weights = dict(
        value_embed=value_embed,
        enc_qkv=enc_qkv,
        enc_out=enc_out,
        enc_ff_in=enc_ff_in,
        enc_ff_out=enc_ff_out,
        dec_qkv=dec_qkv,
        dec_out=dec_out,
        cross_qkv=cross_qkv,
        cross_out=cross_out,
        dec_ff_in=dec_ff_in,
        dec_ff_out=dec_ff_out,
    )
    scalars = dict(item_group=item_group, tau_scale=tau_scale)
    blocks = dict(
        enc_in=enc_in[0],
        series=series[0],
        channel_mask=channel_mask,
        delta_shift=delta_shift,
        dec_in=dec_in[0],
        cotangent=cotangent[0],
        enc_query_bias=enc_query_bias[None],
        enc_bias=enc_bias,
        enc_gain=enc_gain,
        dec_bias=dec_bias,
        dec_gain=dec_gain,
        ff_bias=ff_bias,
    )
    inputs = (scalars, blocks, dict(weight=weights))
    in_specs = [in_smem] * len(scalars) + [anywhere] * (len(blocks) + len(weights))

    def low(*shape):
        return pltpu.VMEM(shape, BF16)

    def full(*shape):
        return pltpu.VMEM(shape, F32)

    def exchanged(features):
        return low(QUAD, rows, features)

    def attention_space():
        packed = low(chips, rows // 2, LANES)
        paired = low(chips, rows, LANES)
        both = low(chips, CORES, rows, LANES)
        return dict(
            query=packed,
            t_query=packed,
            mixed=packed,
            t_mixed=packed,
            grad=packed,
            t_grad=packed,
            query_grad=packed,
            t_query_grad=packed,
            t_pair=paired,
            pair=both,
            t_pair_grad=paired,
            pair_grad=paired,
            t_part=low(CORES, chips, rows, LANES),
            part=paired,
            pair_t=low(LANES, keys_total),
            weights=low(HALVES, keys_total, queries),
            inverse=full(HALVES, 8, queries),
            mixed_t=full(LANES, queries),
        )

    def feed_forward_space():
        return dict(
            hidden=exchanged(width), act=exchanged(hidden), slope=full(rows, hidden)
        )

    def group_space(count, features):
        half = count // 2
        return dict(
            cut=exchanged(features),
            met=exchanged(features),
            part=low(2, depth, half, width),
            item=low(depth, half, width),
            half=low(depth, half, width),
            depth=low(depth - 1, half, width),
            sum=low(2, half, width),
        )

    ff_width = hidden // QUAD
    group_rows = (
        LANES,
        LANES + column,
        4 * column,
        LANES,
        LANES + column,
        3 * column,
        6 * column,
    )
    group_features = (
        ff_width,
        2 * LANES,
        4 * LANES,
        ff_width,
        2 * LANES,
        3 * LANES,
        4 * LANES,
    )
    scratch = dict(
        held={name: low(*value.shape) for name, value in weights.items()},
        held_blocks={
            name: pltpu.VMEM(value.shape, value.dtype) for name, value in blocks.items()
        },
        block_sem=pltpu.SemaphoreType.DMA((len(blocks),)),
        store_sem=pltpu.SemaphoreType.DMA((4 + len(group_rows),)),
        o_dec_result=low(rows, width),
        o_enc_grad=full(rows, width),
        o_dec_grad=full(rows, width),
        o_vectors=full(32, width),
        x_series=exchanged(padded),
        x_enc_hidden=exchanged(width),
        x_dec_in=exchanged(width),
        x_enc_mixed=exchanged(width),
        x_memory=exchanged(width),
        x_self_mixed=exchanged(width),
        x_cross_hidden=exchanged(width),
        x_cross_mixed=exchanged(width),
        enc_ff=feed_forward_space(),
        dec_ff=feed_forward_space(),
        attention=[attention_space() for index in range(3)],
        group=[group_space(*sizes) for sizes in zip(group_rows, group_features)],
        pair_sum=full(CORES, chips, rows, LANES),
        t_shift=full(8, LANES),
        shift=full(chips, CORES, 8, LANES),
        shift_columns=full(keys_total, LANES),
        embedded=full(rows, width),
        first_dec=full(rows, width),
        second_grad=full(rows, width),
        first_grad=full(rows, width),
        enc_first_grad=full(rows, width),
        unit=full(4, rows, width),
        scale=full(4, rows, LANES),
        vec=full(32, width),
        vec_item=full(32, width),
        vec_a=full(32, width),
        vec_core=full(32, width),
        vec_b=full(32, width),
        vec_x=full(32, width),
        vec_c=full(32, width),
        vec_depth=full(depth - 1, 32, width),
        load_sem=pltpu.SemaphoreType.DMA((len(weights),)),
        send_sem=pltpu.SemaphoreType.DMA((LINK_COUNT,)),
        recv_sem=pltpu.SemaphoreType.DMA((LINK_COUNT,)),
    )
    outputs = dict(
        dec_result=jax.ShapeDtypeStruct((rows, width), BF16),
        enc_grad=jax.ShapeDtypeStruct((rows, width), F32),
        dec_grad=jax.ShapeDtypeStruct((rows, width), F32),
        sums=[jax.ShapeDtypeStruct((2, count // 2, width), BF16) for count in group_rows],
        vectors=jax.ShapeDtypeStruct((32, width), F32),
    )
    out_shapes, out_structure = jax.tree.flatten(outputs)
    scratch_shapes, scratch_structure = jax.tree.flatten(scratch)
    operands = jax.tree.leaves(inputs)
    structures = [jax.tree.structure(part) for part in inputs]
    results = pl.pallas_call(
        partial(fused_body, structures + [out_structure, scratch_structure]),
        out_shape=out_shapes,
        in_specs=in_specs,
        out_specs=[anywhere] * len(out_shapes),
        scratch_shapes=scratch_shapes,
        compiler_params=pltpu.CompilerParams(
            collective_id=1, has_side_effects=True, vmem_limit_bytes=VMEM_BYTES
        ),
        name="layers",
    )(*operands)
    results = jax.tree.unflatten(out_structure, results)
    results = [
        results[key] for key in ("dec_result", "enc_grad", "dec_grad")
    ] + results["sums"] + [results["vectors"]]

    final = [
        (rows, width),
        (rows, width),
        (rows, width),
        (column, channels),
        (3, column, width),
        (column, width),
        (width, hidden // (chips * CORES)),
        (column, hidden),
        (1, column),
        (5, column),
        (2, column),
        (3, column, width),
        (column, width),
        (3, column, width),
        (column, width),
        (width, hidden // (chips * CORES)),
        (column, hidden),
        (10, column),
        (3, column),
        (2, hidden // (chips * CORES)),
    ]
    outputs = pl.pallas_call(
        finish_body,
        out_shape=[
            jax.ShapeDtypeStruct(shape, BF16 if index == 0 else F32)
            for index, shape in enumerate(final)
        ],
        in_specs=[in_vmem] * len(results),
        out_specs=[in_vmem] * len(final),
        compiler_params=pltpu.CompilerParams(vmem_limit_bytes=VMEM_BYTES),
        name="columns",
    )(*results)
    outputs = list(outputs)
    for index in range(3):
        outputs[index] = outputs[index][None]
    outputs[8] = outputs[8][0]
    for index in (3, 4, 5, 7, 11, 12, 13, 14, 16):
        outputs[index] = jnp.swapaxes(outputs[index], -1, -2)
    return tuple(outputs)


def solution(mesh):
    in_specs = (
        P(BATCH, SEQ, None),
        P(BATCH, SEQ, None),
        P(),
        P(BATCH),
        P(BATCH),
        P(BATCH, SEQ),
        P(BATCH, SEQ, None),
        P(),
        P(),
        P(),
        P(),
        P(),
        P(),
        P(),
        P(),
        P(),
        P(),
        P(),
        P(),
        P(),
        P(),
        P(),
        P(),
        P(),
        P(BATCH, SEQ, None),
    )
    out_specs = (
        P(BATCH, SEQ, None),
        P(BATCH, SEQ, None),
        P(BATCH, SEQ, None),
        P(None, SEQ),
        P(None, None, SEQ),
        P(None, SEQ),
        P(None, SEQ),
        P(None, SEQ),
        P(SEQ),
        P(None, SEQ),
        P(None, SEQ),
        P(None, None, SEQ),
        P(None, SEQ),
        P(None, None, SEQ),
        P(None, SEQ),
        P(None, SEQ),
        P(None, SEQ),
        P(None, SEQ),
        P(None, SEQ),
        P(None, SEQ),
    )
    fits = mesh.shape[SEQ] == HEADS * CORES and mesh.shape[BATCH] == 2
    return jax.shard_map(
        fused_local if fits else local, mesh=mesh, in_specs=in_specs, out_specs=out_specs, check_vma=False)
```

```python
from functools import partial
import math

import jax
import jax.numpy as jnp
from jax import lax
from jax.experimental import pallas as pl
from jax.experimental.pallas import tpu as pltpu
from jax.sharding import PartitionSpec as P

HEADS = 8
GROUPS = 16
SEQ = "seq"
BATCH = "batch"


epsilon = 1e-05
masked_score = -1e30


def layer_norm(inputs, gain_vector, shift_vector):
    average = jnp.mean(inputs, axis=-1, keepdims=True)
    centred = inputs - average
    variance = jnp.mean(centred * centred, axis=-1, keepdims=True)
    return centred * lax.rsqrt(variance + epsilon) * gain_vector + shift_vector


def norm_backward(inputs, gain_vector, shift_vector, upstream):
    ignored, pullback = jax.vjp(layer_norm, inputs, gain_vector, shift_vector)
    return pullback(upstream)


def project(inputs, weight_matrix):
    return jnp.dot(inputs, weight_matrix, preferred_element_type=jnp.float32)


def project_back(gradient, weight_matrix):
    return jnp.einsum("ilf,kf->ilk", gradient, weight_matrix, preferred_element_type=jnp.float32)


def weight_grad(inputs, gradient):
    return jnp.einsum("ilk,ilf->kf", inputs, gradient, preferred_element_type=jnp.float32)


def row_total(gradient):
    return jnp.sum(gradient.astype(jnp.float32), axis=(0, 1))


def split_heads(values):
    return values.reshape(values.shape[:2] + (HEADS, values.shape[2] // HEADS))


def merge_heads(head_values):
    return jnp.transpose(head_values, (0, 2, 1, 3)).reshape(
        head_values.shape[0], head_values.shape[2], -1
    )


def over_blocks(update, totals, arrays, shard_rows):
    length = arrays[0].shape[1]
    block_rows = shard_rows * math.gcd(length // shard_rows, 8)
    block_count = length // block_rows
    stacked = tuple(
        (
            jnp.moveaxis(
                member.reshape((member.shape[0], block_count, block_rows) + member.shape[2:]), 1, 0
            )
            for member in arrays
        )
    )
    offsets = jnp.arange(block_count, dtype=jnp.int32) * block_rows

    def advance(running, inputs):
        return (update(running, inputs[0], inputs[1]), None)

    totals, ignored = lax.scan(advance, totals, (stacked, offsets))
    return totals


def head_scores(query_heads, key_heads, tau_value, key_shift):
    raw_scores = jnp.einsum(
        "iqhd,ikhd->ihqk", query_heads, key_heads, preferred_element_type=jnp.float32
    )
    return (tau_value[:, None, None, None] * raw_scores + key_shift[:, None, None, :]) * 0.125


def causal_mask(scores, query_pos, key_pos):
    allowed = query_pos[:, None] >= key_pos[None, :]
    return jnp.where(allowed[None, None], scores, masked_score)


def fresh_totals(item_count, row_count, head_size):
    return (
        jnp.full((item_count, HEADS, row_count), masked_score, jnp.float32),
        jnp.zeros((item_count, HEADS, row_count), jnp.float32),
        jnp.zeros((item_count, HEADS, row_count, head_size), jnp.float32),
    )


def finish_forward(totals):
    running_max, running_sum, weighted = totals
    output = merge_heads(weighted / running_sum[..., None])
    log_total = jnp.transpose(running_max + jnp.log(running_sum), (0, 2, 1))
    return (output, log_total)


def row_products(grad_rows, mixed_rows):
    return jnp.sum(split_heads(grad_rows).astype(jnp.float32) * split_heads(mixed_rows), axis=-1)


def scaled_grad(head_totals, tau_value):
    return merge_heads(head_totals * (tau_value * 0.125)[:, None, None, None]).astype(jnp.bfloat16)


def plain_unpack(fetched):
    return (fetched[0], fetched[1], fetched[2].astype(jnp.float32))


def self_unpack(fetched):
    return (fetched[0], fetched[1], jnp.zeros(fetched[0].shape[:2], jnp.float32))


def forward_update(query_heads, tau_value, query_pos, causal, unpack, shard_rows):

    def update(totals, fetched, offset):

        def block_update(running, piece_parts, inner_offset):
            running_max, running_sum, weighted = running
            key_rows, value_rows, key_shift = unpack(piece_parts)
            scores = head_scores(query_heads, split_heads(key_rows), tau_value, key_shift)
            if causal:
                key_pos = inner_offset + jnp.arange(key_rows.shape[1], dtype=jnp.int32)
                scores = causal_mask(scores, query_pos, key_pos)
            new_max = jnp.maximum(running_max, jnp.max(scores, axis=-1))
            factor = jnp.exp(running_max - new_max)
            weights = jnp.exp(scores - new_max[..., None])
            new_sum = running_sum * factor + jnp.sum(weights, axis=-1)
            mixed_values = jnp.einsum(
                "ihqk,ikhd->ihqd",
                weights,
                split_heads(value_rows).astype(jnp.float32),
                preferred_element_type=jnp.float32,
            )
            return (new_max, new_sum, weighted * factor[..., None] + mixed_values)

        return over_blocks(block_update, totals, fetched, shard_rows)

    return update


def query_grad_update(
    query_heads, grad_heads, log_total, row_dot, tau_value, query_pos, causal, unpack, shard_rows
):

    def update(totals, fetched, offset):

        def block_update(running, piece_parts, inner_offset):
            key_rows, value_rows, key_shift = unpack(piece_parts)
            key_heads = split_heads(key_rows)
            scores = head_scores(query_heads, key_heads, tau_value, key_shift)
            if causal:
                key_pos = inner_offset + jnp.arange(key_rows.shape[1], dtype=jnp.int32)
                scores = causal_mask(scores, query_pos, key_pos)
            probabilities = jnp.exp(scores - log_total[..., None])
            prob_grads = jnp.einsum(
                "iqhd,ikhd->ihqk",
                grad_heads,
                split_heads(value_rows),
                preferred_element_type=jnp.float32,
            )
            score_grads = (probabilities * (prob_grads - row_dot[..., None])).astype(jnp.bfloat16)
            return running + jnp.einsum(
                "ihqk,ikhd->ihqd", score_grads, key_heads, preferred_element_type=jnp.float32
            )

        return over_blocks(block_update, totals, fetched, shard_rows)

    return update


def key_grad_update(key_heads, value_heads, key_shift, tau_value, key_pos, causal, shard_rows):

    def update(totals, fetched, offset):

        def block_update(running, piece_parts, inner_offset):
            key_total, value_total = running
            query_heads = split_heads(piece_parts[0].astype(jnp.bfloat16))
            grad_heads = split_heads(piece_parts[1].astype(jnp.bfloat16))
            log_rows = jnp.transpose(piece_parts[2], (0, 2, 1))
            dot_rows = jnp.transpose(piece_parts[3], (0, 2, 1))
            scores = head_scores(query_heads, key_heads, tau_value, key_shift)
            if causal:
                query_pos = inner_offset + jnp.arange(piece_parts[0].shape[1], dtype=jnp.int32)
                scores = causal_mask(scores, query_pos, key_pos)
            probabilities = jnp.exp(scores - log_rows[..., None])
            value_total = value_total + jnp.einsum(
                "ihqk,iqhd->ihkd",
                probabilities,
                grad_heads.astype(jnp.float32),
                preferred_element_type=jnp.float32,
            )
            prob_grads = jnp.einsum(
                "iqhd,ikhd->ihqk", grad_heads, value_heads, preferred_element_type=jnp.float32
            )
            score_grads = (probabilities * (prob_grads - dot_rows[..., None])).astype(jnp.bfloat16)
            key_total = key_total + jnp.einsum(
                "ihqk,iqhd->ihkd", score_grads, query_heads, preferred_element_type=jnp.float32
            )
            return (key_total, value_total)

        return over_blocks(block_update, totals, fetched, shard_rows)

    return update


def feed_forward_back(upstream, hidden, pre_act, activated, weight_in, weight_out):
    out_grad = upstream.astype(jnp.bfloat16)
    out_weight_grad = weight_grad(activated, out_grad)
    out_bias_grad = row_total(out_grad)
    act_grad = project_back(out_grad, weight_out)
    ignored, gelu_back = jax.vjp(partial(jax.nn.gelu, approximate=False), pre_act)
    pre_grad = gelu_back(act_grad)[0].astype(jnp.bfloat16)
    return (
        project_back(pre_grad, weight_in),
        weight_grad(hidden, pre_grad),
        row_total(pre_grad),
        out_weight_grad,
        out_bias_grad,
    )


def local(
    enc_in,
    series,
    channel_mask,
    item_group,
    tau_scale,
    delta_shift,
    dec_in,
    value_embed,
    enc_qkv,
    enc_out,
    enc_ff_in,
    enc_ff_out,
    enc_query_bias,
    enc_bias,
    enc_gain,
    dec_qkv,
    dec_out,
    cross_qkv,
    cross_out,
    dec_ff_in,
    dec_ff_out,
    dec_bias,
    dec_gain,
    ff_bias,
    cotangent,
):
    item_count, enc_rows, width = enc_in.shape
    dec_rows = dec_in.shape[1]
    head_size = width // HEADS
    seq_index = lax.axis_index(SEQ)
    enc_pos = seq_index * enc_rows + jnp.arange(enc_rows, dtype=jnp.int32)
    dec_pos = seq_index * dec_rows + jnp.arange(dec_rows, dtype=jnp.int32)
    enc_shift = delta_shift.astype(jnp.float32)
    chosen = (item_group[:, None] == jnp.arange(GROUPS, dtype=jnp.int32)[None, :]).astype(
        jnp.float32
    )
    channels = jnp.dot(chosen, channel_mask.astype(jnp.float32), precision=lax.Precision.HIGHEST)
    masked_series = (series.astype(jnp.float32) * channels[:, None, :]).astype(jnp.bfloat16)
    embedded = enc_in.astype(jnp.float32) + project(masked_series, value_embed)
    enc_hidden = embedded.astype(jnp.bfloat16)
    enc_query = (project(enc_hidden, enc_qkv[0]) + enc_query_bias).astype(jnp.bfloat16)
    enc_key = project(enc_hidden, enc_qkv[1]).astype(jnp.bfloat16)
    enc_value = (project(enc_hidden, enc_qkv[2]) + enc_bias[0]).astype(jnp.bfloat16)
    enc_update = forward_update(
        split_heads(enc_query), tau_scale, enc_pos, False, plain_unpack, enc_rows
    )
    enc_mixed, enc_log = finish_forward(
        enc_update(
            fresh_totals(item_count, enc_rows, head_size),
            (
                lax.all_gather(enc_key, SEQ, axis=1, tiled=True),
                lax.all_gather(enc_value, SEQ, axis=1, tiled=True),
                lax.all_gather(delta_shift, SEQ, axis=1, tiled=True),
            ),
            jnp.int32(0),
        )
    )
    enc_attended = enc_mixed.astype(jnp.bfloat16)
    enc_first_in = embedded + project(enc_attended, enc_out) + enc_bias[1]
    enc_first = layer_norm(enc_first_in, enc_gain[0], enc_bias[3])
    enc_ff_hidden = enc_first.astype(jnp.bfloat16)
    enc_ff_pre = project(enc_ff_hidden, enc_ff_in) + ff_bias[0]
    enc_ff_act = jax.nn.gelu(enc_ff_pre, approximate=False).astype(jnp.bfloat16)
    enc_second_in = enc_first + project(enc_ff_act, enc_ff_out) + enc_bias[2]
    encoded = layer_norm(enc_second_in, enc_gain[1], enc_bias[4])
    memory = encoded.astype(jnp.bfloat16)
    self_query = (project(dec_in, dec_qkv[0]) + dec_bias[0]).astype(jnp.bfloat16)
    self_key = project(dec_in, dec_qkv[1]).astype(jnp.bfloat16)
    self_value = (project(dec_in, dec_qkv[2]) + dec_bias[1]).astype(jnp.bfloat16)
    self_update = forward_update(
        split_heads(self_query), tau_scale, dec_pos, True, self_unpack, dec_rows
    )
    self_mixed, self_log = finish_forward(
        self_update(
            fresh_totals(item_count, dec_rows, head_size),
            (
                lax.all_gather(self_key, SEQ, axis=1, tiled=True),
                lax.all_gather(self_value, SEQ, axis=1, tiled=True),
            ),
            jnp.int32(0),
        )
    )
    self_attended = self_mixed.astype(jnp.bfloat16)
    dec_first_in = dec_in.astype(jnp.float32) + project(self_attended, dec_out) + dec_bias[2]
    dec_first = layer_norm(dec_first_in, dec_gain[0], dec_bias[7])
    cross_hidden = dec_first.astype(jnp.bfloat16)
    cross_query = (project(cross_hidden, cross_qkv[0]) + dec_bias[3]).astype(jnp.bfloat16)
    cross_key = project(memory, cross_qkv[1]).astype(jnp.bfloat16)
    cross_value = (project(memory, cross_qkv[2]) + dec_bias[4]).astype(jnp.bfloat16)
    cross_start = fresh_totals(item_count, dec_rows, head_size)
    cross_update = forward_update(
        split_heads(cross_query), tau_scale, dec_pos, False, plain_unpack, enc_rows
    )
    cross_totals = cross_update(
        cross_start,
        (
            lax.all_gather(cross_key, SEQ, axis=1, tiled=True),
            lax.all_gather(cross_value, SEQ, axis=1, tiled=True),
            lax.all_gather(delta_shift, SEQ, axis=1, tiled=True),
        ),
        jnp.int32(0),
    )
    cross_mixed, cross_log = finish_forward(cross_totals)
    cross_attended = cross_mixed.astype(jnp.bfloat16)
    dec_second_in = dec_first + project(cross_attended, cross_out) + dec_bias[5]
    dec_second = layer_norm(dec_second_in, dec_gain[1], dec_bias[8])
    dec_ff_hidden = dec_second.astype(jnp.bfloat16)
    dec_ff_pre = project(dec_ff_hidden, dec_ff_in) + ff_bias[1]
    dec_ff_act = jax.nn.gelu(dec_ff_pre, approximate=False).astype(jnp.bfloat16)
    dec_third_in = dec_second + project(dec_ff_act, dec_ff_out) + dec_bias[6]
    decoded = layer_norm(dec_third_in, dec_gain[2], dec_bias[9])
    third_grad, dec_gain_three, dec_bias_three = norm_backward(
        dec_third_in, dec_gain[2], dec_bias[9], cotangent.astype(jnp.float32)
    )
    from_dec_ff, dec_ff_in_grad, dec_ff_bias_grad, dec_ff_out_grad, dec_ff_out_bias = (
        feed_forward_back(third_grad, dec_ff_hidden, dec_ff_pre, dec_ff_act, dec_ff_in, dec_ff_out)
    )
    second_grad, dec_gain_two, dec_bias_two = norm_backward(
        dec_second_in, dec_gain[1], dec_bias[8], third_grad + from_dec_ff
    )
    cross_branch_grad = second_grad.astype(jnp.bfloat16)
    cross_out_grad = weight_grad(cross_attended, cross_branch_grad)
    cross_out_bias = row_total(cross_branch_grad)
    cross_mixed_grad = project_back(cross_branch_grad, cross_out).astype(jnp.bfloat16)
    cross_dot = row_products(cross_mixed_grad, cross_mixed)
    cross_query_start = jnp.zeros((item_count, HEADS, dec_rows, head_size), jnp.float32)
    cross_back = query_grad_update(
        split_heads(cross_query),
        split_heads(cross_mixed_grad),
        jnp.transpose(cross_log, (0, 2, 1)),
        jnp.transpose(cross_dot, (0, 2, 1)),
        tau_scale,
        dec_pos,
        False,
        plain_unpack,
        enc_rows,
    )
    cross_query_total = cross_back(
        cross_query_start,
        (
            lax.all_gather(cross_key, SEQ, axis=1, tiled=True),
            lax.all_gather(cross_value, SEQ, axis=1, tiled=True),
            lax.all_gather(delta_shift, SEQ, axis=1, tiled=True),
        ),
        jnp.int32(0),
    )
    cross_query_grad = scaled_grad(cross_query_total, tau_scale)
    cross_key_update = key_grad_update(
        split_heads(cross_key),
        split_heads(cross_value),
        enc_shift,
        tau_scale,
        enc_pos,
        False,
        dec_rows,
    )
    cross_key_start = (
        jnp.zeros((item_count, HEADS, enc_rows, head_size), jnp.float32),
        jnp.zeros((item_count, HEADS, enc_rows, head_size), jnp.float32),
    )
    cross_key_total, cross_value_total = cross_key_update(
        cross_key_start,
        (
            lax.all_gather(cross_query.astype(jnp.float32), SEQ, axis=1, tiled=True),
            lax.all_gather(cross_mixed_grad.astype(jnp.float32), SEQ, axis=1, tiled=True),
            lax.all_gather(cross_log, SEQ, axis=1, tiled=True),
            lax.all_gather(cross_dot, SEQ, axis=1, tiled=True),
        ),
        jnp.int32(0),
    )
    cross_key_grad = scaled_grad(cross_key_total, tau_scale)
    cross_value_grad = merge_heads(cross_value_total).astype(jnp.bfloat16)
    cross_qkv_grad = jnp.stack(
        [
            weight_grad(cross_hidden, cross_query_grad),
            weight_grad(memory, cross_key_grad),
            weight_grad(memory, cross_value_grad),
        ]
    )
    memory_grad = project_back(cross_key_grad, cross_qkv[1]) + project_back(
        cross_value_grad, cross_qkv[2]
    )
    first_grad, dec_gain_one, dec_bias_one = norm_backward(
        dec_first_in,
        dec_gain[0],
        dec_bias[7],
        second_grad + project_back(cross_query_grad, cross_qkv[0]),
    )
    self_branch_grad = first_grad.astype(jnp.bfloat16)
    dec_out_grad = weight_grad(self_attended, self_branch_grad)
    self_out_bias = row_total(self_branch_grad)
    self_mixed_grad = project_back(self_branch_grad, dec_out).astype(jnp.bfloat16)
    self_dot = row_products(self_mixed_grad, self_mixed)
    self_back = query_grad_update(
        split_heads(self_query),
        split_heads(self_mixed_grad),
        jnp.transpose(self_log, (0, 2, 1)),
        jnp.transpose(self_dot, (0, 2, 1)),
        tau_scale,
        dec_pos,
        True,
        self_unpack,
        dec_rows,
    )
    self_query_total = self_back(
        jnp.zeros((item_count, HEADS, dec_rows, head_size), jnp.float32),
        (
            lax.all_gather(self_key, SEQ, axis=1, tiled=True),
            lax.all_gather(self_value, SEQ, axis=1, tiled=True),
        ),
        jnp.int32(0),
    )
    self_query_grad = scaled_grad(self_query_total, tau_scale)
    self_key_update = key_grad_update(
        split_heads(self_key),
        split_heads(self_value),
        jnp.zeros((item_count, dec_rows), jnp.float32),
        tau_scale,
        dec_pos,
        True,
        dec_rows,
    )
    self_key_start = (
        jnp.zeros((item_count, HEADS, dec_rows, head_size), jnp.float32),
        jnp.zeros((item_count, HEADS, dec_rows, head_size), jnp.float32),
    )
    self_key_total, self_value_total = self_key_update(
        self_key_start,
        (
            lax.all_gather(self_query.astype(jnp.float32), SEQ, axis=1, tiled=True),
            lax.all_gather(self_mixed_grad.astype(jnp.float32), SEQ, axis=1, tiled=True),
            lax.all_gather(self_log, SEQ, axis=1, tiled=True),
            lax.all_gather(self_dot, SEQ, axis=1, tiled=True),
        ),
        jnp.int32(0),
    )
    self_key_grad = scaled_grad(self_key_total, tau_scale)
    self_value_grad = merge_heads(self_value_total).astype(jnp.bfloat16)
    dec_qkv_grad = jnp.stack(
        [
            weight_grad(dec_in, self_query_grad),
            weight_grad(dec_in, self_key_grad),
            weight_grad(dec_in, self_value_grad),
        ]
    )
    dec_in_grad = (
        first_grad
        + project_back(self_query_grad, dec_qkv[0])
        + project_back(self_key_grad, dec_qkv[1])
        + project_back(self_value_grad, dec_qkv[2])
    )
    enc_second_grad, enc_gain_two, enc_bias_two = norm_backward(
        enc_second_in, enc_gain[1], enc_bias[4], memory_grad
    )
    from_enc_ff, enc_ff_in_grad, enc_ff_bias_grad, enc_ff_out_grad, enc_ff_out_bias = (
        feed_forward_back(
            enc_second_grad, enc_ff_hidden, enc_ff_pre, enc_ff_act, enc_ff_in, enc_ff_out
        )
    )
    enc_first_grad, enc_gain_one, enc_bias_one = norm_backward(
        enc_first_in, enc_gain[0], enc_bias[3], enc_second_grad + from_enc_ff
    )
    enc_branch_grad = enc_first_grad.astype(jnp.bfloat16)
    enc_out_grad = weight_grad(enc_attended, enc_branch_grad)
    enc_out_bias = row_total(enc_branch_grad)
    enc_mixed_grad = project_back(enc_branch_grad, enc_out).astype(jnp.bfloat16)
    enc_dot = row_products(enc_mixed_grad, enc_mixed)
    enc_back = query_grad_update(
        split_heads(enc_query),
        split_heads(enc_mixed_grad),
        jnp.transpose(enc_log, (0, 2, 1)),
        jnp.transpose(enc_dot, (0, 2, 1)),
        tau_scale,
        enc_pos,
        False,
        plain_unpack,
        enc_rows,
    )
    enc_query_total = enc_back(
        jnp.zeros((item_count, HEADS, enc_rows, head_size), jnp.float32),
        (
            lax.all_gather(enc_key, SEQ, axis=1, tiled=True),
            lax.all_gather(enc_value, SEQ, axis=1, tiled=True),
            lax.all_gather(delta_shift, SEQ, axis=1, tiled=True),
        ),
        jnp.int32(0),
    )
    enc_query_grad = scaled_grad(enc_query_total, tau_scale)
    enc_key_update = key_grad_update(
        split_heads(enc_key), split_heads(enc_value), enc_shift, tau_scale, enc_pos, False, enc_rows
    )
    enc_key_start = (
        jnp.zeros((item_count, HEADS, enc_rows, head_size), jnp.float32),
        jnp.zeros((item_count, HEADS, enc_rows, head_size), jnp.float32),
    )
    enc_key_total, enc_value_total = enc_key_update(
        enc_key_start,
        (
            lax.all_gather(enc_query.astype(jnp.float32), SEQ, axis=1, tiled=True),
            lax.all_gather(enc_mixed_grad.astype(jnp.float32), SEQ, axis=1, tiled=True),
            lax.all_gather(enc_log, SEQ, axis=1, tiled=True),
            lax.all_gather(enc_dot, SEQ, axis=1, tiled=True),
        ),
        jnp.int32(0),
    )
    enc_key_grad = scaled_grad(enc_key_total, tau_scale)
    enc_value_grad = merge_heads(enc_value_total).astype(jnp.bfloat16)
    enc_qkv_grad = jnp.stack(
        [
            weight_grad(enc_hidden, enc_query_grad),
            weight_grad(enc_hidden, enc_key_grad),
            weight_grad(enc_hidden, enc_value_grad),
        ]
    )
    enc_in_grad = (
        enc_first_grad
        + project_back(enc_query_grad, enc_qkv[0])
        + project_back(enc_key_grad, enc_qkv[1])
        + project_back(enc_value_grad, enc_qkv[2])
    )
    embed_grad = weight_grad(masked_series, enc_in_grad.astype(jnp.bfloat16))
    enc_query_bias_grad = row_total(enc_query_grad)
    enc_bias_grad = jnp.stack(
        [row_total(enc_value_grad), enc_out_bias, enc_ff_out_bias, enc_bias_one, enc_bias_two]
    )
    enc_gain_grad = jnp.stack([enc_gain_one, enc_gain_two])
    dec_bias_grad = jnp.stack(
        [
            row_total(self_query_grad),
            row_total(self_value_grad),
            self_out_bias,
            row_total(cross_query_grad),
            row_total(cross_value_grad),
            cross_out_bias,
            dec_ff_out_bias,
            dec_bias_one,
            dec_bias_two,
            dec_bias_three,
        ]
    )
    dec_gain_grad = jnp.stack([dec_gain_one, dec_gain_two, dec_gain_three])
    ff_bias_grad = jnp.stack([enc_ff_bias_grad, dec_ff_bias_grad])
    shares = (
        lax.psum_scatter(embed_grad, SEQ, scatter_dimension=1, tiled=True),
        lax.psum_scatter(enc_qkv_grad, SEQ, scatter_dimension=2, tiled=True),
        lax.psum_scatter(enc_out_grad, SEQ, scatter_dimension=1, tiled=True),
        lax.psum_scatter(enc_ff_in_grad, SEQ, scatter_dimension=1, tiled=True),
        lax.psum_scatter(enc_ff_out_grad, SEQ, scatter_dimension=1, tiled=True),
        lax.psum_scatter(enc_query_bias_grad, SEQ, scatter_dimension=0, tiled=True),
        lax.psum_scatter(enc_bias_grad, SEQ, scatter_dimension=1, tiled=True),
        lax.psum_scatter(enc_gain_grad, SEQ, scatter_dimension=1, tiled=True),
        lax.psum_scatter(dec_qkv_grad, SEQ, scatter_dimension=2, tiled=True),
        lax.psum_scatter(dec_out_grad, SEQ, scatter_dimension=1, tiled=True),
        lax.psum_scatter(cross_qkv_grad, SEQ, scatter_dimension=2, tiled=True),
        lax.psum_scatter(cross_out_grad, SEQ, scatter_dimension=1, tiled=True),
        lax.psum_scatter(dec_ff_in_grad, SEQ, scatter_dimension=1, tiled=True),
        lax.psum_scatter(dec_ff_out_grad, SEQ, scatter_dimension=1, tiled=True),
        lax.psum_scatter(dec_bias_grad, SEQ, scatter_dimension=1, tiled=True),
        lax.psum_scatter(dec_gain_grad, SEQ, scatter_dimension=1, tiled=True),
        lax.psum_scatter(ff_bias_grad, SEQ, scatter_dimension=1, tiled=True),
    )
    summed = lax.psum(
        (
            shares[0],
            shares[1],
            shares[2],
            shares[3],
            shares[4],
            shares[5],
            shares[6],
            shares[7],
            shares[8],
            shares[9],
            shares[10],
            shares[11],
            shares[12],
            shares[13],
            shares[14],
            shares[15],
            shares[16],
        ),
        BATCH,
    )
    return (
        decoded.astype(jnp.bfloat16),
        enc_in_grad,
        dec_in_grad,
        summed[0],
        summed[1],
        summed[2],
        summed[3],
        summed[4],
        summed[5],
        summed[6],
        summed[7],
        summed[8],
        summed[9],
        summed[10],
        summed[11],
        summed[12],
        summed[13],
        summed[14],
        summed[15],
        summed[16],
    )


F32 = jnp.float32
BF16 = jnp.bfloat16
MESH = pl.DeviceIdType.MESH
QUAD = 4
HALVES = 2
CORES = 2
LANES = 128
LINK_COUNT = 81
ITEM_FIRST = (True, False, True, True, False, True, True)
VMEM_BYTES = 60 << 20
LOAD_FIRST = 3
LOAD_ORDER = (
    "value_embed",
    "enc_qkv",
    "dec_qkv",
    "enc_out",
    "enc_ff_in",
    "enc_ff_out",
    "dec_out",
    "cross_qkv",
    "cross_out",
    "dec_ff_in",
    "dec_ff_out",
)


def mm(left, right):
    return jnp.dot(left, right, preferred_element_type=F32)


def mm_right_t(left, right):
    return lax.dot_general(left, right, (((1,), (1,)), ((), ())), preferred_element_type=F32)


def mm_left_t(left, right):
    return lax.dot_general(left, right, (((0,), (0,)), ((), ())), preferred_element_type=F32)


def lane_index(shape):
    return lax.broadcasted_iota(jnp.int32, shape, len(shape) - 1)


def swap_halves(values):
    return pltpu.roll(values, LANES // 2, axis=1)


def low_lanes(first, second):
    return jnp.where(lane_index(first.shape) < LANES // 2, first, second)


def pack_rows(values):
    half = values.shape[0] // 2
    packed = []
    for pair in range(values.shape[1] // LANES):
        group = values[:, pair * LANES : (pair + 1) * LANES]
        top, bottom = group[:half], group[half:]
        packed.append(low_lanes(top, swap_halves(bottom)))
        packed.append(low_lanes(swap_halves(top), bottom))
    return packed


def unpack_rows(packed):
    groups = []
    for pair in range(len(packed) // 2):
        first, second = packed[2 * pair], packed[2 * pair + 1]
        top = low_lanes(first, swap_halves(second))
        bottom = low_lanes(swap_halves(first), second)
        groups.append(jnp.concatenate([top, bottom], axis=0))
    return jnp.concatenate(groups, axis=1)


def pack_pairs(keys, values):
    packed = []
    for pair in range(keys.shape[1] // LANES):
        key_group = keys[:, pair * LANES : (pair + 1) * LANES]
        value_group = values[:, pair * LANES : (pair + 1) * LANES]
        packed.append(low_lanes(key_group, swap_halves(value_group)))
        packed.append(low_lanes(swap_halves(key_group), value_group))
    return packed


def unpack_pairs(packed):
    keys, values = [], []
    for pair in range(len(packed) // 2):
        first, second = packed[2 * pair], packed[2 * pair + 1]
        keys.append(low_lanes(first, swap_halves(second)))
        values.append(low_lanes(swap_halves(first), second))
    return jnp.concatenate(keys, axis=1), jnp.concatenate(values, axis=1)


def norm_forward(values, gain, shift):
    centred = values - jnp.mean(values, axis=-1, keepdims=True)
    scale = lax.rsqrt(jnp.mean(centred * centred, axis=-1, keepdims=True) + epsilon)
    unit = centred * scale
    return unit * gain + shift, unit, scale


def norm_back(upstream, unit, scale, gain):
    inner = upstream * gain
    result = scale * (
        inner
        - jnp.mean(inner, axis=-1, keepdims=True)
        - unit * jnp.mean(inner * unit, axis=-1, keepdims=True)
    )
    return (
        result,
        jnp.sum(upstream * unit, axis=0, keepdims=True),
        jnp.sum(upstream, axis=0, keepdims=True),
    )


def rounded(values):
    return values.astype(BF16).astype(F32)


class View:
    def __init__(self, entries):
        for name, entry in entries.items():
            if isinstance(entry, dict):
                entry = View(entry)
            elif isinstance(entry, (list, tuple)):
                entry = [View(part) if isinstance(part, dict) else part for part in entry]
            setattr(self, name, entry)


class Weight:
    def __init__(self, copy, held):
        self.copy, self.held, self.here = copy, held, False

    def start(self):
        self.copy.start()

    def __call__(self):
        if not self.here:
            self.copy.wait()
            self.here = True
        return self.held


def fused_body(structures, *refs):
    entries = {}
    for structure in structures:
        count = structure.num_leaves
        entries.update(jax.tree.unflatten(structure, refs[:count]))
        refs = refs[count:]
    ref = View(entries)
    small = View(entries["held_blocks"])
    rows, width = ref.enc_in.shape
    hidden, channels, chips = ref.ff_bias.shape[1], ref.series.shape[1], HEADS
    packed_rows = rows // 2
    keys_total = chips * CORES * rows
    block_queries = chips * packed_rows
    column = width // (chips * CORES)
    depth = chips * CORES // QUAD

    place = lax.axis_index(SEQ)
    item = lax.axis_index(BATCH)
    core = lax.rem(place, 2)
    chip = place // 2
    x_place = lax.rem(chip, 2)
    z_place = chip // 2
    quad = lax.rem(place, QUAD)
    core_dev = (chip * 2 + (1 - core), item)
    x_dev = (z_place * QUAD + (1 - x_place) * 2 + core, item)
    diagonal_dev = (z_place * QUAD + (1 - x_place) * 2 + (1 - core), item)
    item_dev = (place, 1 - item)
    z_high, z_odd = z_place // 2, lax.rem(z_place, 2)
    near_dev = ((z_high * 2 + 1 - z_odd) * QUAD + quad, item)
    far_dev = (((1 - z_high) * 2 + z_odd) * QUAD + quad, item)
    x_quad = (1 - x_place) * 2 + core

    def same_core(step):
        peer = lax.rem(chip + step, chips)
        return peer, (peer * 2 + core, item)

    def z_peer(step):
        peer = lax.rem(z_place + step, depth)
        return peer, (peer * QUAD + quad, item)

    barrier = pltpu.get_barrier_semaphore()
    greeted = [core_dev, diagonal_dev, item_dev] + [same_core(step)[1] for step in range(1, chips)]
    for device in greeted:
        pl.semaphore_signal(barrier, inc=1, device_id=device, device_id_type=MESH)

    blocks = []
    for index, (name, target) in enumerate(entries["held_blocks"].items()):
        blocks.append(pltpu.make_async_copy(entries[name], target, ref.block_sem.at[index]))
        blocks[-1].start()
    loaded = {}
    for index, name in enumerate(LOAD_ORDER):
        source, target = getattr(ref.weight, name), getattr(ref.held, name)
        copy = pltpu.make_async_copy(source, target, ref.load_sem.at[index])
        loaded[name] = Weight(copy, target)
    weight = View(loaded)
    for name in LOAD_ORDER[:LOAD_FIRST]:
        loaded[name].start()
    for copy in blocks:
        copy.wait()

    stores = []

    def store(source, target):
        index = len(stores)
        stores.append(pltpu.make_async_copy(source, target, ref.store_sem.at[index]))
        stores[-1].start()

    batches = []

    def ship(copies, meter=None):
        index = len(batches)
        made = []
        for source, target, device in copies:
            made.append(
                pltpu.make_async_remote_copy(
                    src_ref=source,
                    dst_ref=target,
                    send_sem=ref.send_sem.at[index],
                    recv_sem=ref.recv_sem.at[index],
                    device_id=device,
                    device_id_type=MESH,
                )
            )
            made[-1].start()
        batches.append((index, made, meter))
        return batches[-1]

    def send(source, target, device):
        return ship([(source, target, device)])

    def arrive(batch):
        index, made, meter = batch
        if meter is None:
            made[0].wait_recv()
        else:
            pltpu.make_async_copy(meter, meter, ref.recv_sem.at[index]).wait()

    def depart(batch):
        index, made, meter = batch
        if meter is None:
            made[0].wait_send()
        else:
            pltpu.make_async_copy(meter, meter, ref.send_sem.at[index]).wait()

    def spread(source, target_at):
        copies = []
        for step in range(1, chips):
            peer, device = same_core(step)
            copies.append((source.at[peer], target_at(chip), device))
        return ship(copies, source.at[pl.ds(0, chips - 1)])

    def share(block):
        return [
            block,
            send(block.at[quad], block.at[quad], core_dev),
            send(block.at[quad], block.at[quad], x_dev),
        ]

    def relay(shared):
        block = shared[0]
        arrive(shared[2])
        shared.append(send(block.at[x_quad], block.at[x_quad], core_dev))

    def settle(shared):
        arrive(shared[1])
        arrive(shared[3])

    def gathered(block, start, features):
        value = block[:, :, start : start + features]
        return value.reshape(value.shape[0] * value.shape[1], value.shape[2])

    def cut_columns(values, group, start):
        part = lane_index((rows, LANES)) // column
        for member in range(QUAD):
            total = None
            for level in range(depth):
                cut = values[:, level * LANES : (level + 1) * LANES]
                shift = (column * (level - member)) % LANES
                moved = pltpu.roll(cut, shift, axis=1) if shift else cut
                total = moved if total is None else jnp.where(part == level, moved, total)
            group.cut[member, :, start : start + LANES] = total.astype(BF16)

    def share_columns(group, start, stop):
        source, target = group.cut, group.met
        target[quad, :, start:stop] = source[quad, :, start:stop]
        copies = []
        for device, member in (
            (core_dev, x_place * 2 + 1 - core),
            (x_dev, x_quad),
            (diagonal_dev, (1 - x_place) * 2 + 1 - core),
        ):
            copies.append(
                (
                    source.at[member, :, pl.ds(start, stop - start)],
                    target.at[quad, :, pl.ds(start, stop - start)],
                    device,
                )
            )
        return ship(copies, target.at[pl.ds(0, QUAD - 1), :, pl.ds(start, stop - start)])

    def columns_of(group, start, stop):
        value = group.met[:, :, start:stop]
        return value.reshape(QUAD * rows, stop - start)

    def put_rows(target, level, start, values):
        half = target.shape[3]
        count = values.shape[0]
        done = 0
        while done < count:
            which, offset = divmod(start + done, half)
            take = min(count - done, half - offset)
            target[which, level // 2, level % 2, offset : offset + take, :] = values[
                done : done + take, :
            ]
            done += take

    def put_gradient(target, start, gradient):
        count = gradient.shape[0] // depth
        gradient = gradient.astype(BF16)
        short = -gradient.shape[1] % width
        pieces = gradient.shape[1] // width
        for level in range(depth):
            block = gradient[level * count : (level + 1) * count]
            for piece in range(pieces):
                put_rows(
                    target,
                    level,
                    start + piece * count,
                    block[:, piece * width : (piece + 1) * width],
                )
            if short:
                tail = jnp.concatenate(
                    [block[:, pieces * width :], jnp.zeros((count, short), BF16)], axis=1
                )
                put_rows(target, level, start + pieces * count, tail)

    def both_sums(left, right):
        return (left.astype(F32) + right.astype(F32)).astype(BF16)

    def item_first(group):
        def near():
            group.half[...] = both_sums(group.part[item], group.item[...])
            return send(group.half.at[:, 1 - z_odd], group.near, near_dev)

        def far():
            group.pair[...] = both_sums(group.half[:, z_odd], group.near[...])
            return send(group.pair.at[1 - z_high], group.far, far_dev)

        def last():
            group.sum[item] = both_sums(group.pair[z_high], group.far[...])
            return send(group.sum.at[item], group.sum.at[item], item_dev)

        return [lambda: send(group.part.at[1 - item], group.item, item_dev), near, far, last]

    def depth_first(group):
        def far():
            group.pair[...] = both_sums(group.part[0, :, z_odd], group.near[...])
            return send(group.pair.at[1 - z_high], group.far, far_dev)

        def items():
            group.half[...] = both_sums(group.pair[z_high], group.far[...])
            return send(group.half, group.item, item_dev)

        def last():
            group.sum[0] = both_sums(group.half[...], group.item[...])
            return None

        return [
            lambda: send(group.part.at[0, :, 1 - z_odd], group.near, near_dev),
            far,
            items,
            last,
        ]

    def advance(group):
        if group.batch is not None:
            arrive(group.batch)
        group.batch = group.steps.pop(0)()

    def finish(group):
        if group.batch is not None:
            arrive(group.batch)
        store(group.sum, group.result)

    def set_vector(row, value):
        ref.vec[row : row + 1, :] = value

    att_enc, att_self, att_cross = ref.attention
    for group, result, by_item in zip(ref.group, ref.sums, ITEM_FIRST):
        group.result, group.batch = result, None
        group.steps = item_first(group) if by_item else depth_first(group)
    dec_in_part, dec_out_part, cross_part, enc_in_part, enc_out_part, self_part, last_part = (
        ref.group
    )
    enc_ff = (weight.enc_ff_in, weight.enc_ff_out)
    dec_ff = (weight.dec_ff_in, weight.dec_ff_out)

    def build(group, row, start, features, tokens, wide=False):
        gradient = mm_left_t(columns_of(group, start, start + features), tokens)
        if wide:
            put_gradient(group.part, row, gradient)
            return
        for which in range(features // LANES):
            put_gradient(
                group.part,
                row + which * column,
                gradient[which * LANES : (which + 1) * LANES],
            )

    tau = ref.tau_scale[0]
    group_row = lax.broadcasted_iota(jnp.int32, small.channel_mask.shape, 0)
    chosen = jnp.where(
        group_row == ref.item_group[0], small.channel_mask[...].astype(F32), 0.0
    )
    channel_row = jnp.sum(chosen, axis=0, keepdims=True)
    masked = (small.series[...].astype(F32) * channel_row).astype(BF16)
    dec_hidden = small.dec_in[...]
    ref.x_first[quad, :, 0:width] = dec_hidden
    ref.x_first[quad, :, width:] = jnp.zeros((rows, ref.x_first.shape[2] - width), BF16)
    ref.x_first[quad, :, width : width + channels] = masked
    pl.semaphore_wait(barrier, len(greeted))
    share_first = share(ref.x_first)

    shift_row = small.delta_shift[...].astype(F32)
    ref.t_shift[...] = jnp.broadcast_to(
        jnp.concatenate([shift_row, shift_row], axis=1), ref.t_shift.shape
    )

    embedded = small.enc_in[...].astype(F32) + mm(masked, weight.value_embed()[...])
    ref.embedded[...] = embedded
    enc_hidden = embedded.astype(BF16)
    ref.x_enc_hidden[quad] = enc_hidden
    for name in LOAD_ORDER[LOAD_FIRST:]:
        loaded[name].start()

    def send_queries(own, query):
        for head, packed in enumerate(pack_rows(query)):
            own.t_query[head] = packed.astype(BF16)
        own.query[chip] = own.t_query[chip]
        return spread(own.t_query, lambda at: own.query.at[at])

    def send_pairs(own, keys, values):
        for head, packed in enumerate(pack_pairs(keys, values)):
            own.t_pair[head] = packed.astype(BF16)
        own.pair[chip, core] = own.t_pair[chip]
        return spread(own.t_pair, lambda at: own.pair.at[at, core])

    def pass_on(own):
        block = own.pair
        return send(block.at[:, core], block.at[:, core], core_dev)

    qkv = weight.enc_qkv()
    enc_query = mm(enc_hidden, qkv[0]) + small.enc_query_bias[...]
    enc_key = mm(enc_hidden, qkv[1])
    enc_value = mm(enc_hidden, qkv[2]) + small.enc_bias[0:1, :]
    go_enc_pair = send_pairs(att_enc, enc_key, enc_value)
    go_enc_query = send_queries(att_enc, enc_query)
    ref.shift[chip, core] = ref.t_shift[...]
    go_shift = ship(
        [
            (ref.t_shift, ref.shift.at[chip, core], same_core(step)[1])
            for step in range(1, chips)
        ],
        ref.shift.at[pl.ds(0, chips - 1), 0],
    )

    qkv = weight.dec_qkv()
    self_query = mm(dec_hidden, qkv[0]) + small.dec_bias[0:1, :]
    self_key = mm(dec_hidden, qkv[1])
    self_value = mm(dec_hidden, qkv[2]) + small.dec_bias[1:2, :]
    go_self_pair = send_pairs(att_self, self_key, self_value)
    go_self_query = send_queries(att_self, self_query)
    share_enc_hidden = share(ref.x_enc_hidden)

    def attention(own, shifted, causal):
        pairs = own.pair[...].reshape(keys_total, LANES)
        pairs_t = pairs.T
        own.pair_t[...] = pairs_t
        query_t = own.query[...].reshape(block_queries, LANES).astype(F32).T
        zeros = jnp.zeros((LANES // 2, block_queries), F32)
        for half in range(HALVES):
            part = query_t[half * LANES // 2 : (half + 1) * LANES // 2]
            side = jnp.concatenate([part, zeros], axis=0).astype(BF16)
            scores = mm(pairs, side) * (tau * 0.125)
            if shifted:
                moved = ref.shift_columns[...]
                scores = scores + jnp.concatenate([moved] * (block_queries // LANES), axis=1)
            if causal:
                key_at = lax.broadcasted_iota(jnp.int32, scores.shape, 0)
                lane = lane_index(scores.shape)
                query_at = (
                    (lane // packed_rows * 2 + core) * rows
                    + half * packed_rows
                    + lane % packed_rows
                )
                scores = jnp.where(key_at > query_at, masked_score, scores)
            weights = jnp.exp(scores - jnp.max(scores, axis=0, keepdims=True))
            inverse = 1.0 / jnp.sum(weights, axis=0, keepdims=True)
            low_weights = weights.astype(BF16)
            own.weights[half] = low_weights
            own.inverse[half] = jnp.broadcast_to(inverse, (8, block_queries))
            mixed_t = mm(pairs_t, low_weights)[LANES // 2 :] * inverse
            own.mixed_t[half * LANES // 2 : (half + 1) * LANES // 2, :] = mixed_t
        mixed = own.mixed_t[...].T.astype(BF16)
        own.t_mixed[...] = mixed.reshape(chips, packed_rows, LANES)
        own.mixed[chip] = own.t_mixed[chip]
        return spread(own.t_mixed, lambda at: own.mixed.at[at])

    def mixed_rows(own):
        return unpack_rows(
            [own.mixed[head].astype(F32) for head in range(chips)]
        ).astype(BF16)

    arrive(go_enc_pair)
    on_enc = pass_on(att_enc)
    arrive(go_shift)
    on_shift = send(ref.shift.at[:, core], ref.shift.at[:, core], core_dev)
    arrive(go_enc_query)
    arrive(go_self_pair)
    on_self = pass_on(att_self)
    arrive(on_shift)
    for block in range(chips):
        line = low_lanes(ref.shift[block, 0], ref.shift[block, 1])[0:1, :] * 0.125
        ref.shift_columns[block * LANES : (block + 1) * LANES, :] = jnp.broadcast_to(
            line, (LANES, LANES)
        ).T
    arrive(on_enc)
    back_enc = attention(att_enc, True, False)
    arrive(on_self)
    arrive(go_self_query)
    back_self = attention(att_self, False, True)
    relay(share_first)

    def feed_forward(values, weights, bias_row, out_bias, low_at, act_at, slope):
        low = values.astype(BF16)
        low_at[0][quad, :, low_at[1] : low_at[1] + width] = low
        weight_in, weight_out = weights[0](), weights[1]()
        total = out_bias
        for piece in range(hidden // width):
            cut = slice(piece * width, (piece + 1) * width)
            pre = mm(low, weight_in[:, cut]) + small.ff_bias[bias_row : bias_row + 1, cut]
            normal = 0.5 * (1.0 + lax.erf(pre * 0.7071067811865476))
            act = (pre * normal).astype(BF16)
            slope[:, cut] = normal + pre * (
                jnp.exp(pre * pre * -0.5) * 0.3989422804014327
            )
            at = act_at[1] + piece * width
            act_at[0][quad, :, at : at + width] = act
            total = total + mm(act, weight_out[cut, :])
        return total

    def feed_forward_back(upstream, weights, slope, vector_row, group):
        low = upstream.astype(BF16)
        weight_in, weight_out = weights[0](), weights[1]()
        total = None
        for piece in range(hidden // width):
            cut = slice(piece * width, (piece + 1) * width)
            act_grad = mm_right_t(low, weight_out[cut, :])
            pre_grad = (act_grad * slope[:, cut]).astype(BF16)
            sums = jnp.sum(pre_grad.astype(F32), axis=0, keepdims=True)
            for member in range(QUAD):
                at = piece * LANES
                ref.vec[vector_row + member : vector_row + member + 1, at : at + LANES] = sums[
                    :, member * LANES : (member + 1) * LANES
                ]
                group.cut[member, :, at : at + LANES] = pre_grad[
                    :, member * LANES : (member + 1) * LANES
                ]
            more = mm_right_t(pre_grad, weight_in[:, cut])
            total = more if total is None else total + more
        return total

    def save_norm(index, unit, scale):
        ref.unit[index] = unit
        ref.scale[index] = jnp.broadcast_to(scale, (rows, LANES))

    def saved_norm(index):
        return ref.unit[index], ref.scale[index, :, 0:1]

    arrive(back_enc)
    attended = mixed_rows(att_enc)
    ref.x_early[quad, :, 0:width] = attended
    first, unit, scale = norm_forward(
        embedded + mm(attended, weight.enc_out()[...]) + small.enc_bias[1:2, :],
        small.enc_gain[0:1, :],
        small.enc_bias[3:4, :],
    )
    save_norm(0, unit, scale)
    second, unit, scale = norm_forward(
        first + feed_forward(
            first,
            enc_ff,
            0,
            small.enc_bias[2:3, :],
            (ref.x_early, width),
            (ref.x_act, 0),
            ref.enc_slope,
        ),
        small.enc_gain[1:2, :],
        small.enc_bias[4:5, :],
    )
    save_norm(1, unit, scale)
    memory = second.astype(BF16)
    ref.x_early[quad, :, 2 * width : 3 * width] = memory
    qkv = weight.cross_qkv()
    cross_key = mm(memory, qkv[1])
    cross_value = mm(memory, qkv[2]) + small.dec_bias[4:5, :]
    go_cross_pair = send_pairs(att_cross, cross_key, cross_value)

    arrive(back_self)
    attended = mixed_rows(att_self)
    ref.x_early[quad, :, 3 * width : 4 * width] = attended
    first, unit, scale = norm_forward(
        small.dec_in[...].astype(F32)
        + mm(attended, weight.dec_out()[...])
        + small.dec_bias[2:3, :],
        small.dec_gain[0:1, :],
        small.dec_bias[7:8, :],
    )
    save_norm(2, unit, scale)
    ref.first_dec[...] = first
    low = first.astype(BF16)
    ref.x_early[quad, :, 4 * width : 5 * width] = low
    go_cross_query = send_queries(att_cross, mm(low, qkv[0]) + small.dec_bias[3:4, :])
    share_early = share(ref.x_early)

    arrive(go_cross_pair)
    on_cross = pass_on(att_cross)
    arrive(go_cross_query)
    arrive(on_cross)
    back_cross = attention(att_cross, True, False)
    share_act = share(ref.x_act)
    relay(share_enc_hidden)
    arrive(back_cross)
    attended = mixed_rows(att_cross)
    ref.x_late[quad, :, 0:width] = attended
    second, unit, scale = norm_forward(
        ref.first_dec[...]
        + mm(attended, weight.cross_out()[...])
        + small.dec_bias[5:6, :],
        small.dec_gain[1:2, :],
        small.dec_bias[8:9, :],
    )
    save_norm(3, unit, scale)

    forward = feed_forward(
        second,
        dec_ff,
        1,
        small.dec_bias[6:7, :],
        (ref.x_late, width),
        (ref.x_late_act, 0),
        ref.dec_slope,
    )
    third, unit, scale = norm_forward(
        second + forward,
        small.dec_gain[2:3, :],
        small.dec_bias[9:10, :],
    )
    ref.o_dec_result[...] = third.astype(BF16)
    store(ref.o_dec_result, ref.dec_result)

    def norm_step(index, upstream, gain, gain_row, gain_vector, shift_vector):
        unit, scale = saved_norm(index)
        result, gain_grad, shift_grad = norm_back(
            upstream, unit, scale, gain[gain_row : gain_row + 1, :]
        )
        set_vector(gain_vector, gain_grad)
        set_vector(shift_vector, shift_grad)
        return result

    def column_sum(values):
        return jnp.sum(rounded(values), axis=0, keepdims=True)

    third_grad, gain_grad, shift_grad = norm_back(
        small.cotangent[...].astype(F32), unit, scale, small.dec_gain[2:3, :]
    )
    set_vector(20, gain_grad)
    set_vector(17, shift_grad)
    from_ff = feed_forward_back(third_grad, dec_ff, ref.dec_slope, 25, dec_in_part)
    second_grad = norm_step(3, third_grad + from_ff, small.dec_gain, 1, 19, 16)
    ref.second_grad[...] = second_grad

    def send_mixed_grad(own, branch_grad, out_weight):
        mixed_grad = mm_right_t(branch_grad.astype(BF16), out_weight[...])
        for head, packed in enumerate(pack_rows(mixed_grad)):
            own.t_grad[head] = packed.astype(BF16)
        own.grad[chip] = own.t_grad[chip]
        return spread(own.t_grad, lambda at: own.grad.at[at])

    go_cross_grad = send_mixed_grad(att_cross, second_grad, weight.cross_out())
    share_late_act = share(ref.x_late_act)
    ff_width = hidden // QUAD
    cut_columns(third_grad, dec_out_part, 0)
    cut_columns(second_grad, dec_out_part, LANES)
    set_vector(14, column_sum(third_grad))
    set_vector(13, column_sum(second_grad))
    relay(share_early)

    def attention_back(own):
        pairs = own.pair[...].reshape(keys_total, LANES)
        pairs_t = own.pair_t[...]
        queries = own.query[...].reshape(block_queries, LANES).astype(F32)
        grads = own.grad[...].reshape(block_queries, LANES).astype(F32)
        grads_t = grads.T
        zeros = jnp.zeros((LANES // 2, block_queries), F32)
        blank = jnp.zeros_like(queries)
        query_grads = []
        key_total = value_total = None
        for half in range(HALVES):
            cut = slice(half * LANES // 2, (half + 1) * LANES // 2)
            grad_t = grads_t[cut]
            row_dot = jnp.sum(grad_t * own.mixed_t[cut, :], axis=0, keepdims=True)
            side = jnp.concatenate([zeros, grad_t], axis=0).astype(BF16)
            prob_grads = mm(pairs, side)
            probabilities = own.weights[half].astype(F32) * own.inverse[half, 0:1, :]
            score_grads = (probabilities * (prob_grads - row_dot)).astype(BF16)
            query_grads.append(mm(pairs_t, score_grads)[: LANES // 2])
            if half == 0:
                query_side = low_lanes(queries, blank)
                grad_side = low_lanes(blank, swap_halves(grads))
            else:
                query_side = low_lanes(swap_halves(queries), blank)
                grad_side = low_lanes(blank, grads)
            key_part = mm(score_grads, query_side.astype(BF16))
            value_part = mm(probabilities.astype(BF16), grad_side.astype(BF16))
            key_total = key_part if key_total is None else key_total + key_part
            value_total = value_part if value_total is None else value_total + value_part
        factor = tau * 0.125
        query_grad = (jnp.concatenate(query_grads, axis=0) * factor).T.astype(BF16)
        own.t_query_grad[...] = query_grad.reshape(chips, packed_rows, LANES)
        own.query_grad[chip] = own.t_query_grad[chip]
        go_query = spread(
            own.t_query_grad, lambda at: own.query_grad.at[at]
        )
        pair_grad = (key_total * factor + value_total).reshape(chips, CORES, rows, LANES)
        for which in range(CORES):
            own.pair_sum[which] = pair_grad[:, which]
            own.t_part[which] = pair_grad[:, which].astype(BF16)
        exchange = send(own.t_part.at[1 - core], own.part, core_dev)
        return go_query, exchange

    def attention_back_pairs(own, exchange):
        arrive(exchange)
        total = own.pair_sum[core] + own.part[...].astype(F32)
        own.t_pair_grad[...] = total.astype(BF16)
        own.pair_grad[chip] = own.t_pair_grad[chip]
        return spread(own.t_pair_grad, lambda at: own.pair_grad.at[at])

    def query_grad_rows(own):
        return unpack_rows(
            [own.query_grad[head].astype(F32) for head in range(chips)]
        )

    def pair_grad_rows(own):
        return unpack_pairs([own.pair_grad[head].astype(F32) for head in range(chips)])

    arrive(go_cross_grad)
    go_query, exchange = attention_back(att_cross)
    go_pair = attention_back_pairs(att_cross, exchange)
    share_late = share(ref.x_late)
    columns_dec_in = share_columns(dec_in_part, 0, ff_width)
    columns_dec_out = share_columns(dec_out_part, 0, 2 * LANES)
    relay(share_act)

    qkv = weight.cross_qkv()
    arrive(go_query)
    cross_query_grad = query_grad_rows(att_cross)
    first_grad = norm_step(
        2,
        ref.second_grad[...] + mm_right_t(cross_query_grad.astype(BF16), qkv[0]),
        small.dec_gain,
        0,
        18,
        15,
    )
    ref.first_grad[...] = first_grad
    go_self_grad = send_mixed_grad(att_self, first_grad, weight.dec_out())
    set_vector(10, column_sum(first_grad))

    arrive(go_pair)
    cross_key_grad, cross_value_grad = pair_grad_rows(att_cross)
    memory_grad = mm_right_t(cross_key_grad.astype(BF16), qkv[1]) + mm_right_t(
        cross_value_grad.astype(BF16), qkv[2]
    )
    enc_second_grad = norm_step(1, memory_grad, small.enc_gain, 1, 7, 5)
    from_ff = feed_forward_back(enc_second_grad, enc_ff, ref.enc_slope, 21, enc_in_part)
    enc_first_grad = norm_step(0, enc_second_grad + from_ff, small.enc_gain, 0, 6, 4)
    ref.enc_first_grad[...] = enc_first_grad
    go_enc_grad = send_mixed_grad(att_enc, enc_first_grad, weight.enc_out())
    set_vector(3, column_sum(enc_second_grad))
    set_vector(2, column_sum(enc_first_grad))
    set_vector(11, column_sum(cross_query_grad))
    set_vector(12, column_sum(cross_value_grad))
    for row in (0, 1, 8, 9, 29, 30, 31):
        set_vector(row, jnp.zeros((1, width), F32))
    vec_item = send(ref.vec, ref.vec_item, item_dev)
    columns_enc_in = share_columns(enc_in_part, 0, ff_width)
    cut_columns(enc_second_grad, enc_out_part, 0)
    cut_columns(enc_first_grad, enc_out_part, LANES)
    columns_enc_out = share_columns(enc_out_part, 0, 2 * LANES)
    for index, values in enumerate(
        (cross_query_grad, cross_key_grad, cross_value_grad, first_grad)
    ):
        cut_columns(values, cross_part, index * LANES)
    columns_cross = share_columns(cross_part, 0, 4 * LANES)
    relay(share_late_act)
    relay(share_late)

    settle(share_late)
    arrive(columns_dec_in)
    build(dec_in_part, 0, 0, ff_width, gathered(ref.x_late, width, width), wide=True)
    advance(dec_in_part)
    settle(share_late_act)
    arrive(columns_dec_out)
    build(dec_out_part, 0, 0, LANES, gathered(ref.x_late_act, 0, hidden))
    build(dec_out_part, LANES, LANES, LANES, gathered(ref.x_late, 0, width))
    advance(dec_out_part)

    arrive(go_self_grad)
    go_self_query_grad, exchange_self = attention_back(att_self)
    arrive(go_enc_grad)
    go_enc_query_grad, exchange_enc = attention_back(att_enc)
    go_enc_pair_grad = attention_back_pairs(att_enc, exchange_enc)
    go_self_pair_grad = attention_back_pairs(att_self, exchange_self)
    advance(dec_in_part)

    settle(share_early)
    settle(share_act)
    arrive(columns_enc_in)
    build(enc_in_part, 0, 0, ff_width, gathered(ref.x_early, width, width), wide=True)
    advance(enc_in_part)
    advance(dec_out_part)
    arrive(columns_enc_out)
    build(enc_out_part, 0, 0, LANES, gathered(ref.x_act, 0, hidden))
    build(enc_out_part, LANES, LANES, LANES, gathered(ref.x_early, 0, width))
    advance(enc_out_part)
    arrive(columns_cross)
    build(cross_part, 0, 0, LANES, gathered(ref.x_early, 4 * width, width))
    build(cross_part, column, LANES, 2 * LANES, gathered(ref.x_early, 2 * width, width))
    build(cross_part, 3 * column, 3 * LANES, LANES, gathered(ref.x_early, 3 * width, width))
    advance(cross_part)
    arrive(vec_item)
    ref.vec_a[...] = ref.vec[...] + ref.vec_item[...]
    vec_core = send(ref.vec_a, ref.vec_core, core_dev)

    def input_grad(own, weights, first):
        query_grad = query_grad_rows(own)
        key_grad, value_grad = pair_grad_rows(own)
        total = (
            first[...]
            + mm_right_t(query_grad.astype(BF16), weights[0])
            + mm_right_t(key_grad.astype(BF16), weights[1])
            + mm_right_t(value_grad.astype(BF16), weights[2])
        )
        return total, query_grad, key_grad, value_grad

    arrive(go_enc_query_grad)
    arrive(go_enc_pair_grad)
    total, query_grad, key_grad, value_grad = input_grad(
        att_enc, weight.enc_qkv(), ref.enc_first_grad
    )
    ref.o_enc_grad[...] = total
    store(ref.o_enc_grad, ref.enc_grad)
    for index, values in enumerate((query_grad, key_grad, value_grad, total)):
        cut_columns(values, last_part, index * LANES)
    columns_last = share_columns(last_part, 0, 4 * LANES)
    arrive(vec_core)
    ref.vec_b[...] = ref.vec_a[...] + ref.vec_core[...]
    vec_x = send(ref.vec_b, ref.vec_x, x_dev)
    arrive(go_self_query_grad)
    arrive(go_self_pair_grad)
    total, query_grad, key_grad, value_grad = input_grad(
        att_self, weight.dec_qkv(), ref.first_grad
    )
    ref.o_dec_grad[...] = total
    store(ref.o_dec_grad, ref.dec_grad)
    for index, values in enumerate((query_grad, key_grad, value_grad)):
        cut_columns(values, self_part, index * LANES)
    columns_self = share_columns(self_part, 0, 3 * LANES)
    advance(dec_in_part)
    settle(share_first)
    settle(share_enc_hidden)
    arrive(columns_last)
    build(last_part, 0, 0, 3 * LANES, gathered(ref.x_enc_hidden, 0, width))
    build(
        last_part,
        3 * column,
        3 * LANES,
        LANES,
        gathered(ref.x_first, width, ref.x_first.shape[2] - width),
    )
    arrive(columns_self)
    build(self_part, 0, 0, 3 * LANES, gathered(ref.x_first, 0, width))
    totals = [
        jnp.sum(
            columns_of(group, index * LANES, (index + 1) * LANES).astype(F32),
            axis=0,
            keepdims=True,
        )
        for group, index in ((self_part, 0), (self_part, 2), (last_part, 0), (last_part, 2))
    ]
    totals = jnp.concatenate(totals + [jnp.zeros((column - 4, LANES), F32)], axis=0)
    totals = jnp.concatenate([totals, jnp.zeros((column, width - LANES), F32)], axis=1)
    for level in range(depth):
        put_rows(last_part.part, level, 5 * column, totals.astype(BF16))
    advance(last_part)
    advance(enc_in_part)
    advance(self_part)
    advance(dec_out_part)
    arrive(vec_x)
    ref.vec_c[...] = ref.vec_b[...] + ref.vec_x[...]
    copies = []
    for step in range(1, depth):
        peer, device = z_peer(step)
        lanes = pl.ds(pl.multiple_of(peer * LANES, LANES), LANES)
        copies.append((ref.vec_c.at[:, lanes], ref.vec_depth.at[step - 1], device))
    vec_depth = ship(copies, ref.vec_depth)
    advance(enc_out_part)
    advance(cross_part)
    advance(dec_in_part)
    advance(enc_in_part)
    advance(last_part)
    advance(cross_part)
    advance(enc_out_part)
    advance(self_part)
    advance(enc_in_part)
    arrive(vec_depth)
    lanes = pl.ds(pl.multiple_of(z_place * LANES, LANES), LANES)
    total = ref.vec_c[:, lanes]
    for step in range(1, depth):
        total = total + ref.vec_depth[step - 1]
    ref.o_vectors[...] = total
    store(ref.o_vectors, ref.vectors)
    advance(dec_out_part)
    finish(dec_out_part)
    advance(last_part)
    finish(dec_in_part)
    advance(cross_part)
    advance(self_part)
    advance(enc_out_part)
    finish(enc_out_part)
    finish(enc_in_part)
    advance(last_part)
    finish(cross_part)
    advance(self_part)
    finish(last_part)
    finish(self_part)
    for copy in stores:
        copy.wait()
    for batch in batches:
        depart(batch)
    if len(batches) != LINK_COUNT:
        raise ValueError(len(batches))


def finish_body(*refs):
    (
        dec_in,
        enc_grad_in,
        dec_grad_in,
        ff_in_two,
        ff_out_two,
        cross,
        ff_in_one,
        ff_out_one,
        self_part,
        last,
        vectors,
        dec_out,
        enc_grad,
        dec_grad,
        g_embed,
        g_enc_qkv,
        g_enc_out,
        g_enc_ff_in,
        g_enc_ff_out,
        g_enc_query_bias,
        g_enc_bias,
        g_enc_gain,
        g_dec_qkv,
        g_dec_out,
        g_cross_qkv,
        g_cross_out,
        g_dec_ff_in,
        g_dec_ff_out,
        g_dec_bias,
        g_dec_gain,
        g_ff_bias,
    ) = refs
    place = lax.axis_index(SEQ)
    column, width = g_enc_out.shape
    channels = g_embed.shape[1]
    member = lax.rem(place, QUAD)
    dec_out[...] = dec_in[...]
    enc_grad[...] = enc_grad_in[...]
    dec_grad[...] = dec_grad_in[...]

    def whole(block):
        value = block[...]
        return value.reshape(value.shape[0] * value.shape[1], value.shape[2]).astype(F32)

    def narrow(target, block, start):
        for piece in range(target.shape[1] // width):
            target[:, piece * width : (piece + 1) * width] = block[
                start + piece * column : start + (piece + 1) * column
            ]

    g_dec_ff_in[...] = whole(ff_in_two).T
    block = whole(ff_out_two)
    narrow(g_dec_ff_out, block, 0)
    narrow(g_cross_out, block, LANES)
    block = whole(cross)
    for index in range(3):
        g_cross_qkv[index] = block[index * column : (index + 1) * column]
    narrow(g_dec_out, block, 3 * column)
    g_enc_ff_in[...] = whole(ff_in_one).T
    block = whole(ff_out_one)
    narrow(g_enc_ff_out, block, 0)
    narrow(g_enc_out, block, LANES)
    block = whole(self_part)
    for index in range(3):
        g_dec_qkv[index] = block[index * column : (index + 1) * column]
    block = whole(last)
    for index in range(3):
        g_enc_qkv[index] = block[index * column : (index + 1) * column]
    g_embed[:, 0:width] = block[3 * column : 4 * column]
    g_embed[:, width:channels] = block[4 * column : 5 * column, 0 : channels - width]
    late = block[5 * column : 5 * column + 8, 0:LANES]
    level = place // QUAD
    late = pltpu.roll(late, lax.rem(LANES - level * column, LANES), axis=1)[:, 0:column]

    values = vectors[...]
    moved = pltpu.roll(values, lax.rem(LANES - member * column, LANES), axis=1)
    rows = moved[:, 0:column]
    g_enc_query_bias[...] = late[2:3]
    g_enc_bias[...] = jnp.concatenate([late[3:4], rows[2:6]], axis=0)
    g_enc_gain[...] = rows[6:8]
    g_dec_bias[...] = jnp.concatenate(
        [late[0:2], rows[10:18]], axis=0
    )
    g_dec_gain[...] = rows[18:21]
    row_index = lax.broadcasted_iota(jnp.int32, values.shape, 0)
    for index in range(2):
        chosen = jnp.where(row_index == 21 + QUAD * index + member, values, 0.0)
        g_ff_bias[index : index + 1, :] = jnp.sum(chosen, axis=0, keepdims=True)


def fused_local(
    enc_in,
    series,
    channel_mask,
    item_group,
    tau_scale,
    delta_shift,
    dec_in,
    value_embed,
    enc_qkv,
    enc_out,
    enc_ff_in,
    enc_ff_out,
    enc_query_bias,
    enc_bias,
    enc_gain,
    dec_qkv,
    dec_out,
    cross_qkv,
    cross_out,
    dec_ff_in,
    dec_ff_out,
    dec_bias,
    dec_gain,
    ff_bias,
    cotangent,
):
    rows, width = enc_in.shape[1:]
    hidden = enc_ff_in.shape[1]
    channels = value_embed.shape[0]
    chips = HEADS
    column = width // (chips * CORES)
    depth = chips * CORES // QUAD
    padded = -(-channels // LANES) * LANES
    keys_total = chips * CORES * rows
    queries = chips * rows // 2
    in_smem = pl.BlockSpec(memory_space=pltpu.SMEM)
    in_vmem = pl.BlockSpec(memory_space=pltpu.VMEM)
    anywhere = pl.BlockSpec(memory_space=pl.ANY)

    weights = dict(
        value_embed=value_embed,
        enc_qkv=enc_qkv,
        enc_out=enc_out,
        enc_ff_in=enc_ff_in,
        enc_ff_out=enc_ff_out,
        dec_qkv=dec_qkv,
        dec_out=dec_out,
        cross_qkv=cross_qkv,
        cross_out=cross_out,
        dec_ff_in=dec_ff_in,
        dec_ff_out=dec_ff_out,
    )
    scalars = dict(item_group=item_group, tau_scale=tau_scale)
    blocks = dict(
        enc_in=enc_in[0],
        series=series[0],
        channel_mask=channel_mask,
        delta_shift=delta_shift,
        dec_in=dec_in[0],
        cotangent=cotangent[0],
        enc_query_bias=enc_query_bias[None],
        enc_bias=enc_bias,
        enc_gain=enc_gain,
        dec_bias=dec_bias,
        dec_gain=dec_gain,
        ff_bias=ff_bias,
    )
    inputs = (scalars, blocks, dict(weight=weights))
    in_specs = [in_smem] * len(scalars) + [anywhere] * (len(blocks) + len(weights))

    def low(*shape):
        return pltpu.VMEM(shape, BF16)

    def full(*shape):
        return pltpu.VMEM(shape, F32)

    def exchanged(features):
        return low(QUAD, rows, features)

    def attention_space():
        packed = low(chips, rows // 2, LANES)
        paired = low(chips, rows, LANES)
        both = low(chips, CORES, rows, LANES)
        return dict(
            query=packed,
            t_query=packed,
            mixed=packed,
            t_mixed=packed,
            grad=packed,
            t_grad=packed,
            query_grad=packed,
            t_query_grad=packed,
            t_pair=paired,
            pair=both,
            t_pair_grad=paired,
            pair_grad=paired,
            t_part=low(CORES, chips, rows, LANES),
            part=paired,
            pair_sum=full(CORES, chips, rows, LANES),
            pair_t=low(LANES, keys_total),
            weights=low(HALVES, keys_total, queries),
            inverse=full(HALVES, 8, queries),
            mixed_t=full(LANES, queries),
        )

    def group_space(count, features, by_item):
        halves = 2 if by_item else 1
        half = count // halves
        return dict(
            cut=exchanged(features),
            met=exchanged(features),
            part=low(halves, 2, 2, half, width),
            item=low(2, 2, half, width) if by_item else low(half, width),
            half=low(2, 2, half, width) if by_item else low(half, width),
            near=low(2, half, width),
            pair=low(2, half, width),
            far=low(half, width),
            sum=low(halves, half, width),
        )

    ff_width = hidden // QUAD
    group_rows = (
        LANES,
        LANES + column,
        4 * column,
        LANES,
        LANES + column,
        3 * column,
        6 * column,
    )
    group_features = (
        ff_width,
        2 * LANES,
        4 * LANES,
        ff_width,
        2 * LANES,
        3 * LANES,
        4 * LANES,
    )
    scratch = dict(
        held={name: low(*value.shape) for name, value in weights.items()},
        held_blocks={
            name: pltpu.VMEM(value.shape, value.dtype) for name, value in blocks.items()
        },
        block_sem=pltpu.SemaphoreType.DMA((len(blocks),)),
        store_sem=pltpu.SemaphoreType.DMA((4 + len(group_rows),)),
        o_dec_result=low(rows, width),
        o_enc_grad=full(rows, width),
        o_dec_grad=full(rows, width),
        o_vectors=full(32, LANES),
        x_first=exchanged(width + padded),
        x_enc_hidden=exchanged(width),
        x_early=exchanged(5 * width),
        x_act=exchanged(hidden),
        x_late=exchanged(2 * width),
        x_late_act=exchanged(hidden),
        enc_slope=full(rows, hidden),
        dec_slope=full(rows, hidden),
        attention=[attention_space() for index in range(3)],
        group=[group_space(*sizes) for sizes in zip(group_rows, group_features, ITEM_FIRST)],
        t_shift=full(8, LANES),
        shift=full(chips, CORES, 8, LANES),
        shift_columns=full(keys_total, LANES),
        embedded=full(rows, width),
        first_dec=full(rows, width),
        second_grad=full(rows, width),
        first_grad=full(rows, width),
        enc_first_grad=full(rows, width),
        unit=full(4, rows, width),
        scale=full(4, rows, LANES),
        vec=full(32, width),
        vec_item=full(32, width),
        vec_a=full(32, width),
        vec_core=full(32, width),
        vec_b=full(32, width),
        vec_x=full(32, width),
        vec_c=full(32, width),
        vec_depth=full(depth - 1, 32, LANES),
        load_sem=pltpu.SemaphoreType.DMA((len(weights),)),
        send_sem=pltpu.SemaphoreType.DMA((LINK_COUNT,)),
        recv_sem=pltpu.SemaphoreType.DMA((LINK_COUNT,)),
    )
    outputs = dict(
        dec_result=jax.ShapeDtypeStruct((rows, width), BF16),
        enc_grad=jax.ShapeDtypeStruct((rows, width), F32),
        dec_grad=jax.ShapeDtypeStruct((rows, width), F32),
        sums=[
            jax.ShapeDtypeStruct((2, count // 2, width) if by_item else (1, count, width), BF16)
            for count, by_item in zip(group_rows, ITEM_FIRST)
        ],
        vectors=jax.ShapeDtypeStruct((32, LANES), F32),
    )
    out_shapes, out_structure = jax.tree.flatten(outputs)
    scratch_shapes, scratch_structure = jax.tree.flatten(scratch)
    operands = jax.tree.leaves(inputs)
    structures = [jax.tree.structure(part) for part in inputs]
    results = pl.pallas_call(
        partial(fused_body, structures + [out_structure, scratch_structure]),
        out_shape=out_shapes,
        in_specs=in_specs,
        out_specs=[anywhere] * len(out_shapes),
        scratch_shapes=scratch_shapes,
        compiler_params=pltpu.CompilerParams(
            collective_id=1, has_side_effects=True, vmem_limit_bytes=VMEM_BYTES
        ),
        name="layers",
    )(*operands)
    results = jax.tree.unflatten(out_structure, results)
    results = [
        results[key] for key in ("dec_result", "enc_grad", "dec_grad")
    ] + results["sums"] + [results["vectors"]]

    final = [
        (rows, width),
        (rows, width),
        (rows, width),
        (column, channels),
        (3, column, width),
        (column, width),
        (width, hidden // (chips * CORES)),
        (column, hidden),
        (1, column),
        (5, column),
        (2, column),
        (3, column, width),
        (column, width),
        (3, column, width),
        (column, width),
        (width, hidden // (chips * CORES)),
        (column, hidden),
        (10, column),
        (3, column),
        (2, hidden // (chips * CORES)),
    ]
    outputs = pl.pallas_call(
        finish_body,
        out_shape=[
            jax.ShapeDtypeStruct(shape, BF16 if index == 0 else F32)
            for index, shape in enumerate(final)
        ],
        in_specs=[in_vmem] * len(results),
        out_specs=[in_vmem] * len(final),
        compiler_params=pltpu.CompilerParams(vmem_limit_bytes=VMEM_BYTES),
        name="columns",
    )(*results)
    outputs = list(outputs)
    for index in range(3):
        outputs[index] = outputs[index][None]
    outputs[8] = outputs[8][0]
    for index in (3, 4, 5, 7, 11, 12, 13, 14, 16):
        outputs[index] = jnp.swapaxes(outputs[index], -1, -2)
    return tuple(outputs)


def solution(mesh):
    in_specs = (
        P(BATCH, SEQ, None),
        P(BATCH, SEQ, None),
        P(),
        P(BATCH),
        P(BATCH),
        P(BATCH, SEQ),
        P(BATCH, SEQ, None),
        P(),
        P(),
        P(),
        P(),
        P(),
        P(),
        P(),
        P(),
        P(),
        P(),
        P(),
        P(),
        P(),
        P(),
        P(),
        P(),
        P(),
        P(BATCH, SEQ, None),
    )
    out_specs = (
        P(BATCH, SEQ, None),
        P(BATCH, SEQ, None),
        P(BATCH, SEQ, None),
        P(None, SEQ),
        P(None, None, SEQ),
        P(None, SEQ),
        P(None, SEQ),
        P(None, SEQ),
        P(SEQ),
        P(None, SEQ),
        P(None, SEQ),
        P(None, None, SEQ),
        P(None, SEQ),
        P(None, None, SEQ),
        P(None, SEQ),
        P(None, SEQ),
        P(None, SEQ),
        P(None, SEQ),
        P(None, SEQ),
        P(None, SEQ),
    )
    fits = mesh.shape[SEQ] == HEADS * CORES and mesh.shape[BATCH] == 2
    return jax.shard_map(
        fused_local if fits else local, mesh=mesh, in_specs=in_specs, out_specs=out_specs, check_vma=False)
```

```python
from functools import partial
import math

import jax
import jax.numpy as jnp
from jax import lax
from jax.experimental import pallas as pl
from jax.experimental.pallas import tpu as pltpu
from jax.sharding import PartitionSpec as P

HEADS = 8
GROUPS = 16
SEQ = "seq"
BATCH = "batch"


epsilon = 1e-05
masked_score = -1e30


def layer_norm(inputs, gain_vector, shift_vector):
    average = jnp.mean(inputs, axis=-1, keepdims=True)
    centred = inputs - average
    variance = jnp.mean(centred * centred, axis=-1, keepdims=True)
    return centred * lax.rsqrt(variance + epsilon) * gain_vector + shift_vector


def norm_backward(inputs, gain_vector, shift_vector, upstream):
    ignored, pullback = jax.vjp(layer_norm, inputs, gain_vector, shift_vector)
    return pullback(upstream)


def project(inputs, weight_matrix):
    return jnp.dot(inputs, weight_matrix, preferred_element_type=jnp.float32)


def project_back(gradient, weight_matrix):
    return jnp.einsum("ilf,kf->ilk", gradient, weight_matrix, preferred_element_type=jnp.float32)


def weight_grad(inputs, gradient):
    return jnp.einsum("ilk,ilf->kf", inputs, gradient, preferred_element_type=jnp.float32)


def row_total(gradient):
    return jnp.sum(gradient.astype(jnp.float32), axis=(0, 1))


def split_heads(values):
    return values.reshape(values.shape[:2] + (HEADS, values.shape[2] // HEADS))


def merge_heads(head_values):
    return jnp.transpose(head_values, (0, 2, 1, 3)).reshape(
        head_values.shape[0], head_values.shape[2], -1
    )


def over_blocks(update, totals, arrays, shard_rows):
    length = arrays[0].shape[1]
    block_rows = shard_rows * math.gcd(length // shard_rows, 8)
    block_count = length // block_rows
    stacked = tuple(
        (
            jnp.moveaxis(
                member.reshape((member.shape[0], block_count, block_rows) + member.shape[2:]), 1, 0
            )
            for member in arrays
        )
    )
    offsets = jnp.arange(block_count, dtype=jnp.int32) * block_rows

    def advance(running, inputs):
        return (update(running, inputs[0], inputs[1]), None)

    totals, ignored = lax.scan(advance, totals, (stacked, offsets))
    return totals


def head_scores(query_heads, key_heads, tau_value, key_shift):
    raw_scores = jnp.einsum(
        "iqhd,ikhd->ihqk", query_heads, key_heads, preferred_element_type=jnp.float32
    )
    return (tau_value[:, None, None, None] * raw_scores + key_shift[:, None, None, :]) * 0.125


def causal_mask(scores, query_pos, key_pos):
    allowed = query_pos[:, None] >= key_pos[None, :]
    return jnp.where(allowed[None, None], scores, masked_score)


def fresh_totals(item_count, row_count, head_size):
    return (
        jnp.full((item_count, HEADS, row_count), masked_score, jnp.float32),
        jnp.zeros((item_count, HEADS, row_count), jnp.float32),
        jnp.zeros((item_count, HEADS, row_count, head_size), jnp.float32),
    )


def finish_forward(totals):
    running_max, running_sum, weighted = totals
    output = merge_heads(weighted / running_sum[..., None])
    log_total = jnp.transpose(running_max + jnp.log(running_sum), (0, 2, 1))
    return (output, log_total)


def row_products(grad_rows, mixed_rows):
    return jnp.sum(split_heads(grad_rows).astype(jnp.float32) * split_heads(mixed_rows), axis=-1)


def scaled_grad(head_totals, tau_value):
    return merge_heads(head_totals * (tau_value * 0.125)[:, None, None, None]).astype(jnp.bfloat16)


def plain_unpack(fetched):
    return (fetched[0], fetched[1], fetched[2].astype(jnp.float32))


def self_unpack(fetched):
    return (fetched[0], fetched[1], jnp.zeros(fetched[0].shape[:2], jnp.float32))


def forward_update(query_heads, tau_value, query_pos, causal, unpack, shard_rows):

    def update(totals, fetched, offset):

        def block_update(running, piece_parts, inner_offset):
            running_max, running_sum, weighted = running
            key_rows, value_rows, key_shift = unpack(piece_parts)
            scores = head_scores(query_heads, split_heads(key_rows), tau_value, key_shift)
            if causal:
                key_pos = inner_offset + jnp.arange(key_rows.shape[1], dtype=jnp.int32)
                scores = causal_mask(scores, query_pos, key_pos)
            new_max = jnp.maximum(running_max, jnp.max(scores, axis=-1))
            factor = jnp.exp(running_max - new_max)
            weights = jnp.exp(scores - new_max[..., None])
            new_sum = running_sum * factor + jnp.sum(weights, axis=-1)
            mixed_values = jnp.einsum(
                "ihqk,ikhd->ihqd",
                weights,
                split_heads(value_rows).astype(jnp.float32),
                preferred_element_type=jnp.float32,
            )
            return (new_max, new_sum, weighted * factor[..., None] + mixed_values)

        return over_blocks(block_update, totals, fetched, shard_rows)

    return update


def query_grad_update(
    query_heads, grad_heads, log_total, row_dot, tau_value, query_pos, causal, unpack, shard_rows
):

    def update(totals, fetched, offset):

        def block_update(running, piece_parts, inner_offset):
            key_rows, value_rows, key_shift = unpack(piece_parts)
            key_heads = split_heads(key_rows)
            scores = head_scores(query_heads, key_heads, tau_value, key_shift)
            if causal:
                key_pos = inner_offset + jnp.arange(key_rows.shape[1], dtype=jnp.int32)
                scores = causal_mask(scores, query_pos, key_pos)
            probabilities = jnp.exp(scores - log_total[..., None])
            prob_grads = jnp.einsum(
                "iqhd,ikhd->ihqk",
                grad_heads,
                split_heads(value_rows),
                preferred_element_type=jnp.float32,
            )
            score_grads = (probabilities * (prob_grads - row_dot[..., None])).astype(jnp.bfloat16)
            return running + jnp.einsum(
                "ihqk,ikhd->ihqd", score_grads, key_heads, preferred_element_type=jnp.float32
            )

        return over_blocks(block_update, totals, fetched, shard_rows)

    return update


def key_grad_update(key_heads, value_heads, key_shift, tau_value, key_pos, causal, shard_rows):

    def update(totals, fetched, offset):

        def block_update(running, piece_parts, inner_offset):
            key_total, value_total = running
            query_heads = split_heads(piece_parts[0].astype(jnp.bfloat16))
            grad_heads = split_heads(piece_parts[1].astype(jnp.bfloat16))
            log_rows = jnp.transpose(piece_parts[2], (0, 2, 1))
            dot_rows = jnp.transpose(piece_parts[3], (0, 2, 1))
            scores = head_scores(query_heads, key_heads, tau_value, key_shift)
            if causal:
                query_pos = inner_offset + jnp.arange(piece_parts[0].shape[1], dtype=jnp.int32)
                scores = causal_mask(scores, query_pos, key_pos)
            probabilities = jnp.exp(scores - log_rows[..., None])
            value_total = value_total + jnp.einsum(
                "ihqk,iqhd->ihkd",
                probabilities,
                grad_heads.astype(jnp.float32),
                preferred_element_type=jnp.float32,
            )
            prob_grads = jnp.einsum(
                "iqhd,ikhd->ihqk", grad_heads, value_heads, preferred_element_type=jnp.float32
            )
            score_grads = (probabilities * (prob_grads - dot_rows[..., None])).astype(jnp.bfloat16)
            key_total = key_total + jnp.einsum(
                "ihqk,iqhd->ihkd", score_grads, query_heads, preferred_element_type=jnp.float32
            )
            return (key_total, value_total)

        return over_blocks(block_update, totals, fetched, shard_rows)

    return update


def feed_forward_back(upstream, hidden, pre_act, activated, weight_in, weight_out):
    out_grad = upstream.astype(jnp.bfloat16)
    out_weight_grad = weight_grad(activated, out_grad)
    out_bias_grad = row_total(out_grad)
    act_grad = project_back(out_grad, weight_out)
    ignored, gelu_back = jax.vjp(partial(jax.nn.gelu, approximate=False), pre_act)
    pre_grad = gelu_back(act_grad)[0].astype(jnp.bfloat16)
    return (
        project_back(pre_grad, weight_in),
        weight_grad(hidden, pre_grad),
        row_total(pre_grad),
        out_weight_grad,
        out_bias_grad,
    )


def local(
    enc_in,
    series,
    channel_mask,
    item_group,
    tau_scale,
    delta_shift,
    dec_in,
    value_embed,
    enc_qkv,
    enc_out,
    enc_ff_in,
    enc_ff_out,
    enc_query_bias,
    enc_bias,
    enc_gain,
    dec_qkv,
    dec_out,
    cross_qkv,
    cross_out,
    dec_ff_in,
    dec_ff_out,
    dec_bias,
    dec_gain,
    ff_bias,
    cotangent,
):
    item_count, enc_rows, width = enc_in.shape
    dec_rows = dec_in.shape[1]
    head_size = width // HEADS
    seq_index = lax.axis_index(SEQ)
    enc_pos = seq_index * enc_rows + jnp.arange(enc_rows, dtype=jnp.int32)
    dec_pos = seq_index * dec_rows + jnp.arange(dec_rows, dtype=jnp.int32)
    enc_shift = delta_shift.astype(jnp.float32)
    chosen = (item_group[:, None] == jnp.arange(GROUPS, dtype=jnp.int32)[None, :]).astype(
        jnp.float32
    )
    channels = jnp.dot(chosen, channel_mask.astype(jnp.float32), precision=lax.Precision.HIGHEST)
    masked_series = (series.astype(jnp.float32) * channels[:, None, :]).astype(jnp.bfloat16)
    embedded = enc_in.astype(jnp.float32) + project(masked_series, value_embed)
    enc_hidden = embedded.astype(jnp.bfloat16)
    enc_query = (project(enc_hidden, enc_qkv[0]) + enc_query_bias).astype(jnp.bfloat16)
    enc_key = project(enc_hidden, enc_qkv[1]).astype(jnp.bfloat16)
    enc_value = (project(enc_hidden, enc_qkv[2]) + enc_bias[0]).astype(jnp.bfloat16)
    enc_update = forward_update(
        split_heads(enc_query), tau_scale, enc_pos, False, plain_unpack, enc_rows
    )
    enc_mixed, enc_log = finish_forward(
        enc_update(
            fresh_totals(item_count, enc_rows, head_size),
            (
                lax.all_gather(enc_key, SEQ, axis=1, tiled=True),
                lax.all_gather(enc_value, SEQ, axis=1, tiled=True),
                lax.all_gather(delta_shift, SEQ, axis=1, tiled=True),
            ),
            jnp.int32(0),
        )
    )
    enc_attended = enc_mixed.astype(jnp.bfloat16)
    enc_first_in = embedded + project(enc_attended, enc_out) + enc_bias[1]
    enc_first = layer_norm(enc_first_in, enc_gain[0], enc_bias[3])
    enc_ff_hidden = enc_first.astype(jnp.bfloat16)
    enc_ff_pre = project(enc_ff_hidden, enc_ff_in) + ff_bias[0]
    enc_ff_act = jax.nn.gelu(enc_ff_pre, approximate=False).astype(jnp.bfloat16)
    enc_second_in = enc_first + project(enc_ff_act, enc_ff_out) + enc_bias[2]
    encoded = layer_norm(enc_second_in, enc_gain[1], enc_bias[4])
    memory = encoded.astype(jnp.bfloat16)
    self_query = (project(dec_in, dec_qkv[0]) + dec_bias[0]).astype(jnp.bfloat16)
    self_key = project(dec_in, dec_qkv[1]).astype(jnp.bfloat16)
    self_value = (project(dec_in, dec_qkv[2]) + dec_bias[1]).astype(jnp.bfloat16)
    self_update = forward_update(
        split_heads(self_query), tau_scale, dec_pos, True, self_unpack, dec_rows
    )
    self_mixed, self_log = finish_forward(
        self_update(
            fresh_totals(item_count, dec_rows, head_size),
            (
                lax.all_gather(self_key, SEQ, axis=1, tiled=True),
                lax.all_gather(self_value, SEQ, axis=1, tiled=True),
            ),
            jnp.int32(0),
        )
    )
    self_attended = self_mixed.astype(jnp.bfloat16)
    dec_first_in = dec_in.astype(jnp.float32) + project(self_attended, dec_out) + dec_bias[2]
    dec_first = layer_norm(dec_first_in, dec_gain[0], dec_bias[7])
    cross_hidden = dec_first.astype(jnp.bfloat16)
    cross_query = (project(cross_hidden, cross_qkv[0]) + dec_bias[3]).astype(jnp.bfloat16)
    cross_key = project(memory, cross_qkv[1]).astype(jnp.bfloat16)
    cross_value = (project(memory, cross_qkv[2]) + dec_bias[4]).astype(jnp.bfloat16)
    cross_start = fresh_totals(item_count, dec_rows, head_size)
    cross_update = forward_update(
        split_heads(cross_query), tau_scale, dec_pos, False, plain_unpack, enc_rows
    )
    cross_totals = cross_update(
        cross_start,
        (
            lax.all_gather(cross_key, SEQ, axis=1, tiled=True),
            lax.all_gather(cross_value, SEQ, axis=1, tiled=True),
            lax.all_gather(delta_shift, SEQ, axis=1, tiled=True),
        ),
        jnp.int32(0),
    )
    cross_mixed, cross_log = finish_forward(cross_totals)
    cross_attended = cross_mixed.astype(jnp.bfloat16)
    dec_second_in = dec_first + project(cross_attended, cross_out) + dec_bias[5]
    dec_second = layer_norm(dec_second_in, dec_gain[1], dec_bias[8])
    dec_ff_hidden = dec_second.astype(jnp.bfloat16)
    dec_ff_pre = project(dec_ff_hidden, dec_ff_in) + ff_bias[1]
    dec_ff_act = jax.nn.gelu(dec_ff_pre, approximate=False).astype(jnp.bfloat16)
    dec_third_in = dec_second + project(dec_ff_act, dec_ff_out) + dec_bias[6]
    decoded = layer_norm(dec_third_in, dec_gain[2], dec_bias[9])
    third_grad, dec_gain_three, dec_bias_three = norm_backward(
        dec_third_in, dec_gain[2], dec_bias[9], cotangent.astype(jnp.float32)
    )
    from_dec_ff, dec_ff_in_grad, dec_ff_bias_grad, dec_ff_out_grad, dec_ff_out_bias = (
        feed_forward_back(third_grad, dec_ff_hidden, dec_ff_pre, dec_ff_act, dec_ff_in, dec_ff_out)
    )
    second_grad, dec_gain_two, dec_bias_two = norm_backward(
        dec_second_in, dec_gain[1], dec_bias[8], third_grad + from_dec_ff
    )
    cross_branch_grad = second_grad.astype(jnp.bfloat16)
    cross_out_grad = weight_grad(cross_attended, cross_branch_grad)
    cross_out_bias = row_total(cross_branch_grad)
    cross_mixed_grad = project_back(cross_branch_grad, cross_out).astype(jnp.bfloat16)
    cross_dot = row_products(cross_mixed_grad, cross_mixed)
    cross_query_start = jnp.zeros((item_count, HEADS, dec_rows, head_size), jnp.float32)
    cross_back = query_grad_update(
        split_heads(cross_query),
        split_heads(cross_mixed_grad),
        jnp.transpose(cross_log, (0, 2, 1)),
        jnp.transpose(cross_dot, (0, 2, 1)),
        tau_scale,
        dec_pos,
        False,
        plain_unpack,
        enc_rows,
    )
    cross_query_total = cross_back(
        cross_query_start,
        (
            lax.all_gather(cross_key, SEQ, axis=1, tiled=True),
            lax.all_gather(cross_value, SEQ, axis=1, tiled=True),
            lax.all_gather(delta_shift, SEQ, axis=1, tiled=True),
        ),
        jnp.int32(0),
    )
    cross_query_grad = scaled_grad(cross_query_total, tau_scale)
    cross_key_update = key_grad_update(
        split_heads(cross_key),
        split_heads(cross_value),
        enc_shift,
        tau_scale,
        enc_pos,
        False,
        dec_rows,
    )
    cross_key_start = (
        jnp.zeros((item_count, HEADS, enc_rows, head_size), jnp.float32),
        jnp.zeros((item_count, HEADS, enc_rows, head_size), jnp.float32),
    )
    cross_key_total, cross_value_total = cross_key_update(
        cross_key_start,
        (
            lax.all_gather(cross_query.astype(jnp.float32), SEQ, axis=1, tiled=True),
            lax.all_gather(cross_mixed_grad.astype(jnp.float32), SEQ, axis=1, tiled=True),
            lax.all_gather(cross_log, SEQ, axis=1, tiled=True),
            lax.all_gather(cross_dot, SEQ, axis=1, tiled=True),
        ),
        jnp.int32(0),
    )
    cross_key_grad = scaled_grad(cross_key_total, tau_scale)
    cross_value_grad = merge_heads(cross_value_total).astype(jnp.bfloat16)
    cross_qkv_grad = jnp.stack(
        [
            weight_grad(cross_hidden, cross_query_grad),
            weight_grad(memory, cross_key_grad),
            weight_grad(memory, cross_value_grad),
        ]
    )
    memory_grad = project_back(cross_key_grad, cross_qkv[1]) + project_back(
        cross_value_grad, cross_qkv[2]
    )
    first_grad, dec_gain_one, dec_bias_one = norm_backward(
        dec_first_in,
        dec_gain[0],
        dec_bias[7],
        second_grad + project_back(cross_query_grad, cross_qkv[0]),
    )
    self_branch_grad = first_grad.astype(jnp.bfloat16)
    dec_out_grad = weight_grad(self_attended, self_branch_grad)
    self_out_bias = row_total(self_branch_grad)
    self_mixed_grad = project_back(self_branch_grad, dec_out).astype(jnp.bfloat16)
    self_dot = row_products(self_mixed_grad, self_mixed)
    self_back = query_grad_update(
        split_heads(self_query),
        split_heads(self_mixed_grad),
        jnp.transpose(self_log, (0, 2, 1)),
        jnp.transpose(self_dot, (0, 2, 1)),
        tau_scale,
        dec_pos,
        True,
        self_unpack,
        dec_rows,
    )
    self_query_total = self_back(
        jnp.zeros((item_count, HEADS, dec_rows, head_size), jnp.float32),
        (
            lax.all_gather(self_key, SEQ, axis=1, tiled=True),
            lax.all_gather(self_value, SEQ, axis=1, tiled=True),
        ),
        jnp.int32(0),
    )
    self_query_grad = scaled_grad(self_query_total, tau_scale)
    self_key_update = key_grad_update(
        split_heads(self_key),
        split_heads(self_value),
        jnp.zeros((item_count, dec_rows), jnp.float32),
        tau_scale,
        dec_pos,
        True,
        dec_rows,
    )
    self_key_start = (
        jnp.zeros((item_count, HEADS, dec_rows, head_size), jnp.float32),
        jnp.zeros((item_count, HEADS, dec_rows, head_size), jnp.float32),
    )
    self_key_total, self_value_total = self_key_update(
        self_key_start,
        (
            lax.all_gather(self_query.astype(jnp.float32), SEQ, axis=1, tiled=True),
            lax.all_gather(self_mixed_grad.astype(jnp.float32), SEQ, axis=1, tiled=True),
            lax.all_gather(self_log, SEQ, axis=1, tiled=True),
            lax.all_gather(self_dot, SEQ, axis=1, tiled=True),
        ),
        jnp.int32(0),
    )
    self_key_grad = scaled_grad(self_key_total, tau_scale)
    self_value_grad = merge_heads(self_value_total).astype(jnp.bfloat16)
    dec_qkv_grad = jnp.stack(
        [
            weight_grad(dec_in, self_query_grad),
            weight_grad(dec_in, self_key_grad),
            weight_grad(dec_in, self_value_grad),
        ]
    )
    dec_in_grad = (
        first_grad
        + project_back(self_query_grad, dec_qkv[0])
        + project_back(self_key_grad, dec_qkv[1])
        + project_back(self_value_grad, dec_qkv[2])
    )
    enc_second_grad, enc_gain_two, enc_bias_two = norm_backward(
        enc_second_in, enc_gain[1], enc_bias[4], memory_grad
    )
    from_enc_ff, enc_ff_in_grad, enc_ff_bias_grad, enc_ff_out_grad, enc_ff_out_bias = (
        feed_forward_back(
            enc_second_grad, enc_ff_hidden, enc_ff_pre, enc_ff_act, enc_ff_in, enc_ff_out
        )
    )
    enc_first_grad, enc_gain_one, enc_bias_one = norm_backward(
        enc_first_in, enc_gain[0], enc_bias[3], enc_second_grad + from_enc_ff
    )
    enc_branch_grad = enc_first_grad.astype(jnp.bfloat16)
    enc_out_grad = weight_grad(enc_attended, enc_branch_grad)
    enc_out_bias = row_total(enc_branch_grad)
    enc_mixed_grad = project_back(enc_branch_grad, enc_out).astype(jnp.bfloat16)
    enc_dot = row_products(enc_mixed_grad, enc_mixed)
    enc_back = query_grad_update(
        split_heads(enc_query),
        split_heads(enc_mixed_grad),
        jnp.transpose(enc_log, (0, 2, 1)),
        jnp.transpose(enc_dot, (0, 2, 1)),
        tau_scale,
        enc_pos,
        False,
        plain_unpack,
        enc_rows,
    )
    enc_query_total = enc_back(
        jnp.zeros((item_count, HEADS, enc_rows, head_size), jnp.float32),
        (
            lax.all_gather(enc_key, SEQ, axis=1, tiled=True),
            lax.all_gather(enc_value, SEQ, axis=1, tiled=True),
            lax.all_gather(delta_shift, SEQ, axis=1, tiled=True),
        ),
        jnp.int32(0),
    )
    enc_query_grad = scaled_grad(enc_query_total, tau_scale)
    enc_key_update = key_grad_update(
        split_heads(enc_key), split_heads(enc_value), enc_shift, tau_scale, enc_pos, False, enc_rows
    )
    enc_key_start = (
        jnp.zeros((item_count, HEADS, enc_rows, head_size), jnp.float32),
        jnp.zeros((item_count, HEADS, enc_rows, head_size), jnp.float32),
    )
    enc_key_total, enc_value_total = enc_key_update(
        enc_key_start,
        (
            lax.all_gather(enc_query.astype(jnp.float32), SEQ, axis=1, tiled=True),
            lax.all_gather(enc_mixed_grad.astype(jnp.float32), SEQ, axis=1, tiled=True),
            lax.all_gather(enc_log, SEQ, axis=1, tiled=True),
            lax.all_gather(enc_dot, SEQ, axis=1, tiled=True),
        ),
        jnp.int32(0),
    )
    enc_key_grad = scaled_grad(enc_key_total, tau_scale)
    enc_value_grad = merge_heads(enc_value_total).astype(jnp.bfloat16)
    enc_qkv_grad = jnp.stack(
        [
            weight_grad(enc_hidden, enc_query_grad),
            weight_grad(enc_hidden, enc_key_grad),
            weight_grad(enc_hidden, enc_value_grad),
        ]
    )
    enc_in_grad = (
        enc_first_grad
        + project_back(enc_query_grad, enc_qkv[0])
        + project_back(enc_key_grad, enc_qkv[1])
        + project_back(enc_value_grad, enc_qkv[2])
    )
    embed_grad = weight_grad(masked_series, enc_in_grad.astype(jnp.bfloat16))
    enc_query_bias_grad = row_total(enc_query_grad)
    enc_bias_grad = jnp.stack(
        [row_total(enc_value_grad), enc_out_bias, enc_ff_out_bias, enc_bias_one, enc_bias_two]
    )
    enc_gain_grad = jnp.stack([enc_gain_one, enc_gain_two])
    dec_bias_grad = jnp.stack(
        [
            row_total(self_query_grad),
            row_total(self_value_grad),
            self_out_bias,
            row_total(cross_query_grad),
            row_total(cross_value_grad),
            cross_out_bias,
            dec_ff_out_bias,
            dec_bias_one,
            dec_bias_two,
            dec_bias_three,
        ]
    )
    dec_gain_grad = jnp.stack([dec_gain_one, dec_gain_two, dec_gain_three])
    ff_bias_grad = jnp.stack([enc_ff_bias_grad, dec_ff_bias_grad])
    shares = (
        lax.psum_scatter(embed_grad, SEQ, scatter_dimension=1, tiled=True),
        lax.psum_scatter(enc_qkv_grad, SEQ, scatter_dimension=2, tiled=True),
        lax.psum_scatter(enc_out_grad, SEQ, scatter_dimension=1, tiled=True),
        lax.psum_scatter(enc_ff_in_grad, SEQ, scatter_dimension=1, tiled=True),
        lax.psum_scatter(enc_ff_out_grad, SEQ, scatter_dimension=1, tiled=True),
        lax.psum_scatter(enc_query_bias_grad, SEQ, scatter_dimension=0, tiled=True),
        lax.psum_scatter(enc_bias_grad, SEQ, scatter_dimension=1, tiled=True),
        lax.psum_scatter(enc_gain_grad, SEQ, scatter_dimension=1, tiled=True),
        lax.psum_scatter(dec_qkv_grad, SEQ, scatter_dimension=2, tiled=True),
        lax.psum_scatter(dec_out_grad, SEQ, scatter_dimension=1, tiled=True),
        lax.psum_scatter(cross_qkv_grad, SEQ, scatter_dimension=2, tiled=True),
        lax.psum_scatter(cross_out_grad, SEQ, scatter_dimension=1, tiled=True),
        lax.psum_scatter(dec_ff_in_grad, SEQ, scatter_dimension=1, tiled=True),
        lax.psum_scatter(dec_ff_out_grad, SEQ, scatter_dimension=1, tiled=True),
        lax.psum_scatter(dec_bias_grad, SEQ, scatter_dimension=1, tiled=True),
        lax.psum_scatter(dec_gain_grad, SEQ, scatter_dimension=1, tiled=True),
        lax.psum_scatter(ff_bias_grad, SEQ, scatter_dimension=1, tiled=True),
    )
    summed = lax.psum(
        (
            shares[0],
            shares[1],
            shares[2],
            shares[3],
            shares[4],
            shares[5],
            shares[6],
            shares[7],
            shares[8],
            shares[9],
            shares[10],
            shares[11],
            shares[12],
            shares[13],
            shares[14],
            shares[15],
            shares[16],
        ),
        BATCH,
    )
    return (
        decoded.astype(jnp.bfloat16),
        enc_in_grad,
        dec_in_grad,
        summed[0],
        summed[1],
        summed[2],
        summed[3],
        summed[4],
        summed[5],
        summed[6],
        summed[7],
        summed[8],
        summed[9],
        summed[10],
        summed[11],
        summed[12],
        summed[13],
        summed[14],
        summed[15],
        summed[16],
    )


F32 = jnp.float32
BF16 = jnp.bfloat16
MESH = pl.DeviceIdType.MESH
QUAD = 4
HALVES = 2
CORES = 2
LANES = 128
LINK_COUNT = 83
VMEM_BYTES = 60 << 20
LOAD_FIRST = 3
LOAD_ORDER = (
    "value_embed",
    "enc_qkv",
    "dec_qkv",
    "enc_out",
    "enc_ff_in",
    "enc_ff_out",
    "dec_out",
    "cross_qkv",
    "cross_out",
    "dec_ff_in",
    "dec_ff_out",
)


def mm(left, right):
    return jnp.dot(left, right, preferred_element_type=F32)


def mm_right_t(left, right):
    return lax.dot_general(left, right, (((1,), (1,)), ((), ())), preferred_element_type=F32)


def mm_left_t(left, right):
    return lax.dot_general(left, right, (((0,), (0,)), ((), ())), preferred_element_type=F32)


def lane_index(shape):
    return lax.broadcasted_iota(jnp.int32, shape, len(shape) - 1)


def swap_halves(values):
    return pltpu.roll(values, LANES // 2, axis=1)


def low_lanes(first, second):
    return jnp.where(lane_index(first.shape) < LANES // 2, first, second)


def pack_rows(values):
    half = values.shape[0] // 2
    packed = []
    for pair in range(values.shape[1] // LANES):
        group = values[:, pair * LANES : (pair + 1) * LANES]
        top, bottom = group[:half], group[half:]
        packed.append(low_lanes(top, swap_halves(bottom)))
        packed.append(low_lanes(swap_halves(top), bottom))
    return packed


def unpack_rows(packed):
    groups = []
    for pair in range(len(packed) // 2):
        first, second = packed[2 * pair], packed[2 * pair + 1]
        top = low_lanes(first, swap_halves(second))
        bottom = low_lanes(swap_halves(first), second)
        groups.append(jnp.concatenate([top, bottom], axis=0))
    return jnp.concatenate(groups, axis=1)


def pack_pairs(keys, values):
    packed = []
    for pair in range(keys.shape[1] // LANES):
        key_group = keys[:, pair * LANES : (pair + 1) * LANES]
        value_group = values[:, pair * LANES : (pair + 1) * LANES]
        packed.append(low_lanes(key_group, swap_halves(value_group)))
        packed.append(low_lanes(swap_halves(key_group), value_group))
    return packed


def unpack_pairs(packed):
    keys, values = [], []
    for pair in range(len(packed) // 2):
        first, second = packed[2 * pair], packed[2 * pair + 1]
        keys.append(low_lanes(first, swap_halves(second)))
        values.append(low_lanes(swap_halves(first), second))
    return jnp.concatenate(keys, axis=1), jnp.concatenate(values, axis=1)


def norm_forward(values, gain, shift):
    centred = values - jnp.mean(values, axis=-1, keepdims=True)
    scale = lax.rsqrt(jnp.mean(centred * centred, axis=-1, keepdims=True) + epsilon)
    unit = centred * scale
    return unit * gain + shift, unit, scale


def norm_back(upstream, unit, scale, gain):
    inner = upstream * gain
    result = scale * (
        inner
        - jnp.mean(inner, axis=-1, keepdims=True)
        - unit * jnp.mean(inner * unit, axis=-1, keepdims=True)
    )
    return (
        result,
        jnp.sum(upstream * unit, axis=0, keepdims=True),
        jnp.sum(upstream, axis=0, keepdims=True),
    )


def rounded(values):
    return values.astype(BF16).astype(F32)


class View:
    def __init__(self, entries):
        for name, entry in entries.items():
            if isinstance(entry, dict):
                entry = View(entry)
            elif isinstance(entry, (list, tuple)):
                entry = [View(part) if isinstance(part, dict) else part for part in entry]
            setattr(self, name, entry)


class Weight:
    def __init__(self, copy, held):
        self.copy, self.held, self.here = copy, held, False

    def start(self):
        self.copy.start()

    def __call__(self):
        if not self.here:
            self.copy.wait()
            self.here = True
        return self.held


def fused_body(structures, *refs):
    entries = {}
    for structure in structures:
        count = structure.num_leaves
        entries.update(jax.tree.unflatten(structure, refs[:count]))
        refs = refs[count:]
    ref = View(entries)
    small = View(entries["held_blocks"])
    rows, width = ref.enc_in.shape
    hidden, channels, chips = ref.ff_bias.shape[1], ref.series.shape[1], HEADS
    packed_rows = rows // 2
    keys_total = chips * CORES * rows
    block_queries = chips * packed_rows
    column = width // (chips * CORES)
    depth = chips * CORES // QUAD

    place = lax.axis_index(SEQ)
    item = lax.axis_index(BATCH)
    core = lax.rem(place, 2)
    chip = place // 2
    x_place = lax.rem(chip, 2)
    z_place = chip // 2
    quad = lax.rem(place, QUAD)
    core_dev = (chip * 2 + (1 - core), item)
    x_dev = (z_place * QUAD + (1 - x_place) * 2 + core, item)
    diagonal_dev = (z_place * QUAD + (1 - x_place) * 2 + (1 - core), item)
    item_dev = (place, 1 - item)
    z_high, z_odd = z_place // 2, lax.rem(z_place, 2)
    near_dev = ((z_high * 2 + 1 - z_odd) * QUAD + quad, item)
    far_dev = (((1 - z_high) * 2 + z_odd) * QUAD + quad, item)
    x_quad = (1 - x_place) * 2 + core
    other_dev = (chip * 2 + (1 - core), 1 - item)
    item_quad = item * 2 + core
    next_quad = (1 - item) * 2 + core

    def same_core(step):
        peer = lax.rem(chip + step, chips)
        return peer, (peer * 2 + core, item)

    def z_peer(step):
        peer = lax.rem(z_place + step, depth)
        return peer, (peer * QUAD + quad, item)

    barrier = pltpu.get_barrier_semaphore()
    greeted = [core_dev, diagonal_dev, item_dev, other_dev] + [same_core(step)[1] for step in range(1, chips)]
    for device in greeted:
        pl.semaphore_signal(barrier, inc=1, device_id=device, device_id_type=MESH)

    blocks = []
    for index, (name, target) in enumerate(entries["held_blocks"].items()):
        blocks.append(pltpu.make_async_copy(entries[name], target, ref.block_sem.at[index]))
        blocks[-1].start()
    loaded = {}
    for index, name in enumerate(LOAD_ORDER):
        source, target = getattr(ref.weight, name), getattr(ref.held, name)
        copy = pltpu.make_async_copy(source, target, ref.load_sem.at[index])
        loaded[name] = Weight(copy, target)
    weight = View(loaded)
    for name in LOAD_ORDER[:LOAD_FIRST]:
        loaded[name].start()
    for copy in blocks:
        copy.wait()

    stores = []

    def store(source, target):
        index = len(stores)
        stores.append(pltpu.make_async_copy(source, target, ref.store_sem.at[index]))
        stores[-1].start()

    batches = []

    def ship(copies, meter=None):
        index = len(batches)
        made = []
        for source, target, device in copies:
            made.append(
                pltpu.make_async_remote_copy(
                    src_ref=source,
                    dst_ref=target,
                    send_sem=ref.send_sem.at[index],
                    recv_sem=ref.recv_sem.at[index],
                    device_id=device,
                    device_id_type=MESH,
                )
            )
            made[-1].start()
        batches.append((index, made, meter))
        return batches[-1]

    def send(source, target, device):
        return ship([(source, target, device)])

    def arrive(batch):
        index, made, meter = batch
        if meter is None:
            made[0].wait_recv()
        else:
            pltpu.make_async_copy(meter, meter, ref.recv_sem.at[index]).wait()

    def depart(batch):
        index, made, meter = batch
        if meter is None:
            made[0].wait_send()
        else:
            pltpu.make_async_copy(meter, meter, ref.send_sem.at[index]).wait()

    def spread(source, target_at):
        copies = []
        for step in range(1, chips):
            peer, device = same_core(step)
            copies.append((source.at[peer], target_at(chip), device))
        return ship(copies, source.at[pl.ds(0, chips - 1)])

    def share(block):
        return [
            block,
            send(block.at[quad], block.at[quad], core_dev),
            send(block.at[quad], block.at[quad], x_dev),
        ]

    def relay(shared):
        block = shared[0]
        arrive(shared[2])
        shared.append(send(block.at[x_quad], block.at[x_quad], core_dev))

    def settle(shared):
        arrive(shared[1])
        arrive(shared[3])

    def gathered(block, start, features):
        value = block[:, :, start : start + features]
        return value.reshape(value.shape[0] * value.shape[1], value.shape[2])

    def cut_columns(values, group, start):
        part = lane_index((rows, LANES)) // column
        for member in range(QUAD):
            total = None
            for level in range(depth):
                cut = values[:, level * LANES : (level + 1) * LANES]
                shift = (column * (level - member)) % LANES
                moved = pltpu.roll(cut, shift, axis=1) if shift else cut
                total = moved if total is None else jnp.where(part == level, moved, total)
            group.cut[member, :, start : start + LANES] = total.astype(BF16)

    def share_columns(group, start, stop):
        source, target = group.cut, group.met
        target[quad, :, start:stop] = source[quad, :, start:stop]
        copies = []
        for device, member in (
            (core_dev, x_place * 2 + 1 - core),
            (x_dev, x_quad),
            (diagonal_dev, (1 - x_place) * 2 + 1 - core),
        ):
            copies.append(
                (
                    source.at[member, :, pl.ds(start, stop - start)],
                    target.at[quad, :, pl.ds(start, stop - start)],
                    device,
                )
            )
        return ship(copies, target.at[pl.ds(0, QUAD - 1), :, pl.ds(start, stop - start)])

    def share_item(group):
        group.tokens[item_quad] = group.own[item]
        return [
            group.tokens,
            send(group.own.at[item], group.tokens.at[item_quad], core_dev),
            send(group.own.at[1 - item], group.tokens.at[item_quad], item_dev),
        ]

    def relay_item(shared):
        arrive(shared[2])
        block = shared[0]
        shared.append(send(block.at[next_quad], block.at[next_quad], core_dev))

    def cut_cores(values, group, start):
        part = lane_index((rows, LANES)) // column
        for member in range(CORES):
            for pair in range(depth // 2):
                total = None
                for piece in range(QUAD):
                    level = pair * 2 + piece // 2
                    cut = values[:, level * LANES : (level + 1) * LANES]
                    place_in = 2 * (piece % 2) + member
                    shift = (column * (piece - place_in)) % LANES
                    moved = pltpu.roll(cut, shift, axis=1) if shift else cut
                    total = moved if total is None else jnp.where(part == piece, moved, total)
                at = start + pair * LANES
                group.cut[member, :, at : at + LANES] = total.astype(BF16)

    def share_cores(group):
        group.met[item_quad] = group.cut[core]
        return ship(
            [
                (group.cut.at[1 - core], group.met.at[item_quad], core_dev),
                (group.cut.at[core], group.met.at[item_quad], item_dev),
                (group.cut.at[1 - core], group.met.at[item_quad], other_dev),
            ],
            group.met.at[pl.ds(0, QUAD - 1)],
        )

    def build_cores(group):
        lanes = width // 2
        met = group.met[...].reshape(QUAD * rows, 2 * lanes)
        tokens = group.tokens[...]
        tokens = tokens.reshape(QUAD * rows, tokens.shape[2])
        for index, (start, stop) in enumerate(((0, hidden // 2), (hidden // 2, tokens.shape[1]))):
            gradient = mm_left_t(met[:, index * lanes : (index + 1) * lanes], tokens[:, start:stop])
            gradient = gradient.astype(BF16)
            for at in range(chips):
                group.part[at % 2, at // 4, at // 2 % 2, :, start:stop] = gradient[
                    at * column : (at + 1) * column
                ]

    def columns_of(group, start, stop):
        value = group.met[:, :, start:stop]
        return value.reshape(QUAD * rows, stop - start)

    def put_rows(target, level, start, values):
        half = target.shape[3]
        count = values.shape[0]
        done = 0
        while done < count:
            which, offset = divmod(start + done, half)
            take = min(count - done, half - offset)
            target[which, level // 2, level % 2, offset : offset + take, :] = values[
                done : done + take, :
            ]
            done += take

    def put_gradient(target, start, gradient):
        count = gradient.shape[0] // depth
        gradient = gradient.astype(BF16)
        short = -gradient.shape[1] % width
        pieces = gradient.shape[1] // width
        for level in range(depth):
            block = gradient[level * count : (level + 1) * count]
            for piece in range(pieces):
                put_rows(
                    target,
                    level,
                    start + piece * count,
                    block[:, piece * width : (piece + 1) * width],
                )
            if short:
                tail = jnp.concatenate(
                    [block[:, pieces * width :], jnp.zeros((count, short), BF16)], axis=1
                )
                put_rows(target, level, start + pieces * count, tail)

    def both_sums(left, right):
        return (left.astype(F32) + right.astype(F32)).astype(BF16)

    def steps_of(group, which, device):
        def near():
            group.half[...] = both_sums(group.part[which], group.item[...])
            return send(group.half.at[:, 1 - z_odd], group.near, near_dev)

        def far():
            group.pair[...] = both_sums(group.half[:, z_odd], group.near[...])
            return send(group.pair.at[1 - z_high], group.far, far_dev)

        def last():
            group.sum[item] = both_sums(group.pair[z_high], group.far[...])
            return send(group.sum.at[item], group.sum.at[item], item_dev)

        return [lambda: send(group.part.at[1 - which], group.item, device), near, far, last]

    def advance(group):
        if group.batch is not None:
            arrive(group.batch)
        group.batch = group.steps.pop(0)()

    def finish(group):
        if group.batch is not None:
            arrive(group.batch)
        store(group.sum, group.result)

    def gather_depth(block):
        copies = []
        for step in range(1, depth):
            device = z_peer(step)[1]
            copies.append((block.at[z_place, x_place], block.at[z_place, x_place], device))
        return ship(copies, block.at[pl.ds(0, depth - 1), 0])

    def gather_x(block, batch):
        arrive(batch)
        return send(block.at[:, x_place], block.at[:, x_place], x_dev)

    def head_gradients(own, space, block):
        value = block[...]
        tokens = value.reshape((chips,) + value.shape[2:])
        tokens = jnp.concatenate([tokens, jnp.ones((chips, rows, LANES), BF16)], axis=2)
        features = tokens.shape[2]
        queries = own.t_query_grad[...].reshape(block_queries, LANES)
        total = None
        for half in range(HALVES):
            part = tokens[:, half * packed_rows : (half + 1) * packed_rows]
            part = mm_left_t(queries, part.reshape(block_queries, features))
            part = part[half * LANES // 2 : (half + 1) * LANES // 2]
            total = part if total is None else total + part
        pairs = own.t_pair_grad[...].reshape(chips * rows, LANES)
        both = mm_left_t(pairs, tokens.reshape(chips * rows, features))
        for index, gradient in enumerate((total, both[: LANES // 2], both[LANES // 2 :])):
            for which in range(CORES):
                space.mine[which, index * column : (index + 1) * column, :] = gradient[
                    which * column : (which + 1) * column
                ].astype(BF16)
        return send(space.mine.at[1 - core], space.core, core_dev)

    def heads_item(space, batch):
        arrive(batch)
        space.both[...] = both_sums(space.mine[core], space.core[...])
        return send(space.both, space.item, item_dev)

    def heads_done(space, batch, target):
        arrive(batch)
        space.sum[...] = space.both[...].astype(F32) + space.item[...].astype(F32)
        store(space.sum, target)

    def set_vector(row, value):
        ref.vec[row : row + 1, :] = value

    att_enc, att_self, att_cross = ref.attention
    dec_in_part, cross_part, enc_in_part, embed_part = ref.group
    dec_out_part, enc_out_part = ref.core_group
    for group in ref.group:
        group.steps = steps_of(group, item, item_dev)
    for group in ref.core_group:
        group.steps = steps_of(group, x_place, x_dev)
    for group, result in zip(ref.group + ref.core_group, ref.sums):
        group.result, group.batch = result, None
    enc_ff = (weight.enc_ff_in, weight.enc_ff_out)
    dec_ff = (weight.dec_ff_in, weight.dec_ff_out)

    def build(group, row, start, features, tokens, wide=False):
        gradient = mm_left_t(columns_of(group, start, start + features), tokens)
        if wide:
            put_gradient(group.part, row, gradient)
            return
        for which in range(features // LANES):
            put_gradient(
                group.part,
                row + which * column,
                gradient[which * LANES : (which + 1) * LANES],
            )

    tau = ref.tau_scale[0]
    group_row = lax.broadcasted_iota(jnp.int32, small.channel_mask.shape, 0)
    chosen = jnp.where(
        group_row == ref.item_group[0], small.channel_mask[...].astype(F32), 0.0
    )
    channel_row = jnp.sum(chosen, axis=0, keepdims=True)
    masked = (small.series[...].astype(F32) * channel_row).astype(BF16)
    dec_hidden = small.dec_in[...]
    ref.g_dec_in[z_place, x_place] = dec_hidden
    ref.x_series[quad] = jnp.zeros(ref.x_series.shape[1:], BF16)
    ref.x_series[quad, :, 0:channels] = masked

    shift_row = small.delta_shift[...].astype(F32)
    ref.t_shift[...] = jnp.broadcast_to(
        jnp.concatenate([shift_row, shift_row], axis=1), ref.t_shift.shape
    )
    ref.shift[chip, core] = ref.t_shift[...]
    pl.semaphore_wait(barrier, len(greeted))
    go_shift = ship(
        [
            (ref.t_shift, ref.shift.at[chip, core], same_core(step)[1])
            for step in range(1, chips)
        ],
        ref.shift.at[pl.ds(0, chips - 1), 0],
    )

    embedded = small.enc_in[...].astype(F32) + mm(masked, weight.value_embed()[...])
    ref.embedded[...] = embedded
    enc_hidden = embedded.astype(BF16)
    ref.g_enc_hidden[z_place, x_place] = enc_hidden
    for name in LOAD_ORDER[LOAD_FIRST:]:
        loaded[name].start()

    def send_queries(own, query):
        for head, packed in enumerate(pack_rows(query)):
            own.t_query[head] = packed.astype(BF16)
        own.query[chip] = own.t_query[chip]
        return spread(own.t_query, lambda at: own.query.at[at])

    def send_pairs(own, keys, values):
        for head, packed in enumerate(pack_pairs(keys, values)):
            own.t_pair[head] = packed.astype(BF16)
        own.pair[chip, core] = own.t_pair[chip]
        return spread(own.t_pair, lambda at: own.pair.at[at, core])

    def pass_on(own):
        block = own.pair
        return send(block.at[:, core], block.at[:, core], core_dev)

    qkv = weight.enc_qkv()
    enc_query = mm(enc_hidden, qkv[0]) + small.enc_query_bias[...]
    enc_key = mm(enc_hidden, qkv[1])
    enc_value = mm(enc_hidden, qkv[2]) + small.enc_bias[0:1, :]
    go_enc_pair = send_pairs(att_enc, enc_key, enc_value)
    go_enc_query = send_queries(att_enc, enc_query)
    qkv = weight.dec_qkv()
    self_query = mm(dec_hidden, qkv[0]) + small.dec_bias[0:1, :]
    self_key = mm(dec_hidden, qkv[1])
    self_value = mm(dec_hidden, qkv[2]) + small.dec_bias[1:2, :]
    go_self_pair = send_pairs(att_self, self_key, self_value)
    go_self_query = send_queries(att_self, self_query)

    def attention(own, shifted, causal):
        pairs = own.pair[...].reshape(keys_total, LANES)
        pairs_t = pairs.T
        own.pair_t[...] = pairs_t
        query_t = own.query[...].reshape(block_queries, LANES).astype(F32).T
        zeros = jnp.zeros((LANES // 2, block_queries), F32)
        for half in range(HALVES):
            part = query_t[half * LANES // 2 : (half + 1) * LANES // 2]
            side = jnp.concatenate([part, zeros], axis=0).astype(BF16)
            scores = mm(pairs, side) * (tau * 0.125)
            if shifted:
                moved = ref.shift_columns[...]
                scores = scores + jnp.concatenate([moved] * (block_queries // LANES), axis=1)
            if causal:
                key_at = lax.broadcasted_iota(jnp.int32, scores.shape, 0)
                lane = lane_index(scores.shape)
                query_at = (
                    (lane // packed_rows * 2 + core) * rows
                    + half * packed_rows
                    + lane % packed_rows
                )
                scores = jnp.where(key_at > query_at, masked_score, scores)
            weights = jnp.exp(scores - jnp.max(scores, axis=0, keepdims=True))
            inverse = 1.0 / jnp.sum(weights, axis=0, keepdims=True)
            low_weights = weights.astype(BF16)
            own.weights[half] = low_weights
            own.inverse[half] = jnp.broadcast_to(inverse, (8, block_queries))
            mixed_t = mm(pairs_t, low_weights)[LANES // 2 :] * inverse
            own.mixed_t[half * LANES // 2 : (half + 1) * LANES // 2, :] = mixed_t
        mixed = own.mixed_t[...].T.astype(BF16)
        own.t_mixed[...] = mixed.reshape(chips, packed_rows, LANES)
        own.mixed[chip] = own.t_mixed[chip]
        return spread(own.t_mixed, lambda at: own.mixed.at[at])

    def mixed_rows(own):
        return unpack_rows(
            [own.mixed[head].astype(F32) for head in range(chips)]
        ).astype(BF16)

    arrive(go_shift)
    on_shift = send(ref.shift.at[:, core], ref.shift.at[:, core], core_dev)
    arrive(on_shift)
    for block in range(chips):
        line = low_lanes(ref.shift[block, 0], ref.shift[block, 1])[0:1, :] * 0.125
        ref.shift_columns[block * LANES : (block + 1) * LANES, :] = jnp.broadcast_to(
            line, (LANES, LANES)
        ).T
    arrive(go_enc_pair)
    on_enc = pass_on(att_enc)
    arrive(go_enc_query)
    arrive(on_enc)
    back_enc = attention(att_enc, True, False)
    go_dec_in = gather_depth(ref.g_dec_in)
    share_series = share(ref.x_series)
    arrive(go_self_pair)
    on_self = pass_on(att_self)
    arrive(go_self_query)
    arrive(on_self)
    back_self = attention(att_self, False, True)

    def feed_forward(values, weights, bias_row, out_bias, low_at, group, slope):
        low = values.astype(BF16)
        low_at[quad, :, 0:width] = low
        weight_in, weight_out = weights[0](), weights[1]()
        total = out_bias
        for piece in range(hidden // width):
            cut = slice(piece * width, (piece + 1) * width)
            pre = mm(low, weight_in[:, cut]) + small.ff_bias[bias_row : bias_row + 1, cut]
            normal = 0.5 * (1.0 + lax.erf(pre * 0.7071067811865476))
            act = (pre * normal).astype(BF16)
            slope[:, cut] = normal + pre * (
                jnp.exp(pre * pre * -0.5) * 0.3989422804014327
            )
            half, at = divmod(piece * width, hidden // 2)
            group.own[half, :, at : at + width] = act
            total = total + mm(act, weight_out[cut, :])
        return total

    def feed_forward_back(upstream, weights, slope, vector_row, group):
        low = upstream.astype(BF16)
        weight_in, weight_out = weights[0](), weights[1]()
        total = None
        for piece in range(hidden // width):
            cut = slice(piece * width, (piece + 1) * width)
            act_grad = mm_right_t(low, weight_out[cut, :])
            pre_grad = (act_grad * slope[:, cut]).astype(BF16)
            sums = jnp.sum(pre_grad.astype(F32), axis=0, keepdims=True)
            for member in range(QUAD):
                at = piece * LANES
                ref.vec[vector_row + member : vector_row + member + 1, at : at + LANES] = sums[
                    :, member * LANES : (member + 1) * LANES
                ]
                group.cut[member, :, at : at + LANES] = pre_grad[
                    :, member * LANES : (member + 1) * LANES
                ]
            more = mm_right_t(pre_grad, weight_in[:, cut])
            total = more if total is None else total + more
        return total

    def save_norm(index, unit, scale):
        ref.unit[index] = unit
        ref.scale[index] = jnp.broadcast_to(scale, (rows, LANES))

    def saved_norm(index):
        return ref.unit[index], ref.scale[index, :, 0:1]

    def keep_mixed(group, values):
        for half in range(HALVES):
            group.own[half, :, hidden // 2 :] = values[
                :, half * width // 2 : (half + 1) * width // 2
            ]

    arrive(back_enc)
    attended = mixed_rows(att_enc)
    keep_mixed(enc_out_part, attended)
    first, unit, scale = norm_forward(
        embedded + mm(attended, weight.enc_out()[...]) + small.enc_bias[1:2, :],
        small.enc_gain[0:1, :],
        small.enc_bias[3:4, :],
    )
    save_norm(0, unit, scale)
    second, unit, scale = norm_forward(
        first + feed_forward(
            first,
            enc_ff,
            0,
            small.enc_bias[2:3, :],
            ref.x_early,
            enc_out_part,
            ref.enc_slope,
        ),
        small.enc_gain[1:2, :],
        small.enc_bias[4:5, :],
    )
    save_norm(1, unit, scale)
    memory = second.astype(BF16)
    ref.x_early[quad, :, width : 2 * width] = memory
    share_enc_out = share_item(enc_out_part)
    qkv = weight.cross_qkv()
    cross_key = mm(memory, qkv[1])
    cross_value = mm(memory, qkv[2]) + small.dec_bias[4:5, :]
    go_cross_pair = send_pairs(att_cross, cross_key, cross_value)

    arrive(back_self)
    attended = mixed_rows(att_self)
    ref.x_early[quad, :, 2 * width : 3 * width] = attended
    first, unit, scale = norm_forward(
        small.dec_in[...].astype(F32)
        + mm(attended, weight.dec_out()[...])
        + small.dec_bias[2:3, :],
        small.dec_gain[0:1, :],
        small.dec_bias[7:8, :],
    )
    save_norm(2, unit, scale)
    ref.first_dec[...] = first
    low = first.astype(BF16)
    ref.x_early[quad, :, 3 * width : 4 * width] = low
    go_cross_query = send_queries(att_cross, mm(low, qkv[0]) + small.dec_bias[3:4, :])
    share_early = share(ref.x_early)

    arrive(go_cross_pair)
    on_cross = pass_on(att_cross)
    arrive(go_cross_query)
    arrive(on_cross)
    back_cross = attention(att_cross, True, False)
    go_enc_hidden = gather_depth(ref.g_enc_hidden)
    on_dec_in = gather_x(ref.g_dec_in, go_dec_in)
    relay_item(share_enc_out)
    relay(share_series)
    arrive(back_cross)
    attended = mixed_rows(att_cross)
    keep_mixed(dec_out_part, attended)
    second, unit, scale = norm_forward(
        ref.first_dec[...]
        + mm(attended, weight.cross_out()[...])
        + small.dec_bias[5:6, :],
        small.dec_gain[1:2, :],
        small.dec_bias[8:9, :],
    )
    save_norm(3, unit, scale)

    forward = feed_forward(
        second,
        dec_ff,
        1,
        small.dec_bias[6:7, :],
        ref.x_late,
        dec_out_part,
        ref.dec_slope,
    )
    share_dec_out = share_item(dec_out_part)
    third, unit, scale = norm_forward(
        second + forward,
        small.dec_gain[2:3, :],
        small.dec_bias[9:10, :],
    )
    ref.o_dec_result[...] = third.astype(BF16)
    store(ref.o_dec_result, ref.dec_result)

    def norm_step(index, upstream, gain, gain_row, gain_vector, shift_vector):
        unit, scale = saved_norm(index)
        result, gain_grad, shift_grad = norm_back(
            upstream, unit, scale, gain[gain_row : gain_row + 1, :]
        )
        set_vector(gain_vector, gain_grad)
        set_vector(shift_vector, shift_grad)
        return result

    def column_sum(values):
        return jnp.sum(rounded(values), axis=0, keepdims=True)

    third_grad, gain_grad, shift_grad = norm_back(
        small.cotangent[...].astype(F32), unit, scale, small.dec_gain[2:3, :]
    )
    set_vector(20, gain_grad)
    set_vector(17, shift_grad)
    from_ff = feed_forward_back(third_grad, dec_ff, ref.dec_slope, 25, dec_in_part)
    second_grad = norm_step(3, third_grad + from_ff, small.dec_gain, 1, 19, 16)
    ref.second_grad[...] = second_grad

    def send_mixed_grad(own, branch_grad, out_weight):
        mixed_grad = mm_right_t(branch_grad.astype(BF16), out_weight[...])
        for head, packed in enumerate(pack_rows(mixed_grad)):
            own.t_grad[head] = packed.astype(BF16)
        own.grad[chip] = own.t_grad[chip]
        return spread(own.t_grad, lambda at: own.grad.at[at])

    go_cross_grad = send_mixed_grad(att_cross, second_grad, weight.cross_out())
    ff_width = hidden // QUAD
    cut_cores(third_grad, dec_out_part, 0)
    cut_cores(second_grad, dec_out_part, width // 2)
    columns_dec_out = share_cores(dec_out_part)
    set_vector(14, column_sum(third_grad))
    set_vector(13, column_sum(second_grad))
    share_late = share(ref.x_late)
    columns_dec_in = share_columns(dec_in_part, 0, ff_width)
    relay(share_early)

    def attention_back(own):
        pairs = own.pair[...].reshape(keys_total, LANES)
        pairs_t = own.pair_t[...]
        queries = own.query[...].reshape(block_queries, LANES).astype(F32)
        grads = own.grad[...].reshape(block_queries, LANES).astype(F32)
        grads_t = grads.T
        zeros = jnp.zeros((LANES // 2, block_queries), F32)
        blank = jnp.zeros_like(queries)
        query_grads = []
        key_total = value_total = None
        for half in range(HALVES):
            cut = slice(half * LANES // 2, (half + 1) * LANES // 2)
            grad_t = grads_t[cut]
            row_dot = jnp.sum(grad_t * own.mixed_t[cut, :], axis=0, keepdims=True)
            side = jnp.concatenate([zeros, grad_t], axis=0).astype(BF16)
            prob_grads = mm(pairs, side)
            probabilities = own.weights[half].astype(F32) * own.inverse[half, 0:1, :]
            score_grads = (probabilities * (prob_grads - row_dot)).astype(BF16)
            query_grads.append(mm(pairs_t, score_grads)[: LANES // 2])
            if half == 0:
                query_side = low_lanes(queries, blank)
                grad_side = low_lanes(blank, swap_halves(grads))
            else:
                query_side = low_lanes(swap_halves(queries), blank)
                grad_side = low_lanes(blank, grads)
            key_part = mm(score_grads, query_side.astype(BF16))
            value_part = mm(probabilities.astype(BF16), grad_side.astype(BF16))
            key_total = key_part if key_total is None else key_total + key_part
            value_total = value_part if value_total is None else value_total + value_part
        factor = tau * 0.125
        query_grad = (jnp.concatenate(query_grads, axis=0) * factor).T.astype(BF16)
        own.t_query_grad[...] = query_grad.reshape(chips, packed_rows, LANES)
        own.query_grad[chip] = own.t_query_grad[chip]
        go_query = spread(
            own.t_query_grad, lambda at: own.query_grad.at[at]
        )
        pair_grad = (key_total * factor + value_total).reshape(chips, CORES, rows, LANES)
        for which in range(CORES):
            own.pair_sum[which] = pair_grad[:, which]
            own.t_part[which] = pair_grad[:, which].astype(BF16)
        exchange = send(own.t_part.at[1 - core], own.part, core_dev)
        return go_query, exchange

    def attention_back_pairs(own, exchange):
        arrive(exchange)
        total = own.pair_sum[core] + own.part[...].astype(F32)
        own.t_pair_grad[...] = total.astype(BF16)
        own.pair_grad[chip] = own.t_pair_grad[chip]
        return spread(own.t_pair_grad, lambda at: own.pair_grad.at[at])

    def query_grad_rows(own):
        return unpack_rows(
            [own.query_grad[head].astype(F32) for head in range(chips)]
        )

    def pair_grad_rows(own):
        return unpack_pairs([own.pair_grad[head].astype(F32) for head in range(chips)])

    arrive(go_cross_grad)
    go_query, exchange = attention_back(att_cross)
    relay(share_late)
    relay_item(share_dec_out)
    go_pair = attention_back_pairs(att_cross, exchange)
    settle(share_late)
    arrive(columns_dec_in)
    build(dec_in_part, 0, 0, ff_width, gathered(ref.x_late, 0, width), wide=True)
    advance(dec_in_part)
    settle(share_dec_out)
    arrive(columns_dec_out)
    build_cores(dec_out_part)
    advance(dec_out_part)

    qkv = weight.cross_qkv()
    arrive(go_query)
    cross_query_grad = query_grad_rows(att_cross)
    first_grad = norm_step(
        2,
        ref.second_grad[...] + mm_right_t(cross_query_grad.astype(BF16), qkv[0]),
        small.dec_gain,
        0,
        18,
        15,
    )
    ref.first_grad[...] = first_grad
    go_self_grad = send_mixed_grad(att_self, first_grad, weight.dec_out())
    set_vector(10, column_sum(first_grad))

    arrive(go_pair)
    cross_key_grad, cross_value_grad = pair_grad_rows(att_cross)
    memory_grad = mm_right_t(cross_key_grad.astype(BF16), qkv[1]) + mm_right_t(
        cross_value_grad.astype(BF16), qkv[2]
    )
    enc_second_grad = norm_step(1, memory_grad, small.enc_gain, 1, 7, 5)
    from_ff = feed_forward_back(enc_second_grad, enc_ff, ref.enc_slope, 21, enc_in_part)
    enc_first_grad = norm_step(0, enc_second_grad + from_ff, small.enc_gain, 0, 6, 4)
    ref.enc_first_grad[...] = enc_first_grad
    go_enc_grad = send_mixed_grad(att_enc, enc_first_grad, weight.enc_out())
    set_vector(3, column_sum(enc_second_grad))
    set_vector(2, column_sum(enc_first_grad))
    set_vector(11, column_sum(cross_query_grad))
    set_vector(12, column_sum(cross_value_grad))
    for row in (0, 1, 8, 9, 29, 30, 31):
        set_vector(row, jnp.zeros((1, width), F32))
    vec_item = send(ref.vec, ref.vec_item, item_dev)
    columns_enc_in = share_columns(enc_in_part, 0, ff_width)
    for index, values in enumerate(
        (cross_query_grad, cross_key_grad, cross_value_grad, first_grad)
    ):
        cut_columns(values, cross_part, index * LANES)
    columns_cross = share_columns(cross_part, 0, 4 * LANES)
    cut_cores(enc_second_grad, enc_out_part, 0)
    cut_cores(enc_first_grad, enc_out_part, width // 2)
    columns_enc_out = share_cores(enc_out_part)
    advance(dec_in_part)
    advance(dec_out_part)
    arrive(go_self_grad)
    go_self_query_grad, exchange_self = attention_back(att_self)
    arrive(go_enc_grad)
    go_enc_query_grad, exchange_enc = attention_back(att_enc)
    go_enc_pair_grad = attention_back_pairs(att_enc, exchange_enc)
    go_self_pair_grad = attention_back_pairs(att_self, exchange_self)
    advance(dec_in_part)
    advance(dec_out_part)

    settle(share_early)
    arrive(columns_enc_in)
    build(enc_in_part, 0, 0, ff_width, gathered(ref.x_early, 0, width), wide=True)
    advance(enc_in_part)
    settle(share_enc_out)
    arrive(columns_enc_out)
    build_cores(enc_out_part)
    advance(enc_out_part)
    arrive(columns_cross)
    build(cross_part, 0, 0, LANES, gathered(ref.x_early, 3 * width, width))
    build(cross_part, column, LANES, 2 * LANES, gathered(ref.x_early, width, width))
    build(cross_part, 3 * column, 3 * LANES, LANES, gathered(ref.x_early, 2 * width, width))
    advance(cross_part)
    arrive(vec_item)
    ref.vec_a[...] = ref.vec[...] + ref.vec_item[...]
    vec_core = send(ref.vec_a, ref.vec_core, core_dev)
    arrive(on_dec_in)
    core_self = head_gradients(att_self, ref.head_self, ref.g_dec_in)

    def input_grad(own, weights, first):
        query_grad = query_grad_rows(own)
        key_grad, value_grad = pair_grad_rows(own)
        return (
            first[...]
            + mm_right_t(query_grad.astype(BF16), weights[0])
            + mm_right_t(key_grad.astype(BF16), weights[1])
            + mm_right_t(value_grad.astype(BF16), weights[2])
        )

    arrive(go_enc_query_grad)
    arrive(go_enc_pair_grad)
    total = input_grad(att_enc, weight.enc_qkv(), ref.enc_first_grad)
    ref.o_enc_grad[...] = total
    store(ref.o_enc_grad, ref.enc_grad)
    cut_columns(total, embed_part, 0)
    columns_embed = share_columns(embed_part, 0, LANES)
    on_enc_hidden = gather_x(ref.g_enc_hidden, go_enc_hidden)
    item_self = heads_item(ref.head_self, core_self)
    arrive(vec_core)
    ref.vec_b[...] = ref.vec_a[...] + ref.vec_core[...]
    vec_x = send(ref.vec_b, ref.vec_x, x_dev)
    arrive(go_self_query_grad)
    arrive(go_self_pair_grad)
    total = input_grad(att_self, weight.dec_qkv(), ref.first_grad)
    ref.o_dec_grad[...] = total
    store(ref.o_dec_grad, ref.dec_grad)
    advance(enc_in_part)
    settle(share_series)
    arrive(columns_embed)
    build(embed_part, 0, 0, LANES, gathered(ref.x_series, 0, ref.x_series.shape[2]))
    advance(embed_part)
    advance(enc_out_part)
    advance(dec_in_part)
    advance(dec_out_part)
    arrive(on_enc_hidden)
    core_enc = head_gradients(att_enc, ref.head_enc, ref.g_enc_hidden)
    advance(enc_in_part)
    advance(cross_part)
    heads_done(ref.head_self, item_self, ref.heads[1])
    item_enc = heads_item(ref.head_enc, core_enc)
    arrive(vec_x)
    ref.vec_c[...] = ref.vec_b[...] + ref.vec_x[...]
    copies = []
    for step in range(1, depth):
        peer, device = z_peer(step)
        lanes = pl.ds(pl.multiple_of(peer * LANES, LANES), LANES)
        copies.append((ref.vec_c.at[:, lanes], ref.vec_depth.at[step - 1], device))
    vec_depth = ship(copies, ref.vec_depth)
    advance(enc_out_part)
    finish(dec_in_part)
    finish(dec_out_part)
    advance(enc_in_part)
    advance(embed_part)
    advance(cross_part)
    heads_done(ref.head_enc, item_enc, ref.heads[0])
    arrive(vec_depth)
    lanes = pl.ds(pl.multiple_of(z_place * LANES, LANES), LANES)
    total = ref.vec_c[:, lanes]
    for step in range(1, depth):
        total = total + ref.vec_depth[step - 1]
    ref.o_vectors[...] = total
    store(ref.o_vectors, ref.vectors)
    advance(embed_part)
    advance(enc_out_part)
    finish(enc_in_part)
    advance(cross_part)
    advance(embed_part)
    finish(enc_out_part)
    finish(cross_part)
    finish(embed_part)
    for copy in stores:
        copy.wait()
    for batch in batches:
        depart(batch)
    if len(batches) != LINK_COUNT:
        raise ValueError(len(batches))


def finish_body(*refs):
    (
        dec_in,
        enc_grad_in,
        dec_grad_in,
        ff_in_two,
        cross,
        ff_in_one,
        embed,
        ff_out_two,
        ff_out_one,
        head_enc,
        head_self,
        vectors,
        dec_out,
        enc_grad,
        dec_grad,
        g_embed,
        g_enc_qkv,
        g_enc_out,
        g_enc_ff_in,
        g_enc_ff_out,
        g_enc_query_bias,
        g_enc_bias,
        g_enc_gain,
        g_dec_qkv,
        g_dec_out,
        g_cross_qkv,
        g_cross_out,
        g_dec_ff_in,
        g_dec_ff_out,
        g_dec_bias,
        g_dec_gain,
        g_ff_bias,
    ) = refs
    place = lax.axis_index(SEQ)
    column, width = g_enc_out.shape
    channels = g_embed.shape[1]
    member = lax.rem(place, QUAD)
    dec_out[...] = dec_in[...]
    enc_grad[...] = enc_grad_in[...]
    dec_grad[...] = dec_grad_in[...]

    def whole(block):
        value = block[...]
        return value.reshape(value.shape[0] * value.shape[1], value.shape[2]).astype(F32)

    g_dec_ff_in[...] = whole(ff_in_two).T
    g_enc_ff_in[...] = whole(ff_in_one).T
    block = whole(cross)
    for index in range(3):
        g_cross_qkv[index] = block[index * column : (index + 1) * column]
    g_dec_out[...] = block[3 * column : 4 * column]
    for block, wide, narrow in (
        (ff_out_two, g_dec_ff_out, g_cross_out),
        (ff_out_one, g_enc_ff_out, g_enc_out),
    ):
        for half in range(HALVES):
            value = block[half].astype(F32)
            step = wide.shape[1] // 2
            wide[:, half * step : (half + 1) * step] = value[:, 0:step]
            rest = width // 2
            narrow[:, half * rest : (half + 1) * rest] = value[:, step : step + rest]
    late = []
    for block, target in ((head_enc, g_enc_qkv), (head_self, g_dec_qkv)):
        for index in range(3):
            target[index] = block[index * column : (index + 1) * column, 0:width]
        late.append(block[:, width : width + LANES].T[0:1])
    late_enc, late_self = late
    block = whole(embed)
    g_embed[:, 0:width] = block[0:column]
    g_embed[:, width:channels] = block[column : 2 * column, 0 : channels - width]

    values = vectors[...]
    moved = pltpu.roll(values, lax.rem(LANES - member * column, LANES), axis=1)
    rows = moved[:, 0:column]
    g_enc_query_bias[...] = late_enc[:, 0:column]
    g_enc_bias[...] = jnp.concatenate([late_enc[:, 2 * column : 3 * column], rows[2:6]], axis=0)
    g_enc_gain[...] = rows[6:8]
    g_dec_bias[...] = jnp.concatenate(
        [late_self[:, 0:column], late_self[:, 2 * column : 3 * column], rows[10:18]], axis=0
    )
    g_dec_gain[...] = rows[18:21]
    row_index = lax.broadcasted_iota(jnp.int32, values.shape, 0)
    for index in range(2):
        chosen = jnp.where(row_index == 21 + QUAD * index + member, values, 0.0)
        g_ff_bias[index : index + 1, :] = jnp.sum(chosen, axis=0, keepdims=True)


def fused_local(
    enc_in,
    series,
    channel_mask,
    item_group,
    tau_scale,
    delta_shift,
    dec_in,
    value_embed,
    enc_qkv,
    enc_out,
    enc_ff_in,
    enc_ff_out,
    enc_query_bias,
    enc_bias,
    enc_gain,
    dec_qkv,
    dec_out,
    cross_qkv,
    cross_out,
    dec_ff_in,
    dec_ff_out,
    dec_bias,
    dec_gain,
    ff_bias,
    cotangent,
):
    rows, width = enc_in.shape[1:]
    hidden = enc_ff_in.shape[1]
    channels = value_embed.shape[0]
    chips = HEADS
    column = width // (chips * CORES)
    depth = chips * CORES // QUAD
    padded = -(-channels // LANES) * LANES
    keys_total = chips * CORES * rows
    queries = chips * rows // 2
    in_smem = pl.BlockSpec(memory_space=pltpu.SMEM)
    in_vmem = pl.BlockSpec(memory_space=pltpu.VMEM)
    anywhere = pl.BlockSpec(memory_space=pl.ANY)

    weights = dict(
        value_embed=value_embed,
        enc_qkv=enc_qkv,
        enc_out=enc_out,
        enc_ff_in=enc_ff_in,
        enc_ff_out=enc_ff_out,
        dec_qkv=dec_qkv,
        dec_out=dec_out,
        cross_qkv=cross_qkv,
        cross_out=cross_out,
        dec_ff_in=dec_ff_in,
        dec_ff_out=dec_ff_out,
    )
    scalars = dict(item_group=item_group, tau_scale=tau_scale)
    blocks = dict(
        enc_in=enc_in[0],
        series=series[0],
        channel_mask=channel_mask,
        delta_shift=delta_shift,
        dec_in=dec_in[0],
        cotangent=cotangent[0],
        enc_query_bias=enc_query_bias[None],
        enc_bias=enc_bias,
        enc_gain=enc_gain,
        dec_bias=dec_bias,
        dec_gain=dec_gain,
        ff_bias=ff_bias,
    )
    inputs = (scalars, blocks, dict(weight=weights))
    in_specs = [in_smem] * len(scalars) + [anywhere] * (len(blocks) + len(weights))

    def low(*shape):
        return pltpu.VMEM(shape, BF16)

    def full(*shape):
        return pltpu.VMEM(shape, F32)

    def exchanged(features):
        return low(QUAD, rows, features)

    def attention_space():
        packed = low(chips, rows // 2, LANES)
        paired = low(chips, rows, LANES)
        both = low(chips, CORES, rows, LANES)
        return dict(
            query=packed,
            t_query=packed,
            mixed=packed,
            t_mixed=packed,
            grad=packed,
            t_grad=packed,
            query_grad=packed,
            t_query_grad=packed,
            t_pair=paired,
            pair=both,
            t_pair_grad=paired,
            pair_grad=paired,
            t_part=low(CORES, chips, rows, LANES),
            part=paired,
            pair_sum=full(CORES, chips, rows, LANES),
            pair_t=low(LANES, keys_total),
            weights=low(HALVES, keys_total, queries),
            inverse=full(HALVES, 8, queries),
            mixed_t=full(LANES, queries),
        )

    def sum_space(half, features):
        return dict(
            part=low(2, 2, 2, half, features),
            item=low(2, 2, half, features),
            half=low(2, 2, half, features),
            near=low(2, half, features),
            pair=low(2, half, features),
            far=low(half, features),
            sum=low(2, half, features),
        )

    def group_space(count, features):
        return dict(
            cut=exchanged(features), met=exchanged(features), **sum_space(count // 2, width)
        )

    def core_group_space():
        features = (hidden + width) // 2
        return dict(
            own=low(HALVES, rows, features),
            tokens=exchanged(features),
            cut=low(CORES, rows, width),
            met=exchanged(width),
            **sum_space(column, features),
        )

    def head_space():
        shape = (3 * column, width + LANES)
        return dict(
            mine=low(CORES, *shape),
            core=low(*shape),
            both=low(*shape),
            item=low(*shape),
            sum=full(*shape),
        )

    ff_width = hidden // QUAD
    group_rows = (LANES, 4 * column, LANES, 2 * column)
    group_features = (ff_width, 4 * LANES, ff_width, LANES)
    scratch = dict(
        held={name: low(*value.shape) for name, value in weights.items()},
        held_blocks={
            name: pltpu.VMEM(value.shape, value.dtype) for name, value in blocks.items()
        },
        block_sem=pltpu.SemaphoreType.DMA((len(blocks),)),
        store_sem=pltpu.SemaphoreType.DMA((8 + len(group_rows),)),
        o_dec_result=low(rows, width),
        o_enc_grad=full(rows, width),
        o_dec_grad=full(rows, width),
        o_vectors=full(32, LANES),
        g_dec_in=low(depth, 2, rows, width),
        g_enc_hidden=low(depth, 2, rows, width),
        x_series=exchanged(padded),
        x_early=exchanged(4 * width),
        x_late=exchanged(width),
        enc_slope=full(rows, hidden),
        dec_slope=full(rows, hidden),
        attention=[attention_space() for index in range(3)],
        group=[group_space(*sizes) for sizes in zip(group_rows, group_features)],
        core_group=[core_group_space() for index in range(2)],
        head_enc=head_space(),
        head_self=head_space(),
        t_shift=full(8, LANES),
        shift=full(chips, CORES, 8, LANES),
        shift_columns=full(keys_total, LANES),
        embedded=full(rows, width),
        first_dec=full(rows, width),
        second_grad=full(rows, width),
        first_grad=full(rows, width),
        enc_first_grad=full(rows, width),
        unit=full(4, rows, width),
        scale=full(4, rows, LANES),
        vec=full(32, width),
        vec_item=full(32, width),
        vec_a=full(32, width),
        vec_core=full(32, width),
        vec_b=full(32, width),
        vec_x=full(32, width),
        vec_c=full(32, width),
        vec_depth=full(depth - 1, 32, LANES),
        load_sem=pltpu.SemaphoreType.DMA((len(weights),)),
        send_sem=pltpu.SemaphoreType.DMA((LINK_COUNT,)),
        recv_sem=pltpu.SemaphoreType.DMA((LINK_COUNT,)),
    )
    outputs = dict(
        dec_result=jax.ShapeDtypeStruct((rows, width), BF16),
        enc_grad=jax.ShapeDtypeStruct((rows, width), F32),
        dec_grad=jax.ShapeDtypeStruct((rows, width), F32),
        sums=[jax.ShapeDtypeStruct((2, count // 2, width), BF16) for count in group_rows]
        + [jax.ShapeDtypeStruct((2, column, (hidden + width) // 2), BF16)] * 2,
        heads=[jax.ShapeDtypeStruct((3 * column, width + LANES), F32)] * 2,
        vectors=jax.ShapeDtypeStruct((32, LANES), F32),
    )
    out_shapes, out_structure = jax.tree.flatten(outputs)
    scratch_shapes, scratch_structure = jax.tree.flatten(scratch)
    operands = jax.tree.leaves(inputs)
    structures = [jax.tree.structure(part) for part in inputs]
    results = pl.pallas_call(
        partial(fused_body, structures + [out_structure, scratch_structure]),
        out_shape=out_shapes,
        in_specs=in_specs,
        out_specs=[anywhere] * len(out_shapes),
        scratch_shapes=scratch_shapes,
        compiler_params=pltpu.CompilerParams(
            collective_id=1, has_side_effects=True, vmem_limit_bytes=VMEM_BYTES
        ),
        name="layers",
    )(*operands)
    results = jax.tree.unflatten(out_structure, results)
    results = [
        results[key] for key in ("dec_result", "enc_grad", "dec_grad")
    ] + results["sums"] + results["heads"] + [results["vectors"]]

    final = [
        (rows, width),
        (rows, width),
        (rows, width),
        (column, channels),
        (3, column, width),
        (column, width),
        (width, hidden // (chips * CORES)),
        (column, hidden),
        (1, column),
        (5, column),
        (2, column),
        (3, column, width),
        (column, width),
        (3, column, width),
        (column, width),
        (width, hidden // (chips * CORES)),
        (column, hidden),
        (10, column),
        (3, column),
        (2, hidden // (chips * CORES)),
    ]
    outputs = pl.pallas_call(
        finish_body,
        out_shape=[
            jax.ShapeDtypeStruct(shape, BF16 if index == 0 else F32)
            for index, shape in enumerate(final)
        ],
        in_specs=[in_vmem] * len(results),
        out_specs=[in_vmem] * len(final),
        compiler_params=pltpu.CompilerParams(vmem_limit_bytes=VMEM_BYTES),
        name="columns",
    )(*results)
    outputs = list(outputs)
    for index in range(3):
        outputs[index] = outputs[index][None]
    outputs[8] = outputs[8][0]
    for index in (3, 4, 5, 7, 11, 12, 13, 14, 16):
        outputs[index] = jnp.swapaxes(outputs[index], -1, -2)
    return tuple(outputs)


def solution(mesh):
    in_specs = (
        P(BATCH, SEQ, None),
        P(BATCH, SEQ, None),
        P(),
        P(BATCH),
        P(BATCH),
        P(BATCH, SEQ),
        P(BATCH, SEQ, None),
        P(),
        P(),
        P(),
        P(),
        P(),
        P(),
        P(),
        P(),
        P(),
        P(),
        P(),
        P(),
        P(),
        P(),
        P(),
        P(),
        P(),
        P(BATCH, SEQ, None),
    )
    out_specs = (
        P(BATCH, SEQ, None),
        P(BATCH, SEQ, None),
        P(BATCH, SEQ, None),
        P(None, SEQ),
        P(None, None, SEQ),
        P(None, SEQ),
        P(None, SEQ),
        P(None, SEQ),
        P(SEQ),
        P(None, SEQ),
        P(None, SEQ),
        P(None, None, SEQ),
        P(None, SEQ),
        P(None, None, SEQ),
        P(None, SEQ),
        P(None, SEQ),
        P(None, SEQ),
        P(None, SEQ),
        P(None, SEQ),
        P(None, SEQ),
    )
    fits = mesh.shape[SEQ] == HEADS * CORES and mesh.shape[BATCH] == 2
    return jax.shard_map(
        fused_local if fits else local, mesh=mesh, in_specs=in_specs, out_specs=out_specs, check_vma=False)
```

```python
from functools import partial
from types import SimpleNamespace
import math

import jax
import jax.numpy as jnp
from jax import lax
from jax.experimental import pallas as pl
from jax.experimental.pallas import tpu as pltpu
from jax.sharding import PartitionSpec as P

HEADS = 8
GROUPS = 16
SEQ = "seq"
BATCH = "batch"


epsilon = 1e-05
masked_score = -1e30


def layer_norm(inputs, gain_vector, shift_vector):
    average = jnp.mean(inputs, axis=-1, keepdims=True)
    centred = inputs - average
    variance = jnp.mean(centred * centred, axis=-1, keepdims=True)
    return centred * lax.rsqrt(variance + epsilon) * gain_vector + shift_vector


def norm_backward(inputs, gain_vector, shift_vector, upstream):
    ignored, pullback = jax.vjp(layer_norm, inputs, gain_vector, shift_vector)
    return pullback(upstream)


def project(inputs, weight_matrix):
    return jnp.dot(inputs, weight_matrix, preferred_element_type=jnp.float32)


def project_back(gradient, weight_matrix):
    return jnp.einsum("ilf,kf->ilk", gradient, weight_matrix, preferred_element_type=jnp.float32)


def weight_grad(inputs, gradient):
    return jnp.einsum("ilk,ilf->kf", inputs, gradient, preferred_element_type=jnp.float32)


def row_total(gradient):
    return jnp.sum(gradient.astype(jnp.float32), axis=(0, 1))


def split_heads(values):
    return values.reshape(values.shape[:2] + (HEADS, values.shape[2] // HEADS))


def merge_heads(head_values):
    return jnp.transpose(head_values, (0, 2, 1, 3)).reshape(
        head_values.shape[0], head_values.shape[2], -1
    )


def over_blocks(update, totals, arrays, shard_rows):
    length = arrays[0].shape[1]
    block_rows = shard_rows * math.gcd(length // shard_rows, 8)
    block_count = length // block_rows
    stacked = tuple(
        (
            jnp.moveaxis(
                member.reshape((member.shape[0], block_count, block_rows) + member.shape[2:]), 1, 0
            )
            for member in arrays
        )
    )
    offsets = jnp.arange(block_count, dtype=jnp.int32) * block_rows

    def advance(running, inputs):
        return (update(running, inputs[0], inputs[1]), None)

    totals, ignored = lax.scan(advance, totals, (stacked, offsets))
    return totals


def head_scores(query_heads, key_heads, tau_value, key_shift):
    raw_scores = jnp.einsum(
        "iqhd,ikhd->ihqk", query_heads, key_heads, preferred_element_type=jnp.float32
    )
    return (tau_value[:, None, None, None] * raw_scores + key_shift[:, None, None, :]) * 0.125


def causal_mask(scores, query_pos, key_pos):
    allowed = query_pos[:, None] >= key_pos[None, :]
    return jnp.where(allowed[None, None], scores, masked_score)


def fresh_totals(item_count, row_count, head_size):
    return (
        jnp.full((item_count, HEADS, row_count), masked_score, jnp.float32),
        jnp.zeros((item_count, HEADS, row_count), jnp.float32),
        jnp.zeros((item_count, HEADS, row_count, head_size), jnp.float32),
    )


def finish_forward(totals):
    running_max, running_sum, weighted = totals
    output = merge_heads(weighted / running_sum[..., None])
    log_total = jnp.transpose(running_max + jnp.log(running_sum), (0, 2, 1))
    return (output, log_total)


def row_products(grad_rows, mixed_rows):
    return jnp.sum(split_heads(grad_rows).astype(jnp.float32) * split_heads(mixed_rows), axis=-1)


def scaled_grad(head_totals, tau_value):
    return merge_heads(head_totals * (tau_value * 0.125)[:, None, None, None]).astype(jnp.bfloat16)


def plain_unpack(fetched):
    return (fetched[0], fetched[1], fetched[2].astype(jnp.float32))


def self_unpack(fetched):
    return (fetched[0], fetched[1], jnp.zeros(fetched[0].shape[:2], jnp.float32))


def forward_update(query_heads, tau_value, query_pos, causal, unpack, shard_rows):

    def update(totals, fetched, offset):

        def block_update(running, piece_parts, inner_offset):
            running_max, running_sum, weighted = running
            key_rows, value_rows, key_shift = unpack(piece_parts)
            scores = head_scores(query_heads, split_heads(key_rows), tau_value, key_shift)
            if causal:
                key_pos = inner_offset + jnp.arange(key_rows.shape[1], dtype=jnp.int32)
                scores = causal_mask(scores, query_pos, key_pos)
            new_max = jnp.maximum(running_max, jnp.max(scores, axis=-1))
            factor = jnp.exp(running_max - new_max)
            weights = jnp.exp(scores - new_max[..., None])
            new_sum = running_sum * factor + jnp.sum(weights, axis=-1)
            mixed_values = jnp.einsum(
                "ihqk,ikhd->ihqd",
                weights,
                split_heads(value_rows).astype(jnp.float32),
                preferred_element_type=jnp.float32,
            )
            return (new_max, new_sum, weighted * factor[..., None] + mixed_values)

        return over_blocks(block_update, totals, fetched, shard_rows)

    return update


def query_grad_update(
    query_heads, grad_heads, log_total, row_dot, tau_value, query_pos, causal, unpack, shard_rows
):

    def update(totals, fetched, offset):

        def block_update(running, piece_parts, inner_offset):
            key_rows, value_rows, key_shift = unpack(piece_parts)
            key_heads = split_heads(key_rows)
            scores = head_scores(query_heads, key_heads, tau_value, key_shift)
            if causal:
                key_pos = inner_offset + jnp.arange(key_rows.shape[1], dtype=jnp.int32)
                scores = causal_mask(scores, query_pos, key_pos)
            probabilities = jnp.exp(scores - log_total[..., None])
            prob_grads = jnp.einsum(
                "iqhd,ikhd->ihqk",
                grad_heads,
                split_heads(value_rows),
                preferred_element_type=jnp.float32,
            )
            score_grads = (probabilities * (prob_grads - row_dot[..., None])).astype(jnp.bfloat16)
            return running + jnp.einsum(
                "ihqk,ikhd->ihqd", score_grads, key_heads, preferred_element_type=jnp.float32
            )

        return over_blocks(block_update, totals, fetched, shard_rows)

    return update


def key_grad_update(key_heads, value_heads, key_shift, tau_value, key_pos, causal, shard_rows):

    def update(totals, fetched, offset):

        def block_update(running, piece_parts, inner_offset):
            key_total, value_total = running
            query_heads = split_heads(piece_parts[0].astype(jnp.bfloat16))
            grad_heads = split_heads(piece_parts[1].astype(jnp.bfloat16))
            log_rows = jnp.transpose(piece_parts[2], (0, 2, 1))
            dot_rows = jnp.transpose(piece_parts[3], (0, 2, 1))
            scores = head_scores(query_heads, key_heads, tau_value, key_shift)
            if causal:
                query_pos = inner_offset + jnp.arange(piece_parts[0].shape[1], dtype=jnp.int32)
                scores = causal_mask(scores, query_pos, key_pos)
            probabilities = jnp.exp(scores - log_rows[..., None])
            value_total = value_total + jnp.einsum(
                "ihqk,iqhd->ihkd",
                probabilities,
                grad_heads.astype(jnp.float32),
                preferred_element_type=jnp.float32,
            )
            prob_grads = jnp.einsum(
                "iqhd,ikhd->ihqk", grad_heads, value_heads, preferred_element_type=jnp.float32
            )
            score_grads = (probabilities * (prob_grads - dot_rows[..., None])).astype(jnp.bfloat16)
            key_total = key_total + jnp.einsum(
                "ihqk,iqhd->ihkd", score_grads, query_heads, preferred_element_type=jnp.float32
            )
            return (key_total, value_total)

        return over_blocks(block_update, totals, fetched, shard_rows)

    return update


def feed_forward_back(upstream, hidden, pre_act, activated, weight_in, weight_out):
    out_grad = upstream.astype(jnp.bfloat16)
    out_weight_grad = weight_grad(activated, out_grad)
    out_bias_grad = row_total(out_grad)
    act_grad = project_back(out_grad, weight_out)
    ignored, gelu_back = jax.vjp(partial(jax.nn.gelu, approximate=False), pre_act)
    pre_grad = gelu_back(act_grad)[0].astype(jnp.bfloat16)
    return (
        project_back(pre_grad, weight_in),
        weight_grad(hidden, pre_grad),
        row_total(pre_grad),
        out_weight_grad,
        out_bias_grad,
    )


def local(
    enc_in,
    series,
    channel_mask,
    item_group,
    tau_scale,
    delta_shift,
    dec_in,
    value_embed,
    enc_qkv,
    enc_out,
    enc_ff_in,
    enc_ff_out,
    enc_query_bias,
    enc_bias,
    enc_gain,
    dec_qkv,
    dec_out,
    cross_qkv,
    cross_out,
    dec_ff_in,
    dec_ff_out,
    dec_bias,
    dec_gain,
    ff_bias,
    cotangent,
):
    item_count, enc_rows, width = enc_in.shape
    dec_rows = dec_in.shape[1]
    head_size = width // HEADS
    seq_index = lax.axis_index(SEQ)
    enc_pos = seq_index * enc_rows + jnp.arange(enc_rows, dtype=jnp.int32)
    dec_pos = seq_index * dec_rows + jnp.arange(dec_rows, dtype=jnp.int32)
    enc_shift = delta_shift.astype(jnp.float32)
    chosen = (item_group[:, None] == jnp.arange(GROUPS, dtype=jnp.int32)[None, :]).astype(
        jnp.float32
    )
    channels = jnp.dot(chosen, channel_mask.astype(jnp.float32), precision=lax.Precision.HIGHEST)
    masked_series = (series.astype(jnp.float32) * channels[:, None, :]).astype(jnp.bfloat16)
    embedded = enc_in.astype(jnp.float32) + project(masked_series, value_embed)
    enc_hidden = embedded.astype(jnp.bfloat16)
    enc_query = (project(enc_hidden, enc_qkv[0]) + enc_query_bias).astype(jnp.bfloat16)
    enc_key = project(enc_hidden, enc_qkv[1]).astype(jnp.bfloat16)
    enc_value = (project(enc_hidden, enc_qkv[2]) + enc_bias[0]).astype(jnp.bfloat16)
    enc_update = forward_update(
        split_heads(enc_query), tau_scale, enc_pos, False, plain_unpack, enc_rows
    )
    enc_mixed, enc_log = finish_forward(
        enc_update(
            fresh_totals(item_count, enc_rows, head_size),
            (
                lax.all_gather(enc_key, SEQ, axis=1, tiled=True),
                lax.all_gather(enc_value, SEQ, axis=1, tiled=True),
                lax.all_gather(delta_shift, SEQ, axis=1, tiled=True),
            ),
            jnp.int32(0),
        )
    )
    enc_attended = enc_mixed.astype(jnp.bfloat16)
    enc_first_in = embedded + project(enc_attended, enc_out) + enc_bias[1]
    enc_first = layer_norm(enc_first_in, enc_gain[0], enc_bias[3])
    enc_ff_hidden = enc_first.astype(jnp.bfloat16)
    enc_ff_pre = project(enc_ff_hidden, enc_ff_in) + ff_bias[0]
    enc_ff_act = jax.nn.gelu(enc_ff_pre, approximate=False).astype(jnp.bfloat16)
    enc_second_in = enc_first + project(enc_ff_act, enc_ff_out) + enc_bias[2]
    encoded = layer_norm(enc_second_in, enc_gain[1], enc_bias[4])
    memory = encoded.astype(jnp.bfloat16)
    self_query = (project(dec_in, dec_qkv[0]) + dec_bias[0]).astype(jnp.bfloat16)
    self_key = project(dec_in, dec_qkv[1]).astype(jnp.bfloat16)
    self_value = (project(dec_in, dec_qkv[2]) + dec_bias[1]).astype(jnp.bfloat16)
    self_update = forward_update(
        split_heads(self_query), tau_scale, dec_pos, True, self_unpack, dec_rows
    )
    self_mixed, self_log = finish_forward(
        self_update(
            fresh_totals(item_count, dec_rows, head_size),
            (
                lax.all_gather(self_key, SEQ, axis=1, tiled=True),
                lax.all_gather(self_value, SEQ, axis=1, tiled=True),
            ),
            jnp.int32(0),
        )
    )
    self_attended = self_mixed.astype(jnp.bfloat16)
    dec_first_in = dec_in.astype(jnp.float32) + project(self_attended, dec_out) + dec_bias[2]
    dec_first = layer_norm(dec_first_in, dec_gain[0], dec_bias[7])
    cross_hidden = dec_first.astype(jnp.bfloat16)
    cross_query = (project(cross_hidden, cross_qkv[0]) + dec_bias[3]).astype(jnp.bfloat16)
    cross_key = project(memory, cross_qkv[1]).astype(jnp.bfloat16)
    cross_value = (project(memory, cross_qkv[2]) + dec_bias[4]).astype(jnp.bfloat16)
    cross_start = fresh_totals(item_count, dec_rows, head_size)
    cross_update = forward_update(
        split_heads(cross_query), tau_scale, dec_pos, False, plain_unpack, enc_rows
    )
    cross_totals = cross_update(
        cross_start,
        (
            lax.all_gather(cross_key, SEQ, axis=1, tiled=True),
            lax.all_gather(cross_value, SEQ, axis=1, tiled=True),
            lax.all_gather(delta_shift, SEQ, axis=1, tiled=True),
        ),
        jnp.int32(0),
    )
    cross_mixed, cross_log = finish_forward(cross_totals)
    cross_attended = cross_mixed.astype(jnp.bfloat16)
    dec_second_in = dec_first + project(cross_attended, cross_out) + dec_bias[5]
    dec_second = layer_norm(dec_second_in, dec_gain[1], dec_bias[8])
    dec_ff_hidden = dec_second.astype(jnp.bfloat16)
    dec_ff_pre = project(dec_ff_hidden, dec_ff_in) + ff_bias[1]
    dec_ff_act = jax.nn.gelu(dec_ff_pre, approximate=False).astype(jnp.bfloat16)
    dec_third_in = dec_second + project(dec_ff_act, dec_ff_out) + dec_bias[6]
    decoded = layer_norm(dec_third_in, dec_gain[2], dec_bias[9])
    third_grad, dec_gain_three, dec_bias_three = norm_backward(
        dec_third_in, dec_gain[2], dec_bias[9], cotangent.astype(jnp.float32)
    )
    from_dec_ff, dec_ff_in_grad, dec_ff_bias_grad, dec_ff_out_grad, dec_ff_out_bias = (
        feed_forward_back(third_grad, dec_ff_hidden, dec_ff_pre, dec_ff_act, dec_ff_in, dec_ff_out)
    )
    second_grad, dec_gain_two, dec_bias_two = norm_backward(
        dec_second_in, dec_gain[1], dec_bias[8], third_grad + from_dec_ff
    )
    cross_branch_grad = second_grad.astype(jnp.bfloat16)
    cross_out_grad = weight_grad(cross_attended, cross_branch_grad)
    cross_out_bias = row_total(cross_branch_grad)
    cross_mixed_grad = project_back(cross_branch_grad, cross_out).astype(jnp.bfloat16)
    cross_dot = row_products(cross_mixed_grad, cross_mixed)
    cross_query_start = jnp.zeros((item_count, HEADS, dec_rows, head_size), jnp.float32)
    cross_back = query_grad_update(
        split_heads(cross_query),
        split_heads(cross_mixed_grad),
        jnp.transpose(cross_log, (0, 2, 1)),
        jnp.transpose(cross_dot, (0, 2, 1)),
        tau_scale,
        dec_pos,
        False,
        plain_unpack,
        enc_rows,
    )
    cross_query_total = cross_back(
        cross_query_start,
        (
            lax.all_gather(cross_key, SEQ, axis=1, tiled=True),
            lax.all_gather(cross_value, SEQ, axis=1, tiled=True),
            lax.all_gather(delta_shift, SEQ, axis=1, tiled=True),
        ),
        jnp.int32(0),
    )
    cross_query_grad = scaled_grad(cross_query_total, tau_scale)
    cross_key_update = key_grad_update(
        split_heads(cross_key),
        split_heads(cross_value),
        enc_shift,
        tau_scale,
        enc_pos,
        False,
        dec_rows,
    )
    cross_key_start = (
        jnp.zeros((item_count, HEADS, enc_rows, head_size), jnp.float32),
        jnp.zeros((item_count, HEADS, enc_rows, head_size), jnp.float32),
    )
    cross_key_total, cross_value_total = cross_key_update(
        cross_key_start,
        (
            lax.all_gather(cross_query.astype(jnp.float32), SEQ, axis=1, tiled=True),
            lax.all_gather(cross_mixed_grad.astype(jnp.float32), SEQ, axis=1, tiled=True),
            lax.all_gather(cross_log, SEQ, axis=1, tiled=True),
            lax.all_gather(cross_dot, SEQ, axis=1, tiled=True),
        ),
        jnp.int32(0),
    )
    cross_key_grad = scaled_grad(cross_key_total, tau_scale)
    cross_value_grad = merge_heads(cross_value_total).astype(jnp.bfloat16)
    cross_qkv_grad = jnp.stack(
        [
            weight_grad(cross_hidden, cross_query_grad),
            weight_grad(memory, cross_key_grad),
            weight_grad(memory, cross_value_grad),
        ]
    )
    memory_grad = project_back(cross_key_grad, cross_qkv[1]) + project_back(
        cross_value_grad, cross_qkv[2]
    )
    first_grad, dec_gain_one, dec_bias_one = norm_backward(
        dec_first_in,
        dec_gain[0],
        dec_bias[7],
        second_grad + project_back(cross_query_grad, cross_qkv[0]),
    )
    self_branch_grad = first_grad.astype(jnp.bfloat16)
    dec_out_grad = weight_grad(self_attended, self_branch_grad)
    self_out_bias = row_total(self_branch_grad)
    self_mixed_grad = project_back(self_branch_grad, dec_out).astype(jnp.bfloat16)
    self_dot = row_products(self_mixed_grad, self_mixed)
    self_back = query_grad_update(
        split_heads(self_query),
        split_heads(self_mixed_grad),
        jnp.transpose(self_log, (0, 2, 1)),
        jnp.transpose(self_dot, (0, 2, 1)),
        tau_scale,
        dec_pos,
        True,
        self_unpack,
        dec_rows,
    )
    self_query_total = self_back(
        jnp.zeros((item_count, HEADS, dec_rows, head_size), jnp.float32),
        (
            lax.all_gather(self_key, SEQ, axis=1, tiled=True),
            lax.all_gather(self_value, SEQ, axis=1, tiled=True),
        ),
        jnp.int32(0),
    )
    self_query_grad = scaled_grad(self_query_total, tau_scale)
    self_key_update = key_grad_update(
        split_heads(self_key),
        split_heads(self_value),
        jnp.zeros((item_count, dec_rows), jnp.float32),
        tau_scale,
        dec_pos,
        True,
        dec_rows,
    )
    self_key_start = (
        jnp.zeros((item_count, HEADS, dec_rows, head_size), jnp.float32),
        jnp.zeros((item_count, HEADS, dec_rows, head_size), jnp.float32),
    )
    self_key_total, self_value_total = self_key_update(
        self_key_start,
        (
            lax.all_gather(self_query.astype(jnp.float32), SEQ, axis=1, tiled=True),
            lax.all_gather(self_mixed_grad.astype(jnp.float32), SEQ, axis=1, tiled=True),
            lax.all_gather(self_log, SEQ, axis=1, tiled=True),
            lax.all_gather(self_dot, SEQ, axis=1, tiled=True),
        ),
        jnp.int32(0),
    )
    self_key_grad = scaled_grad(self_key_total, tau_scale)
    self_value_grad = merge_heads(self_value_total).astype(jnp.bfloat16)
    dec_qkv_grad = jnp.stack(
        [
            weight_grad(dec_in, self_query_grad),
            weight_grad(dec_in, self_key_grad),
            weight_grad(dec_in, self_value_grad),
        ]
    )
    dec_in_grad = (
        first_grad
        + project_back(self_query_grad, dec_qkv[0])
        + project_back(self_key_grad, dec_qkv[1])
        + project_back(self_value_grad, dec_qkv[2])
    )
    enc_second_grad, enc_gain_two, enc_bias_two = norm_backward(
        enc_second_in, enc_gain[1], enc_bias[4], memory_grad
    )
    from_enc_ff, enc_ff_in_grad, enc_ff_bias_grad, enc_ff_out_grad, enc_ff_out_bias = (
        feed_forward_back(
            enc_second_grad, enc_ff_hidden, enc_ff_pre, enc_ff_act, enc_ff_in, enc_ff_out
        )
    )
    enc_first_grad, enc_gain_one, enc_bias_one = norm_backward(
        enc_first_in, enc_gain[0], enc_bias[3], enc_second_grad + from_enc_ff
    )
    enc_branch_grad = enc_first_grad.astype(jnp.bfloat16)
    enc_out_grad = weight_grad(enc_attended, enc_branch_grad)
    enc_out_bias = row_total(enc_branch_grad)
    enc_mixed_grad = project_back(enc_branch_grad, enc_out).astype(jnp.bfloat16)
    enc_dot = row_products(enc_mixed_grad, enc_mixed)
    enc_back = query_grad_update(
        split_heads(enc_query),
        split_heads(enc_mixed_grad),
        jnp.transpose(enc_log, (0, 2, 1)),
        jnp.transpose(enc_dot, (0, 2, 1)),
        tau_scale,
        enc_pos,
        False,
        plain_unpack,
        enc_rows,
    )
    enc_query_total = enc_back(
        jnp.zeros((item_count, HEADS, enc_rows, head_size), jnp.float32),
        (
            lax.all_gather(enc_key, SEQ, axis=1, tiled=True),
            lax.all_gather(enc_value, SEQ, axis=1, tiled=True),
            lax.all_gather(delta_shift, SEQ, axis=1, tiled=True),
        ),
        jnp.int32(0),
    )
    enc_query_grad = scaled_grad(enc_query_total, tau_scale)
    enc_key_update = key_grad_update(
        split_heads(enc_key), split_heads(enc_value), enc_shift, tau_scale, enc_pos, False, enc_rows
    )
    enc_key_start = (
        jnp.zeros((item_count, HEADS, enc_rows, head_size), jnp.float32),
        jnp.zeros((item_count, HEADS, enc_rows, head_size), jnp.float32),
    )
    enc_key_total, enc_value_total = enc_key_update(
        enc_key_start,
        (
            lax.all_gather(enc_query.astype(jnp.float32), SEQ, axis=1, tiled=True),
            lax.all_gather(enc_mixed_grad.astype(jnp.float32), SEQ, axis=1, tiled=True),
            lax.all_gather(enc_log, SEQ, axis=1, tiled=True),
            lax.all_gather(enc_dot, SEQ, axis=1, tiled=True),
        ),
        jnp.int32(0),
    )
    enc_key_grad = scaled_grad(enc_key_total, tau_scale)
    enc_value_grad = merge_heads(enc_value_total).astype(jnp.bfloat16)
    enc_qkv_grad = jnp.stack(
        [
            weight_grad(enc_hidden, enc_query_grad),
            weight_grad(enc_hidden, enc_key_grad),
            weight_grad(enc_hidden, enc_value_grad),
        ]
    )
    enc_in_grad = (
        enc_first_grad
        + project_back(enc_query_grad, enc_qkv[0])
        + project_back(enc_key_grad, enc_qkv[1])
        + project_back(enc_value_grad, enc_qkv[2])
    )
    embed_grad = weight_grad(masked_series, enc_in_grad.astype(jnp.bfloat16))
    enc_query_bias_grad = row_total(enc_query_grad)
    enc_bias_grad = jnp.stack(
        [row_total(enc_value_grad), enc_out_bias, enc_ff_out_bias, enc_bias_one, enc_bias_two]
    )
    enc_gain_grad = jnp.stack([enc_gain_one, enc_gain_two])
    dec_bias_grad = jnp.stack(
        [
            row_total(self_query_grad),
            row_total(self_value_grad),
            self_out_bias,
            row_total(cross_query_grad),
            row_total(cross_value_grad),
            cross_out_bias,
            dec_ff_out_bias,
            dec_bias_one,
            dec_bias_two,
            dec_bias_three,
        ]
    )
    dec_gain_grad = jnp.stack([dec_gain_one, dec_gain_two, dec_gain_three])
    ff_bias_grad = jnp.stack([enc_ff_bias_grad, dec_ff_bias_grad])
    shares = (
        lax.psum_scatter(embed_grad, SEQ, scatter_dimension=1, tiled=True),
        lax.psum_scatter(enc_qkv_grad, SEQ, scatter_dimension=2, tiled=True),
        lax.psum_scatter(enc_out_grad, SEQ, scatter_dimension=1, tiled=True),
        lax.psum_scatter(enc_ff_in_grad, SEQ, scatter_dimension=1, tiled=True),
        lax.psum_scatter(enc_ff_out_grad, SEQ, scatter_dimension=1, tiled=True),
        lax.psum_scatter(enc_query_bias_grad, SEQ, scatter_dimension=0, tiled=True),
        lax.psum_scatter(enc_bias_grad, SEQ, scatter_dimension=1, tiled=True),
        lax.psum_scatter(enc_gain_grad, SEQ, scatter_dimension=1, tiled=True),
        lax.psum_scatter(dec_qkv_grad, SEQ, scatter_dimension=2, tiled=True),
        lax.psum_scatter(dec_out_grad, SEQ, scatter_dimension=1, tiled=True),
        lax.psum_scatter(cross_qkv_grad, SEQ, scatter_dimension=2, tiled=True),
        lax.psum_scatter(cross_out_grad, SEQ, scatter_dimension=1, tiled=True),
        lax.psum_scatter(dec_ff_in_grad, SEQ, scatter_dimension=1, tiled=True),
        lax.psum_scatter(dec_ff_out_grad, SEQ, scatter_dimension=1, tiled=True),
        lax.psum_scatter(dec_bias_grad, SEQ, scatter_dimension=1, tiled=True),
        lax.psum_scatter(dec_gain_grad, SEQ, scatter_dimension=1, tiled=True),
        lax.psum_scatter(ff_bias_grad, SEQ, scatter_dimension=1, tiled=True),
    )
    summed = lax.psum(
        (
            shares[0],
            shares[1],
            shares[2],
            shares[3],
            shares[4],
            shares[5],
            shares[6],
            shares[7],
            shares[8],
            shares[9],
            shares[10],
            shares[11],
            shares[12],
            shares[13],
            shares[14],
            shares[15],
            shares[16],
        ),
        BATCH,
    )
    return (
        decoded.astype(jnp.bfloat16),
        enc_in_grad,
        dec_in_grad,
        summed[0],
        summed[1],
        summed[2],
        summed[3],
        summed[4],
        summed[5],
        summed[6],
        summed[7],
        summed[8],
        summed[9],
        summed[10],
        summed[11],
        summed[12],
        summed[13],
        summed[14],
        summed[15],
        summed[16],
    )


F32 = jnp.float32
BF16 = jnp.bfloat16
MESH = pl.DeviceIdType.MESH
QUAD = 4
HALVES = 2
CORES = 2
LANES = 128
LINK_COUNT = 90
ORDER = (
    0, 1, 2, 3, 4, 5, 8, 6, 7, 9, 10, 12, 13, 15, 16, 17,
    41, 14, 18, 19, 20, 21, 22, 11, 23, 24, 42, 37, 27, 25, 30, 49,
    26, 32, 28, 38, 31, 43, 45, 36, 50, 53, 46, 57, 29, 54, 47, 33,
    61, 34, 39, 51, 58, 44, 55, 62, 48, 52, 40, 35, 59, 63, 56, 60,
    64,
)
VMEM_BYTES = 56 << 20
LOAD_FIRST = 3
LOAD_ORDER = (
    "value_embed",
    "enc_qkv",
    "dec_qkv",
    "enc_out",
    "enc_ff_in",
    "enc_ff_out",
    "dec_out",
    "cross_qkv",
    "cross_out",
    "dec_ff_in",
    "dec_ff_out",
)


def mm(left, right):
    return jnp.dot(left, right, preferred_element_type=F32)


def mm_right_t(left, right):
    return lax.dot_general(left, right, (((1,), (1,)), ((), ())), preferred_element_type=F32)


def mm_left_t(left, right):
    return lax.dot_general(left, right, (((0,), (0,)), ((), ())), preferred_element_type=F32)


def lane_index(shape):
    return lax.broadcasted_iota(jnp.int32, shape, len(shape) - 1)


def swap_halves(values):
    return pltpu.roll(values, LANES // 2, axis=1)


def low_lanes(first, second):
    return jnp.where(lane_index(first.shape) < LANES // 2, first, second)


def pack_rows(values):
    half = values.shape[0] // 2
    packed = []
    for pair in range(values.shape[1] // LANES):
        group = values[:, pair * LANES : (pair + 1) * LANES]
        top, bottom = group[:half], group[half:]
        packed.append(low_lanes(top, swap_halves(bottom)))
        packed.append(low_lanes(swap_halves(top), bottom))
    return packed


def unpack_rows(packed):
    groups = []
    for pair in range(len(packed) // 2):
        first, second = packed[2 * pair], packed[2 * pair + 1]
        top = low_lanes(first, swap_halves(second))
        bottom = low_lanes(swap_halves(first), second)
        groups.append(jnp.concatenate([top, bottom], axis=0))
    return jnp.concatenate(groups, axis=1)


def pack_pairs(keys, values):
    packed = []
    for pair in range(keys.shape[1] // LANES):
        key_group = keys[:, pair * LANES : (pair + 1) * LANES]
        value_group = values[:, pair * LANES : (pair + 1) * LANES]
        packed.append(low_lanes(key_group, swap_halves(value_group)))
        packed.append(low_lanes(swap_halves(key_group), value_group))
    return packed


def unpack_pairs(packed):
    keys, values = [], []
    for pair in range(len(packed) // 2):
        first, second = packed[2 * pair], packed[2 * pair + 1]
        keys.append(low_lanes(first, swap_halves(second)))
        values.append(low_lanes(swap_halves(first), second))
    return jnp.concatenate(keys, axis=1), jnp.concatenate(values, axis=1)


def norm_forward(values, gain, shift):
    centred = values - jnp.mean(values, axis=-1, keepdims=True)
    scale = lax.rsqrt(jnp.mean(centred * centred, axis=-1, keepdims=True) + epsilon)
    unit = centred * scale
    return unit * gain + shift, unit, scale


def norm_back(upstream, unit, scale, gain):
    inner = upstream * gain
    result = scale * (
        inner
        - jnp.mean(inner, axis=-1, keepdims=True)
        - unit * jnp.mean(inner * unit, axis=-1, keepdims=True)
    )
    return (
        result,
        jnp.sum(upstream * unit, axis=0, keepdims=True),
        jnp.sum(upstream, axis=0, keepdims=True),
    )


def rounded(values):
    return values.astype(BF16).astype(F32)


class View:
    def __init__(self, entries):
        for name, entry in entries.items():
            if isinstance(entry, dict):
                entry = View(entry)
            elif isinstance(entry, (list, tuple)):
                entry = [View(part) if isinstance(part, dict) else part for part in entry]
            setattr(self, name, entry)


class Weight:
    def __init__(self, copy, held):
        self.copy, self.held, self.here = copy, held, False

    def start(self):
        self.copy.start()

    def __call__(self):
        if not self.here:
            self.copy.wait()
            self.here = True
        return self.held


def fused_body(structures, *refs):
    entries = {}
    for structure in structures:
        count = structure.num_leaves
        entries.update(jax.tree.unflatten(structure, refs[:count]))
        refs = refs[count:]
    ref = View(entries)
    small = View(entries["held_blocks"])
    rows, width = ref.enc_in.shape
    hidden, channels, chips = ref.ff_bias.shape[1], ref.series.shape[1], HEADS
    packed_rows = rows // 2
    keys_total = chips * CORES * rows
    block_queries = chips * packed_rows
    column = width // (chips * CORES)
    depth = chips * CORES // QUAD

    place = lax.axis_index(SEQ)
    item = lax.axis_index(BATCH)
    core = lax.rem(place, 2)
    chip = place // 2
    x_place = lax.rem(chip, 2)
    z_place = chip // 2
    quad = lax.rem(place, QUAD)
    core_dev = (chip * 2 + (1 - core), item)
    x_dev = (z_place * QUAD + (1 - x_place) * 2 + core, item)
    diagonal_dev = (z_place * QUAD + (1 - x_place) * 2 + (1 - core), item)
    item_dev = (place, 1 - item)
    z_high, z_odd = z_place // 2, lax.rem(z_place, 2)
    near_dev = ((z_high * 2 + 1 - z_odd) * QUAD + quad, item)
    far_dev = (((1 - z_high) * 2 + z_odd) * QUAD + quad, item)
    x_quad = (1 - x_place) * 2 + core
    other_dev = (chip * 2 + (1 - core), 1 - item)
    item_quad = item * 2 + core
    next_quad = (1 - item) * 2 + core

    def same_core(step):
        peer = lax.rem(chip + step, chips)
        return peer, (peer * 2 + core, item)

    def z_peer(step):
        peer = lax.rem(z_place + step, depth)
        return peer, (peer * QUAD + quad, item)

    barrier = pltpu.get_barrier_semaphore()
    greeted = [core_dev, diagonal_dev, item_dev, other_dev] + [same_core(step)[1] for step in range(1, chips)]
    for device in greeted:
        pl.semaphore_signal(barrier, inc=1, device_id=device, device_id_type=MESH)

    blocks = []
    for index, (name, target) in enumerate(entries["held_blocks"].items()):
        blocks.append(pltpu.make_async_copy(entries[name], target, ref.block_sem.at[index]))
        blocks[-1].start()
    loaded = {}
    for index, name in enumerate(LOAD_ORDER):
        source, target = getattr(ref.weight, name), getattr(ref.held, name)
        copy = pltpu.make_async_copy(source, target, ref.load_sem.at[index])
        loaded[name] = Weight(copy, target)
    weight = View(loaded)
    for name in LOAD_ORDER[:LOAD_FIRST]:
        loaded[name].start()
    for copy in blocks:
        copy.wait()

    batches = []

    def ship(copies, meter=None):
        index = len(batches)
        made = []
        for source, target, device in copies:
            made.append(
                pltpu.make_async_remote_copy(
                    src_ref=source,
                    dst_ref=target,
                    send_sem=ref.send_sem.at[index],
                    recv_sem=ref.recv_sem.at[index],
                    device_id=device,
                    device_id_type=MESH,
                )
            )
            made[-1].start()
        batches.append((index, made, meter))
        return batches[-1]

    def send(source, target, device):
        return ship([(source, target, device)])

    def arrive(batch):
        index, made, meter = batch
        if meter is None:
            made[0].wait_recv()
        else:
            pltpu.make_async_copy(meter, meter, ref.recv_sem.at[index]).wait()

    def depart(batch):
        index, made, meter = batch
        if meter is None:
            made[0].wait_send()
        else:
            pltpu.make_async_copy(meter, meter, ref.send_sem.at[index]).wait()

    def spread(source, target_at):
        copies = []
        for step in range(1, chips):
            peer, device = same_core(step)
            copies.append((source.at[peer], target_at(chip), device))
        return ship(copies, source.at[pl.ds(0, chips - 1)])

    def share(block):
        return [
            block,
            send(block.at[quad], block.at[quad], core_dev),
            send(block.at[quad], block.at[quad], x_dev),
        ]

    def relay(shared):
        block = shared[0]
        arrive(shared.pop())
        shared.append(send(block.at[x_quad], block.at[x_quad], core_dev))

    def settle(shared):
        while len(shared) > 1:
            arrive(shared.pop())

    def gathered(block, start, features):
        value = block[:, :, start : start + features]
        return value.reshape(value.shape[0] * value.shape[1], value.shape[2])

    def cut_columns(values, group, start):
        part = lane_index((rows, LANES)) // column
        for member in range(QUAD):
            total = None
            for level in range(depth):
                cut = values[:, level * LANES : (level + 1) * LANES]
                shift = (column * (level - member)) % LANES
                moved = pltpu.roll(cut, shift, axis=1) if shift else cut
                total = moved if total is None else jnp.where(part == level, moved, total)
            group.cut[member, :, start : start + LANES] = total.astype(BF16)

    def share_columns(group, start, stop):
        source, target = group.cut, group.met
        target[quad, :, start:stop] = source[quad, :, start:stop]
        copies = []
        for device, member in (
            (core_dev, x_place * 2 + 1 - core),
            (x_dev, x_quad),
            (diagonal_dev, (1 - x_place) * 2 + 1 - core),
        ):
            copies.append(
                (
                    source.at[member, :, pl.ds(start, stop - start)],
                    target.at[quad, :, pl.ds(start, stop - start)],
                    device,
                )
            )
        return ship(copies, target.at[pl.ds(0, QUAD - 1), :, pl.ds(start, stop - start)])

    def share_item(group):
        group.tokens[item_quad] = group.own[item]
        return [
            group.tokens,
            send(group.own.at[item], group.tokens.at[item_quad], core_dev),
            send(group.own.at[1 - item], group.tokens.at[item_quad], item_dev),
        ]

    def relay_item(shared):
        arrive(shared.pop())
        block = shared[0]
        shared.append(send(block.at[next_quad], block.at[next_quad], core_dev))

    def cut_cores(values, group, start):
        part = lane_index((rows, LANES)) // column
        for member in range(CORES):
            for pair in range(depth // 2):
                total = None
                for piece in range(QUAD):
                    level = pair * 2 + piece // 2
                    cut = values[:, level * LANES : (level + 1) * LANES]
                    place_in = 2 * (piece % 2) + member
                    shift = (column * (piece - place_in)) % LANES
                    moved = pltpu.roll(cut, shift, axis=1) if shift else cut
                    total = moved if total is None else jnp.where(part == piece, moved, total)
                at = start + pair * LANES
                group.cut[member, :, at : at + LANES] = total.astype(BF16)

    def share_cores(group):
        group.met[item_quad] = group.cut[core]
        return ship(
            [
                (group.cut.at[1 - core], group.met.at[item_quad], core_dev),
                (group.cut.at[core], group.met.at[item_quad], item_dev),
                (group.cut.at[1 - core], group.met.at[item_quad], other_dev),
            ],
            group.met.at[pl.ds(0, QUAD - 1)],
        )

    def build_cores(group):
        lanes = width // 2
        met = group.met[...].reshape(QUAD * rows, 2 * lanes)
        tokens = group.tokens[...]
        tokens = tokens.reshape(QUAD * rows, tokens.shape[2])
        for index, (start, stop) in enumerate(((0, hidden // 2), (hidden // 2, tokens.shape[1]))):
            gradient = mm_left_t(met[:, index * lanes : (index + 1) * lanes], tokens[:, start:stop])
            gradient = gradient.astype(BF16)
            for at in range(chips):
                group.part[at % 2, at // 4, at // 2 % 2, :, start:stop] = gradient[
                    at * column : (at + 1) * column
                ]

    def columns_of(group, start, stop):
        value = group.met[:, :, start:stop]
        return value.reshape(QUAD * rows, stop - start)

    def put_rows(target, level, start, values):
        half = target.shape[3]
        count = values.shape[0]
        done = 0
        while done < count:
            which, offset = divmod(start + done, half)
            take = min(count - done, half - offset)
            target[which, level // 2, level % 2, offset : offset + take, :] = values[
                done : done + take, :
            ]
            done += take

    def put_gradient(target, start, gradient):
        count = gradient.shape[0] // depth
        gradient = gradient.astype(BF16)
        short = -gradient.shape[1] % width
        pieces = gradient.shape[1] // width
        for level in range(depth):
            block = gradient[level * count : (level + 1) * count]
            for piece in range(pieces):
                put_rows(
                    target,
                    level,
                    start + piece * count,
                    block[:, piece * width : (piece + 1) * width],
                )
            if short:
                tail = jnp.concatenate(
                    [block[:, pieces * width :], jnp.zeros((count, short), BF16)], axis=1
                )
                put_rows(target, level, start + pieces * count, tail)

    def both_sums(left, right):
        return (left.astype(F32) + right.astype(F32)).astype(BF16)

    def steps_of(group, which, device):
        def near():
            group.half[...] = both_sums(group.part[which], group.item[...])
            return send(group.half.at[:, 1 - z_odd], group.near, near_dev)

        def far():
            group.pair[...] = both_sums(group.half[:, z_odd], group.near[...])
            return send(group.pair.at[1 - z_high], group.far, far_dev)

        def last():
            group.sum[item] = both_sums(group.pair[z_high], group.far[...])
            return send(group.sum.at[item], group.sum.at[item], item_dev)

        for level in range(2):
            group.pushes.append(
                partial(send, group.part.at[1 - which, level], group.item.at[level], device)
            )
        return [near, far, last]

    def advance(group):
        for batch in group.batches:
            arrive(batch)
        group.batches = [group.steps.pop(0)()]

    def push(group, count=1):
        for index in range(count):
            group.batches.append(group.pushes.pop(0)())

    def finish(group):
        for batch in group.batches:
            arrive(batch)

    def gather_depth(block, part, parts):
        count = rows // parts
        cut = pl.ds(part * count, count)
        here = block.at[z_place, x_place, cut]
        copies = [(here, here, z_peer(step)[1]) for step in range(1, depth)]
        return ship(copies, block.at[pl.ds(0, depth - 1), 0, cut])

    def gather_x(block, gathers):
        for batch in gathers:
            arrive(batch)
        return send(block.at[:, x_place], block.at[:, x_place], x_dev)

    def head_gradients(own, space, block):
        value = block[...]
        tokens = value.reshape((chips,) + value.shape[2:])
        tokens = jnp.concatenate([tokens, jnp.ones((chips, rows, LANES), BF16)], axis=2)
        features = tokens.shape[2]
        queries = own.t_query_grad[...].reshape(block_queries, LANES)
        total = None
        for half in range(HALVES):
            part = tokens[:, half * packed_rows : (half + 1) * packed_rows]
            part = mm_left_t(queries, part.reshape(block_queries, features))
            part = part[half * LANES // 2 : (half + 1) * LANES // 2]
            total = part if total is None else total + part
        pairs = own.t_pair_grad[...].reshape(chips * rows, LANES)
        both = mm_left_t(pairs, tokens.reshape(chips * rows, features))
        for index, gradient in enumerate((total, both[: LANES // 2], both[LANES // 2 :])):
            for which in range(CORES):
                space.mine[which, index * column : (index + 1) * column, :] = gradient[
                    which * column : (which + 1) * column
                ].astype(BF16)
        return send(space.mine.at[1 - core], space.core, core_dev)

    def heads_item(space, batch):
        arrive(batch)
        space.both[...] = both_sums(space.mine[core], space.core[...])
        return send(space.both, space.item, item_dev)

    def heads_done(space, batch, target):
        arrive(batch)
        target[...] = space.both[...].astype(F32) + space.item[...].astype(F32)

    def set_vector(row, value):
        ref.vec[row : row + 1, :] = value

    att_enc, att_self, att_cross = ref.attention
    dec_in_part, cross_part, enc_in_part, embed_part = ref.group
    dec_out_part, enc_out_part = ref.core_group
    for group in ref.group + ref.core_group:
        group.batches, group.pushes = [], []
    for group in ref.group:
        group.steps = steps_of(group, item, item_dev)
    for group in ref.core_group:
        group.steps = steps_of(group, x_place, x_dev)
    for group, result in zip(ref.group + ref.core_group, ref.sums):
        group.sum = result
    enc_ff = (weight.enc_ff_in, weight.enc_ff_out)
    dec_ff = (weight.dec_ff_in, weight.dec_ff_out)

    def build(group, row, start, features, tokens, wide=False):
        gradient = mm_left_t(columns_of(group, start, start + features), tokens)
        if wide:
            put_gradient(group.part, row, gradient)
            return
        for which in range(features // LANES):
            put_gradient(
                group.part,
                row + which * column,
                gradient[which * LANES : (which + 1) * LANES],
            )

    tau = ref.tau_scale[0]
    group_row = lax.broadcasted_iota(jnp.int32, small.channel_mask.shape, 0)
    chosen = jnp.where(
        group_row == ref.item_group[0], small.channel_mask[...].astype(F32), 0.0
    )
    channel_row = jnp.sum(chosen, axis=0, keepdims=True)
    masked = (small.series[...].astype(F32) * channel_row).astype(BF16)
    dec_hidden = small.dec_in[...]
    ref.g_dec_in[z_place, x_place] = dec_hidden
    ref.x_series[quad] = jnp.zeros(ref.x_series.shape[1:], BF16)
    ref.x_series[quad, :, 0:channels] = masked

    shift_row = small.delta_shift[...].astype(F32)
    ref.t_shift[...] = jnp.broadcast_to(
        jnp.concatenate([shift_row, shift_row], axis=1), ref.t_shift.shape
    )
    ref.shift[chip, core] = ref.t_shift[...]
    pl.semaphore_wait(barrier, len(greeted))
    go_shift = ship(
        [
            (ref.t_shift, ref.shift.at[chip, core], same_core(step)[1])
            for step in range(1, chips)
        ],
        ref.shift.at[pl.ds(0, chips - 1), 0],
    )

    embedded = small.enc_in[...].astype(F32) + mm(masked, weight.value_embed()[...])
    ref.embedded[...] = embedded
    enc_hidden = embedded.astype(BF16)
    ref.g_enc_hidden[z_place, x_place] = enc_hidden
    for name in LOAD_ORDER[LOAD_FIRST:]:
        loaded[name].start()

    def send_queries(own, query):
        for head, packed in enumerate(pack_rows(query)):
            own.t_query[head] = packed.astype(BF16)
        own.query[chip] = own.t_query[chip]
        return spread(own.t_query, lambda at: own.query.at[at])

    def send_pairs(own, keys, values):
        for head, packed in enumerate(pack_pairs(keys, values)):
            own.t_pair[head] = packed.astype(BF16)
        own.pair[chip, core] = own.t_pair[chip]
        return spread(own.t_pair, lambda at: own.pair.at[at, core])

    def pass_on(own):
        block = own.pair
        return send(block.at[:, core], block.at[:, core], core_dev)

    qkv = weight.enc_qkv()
    enc_query = mm(enc_hidden, qkv[0]) + small.enc_query_bias[...]
    enc_key = mm(enc_hidden, qkv[1])
    enc_value = mm(enc_hidden, qkv[2]) + small.enc_bias[0:1, :]
    go_enc_pair = send_pairs(att_enc, enc_key, enc_value)
    go_enc_query = send_queries(att_enc, enc_query)
    qkv = weight.dec_qkv()
    self_query = mm(dec_hidden, qkv[0]) + small.dec_bias[0:1, :]
    self_key = mm(dec_hidden, qkv[1])
    self_value = mm(dec_hidden, qkv[2]) + small.dec_bias[1:2, :]
    go_self_pair = send_pairs(att_self, self_key, self_value)
    go_self_query = send_queries(att_self, self_query)

    def attention(own, shifted, causal):
        pairs = own.pair[...].reshape(keys_total, LANES)
        pairs_t = pairs.T
        own.pair_t[...] = pairs_t
        query_t = own.query[...].reshape(block_queries, LANES).astype(F32).T
        zeros = jnp.zeros((LANES // 2, block_queries), F32)
        for half in range(HALVES):
            part = query_t[half * LANES // 2 : (half + 1) * LANES // 2]
            side = jnp.concatenate([part, zeros], axis=0).astype(BF16)
            scores = mm(pairs, side) * (tau * 0.125)
            if shifted:
                moved = ref.shift_columns[...]
                scores = scores + jnp.concatenate([moved] * (block_queries // LANES), axis=1)
            if causal:
                key_at = lax.broadcasted_iota(jnp.int32, scores.shape, 0)
                lane = lane_index(scores.shape)
                query_at = (
                    (lane // packed_rows * 2 + core) * rows
                    + half * packed_rows
                    + lane % packed_rows
                )
                scores = jnp.where(key_at > query_at, masked_score, scores)
            weights = jnp.exp(scores - jnp.max(scores, axis=0, keepdims=True))
            inverse = 1.0 / jnp.sum(weights, axis=0, keepdims=True)
            low_weights = weights.astype(BF16)
            own.weights[half] = low_weights
            own.inverse[half] = jnp.broadcast_to(inverse, (8, block_queries))
            mixed_t = mm(pairs_t, low_weights)[LANES // 2 :] * inverse
            own.mixed_t[half * LANES // 2 : (half + 1) * LANES // 2, :] = mixed_t
        mixed = own.mixed_t[...].T.astype(BF16)
        own.t_mixed[...] = mixed.reshape(chips, packed_rows, LANES)
        own.mixed[chip] = own.t_mixed[chip]
        return spread(own.t_mixed, lambda at: own.mixed.at[at])

    def mixed_rows(own):
        return unpack_rows(
            [own.mixed[head].astype(F32) for head in range(chips)]
        ).astype(BF16)

    arrive(go_shift)
    on_shift = send(ref.shift.at[:, core], ref.shift.at[:, core], core_dev)
    arrive(on_shift)
    for block in range(chips):
        line = low_lanes(ref.shift[block, 0], ref.shift[block, 1])[0:1, :] * 0.125
        ref.shift_columns[block * LANES : (block + 1) * LANES, :] = jnp.broadcast_to(
            line, (LANES, LANES)
        ).T
    arrive(go_enc_pair)
    on_enc = pass_on(att_enc)
    arrive(go_enc_query)
    arrive(on_enc)
    back_enc = attention(att_enc, True, False)
    go_dec_in = [gather_depth(ref.g_dec_in, 0, 2)]
    share_series = share(ref.x_series)
    arrive(go_self_pair)
    on_self = pass_on(att_self)
    arrive(go_self_query)
    arrive(on_self)
    back_self = attention(att_self, False, True)

    def feed_forward(values, weights, bias_row, out_bias, low_at, group, slope):
        low = values.astype(BF16)
        low_at[quad, :, 0:width] = low
        weight_in, weight_out = weights[0](), weights[1]()
        total = out_bias
        for piece in range(hidden // width):
            cut = slice(piece * width, (piece + 1) * width)
            pre = mm(low, weight_in[:, cut]) + small.ff_bias[bias_row : bias_row + 1, cut]
            normal = 0.5 * (1.0 + lax.erf(pre * 0.7071067811865476))
            act = (pre * normal).astype(BF16)
            slope[:, cut] = normal + pre * (
                jnp.exp(pre * pre * -0.5) * 0.3989422804014327
            )
            half, at = divmod(piece * width, hidden // 2)
            group.own[half, :, at : at + width] = act
            total = total + mm(act, weight_out[cut, :])
        return total

    def feed_forward_back(upstream, weights, slope, vector_row, group):
        low = upstream.astype(BF16)
        weight_in, weight_out = weights[0](), weights[1]()
        total = None
        for piece in range(hidden // width):
            cut = slice(piece * width, (piece + 1) * width)
            act_grad = mm_right_t(low, weight_out[cut, :])
            pre_grad = (act_grad * slope[:, cut]).astype(BF16)
            sums = jnp.sum(pre_grad.astype(F32), axis=0, keepdims=True)
            for member in range(QUAD):
                at = piece * LANES
                ref.vec[vector_row + member : vector_row + member + 1, at : at + LANES] = sums[
                    :, member * LANES : (member + 1) * LANES
                ]
                group.cut[member, :, at : at + LANES] = pre_grad[
                    :, member * LANES : (member + 1) * LANES
                ]
            more = mm_right_t(pre_grad, weight_in[:, cut])
            total = more if total is None else total + more
        return total

    def save_norm(index, unit, scale):
        ref.unit[index] = unit
        ref.scale[index] = jnp.broadcast_to(scale, (rows, LANES))

    def saved_norm(index):
        return ref.unit[index], ref.scale[index, :, 0:1]

    def keep_mixed(group, values):
        for half in range(HALVES):
            group.own[half, :, hidden // 2 :] = values[
                :, half * width // 2 : (half + 1) * width // 2
            ]

    arrive(back_enc)
    attended = mixed_rows(att_enc)
    keep_mixed(enc_out_part, attended)
    first, unit, scale = norm_forward(
        embedded + mm(attended, weight.enc_out()[...]) + small.enc_bias[1:2, :],
        small.enc_gain[0:1, :],
        small.enc_bias[3:4, :],
    )
    save_norm(0, unit, scale)
    second, unit, scale = norm_forward(
        first + feed_forward(
            first,
            enc_ff,
            0,
            small.enc_bias[2:3, :],
            ref.x_early,
            enc_out_part,
            ref.enc_slope,
        ),
        small.enc_gain[1:2, :],
        small.enc_bias[4:5, :],
    )
    save_norm(1, unit, scale)
    memory = second.astype(BF16)
    ref.x_early[quad, :, width : 2 * width] = memory
    share_enc_out = share_item(enc_out_part)
    qkv = weight.cross_qkv()
    cross_key = mm(memory, qkv[1])
    cross_value = mm(memory, qkv[2]) + small.dec_bias[4:5, :]
    go_cross_pair = send_pairs(att_cross, cross_key, cross_value)

    arrive(back_self)
    attended = mixed_rows(att_self)
    ref.x_early[quad, :, 2 * width : 3 * width] = attended
    first, unit, scale = norm_forward(
        small.dec_in[...].astype(F32)
        + mm(attended, weight.dec_out()[...])
        + small.dec_bias[2:3, :],
        small.dec_gain[0:1, :],
        small.dec_bias[7:8, :],
    )
    save_norm(2, unit, scale)
    ref.first_dec[...] = first
    low = first.astype(BF16)
    ref.x_early[quad, :, 3 * width : 4 * width] = low
    go_cross_query = send_queries(att_cross, mm(low, qkv[0]) + small.dec_bias[3:4, :])
    share_early = share(ref.x_early)
    go_dec_in.append(gather_depth(ref.g_dec_in, 1, 2))

    arrive(go_cross_pair)
    on_cross = pass_on(att_cross)
    arrive(go_cross_query)
    arrive(on_cross)
    back_cross = attention(att_cross, True, False)
    go_enc_hidden = [gather_depth(ref.g_enc_hidden, 0, 1)]
    on_dec_in = gather_x(ref.g_dec_in, go_dec_in)
    relay_item(share_enc_out)
    relay(share_series)
    arrive(back_cross)
    attended = mixed_rows(att_cross)
    keep_mixed(dec_out_part, attended)
    second, unit, scale = norm_forward(
        ref.first_dec[...]
        + mm(attended, weight.cross_out()[...])
        + small.dec_bias[5:6, :],
        small.dec_gain[1:2, :],
        small.dec_bias[8:9, :],
    )
    save_norm(3, unit, scale)

    forward = feed_forward(
        second,
        dec_ff,
        1,
        small.dec_bias[6:7, :],
        ref.x_late,
        dec_out_part,
        ref.dec_slope,
    )
    share_dec_out = share_item(dec_out_part)
    third, unit, scale = norm_forward(
        second + forward,
        small.dec_gain[2:3, :],
        small.dec_bias[9:10, :],
    )
    ref.dec_result[...] = third.astype(BF16)

    def norm_step(index, upstream, gain, gain_row, gain_vector, shift_vector):
        unit, scale = saved_norm(index)
        result, gain_grad, shift_grad = norm_back(
            upstream, unit, scale, gain[gain_row : gain_row + 1, :]
        )
        set_vector(gain_vector, gain_grad)
        set_vector(shift_vector, shift_grad)
        return result

    def column_sum(values):
        return jnp.sum(rounded(values), axis=0, keepdims=True)

    third_grad, gain_grad, shift_grad = norm_back(
        small.cotangent[...].astype(F32), unit, scale, small.dec_gain[2:3, :]
    )
    set_vector(20, gain_grad)
    set_vector(17, shift_grad)
    from_ff = feed_forward_back(third_grad, dec_ff, ref.dec_slope, 25, dec_in_part)
    second_grad = norm_step(3, third_grad + from_ff, small.dec_gain, 1, 19, 16)
    ref.second_grad[...] = second_grad

    def send_mixed_grad(own, branch_grad, out_weight):
        mixed_grad = mm_right_t(branch_grad.astype(BF16), out_weight[...])
        for head, packed in enumerate(pack_rows(mixed_grad)):
            own.t_grad[head] = packed.astype(BF16)
        own.grad[chip] = own.t_grad[chip]
        return spread(own.t_grad, lambda at: own.grad.at[at])

    go_cross_grad = send_mixed_grad(att_cross, second_grad, weight.cross_out())
    ff_width = hidden // QUAD

    def attention_back(own):
        pairs = own.pair[...].reshape(keys_total, LANES)
        pairs_t = own.pair_t[...]
        queries = own.query[...].reshape(block_queries, LANES).astype(F32)
        grads = own.grad[...].reshape(block_queries, LANES).astype(F32)
        grads_t = grads.T
        zeros = jnp.zeros((LANES // 2, block_queries), F32)
        blank = jnp.zeros_like(queries)
        query_grads = []
        key_total = value_total = None
        for half in range(HALVES):
            cut = slice(half * LANES // 2, (half + 1) * LANES // 2)
            grad_t = grads_t[cut]
            row_dot = jnp.sum(grad_t * own.mixed_t[cut, :], axis=0, keepdims=True)
            side = jnp.concatenate([zeros, grad_t], axis=0).astype(BF16)
            prob_grads = mm(pairs, side)
            probabilities = own.weights[half].astype(F32) * own.inverse[half, 0:1, :]
            score_grads = (probabilities * (prob_grads - row_dot)).astype(BF16)
            query_grads.append(mm(pairs_t, score_grads)[: LANES // 2])
            if half == 0:
                query_side = low_lanes(queries, blank)
                grad_side = low_lanes(blank, swap_halves(grads))
            else:
                query_side = low_lanes(swap_halves(queries), blank)
                grad_side = low_lanes(blank, grads)
            key_part = mm(score_grads, query_side.astype(BF16))
            value_part = mm(probabilities.astype(BF16), grad_side.astype(BF16))
            key_total = key_part if key_total is None else key_total + key_part
            value_total = value_part if value_total is None else value_total + value_part
        factor = tau * 0.125
        query_grad = (jnp.concatenate(query_grads, axis=0) * factor).T.astype(BF16)
        own.t_query_grad[...] = query_grad.reshape(chips, packed_rows, LANES)
        own.query_grad[chip] = own.t_query_grad[chip]
        go_query = spread(
            own.t_query_grad, lambda at: own.query_grad.at[at]
        )
        pair_grad = (key_total * factor + value_total).reshape(chips, CORES, rows, LANES)
        for which in range(CORES):
            own.pair_sum[which] = pair_grad[:, which]
            own.t_part[which] = pair_grad[:, which].astype(BF16)
        exchange = send(own.t_part.at[1 - core], own.part, core_dev)
        return go_query, exchange

    def attention_back_pairs(own, exchange):
        arrive(exchange)
        total = own.pair_sum[core] + own.part[...].astype(F32)
        own.t_pair_grad[...] = total.astype(BF16)
        own.pair_grad[chip] = own.t_pair_grad[chip]
        return spread(own.t_pair_grad, lambda at: own.pair_grad.at[at])

    def query_grad_rows(own):
        return unpack_rows(
            [own.query_grad[head].astype(F32) for head in range(chips)]
        )

    def pair_grad_rows(own):
        return unpack_pairs([own.pair_grad[head].astype(F32) for head in range(chips)])

    def input_grad(own, weights, first):
        query_grad = query_grad_rows(own)
        key_grad, value_grad = pair_grad_rows(own)
        return (
            first[...]
            + mm_right_t(query_grad.astype(BF16), weights[0])
            + mm_right_t(key_grad.astype(BF16), weights[1])
            + mm_right_t(value_grad.astype(BF16), weights[2])
        )

    now = SimpleNamespace()
    steps = []

    def step(body):
        steps.append(body)

    @step
    def late_rows():
        now.share_late = share(ref.x_late)

    @step
    def dec_in_columns():
        now.columns_dec_in = share_columns(dec_in_part, 0, ff_width)

    @step
    def dec_out_columns():
        cut_cores(third_grad, dec_out_part, 0)
        cut_cores(second_grad, dec_out_part, width // 2)
        now.columns_dec_out = share_cores(dec_out_part)
        set_vector(14, column_sum(third_grad))
        set_vector(13, column_sum(second_grad))

    @step
    def early_relay():
        relay(share_early)

    @step
    def cross_back():
        arrive(go_cross_grad)
        now.go_query, now.exchange = attention_back(att_cross)

    @step
    def late_relay():
        relay(now.share_late)

    @step
    def dec_out_relay():
        relay_item(share_dec_out)

    @step
    def cross_pairs():
        now.go_pair = attention_back_pairs(att_cross, now.exchange)

    @step
    def dec_in_build():
        settle(now.share_late)
        arrive(now.columns_dec_in)
        build(dec_in_part, 0, 0, ff_width, gathered(ref.x_late, 0, width), wide=True)
        push(dec_in_part, 2)

    @step
    def dec_out_build():
        settle(share_dec_out)
        arrive(now.columns_dec_out)
        build_cores(dec_out_part)

    @step
    def dec_out_push():
        push(dec_out_part)

    @step
    def dec_out_push_two():
        push(dec_out_part)

    @step
    def self_branch():
        arrive(now.go_query)
        now.cross_query_grad = query_grad_rows(att_cross)
        now.first_grad = norm_step(
            2,
            ref.second_grad[...]
            + mm_right_t(now.cross_query_grad.astype(BF16), weight.cross_qkv()[0]),
            small.dec_gain,
            0,
            18,
            15,
        )
        ref.first_grad[...] = now.first_grad
        now.go_self_grad = send_mixed_grad(att_self, now.first_grad, weight.dec_out())
        set_vector(10, column_sum(now.first_grad))

    @step
    def encoder_back():
        arrive(now.go_pair)
        qkv = weight.cross_qkv()
        now.cross_key_grad, now.cross_value_grad = pair_grad_rows(att_cross)
        memory_grad = mm_right_t(now.cross_key_grad.astype(BF16), qkv[1]) + mm_right_t(
            now.cross_value_grad.astype(BF16), qkv[2]
        )
        now.second = norm_step(1, memory_grad, small.enc_gain, 1, 7, 5)
        from_ff = feed_forward_back(now.second, enc_ff, ref.enc_slope, 21, enc_in_part)
        now.first = norm_step(0, now.second + from_ff, small.enc_gain, 0, 6, 4)
        ref.enc_first_grad[...] = now.first
        now.go_enc_grad = send_mixed_grad(att_enc, now.first, weight.enc_out())

    @step
    def vector_sums():
        set_vector(3, column_sum(now.second))
        set_vector(2, column_sum(now.first))
        set_vector(11, column_sum(now.cross_query_grad))
        set_vector(12, column_sum(now.cross_value_grad))
        for row in (0, 1, 8, 9, 29, 30, 31):
            set_vector(row, jnp.zeros((1, width), F32))
        now.vec_item = send(ref.vec, ref.vec_item, item_dev)

    @step
    def cross_columns():
        for index, values in enumerate(
            (now.cross_query_grad, now.cross_key_grad, now.cross_value_grad, now.first_grad)
        ):
            cut_columns(values, cross_part, index * LANES)
        now.columns_cross = share_columns(cross_part, 0, 4 * LANES)

    @step
    def enc_in_columns():
        now.columns_enc_in = share_columns(enc_in_part, 0, ff_width)

    @step
    def enc_out_columns():
        cut_cores(now.second, enc_out_part, 0)
        cut_cores(now.first, enc_out_part, width // 2)
        now.columns_enc_out = share_cores(enc_out_part)

    @step
    def self_back():
        arrive(now.go_self_grad)
        now.go_self_query_grad, now.exchange_self = attention_back(att_self)

    @step
    def enc_back():
        arrive(now.go_enc_grad)
        now.go_enc_query_grad, now.exchange_enc = attention_back(att_enc)

    @step
    def cross_build():
        settle(share_early)
        arrive(now.columns_cross)
        build(cross_part, 0, 0, LANES, gathered(ref.x_early, 3 * width, width))
        build(cross_part, column, LANES, 2 * LANES, gathered(ref.x_early, width, width))
        build(cross_part, 3 * column, 3 * LANES, LANES, gathered(ref.x_early, 2 * width, width))
        push(cross_part, 2)

    @step
    def enc_pairs():
        now.go_enc_pair_grad = attention_back_pairs(att_enc, now.exchange_enc)

    @step
    def self_pairs():
        now.go_self_pair_grad = attention_back_pairs(att_self, now.exchange_self)

    @step
    def enc_in_build():
        settle(share_early)
        arrive(now.columns_enc_in)
        build(enc_in_part, 0, 0, ff_width, gathered(ref.x_early, 0, width), wide=True)
        push(enc_in_part, 2)

    @step
    def enc_out_build():
        settle(share_enc_out)
        arrive(now.columns_enc_out)
        build_cores(enc_out_part)

    @step
    def enc_out_push():
        push(enc_out_part)

    @step
    def enc_out_push_two():
        push(enc_out_part)

    @step
    def self_heads():
        arrive(on_dec_in)
        now.core_self = head_gradients(att_self, ref.head_self, ref.g_dec_in)

    @step
    def self_heads_item():
        now.item_self = heads_item(ref.head_self, now.core_self)

    @step
    def self_heads_done():
        heads_done(ref.head_self, now.item_self, ref.heads[1])

    @step
    def enc_input():
        arrive(now.go_enc_query_grad)
        arrive(now.go_enc_pair_grad)
        total = input_grad(att_enc, weight.enc_qkv(), ref.enc_first_grad)
        ref.enc_grad[...] = total
        cut_columns(total, embed_part, 0)
        now.columns_embed = share_columns(embed_part, 0, LANES)

    @step
    def self_input():
        arrive(now.go_self_query_grad)
        arrive(now.go_self_pair_grad)
        ref.dec_grad[...] = input_grad(att_self, weight.dec_qkv(), ref.first_grad)

    @step
    def enc_hidden_hop():
        now.on_enc_hidden = gather_x(ref.g_enc_hidden, go_enc_hidden)

    @step
    def enc_heads():
        arrive(now.on_enc_hidden)
        now.core_enc = head_gradients(att_enc, ref.head_enc, ref.g_enc_hidden)

    @step
    def enc_heads_item():
        now.item_enc = heads_item(ref.head_enc, now.core_enc)

    @step
    def enc_heads_done():
        heads_done(ref.head_enc, now.item_enc, ref.heads[0])

    @step
    def embed_build():
        settle(share_series)
        arrive(now.columns_embed)
        build(embed_part, 0, 0, LANES, gathered(ref.x_series, 0, ref.x_series.shape[2]))
        push(embed_part, 2)

    @step
    def vector_core():
        arrive(now.vec_item)
        ref.vec_a[...] = ref.vec[...] + ref.vec_item[...]
        now.vec_core = send(ref.vec_a, ref.vec_core, core_dev)

    @step
    def vector_x():
        arrive(now.vec_core)
        ref.vec_b[...] = ref.vec_a[...] + ref.vec_core[...]
        now.vec_x = send(ref.vec_b, ref.vec_x, x_dev)

    @step
    def vector_depth():
        arrive(now.vec_x)
        ref.vec_c[...] = ref.vec_b[...] + ref.vec_x[...]
        copies = []
        for distance in range(1, depth):
            peer, device = z_peer(distance)
            lanes = pl.ds(pl.multiple_of(peer * LANES, LANES), LANES)
            copies.append((ref.vec_c.at[:, lanes], ref.vec_depth.at[distance - 1], device))
        now.vec_depth = ship(copies, ref.vec_depth)

    @step
    def vector_done():
        arrive(now.vec_depth)
        lanes = pl.ds(pl.multiple_of(z_place * LANES, LANES), LANES)
        total = ref.vec_c[:, lanes]
        for distance in range(1, depth):
            total = total + ref.vec_depth[distance - 1]
        ref.vectors[...] = total

    for group in (dec_in_part, dec_out_part, cross_part, enc_in_part, enc_out_part, embed_part):
        steps += [partial(advance, group)] * 3 + [partial(finish, group)]
    for index in ORDER:
        steps[index]()
    for batch in batches:
        depart(batch)
    if len(batches) != LINK_COUNT:
        raise ValueError(len(batches))


def finish_body(*refs):
    (
        dec_in,
        enc_grad_in,
        dec_grad_in,
        ff_in_two,
        cross,
        ff_in_one,
        embed,
        ff_out_two,
        ff_out_one,
        head_enc,
        head_self,
        vectors,
        dec_out,
        enc_grad,
        dec_grad,
        g_embed,
        g_enc_qkv,
        g_enc_out,
        g_enc_ff_in,
        g_enc_ff_out,
        g_enc_query_bias,
        g_enc_bias,
        g_enc_gain,
        g_dec_qkv,
        g_dec_out,
        g_cross_qkv,
        g_cross_out,
        g_dec_ff_in,
        g_dec_ff_out,
        g_dec_bias,
        g_dec_gain,
        g_ff_bias,
    ) = refs
    place = lax.axis_index(SEQ)
    column, width = g_enc_out.shape
    channels = g_embed.shape[1]
    member = lax.rem(place, QUAD)
    dec_out[...] = dec_in[...]
    enc_grad[...] = enc_grad_in[...]
    dec_grad[...] = dec_grad_in[...]

    def whole(block):
        value = block[...]
        return value.reshape(value.shape[0] * value.shape[1], value.shape[2]).astype(F32)

    g_dec_ff_in[...] = whole(ff_in_two).T
    g_enc_ff_in[...] = whole(ff_in_one).T
    block = whole(cross)
    for index in range(3):
        g_cross_qkv[index] = block[index * column : (index + 1) * column]
    g_dec_out[...] = block[3 * column : 4 * column]
    for block, wide, narrow in (
        (ff_out_two, g_dec_ff_out, g_cross_out),
        (ff_out_one, g_enc_ff_out, g_enc_out),
    ):
        for half in range(HALVES):
            value = block[half].astype(F32)
            step = wide.shape[1] // 2
            wide[:, half * step : (half + 1) * step] = value[:, 0:step]
            rest = width // 2
            narrow[:, half * rest : (half + 1) * rest] = value[:, step : step + rest]
    late = []
    for block, target in ((head_enc, g_enc_qkv), (head_self, g_dec_qkv)):
        for index in range(3):
            target[index] = block[index * column : (index + 1) * column, 0:width]
        late.append(block[:, width : width + LANES].T[0:1])
    late_enc, late_self = late
    block = whole(embed)
    g_embed[:, 0:width] = block[0:column]
    g_embed[:, width:channels] = block[column : 2 * column, 0 : channels - width]

    values = vectors[...]
    moved = pltpu.roll(values, lax.rem(LANES - member * column, LANES), axis=1)
    rows = moved[:, 0:column]
    g_enc_query_bias[...] = late_enc[:, 0:column]
    g_enc_bias[...] = jnp.concatenate([late_enc[:, 2 * column : 3 * column], rows[2:6]], axis=0)
    g_enc_gain[...] = rows[6:8]
    g_dec_bias[...] = jnp.concatenate(
        [late_self[:, 0:column], late_self[:, 2 * column : 3 * column], rows[10:18]], axis=0
    )
    g_dec_gain[...] = rows[18:21]
    row_index = lax.broadcasted_iota(jnp.int32, values.shape, 0)
    for index in range(2):
        chosen = jnp.where(row_index == 21 + QUAD * index + member, values, 0.0)
        g_ff_bias[index : index + 1, :] = jnp.sum(chosen, axis=0, keepdims=True)


def fused_local(
    enc_in,
    series,
    channel_mask,
    item_group,
    tau_scale,
    delta_shift,
    dec_in,
    value_embed,
    enc_qkv,
    enc_out,
    enc_ff_in,
    enc_ff_out,
    enc_query_bias,
    enc_bias,
    enc_gain,
    dec_qkv,
    dec_out,
    cross_qkv,
    cross_out,
    dec_ff_in,
    dec_ff_out,
    dec_bias,
    dec_gain,
    ff_bias,
    cotangent,
):
    rows, width = enc_in.shape[1:]
    hidden = enc_ff_in.shape[1]
    channels = value_embed.shape[0]
    chips = HEADS
    column = width // (chips * CORES)
    depth = chips * CORES // QUAD
    padded = -(-channels // LANES) * LANES
    keys_total = chips * CORES * rows
    queries = chips * rows // 2
    in_smem = pl.BlockSpec(memory_space=pltpu.SMEM)
    in_vmem = pl.BlockSpec(memory_space=pltpu.VMEM)
    anywhere = pl.BlockSpec(memory_space=pl.ANY)

    weights = dict(
        value_embed=value_embed,
        enc_qkv=enc_qkv,
        enc_out=enc_out,
        enc_ff_in=enc_ff_in,
        enc_ff_out=enc_ff_out,
        dec_qkv=dec_qkv,
        dec_out=dec_out,
        cross_qkv=cross_qkv,
        cross_out=cross_out,
        dec_ff_in=dec_ff_in,
        dec_ff_out=dec_ff_out,
    )
    scalars = dict(item_group=item_group, tau_scale=tau_scale)
    blocks = dict(
        enc_in=enc_in[0],
        series=series[0],
        channel_mask=channel_mask,
        delta_shift=delta_shift,
        dec_in=dec_in[0],
        cotangent=cotangent[0],
        enc_query_bias=enc_query_bias[None],
        enc_bias=enc_bias,
        enc_gain=enc_gain,
        dec_bias=dec_bias,
        dec_gain=dec_gain,
        ff_bias=ff_bias,
    )
    inputs = (scalars, blocks, dict(weight=weights))
    in_specs = [in_smem] * len(scalars) + [anywhere] * (len(blocks) + len(weights))

    def low(*shape):
        return pltpu.VMEM(shape, BF16)

    def full(*shape):
        return pltpu.VMEM(shape, F32)

    def exchanged(features):
        return low(QUAD, rows, features)

    def attention_space():
        packed = low(chips, rows // 2, LANES)
        paired = low(chips, rows, LANES)
        both = low(chips, CORES, rows, LANES)
        return dict(
            query=packed,
            t_query=packed,
            mixed=packed,
            t_mixed=packed,
            grad=packed,
            t_grad=packed,
            query_grad=packed,
            t_query_grad=packed,
            t_pair=paired,
            pair=both,
            t_pair_grad=paired,
            pair_grad=paired,
            t_part=low(CORES, chips, rows, LANES),
            part=paired,
            pair_sum=full(CORES, chips, rows, LANES),
            pair_t=low(LANES, keys_total),
            weights=low(HALVES, keys_total, queries),
            inverse=full(HALVES, 8, queries),
            mixed_t=full(LANES, queries),
        )

    def sum_space(half, features):
        return dict(
            part=low(2, 2, 2, half, features),
            item=low(2, 2, half, features),
            half=low(2, 2, half, features),
            near=low(2, half, features),
            pair=low(2, half, features),
            far=low(half, features),
        )

    def group_space(count, features):
        return dict(
            cut=exchanged(features), met=exchanged(features), **sum_space(count // 2, width)
        )

    def core_group_space():
        features = (hidden + width) // 2
        return dict(
            own=low(HALVES, rows, features),
            tokens=exchanged(features),
            cut=low(CORES, rows, width),
            met=exchanged(width),
            **sum_space(column, features),
        )

    def head_space():
        shape = (3 * column, width + LANES)
        return dict(
            mine=low(CORES, *shape),
            core=low(*shape),
            both=low(*shape),
            item=low(*shape),
        )

    ff_width = hidden // QUAD
    group_rows = (LANES, 4 * column, LANES, 2 * column)
    group_features = (ff_width, 4 * LANES, ff_width, LANES)
    scratch = dict(
        held={name: low(*value.shape) for name, value in weights.items()},
        held_blocks={
            name: pltpu.VMEM(value.shape, value.dtype) for name, value in blocks.items()
        },
        block_sem=pltpu.SemaphoreType.DMA((len(blocks),)),
        g_dec_in=low(depth, 2, rows, width),
        g_enc_hidden=low(depth, 2, rows, width),
        x_series=exchanged(padded),
        x_early=exchanged(4 * width),
        x_late=exchanged(width),
        enc_slope=full(rows, hidden),
        dec_slope=full(rows, hidden),
        attention=[attention_space() for index in range(3)],
        group=[group_space(*sizes) for sizes in zip(group_rows, group_features)],
        core_group=[core_group_space() for index in range(2)],
        head_enc=head_space(),
        head_self=head_space(),
        t_shift=full(8, LANES),
        shift=full(chips, CORES, 8, LANES),
        shift_columns=full(keys_total, LANES),
        embedded=full(rows, width),
        first_dec=full(rows, width),
        second_grad=full(rows, width),
        first_grad=full(rows, width),
        enc_first_grad=full(rows, width),
        unit=full(4, rows, width),
        scale=full(4, rows, LANES),
        vec=full(32, width),
        vec_item=full(32, width),
        vec_a=full(32, width),
        vec_core=full(32, width),
        vec_b=full(32, width),
        vec_x=full(32, width),
        vec_c=full(32, width),
        vec_depth=full(depth - 1, 32, LANES),
        load_sem=pltpu.SemaphoreType.DMA((len(weights),)),
        send_sem=pltpu.SemaphoreType.DMA((LINK_COUNT,)),
        recv_sem=pltpu.SemaphoreType.DMA((LINK_COUNT,)),
    )
    outputs = dict(
        dec_result=jax.ShapeDtypeStruct((rows, width), BF16),
        enc_grad=jax.ShapeDtypeStruct((rows, width), F32),
        dec_grad=jax.ShapeDtypeStruct((rows, width), F32),
        sums=[jax.ShapeDtypeStruct((2, count // 2, width), BF16) for count in group_rows]
        + [jax.ShapeDtypeStruct((2, column, (hidden + width) // 2), BF16)] * 2,
        heads=[jax.ShapeDtypeStruct((3 * column, width + LANES), F32)] * 2,
        vectors=jax.ShapeDtypeStruct((32, LANES), F32),
    )
    out_shapes, out_structure = jax.tree.flatten(outputs)
    scratch_shapes, scratch_structure = jax.tree.flatten(scratch)
    operands = jax.tree.leaves(inputs)
    structures = [jax.tree.structure(part) for part in inputs]
    results = pl.pallas_call(
        partial(fused_body, structures + [out_structure, scratch_structure]),
        out_shape=[pltpu.VMEM(leaf.shape, leaf.dtype) for leaf in out_shapes],
        in_specs=in_specs,
        out_specs=[in_vmem] * len(out_shapes),
        scratch_shapes=scratch_shapes,
        compiler_params=pltpu.CompilerParams(
            collective_id=1, has_side_effects=True, vmem_limit_bytes=VMEM_BYTES
        ),
        name="layers",
    )(*operands)
    results = jax.tree.unflatten(out_structure, results)
    results = [
        results[key] for key in ("dec_result", "enc_grad", "dec_grad")
    ] + results["sums"] + results["heads"] + [results["vectors"]]

    final = [
        (rows, width),
        (rows, width),
        (rows, width),
        (column, channels),
        (3, column, width),
        (column, width),
        (width, hidden // (chips * CORES)),
        (column, hidden),
        (1, column),
        (5, column),
        (2, column),
        (3, column, width),
        (column, width),
        (3, column, width),
        (column, width),
        (width, hidden // (chips * CORES)),
        (column, hidden),
        (10, column),
        (3, column),
        (2, hidden // (chips * CORES)),
    ]
    outputs = pl.pallas_call(
        finish_body,
        out_shape=[
            jax.ShapeDtypeStruct(shape, BF16 if index == 0 else F32)
            for index, shape in enumerate(final)
        ],
        in_specs=[in_vmem] * len(results),
        out_specs=[in_vmem] * len(final),
        compiler_params=pltpu.CompilerParams(vmem_limit_bytes=12 << 20),
        name="columns",
    )(*results)
    outputs = list(outputs)
    for index in range(3):
        outputs[index] = outputs[index][None]
    outputs[8] = outputs[8][0]
    for index in (3, 4, 5, 7, 11, 12, 13, 14, 16):
        outputs[index] = jnp.swapaxes(outputs[index], -1, -2)
    return tuple(outputs)


def solution(mesh):
    in_specs = (
        P(BATCH, SEQ, None),
        P(BATCH, SEQ, None),
        P(),
        P(BATCH),
        P(BATCH),
        P(BATCH, SEQ),
        P(BATCH, SEQ, None),
        P(),
        P(),
        P(),
        P(),
        P(),
        P(),
        P(),
        P(),
        P(),
        P(),
        P(),
        P(),
        P(),
        P(),
        P(),
        P(),
        P(),
        P(BATCH, SEQ, None),
    )
    out_specs = (
        P(BATCH, SEQ, None),
        P(BATCH, SEQ, None),
        P(BATCH, SEQ, None),
        P(None, SEQ),
        P(None, None, SEQ),
        P(None, SEQ),
        P(None, SEQ),
        P(None, SEQ),
        P(SEQ),
        P(None, SEQ),
        P(None, SEQ),
        P(None, None, SEQ),
        P(None, SEQ),
        P(None, None, SEQ),
        P(None, SEQ),
        P(None, SEQ),
        P(None, SEQ),
        P(None, SEQ),
        P(None, SEQ),
        P(None, SEQ),
    )
    fits = mesh.shape[SEQ] == HEADS * CORES and mesh.shape[BATCH] == 2
    return jax.shard_map(
        fused_local if fits else local, mesh=mesh, in_specs=in_specs, out_specs=out_specs, check_vma=False)
```

```python
from functools import partial
from types import SimpleNamespace
import math

import jax
import jax.numpy as jnp
from jax import lax
from jax.experimental import pallas as pl
from jax.experimental.pallas import tpu as pltpu
from jax.sharding import PartitionSpec as P

HEADS = 8
GROUPS = 16
SEQ = "seq"
BATCH = "batch"


epsilon = 1e-05
masked_score = -1e30


def layer_norm(inputs, gain_vector, shift_vector):
    average = jnp.mean(inputs, axis=-1, keepdims=True)
    centred = inputs - average
    variance = jnp.mean(centred * centred, axis=-1, keepdims=True)
    return centred * lax.rsqrt(variance + epsilon) * gain_vector + shift_vector


def norm_backward(inputs, gain_vector, shift_vector, upstream):
    ignored, pullback = jax.vjp(layer_norm, inputs, gain_vector, shift_vector)
    return pullback(upstream)


def project(inputs, weight_matrix):
    return jnp.dot(inputs, weight_matrix, preferred_element_type=jnp.float32)


def project_back(gradient, weight_matrix):
    return jnp.einsum("ilf,kf->ilk", gradient, weight_matrix, preferred_element_type=jnp.float32)


def weight_grad(inputs, gradient):
    return jnp.einsum("ilk,ilf->kf", inputs, gradient, preferred_element_type=jnp.float32)


def row_total(gradient):
    return jnp.sum(gradient.astype(jnp.float32), axis=(0, 1))


def split_heads(values):
    return values.reshape(values.shape[:2] + (HEADS, values.shape[2] // HEADS))


def merge_heads(head_values):
    return jnp.transpose(head_values, (0, 2, 1, 3)).reshape(
        head_values.shape[0], head_values.shape[2], -1
    )


def over_blocks(update, totals, arrays, shard_rows):
    length = arrays[0].shape[1]
    block_rows = shard_rows * math.gcd(length // shard_rows, 8)
    block_count = length // block_rows
    stacked = tuple(
        (
            jnp.moveaxis(
                member.reshape((member.shape[0], block_count, block_rows) + member.shape[2:]), 1, 0
            )
            for member in arrays
        )
    )
    offsets = jnp.arange(block_count, dtype=jnp.int32) * block_rows

    def advance(running, inputs):
        return (update(running, inputs[0], inputs[1]), None)

    totals, ignored = lax.scan(advance, totals, (stacked, offsets))
    return totals


def head_scores(query_heads, key_heads, tau_value, key_shift):
    raw_scores = jnp.einsum(
        "iqhd,ikhd->ihqk", query_heads, key_heads, preferred_element_type=jnp.float32
    )
    return (tau_value[:, None, None, None] * raw_scores + key_shift[:, None, None, :]) * 0.125


def causal_mask(scores, query_pos, key_pos):
    allowed = query_pos[:, None] >= key_pos[None, :]
    return jnp.where(allowed[None, None], scores, masked_score)


def fresh_totals(item_count, row_count, head_size):
    return (
        jnp.full((item_count, HEADS, row_count), masked_score, jnp.float32),
        jnp.zeros((item_count, HEADS, row_count), jnp.float32),
        jnp.zeros((item_count, HEADS, row_count, head_size), jnp.float32),
    )


def finish_forward(totals):
    running_max, running_sum, weighted = totals
    output = merge_heads(weighted / running_sum[..., None])
    log_total = jnp.transpose(running_max + jnp.log(running_sum), (0, 2, 1))
    return (output, log_total)


def row_products(grad_rows, mixed_rows):
    return jnp.sum(split_heads(grad_rows).astype(jnp.float32) * split_heads(mixed_rows), axis=-1)


def scaled_grad(head_totals, tau_value):
    return merge_heads(head_totals * (tau_value * 0.125)[:, None, None, None]).astype(jnp.bfloat16)


def plain_unpack(fetched):
    return (fetched[0], fetched[1], fetched[2].astype(jnp.float32))


def self_unpack(fetched):
    return (fetched[0], fetched[1], jnp.zeros(fetched[0].shape[:2], jnp.float32))


def forward_update(query_heads, tau_value, query_pos, causal, unpack, shard_rows):

    def update(totals, fetched, offset):

        def block_update(running, piece_parts, inner_offset):
            running_max, running_sum, weighted = running
            key_rows, value_rows, key_shift = unpack(piece_parts)
            scores = head_scores(query_heads, split_heads(key_rows), tau_value, key_shift)
            if causal:
                key_pos = inner_offset + jnp.arange(key_rows.shape[1], dtype=jnp.int32)
                scores = causal_mask(scores, query_pos, key_pos)
            new_max = jnp.maximum(running_max, jnp.max(scores, axis=-1))
            factor = jnp.exp(running_max - new_max)
            weights = jnp.exp(scores - new_max[..., None])
            new_sum = running_sum * factor + jnp.sum(weights, axis=-1)
            mixed_values = jnp.einsum(
                "ihqk,ikhd->ihqd",
                weights,
                split_heads(value_rows).astype(jnp.float32),
                preferred_element_type=jnp.float32,
            )
            return (new_max, new_sum, weighted * factor[..., None] + mixed_values)

        return over_blocks(block_update, totals, fetched, shard_rows)

    return update


def query_grad_update(
    query_heads, grad_heads, log_total, row_dot, tau_value, query_pos, causal, unpack, shard_rows
):

    def update(totals, fetched, offset):

        def block_update(running, piece_parts, inner_offset):
            key_rows, value_rows, key_shift = unpack(piece_parts)
            key_heads = split_heads(key_rows)
            scores = head_scores(query_heads, key_heads, tau_value, key_shift)
            if causal:
                key_pos = inner_offset + jnp.arange(key_rows.shape[1], dtype=jnp.int32)
                scores = causal_mask(scores, query_pos, key_pos)
            probabilities = jnp.exp(scores - log_total[..., None])
            prob_grads = jnp.einsum(
                "iqhd,ikhd->ihqk",
                grad_heads,
                split_heads(value_rows),
                preferred_element_type=jnp.float32,
            )
            score_grads = (probabilities * (prob_grads - row_dot[..., None])).astype(jnp.bfloat16)
            return running + jnp.einsum(
                "ihqk,ikhd->ihqd", score_grads, key_heads, preferred_element_type=jnp.float32
            )

        return over_blocks(block_update, totals, fetched, shard_rows)

    return update


def key_grad_update(key_heads, value_heads, key_shift, tau_value, key_pos, causal, shard_rows):

    def update(totals, fetched, offset):

        def block_update(running, piece_parts, inner_offset):
            key_total, value_total = running
            query_heads = split_heads(piece_parts[0].astype(jnp.bfloat16))
            grad_heads = split_heads(piece_parts[1].astype(jnp.bfloat16))
            log_rows = jnp.transpose(piece_parts[2], (0, 2, 1))
            dot_rows = jnp.transpose(piece_parts[3], (0, 2, 1))
            scores = head_scores(query_heads, key_heads, tau_value, key_shift)
            if causal:
                query_pos = inner_offset + jnp.arange(piece_parts[0].shape[1], dtype=jnp.int32)
                scores = causal_mask(scores, query_pos, key_pos)
            probabilities = jnp.exp(scores - log_rows[..., None])
            value_total = value_total + jnp.einsum(
                "ihqk,iqhd->ihkd",
                probabilities,
                grad_heads.astype(jnp.float32),
                preferred_element_type=jnp.float32,
            )
            prob_grads = jnp.einsum(
                "iqhd,ikhd->ihqk", grad_heads, value_heads, preferred_element_type=jnp.float32
            )
            score_grads = (probabilities * (prob_grads - dot_rows[..., None])).astype(jnp.bfloat16)
            key_total = key_total + jnp.einsum(
                "ihqk,iqhd->ihkd", score_grads, query_heads, preferred_element_type=jnp.float32
            )
            return (key_total, value_total)

        return over_blocks(block_update, totals, fetched, shard_rows)

    return update


def feed_forward_back(upstream, hidden, pre_act, activated, weight_in, weight_out):
    out_grad = upstream.astype(jnp.bfloat16)
    out_weight_grad = weight_grad(activated, out_grad)
    out_bias_grad = row_total(out_grad)
    act_grad = project_back(out_grad, weight_out)
    ignored, gelu_back = jax.vjp(partial(jax.nn.gelu, approximate=False), pre_act)
    pre_grad = gelu_back(act_grad)[0].astype(jnp.bfloat16)
    return (
        project_back(pre_grad, weight_in),
        weight_grad(hidden, pre_grad),
        row_total(pre_grad),
        out_weight_grad,
        out_bias_grad,
    )


def local(
    enc_in,
    series,
    channel_mask,
    item_group,
    tau_scale,
    delta_shift,
    dec_in,
    value_embed,
    enc_qkv,
    enc_out,
    enc_ff_in,
    enc_ff_out,
    enc_query_bias,
    enc_bias,
    enc_gain,
    dec_qkv,
    dec_out,
    cross_qkv,
    cross_out,
    dec_ff_in,
    dec_ff_out,
    dec_bias,
    dec_gain,
    ff_bias,
    cotangent,
):
    item_count, enc_rows, width = enc_in.shape
    dec_rows = dec_in.shape[1]
    head_size = width // HEADS
    seq_index = lax.axis_index(SEQ)
    enc_pos = seq_index * enc_rows + jnp.arange(enc_rows, dtype=jnp.int32)
    dec_pos = seq_index * dec_rows + jnp.arange(dec_rows, dtype=jnp.int32)
    enc_shift = delta_shift.astype(jnp.float32)
    chosen = (item_group[:, None] == jnp.arange(GROUPS, dtype=jnp.int32)[None, :]).astype(
        jnp.float32
    )
    channels = jnp.dot(chosen, channel_mask.astype(jnp.float32), precision=lax.Precision.HIGHEST)
    masked_series = (series.astype(jnp.float32) * channels[:, None, :]).astype(jnp.bfloat16)
    embedded = enc_in.astype(jnp.float32) + project(masked_series, value_embed)
    enc_hidden = embedded.astype(jnp.bfloat16)
    enc_query = (project(enc_hidden, enc_qkv[0]) + enc_query_bias).astype(jnp.bfloat16)
    enc_key = project(enc_hidden, enc_qkv[1]).astype(jnp.bfloat16)
    enc_value = (project(enc_hidden, enc_qkv[2]) + enc_bias[0]).astype(jnp.bfloat16)
    enc_update = forward_update(
        split_heads(enc_query), tau_scale, enc_pos, False, plain_unpack, enc_rows
    )
    enc_mixed, enc_log = finish_forward(
        enc_update(
            fresh_totals(item_count, enc_rows, head_size),
            (
                lax.all_gather(enc_key, SEQ, axis=1, tiled=True),
                lax.all_gather(enc_value, SEQ, axis=1, tiled=True),
                lax.all_gather(delta_shift, SEQ, axis=1, tiled=True),
            ),
            jnp.int32(0),
        )
    )
    enc_attended = enc_mixed.astype(jnp.bfloat16)
    enc_first_in = embedded + project(enc_attended, enc_out) + enc_bias[1]
    enc_first = layer_norm(enc_first_in, enc_gain[0], enc_bias[3])
    enc_ff_hidden = enc_first.astype(jnp.bfloat16)
    enc_ff_pre = project(enc_ff_hidden, enc_ff_in) + ff_bias[0]
    enc_ff_act = jax.nn.gelu(enc_ff_pre, approximate=False).astype(jnp.bfloat16)
    enc_second_in = enc_first + project(enc_ff_act, enc_ff_out) + enc_bias[2]
    encoded = layer_norm(enc_second_in, enc_gain[1], enc_bias[4])
    memory = encoded.astype(jnp.bfloat16)
    self_query = (project(dec_in, dec_qkv[0]) + dec_bias[0]).astype(jnp.bfloat16)
    self_key = project(dec_in, dec_qkv[1]).astype(jnp.bfloat16)
    self_value = (project(dec_in, dec_qkv[2]) + dec_bias[1]).astype(jnp.bfloat16)
    self_update = forward_update(
        split_heads(self_query), tau_scale, dec_pos, True, self_unpack, dec_rows
    )
    self_mixed, self_log = finish_forward(
        self_update(
            fresh_totals(item_count, dec_rows, head_size),
            (
                lax.all_gather(self_key, SEQ, axis=1, tiled=True),
                lax.all_gather(self_value, SEQ, axis=1, tiled=True),
            ),
            jnp.int32(0),
        )
    )
    self_attended = self_mixed.astype(jnp.bfloat16)
    dec_first_in = dec_in.astype(jnp.float32) + project(self_attended, dec_out) + dec_bias[2]
    dec_first = layer_norm(dec_first_in, dec_gain[0], dec_bias[7])
    cross_hidden = dec_first.astype(jnp.bfloat16)
    cross_query = (project(cross_hidden, cross_qkv[0]) + dec_bias[3]).astype(jnp.bfloat16)
    cross_key = project(memory, cross_qkv[1]).astype(jnp.bfloat16)
    cross_value = (project(memory, cross_qkv[2]) + dec_bias[4]).astype(jnp.bfloat16)
    cross_start = fresh_totals(item_count, dec_rows, head_size)
    cross_update = forward_update(
        split_heads(cross_query), tau_scale, dec_pos, False, plain_unpack, enc_rows
    )
    cross_totals = cross_update(
        cross_start,
        (
            lax.all_gather(cross_key, SEQ, axis=1, tiled=True),
            lax.all_gather(cross_value, SEQ, axis=1, tiled=True),
            lax.all_gather(delta_shift, SEQ, axis=1, tiled=True),
        ),
        jnp.int32(0),
    )
    cross_mixed, cross_log = finish_forward(cross_totals)
    cross_attended = cross_mixed.astype(jnp.bfloat16)
    dec_second_in = dec_first + project(cross_attended, cross_out) + dec_bias[5]
    dec_second = layer_norm(dec_second_in, dec_gain[1], dec_bias[8])
    dec_ff_hidden = dec_second.astype(jnp.bfloat16)
    dec_ff_pre = project(dec_ff_hidden, dec_ff_in) + ff_bias[1]
    dec_ff_act = jax.nn.gelu(dec_ff_pre, approximate=False).astype(jnp.bfloat16)
    dec_third_in = dec_second + project(dec_ff_act, dec_ff_out) + dec_bias[6]
    decoded = layer_norm(dec_third_in, dec_gain[2], dec_bias[9])
    third_grad, dec_gain_three, dec_bias_three = norm_backward(
        dec_third_in, dec_gain[2], dec_bias[9], cotangent.astype(jnp.float32)
    )
    from_dec_ff, dec_ff_in_grad, dec_ff_bias_grad, dec_ff_out_grad, dec_ff_out_bias = (
        feed_forward_back(third_grad, dec_ff_hidden, dec_ff_pre, dec_ff_act, dec_ff_in, dec_ff_out)
    )
    second_grad, dec_gain_two, dec_bias_two = norm_backward(
        dec_second_in, dec_gain[1], dec_bias[8], third_grad + from_dec_ff
    )
    cross_branch_grad = second_grad.astype(jnp.bfloat16)
    cross_out_grad = weight_grad(cross_attended, cross_branch_grad)
    cross_out_bias = row_total(cross_branch_grad)
    cross_mixed_grad = project_back(cross_branch_grad, cross_out).astype(jnp.bfloat16)
    cross_dot = row_products(cross_mixed_grad, cross_mixed)
    cross_query_start = jnp.zeros((item_count, HEADS, dec_rows, head_size), jnp.float32)
    cross_back = query_grad_update(
        split_heads(cross_query),
        split_heads(cross_mixed_grad),
        jnp.transpose(cross_log, (0, 2, 1)),
        jnp.transpose(cross_dot, (0, 2, 1)),
        tau_scale,
        dec_pos,
        False,
        plain_unpack,
        enc_rows,
    )
    cross_query_total = cross_back(
        cross_query_start,
        (
            lax.all_gather(cross_key, SEQ, axis=1, tiled=True),
            lax.all_gather(cross_value, SEQ, axis=1, tiled=True),
            lax.all_gather(delta_shift, SEQ, axis=1, tiled=True),
        ),
        jnp.int32(0),
    )
    cross_query_grad = scaled_grad(cross_query_total, tau_scale)
    cross_key_update = key_grad_update(
        split_heads(cross_key),
        split_heads(cross_value),
        enc_shift,
        tau_scale,
        enc_pos,
        False,
        dec_rows,
    )
    cross_key_start = (
        jnp.zeros((item_count, HEADS, enc_rows, head_size), jnp.float32),
        jnp.zeros((item_count, HEADS, enc_rows, head_size), jnp.float32),
    )
    cross_key_total, cross_value_total = cross_key_update(
        cross_key_start,
        (
            lax.all_gather(cross_query.astype(jnp.float32), SEQ, axis=1, tiled=True),
            lax.all_gather(cross_mixed_grad.astype(jnp.float32), SEQ, axis=1, tiled=True),
            lax.all_gather(cross_log, SEQ, axis=1, tiled=True),
            lax.all_gather(cross_dot, SEQ, axis=1, tiled=True),
        ),
        jnp.int32(0),
    )
    cross_key_grad = scaled_grad(cross_key_total, tau_scale)
    cross_value_grad = merge_heads(cross_value_total).astype(jnp.bfloat16)
    cross_qkv_grad = jnp.stack(
        [
            weight_grad(cross_hidden, cross_query_grad),
            weight_grad(memory, cross_key_grad),
            weight_grad(memory, cross_value_grad),
        ]
    )
    memory_grad = project_back(cross_key_grad, cross_qkv[1]) + project_back(
        cross_value_grad, cross_qkv[2]
    )
    first_grad, dec_gain_one, dec_bias_one = norm_backward(
        dec_first_in,
        dec_gain[0],
        dec_bias[7],
        second_grad + project_back(cross_query_grad, cross_qkv[0]),
    )
    self_branch_grad = first_grad.astype(jnp.bfloat16)
    dec_out_grad = weight_grad(self_attended, self_branch_grad)
    self_out_bias = row_total(self_branch_grad)
    self_mixed_grad = project_back(self_branch_grad, dec_out).astype(jnp.bfloat16)
    self_dot = row_products(self_mixed_grad, self_mixed)
    self_back = query_grad_update(
        split_heads(self_query),
        split_heads(self_mixed_grad),
        jnp.transpose(self_log, (0, 2, 1)),
        jnp.transpose(self_dot, (0, 2, 1)),
        tau_scale,
        dec_pos,
        True,
        self_unpack,
        dec_rows,
    )
    self_query_total = self_back(
        jnp.zeros((item_count, HEADS, dec_rows, head_size), jnp.float32),
        (
            lax.all_gather(self_key, SEQ, axis=1, tiled=True),
            lax.all_gather(self_value, SEQ, axis=1, tiled=True),
        ),
        jnp.int32(0),
    )
    self_query_grad = scaled_grad(self_query_total, tau_scale)
    self_key_update = key_grad_update(
        split_heads(self_key),
        split_heads(self_value),
        jnp.zeros((item_count, dec_rows), jnp.float32),
        tau_scale,
        dec_pos,
        True,
        dec_rows,
    )
    self_key_start = (
        jnp.zeros((item_count, HEADS, dec_rows, head_size), jnp.float32),
        jnp.zeros((item_count, HEADS, dec_rows, head_size), jnp.float32),
    )
    self_key_total, self_value_total = self_key_update(
        self_key_start,
        (
            lax.all_gather(self_query.astype(jnp.float32), SEQ, axis=1, tiled=True),
            lax.all_gather(self_mixed_grad.astype(jnp.float32), SEQ, axis=1, tiled=True),
            lax.all_gather(self_log, SEQ, axis=1, tiled=True),
            lax.all_gather(self_dot, SEQ, axis=1, tiled=True),
        ),
        jnp.int32(0),
    )
    self_key_grad = scaled_grad(self_key_total, tau_scale)
    self_value_grad = merge_heads(self_value_total).astype(jnp.bfloat16)
    dec_qkv_grad = jnp.stack(
        [
            weight_grad(dec_in, self_query_grad),
            weight_grad(dec_in, self_key_grad),
            weight_grad(dec_in, self_value_grad),
        ]
    )
    dec_in_grad = (
        first_grad
        + project_back(self_query_grad, dec_qkv[0])
        + project_back(self_key_grad, dec_qkv[1])
        + project_back(self_value_grad, dec_qkv[2])
    )
    enc_second_grad, enc_gain_two, enc_bias_two = norm_backward(
        enc_second_in, enc_gain[1], enc_bias[4], memory_grad
    )
    from_enc_ff, enc_ff_in_grad, enc_ff_bias_grad, enc_ff_out_grad, enc_ff_out_bias = (
        feed_forward_back(
            enc_second_grad, enc_ff_hidden, enc_ff_pre, enc_ff_act, enc_ff_in, enc_ff_out
        )
    )
    enc_first_grad, enc_gain_one, enc_bias_one = norm_backward(
        enc_first_in, enc_gain[0], enc_bias[3], enc_second_grad + from_enc_ff
    )
    enc_branch_grad = enc_first_grad.astype(jnp.bfloat16)
    enc_out_grad = weight_grad(enc_attended, enc_branch_grad)
    enc_out_bias = row_total(enc_branch_grad)
    enc_mixed_grad = project_back(enc_branch_grad, enc_out).astype(jnp.bfloat16)
    enc_dot = row_products(enc_mixed_grad, enc_mixed)
    enc_back = query_grad_update(
        split_heads(enc_query),
        split_heads(enc_mixed_grad),
        jnp.transpose(enc_log, (0, 2, 1)),
        jnp.transpose(enc_dot, (0, 2, 1)),
        tau_scale,
        enc_pos,
        False,
        plain_unpack,
        enc_rows,
    )
    enc_query_total = enc_back(
        jnp.zeros((item_count, HEADS, enc_rows, head_size), jnp.float32),
        (
            lax.all_gather(enc_key, SEQ, axis=1, tiled=True),
            lax.all_gather(enc_value, SEQ, axis=1, tiled=True),
            lax.all_gather(delta_shift, SEQ, axis=1, tiled=True),
        ),
        jnp.int32(0),
    )
    enc_query_grad = scaled_grad(enc_query_total, tau_scale)
    enc_key_update = key_grad_update(
        split_heads(enc_key), split_heads(enc_value), enc_shift, tau_scale, enc_pos, False, enc_rows
    )
    enc_key_start = (
        jnp.zeros((item_count, HEADS, enc_rows, head_size), jnp.float32),
        jnp.zeros((item_count, HEADS, enc_rows, head_size), jnp.float32),
    )
    enc_key_total, enc_value_total = enc_key_update(
        enc_key_start,
        (
            lax.all_gather(enc_query.astype(jnp.float32), SEQ, axis=1, tiled=True),
            lax.all_gather(enc_mixed_grad.astype(jnp.float32), SEQ, axis=1, tiled=True),
            lax.all_gather(enc_log, SEQ, axis=1, tiled=True),
            lax.all_gather(enc_dot, SEQ, axis=1, tiled=True),
        ),
        jnp.int32(0),
    )
    enc_key_grad = scaled_grad(enc_key_total, tau_scale)
    enc_value_grad = merge_heads(enc_value_total).astype(jnp.bfloat16)
    enc_qkv_grad = jnp.stack(
        [
            weight_grad(enc_hidden, enc_query_grad),
            weight_grad(enc_hidden, enc_key_grad),
            weight_grad(enc_hidden, enc_value_grad),
        ]
    )
    enc_in_grad = (
        enc_first_grad
        + project_back(enc_query_grad, enc_qkv[0])
        + project_back(enc_key_grad, enc_qkv[1])
        + project_back(enc_value_grad, enc_qkv[2])
    )
    embed_grad = weight_grad(masked_series, enc_in_grad.astype(jnp.bfloat16))
    enc_query_bias_grad = row_total(enc_query_grad)
    enc_bias_grad = jnp.stack(
        [row_total(enc_value_grad), enc_out_bias, enc_ff_out_bias, enc_bias_one, enc_bias_two]
    )
    enc_gain_grad = jnp.stack([enc_gain_one, enc_gain_two])
    dec_bias_grad = jnp.stack(
        [
            row_total(self_query_grad),
            row_total(self_value_grad),
            self_out_bias,
            row_total(cross_query_grad),
            row_total(cross_value_grad),
            cross_out_bias,
            dec_ff_out_bias,
            dec_bias_one,
            dec_bias_two,
            dec_bias_three,
        ]
    )
    dec_gain_grad = jnp.stack([dec_gain_one, dec_gain_two, dec_gain_three])
    ff_bias_grad = jnp.stack([enc_ff_bias_grad, dec_ff_bias_grad])
    shares = (
        lax.psum_scatter(embed_grad, SEQ, scatter_dimension=1, tiled=True),
        lax.psum_scatter(enc_qkv_grad, SEQ, scatter_dimension=2, tiled=True),
        lax.psum_scatter(enc_out_grad, SEQ, scatter_dimension=1, tiled=True),
        lax.psum_scatter(enc_ff_in_grad, SEQ, scatter_dimension=1, tiled=True),
        lax.psum_scatter(enc_ff_out_grad, SEQ, scatter_dimension=1, tiled=True),
        lax.psum_scatter(enc_query_bias_grad, SEQ, scatter_dimension=0, tiled=True),
        lax.psum_scatter(enc_bias_grad, SEQ, scatter_dimension=1, tiled=True),
        lax.psum_scatter(enc_gain_grad, SEQ, scatter_dimension=1, tiled=True),
        lax.psum_scatter(dec_qkv_grad, SEQ, scatter_dimension=2, tiled=True),
        lax.psum_scatter(dec_out_grad, SEQ, scatter_dimension=1, tiled=True),
        lax.psum_scatter(cross_qkv_grad, SEQ, scatter_dimension=2, tiled=True),
        lax.psum_scatter(cross_out_grad, SEQ, scatter_dimension=1, tiled=True),
        lax.psum_scatter(dec_ff_in_grad, SEQ, scatter_dimension=1, tiled=True),
        lax.psum_scatter(dec_ff_out_grad, SEQ, scatter_dimension=1, tiled=True),
        lax.psum_scatter(dec_bias_grad, SEQ, scatter_dimension=1, tiled=True),
        lax.psum_scatter(dec_gain_grad, SEQ, scatter_dimension=1, tiled=True),
        lax.psum_scatter(ff_bias_grad, SEQ, scatter_dimension=1, tiled=True),
    )
    summed = lax.psum(
        (
            shares[0],
            shares[1],
            shares[2],
            shares[3],
            shares[4],
            shares[5],
            shares[6],
            shares[7],
            shares[8],
            shares[9],
            shares[10],
            shares[11],
            shares[12],
            shares[13],
            shares[14],
            shares[15],
            shares[16],
        ),
        BATCH,
    )
    return (
        decoded.astype(jnp.bfloat16),
        enc_in_grad,
        dec_in_grad,
        summed[0],
        summed[1],
        summed[2],
        summed[3],
        summed[4],
        summed[5],
        summed[6],
        summed[7],
        summed[8],
        summed[9],
        summed[10],
        summed[11],
        summed[12],
        summed[13],
        summed[14],
        summed[15],
        summed[16],
    )


F32 = jnp.float32
BF16 = jnp.bfloat16
MESH = pl.DeviceIdType.MESH
QUAD = 4
HALVES = 2
CORES = 2
LANES = 128
LINK_COUNT = 90
SENT_ROWS = 40496
ORDER = (
    0, 1, 2, 3, 4, 5, 8, 6, 7, 9, 10, 12, 13, 15, 16, 17,
    41, 14, 18, 19, 20, 21, 22, 11, 23, 24, 42, 37, 27, 25, 30, 49,
    26, 32, 28, 38, 31, 43, 45, 36, 50, 53, 46, 57, 29, 54, 47, 33,
    61, 34, 39, 51, 58, 44, 55, 62, 48, 52, 40, 35, 59, 63, 56, 60,
    64,
)
VMEM_BYTES = 56 << 20
LOAD_FIRST = 3
LOAD_ORDER = (
    "value_embed",
    "enc_qkv",
    "dec_qkv",
    "enc_out",
    "enc_ff_in",
    "enc_ff_out",
    "dec_out",
    "cross_qkv",
    "cross_out",
    "dec_ff_in",
    "dec_ff_out",
)


def mm(left, right):
    return jnp.dot(left, right, preferred_element_type=F32)


def mm_right_t(left, right):
    return lax.dot_general(left, right, (((1,), (1,)), ((), ())), preferred_element_type=F32)


def mm_left_t(left, right):
    return lax.dot_general(left, right, (((0,), (0,)), ((), ())), preferred_element_type=F32)


def lane_index(shape):
    return lax.broadcasted_iota(jnp.int32, shape, len(shape) - 1)


def swap_halves(values):
    return pltpu.roll(values, LANES // 2, axis=1)


def low_lanes(first, second):
    return jnp.where(lane_index(first.shape) < LANES // 2, first, second)


def pack_rows(values):
    half = values.shape[0] // 2
    packed = []
    for pair in range(values.shape[1] // LANES):
        group = values[:, pair * LANES : (pair + 1) * LANES]
        top, bottom = group[:half], group[half:]
        packed.append(low_lanes(top, swap_halves(bottom)))
        packed.append(low_lanes(swap_halves(top), bottom))
    return packed


def unpack_rows(packed):
    groups = []
    for pair in range(len(packed) // 2):
        first, second = packed[2 * pair], packed[2 * pair + 1]
        top = low_lanes(first, swap_halves(second))
        bottom = low_lanes(swap_halves(first), second)
        groups.append(jnp.concatenate([top, bottom], axis=0))
    return jnp.concatenate(groups, axis=1)


def pack_pairs(keys, values):
    packed = []
    for pair in range(keys.shape[1] // LANES):
        key_group = keys[:, pair * LANES : (pair + 1) * LANES]
        value_group = values[:, pair * LANES : (pair + 1) * LANES]
        packed.append(low_lanes(key_group, swap_halves(value_group)))
        packed.append(low_lanes(swap_halves(key_group), value_group))
    return packed


def unpack_pairs(packed):
    keys, values = [], []
    for pair in range(len(packed) // 2):
        first, second = packed[2 * pair], packed[2 * pair + 1]
        keys.append(low_lanes(first, swap_halves(second)))
        values.append(low_lanes(swap_halves(first), second))
    return jnp.concatenate(keys, axis=1), jnp.concatenate(values, axis=1)


def norm_forward(values, gain, shift):
    centred = values - jnp.mean(values, axis=-1, keepdims=True)
    scale = lax.rsqrt(jnp.mean(centred * centred, axis=-1, keepdims=True) + epsilon)
    unit = centred * scale
    return unit * gain + shift, unit, scale


def norm_back(upstream, unit, scale, gain):
    inner = upstream * gain
    result = scale * (
        inner
        - jnp.mean(inner, axis=-1, keepdims=True)
        - unit * jnp.mean(inner * unit, axis=-1, keepdims=True)
    )
    return (
        result,
        jnp.sum(upstream * unit, axis=0, keepdims=True),
        jnp.sum(upstream, axis=0, keepdims=True),
    )


def rounded(values):
    return values.astype(BF16).astype(F32)


class View:
    def __init__(self, entries):
        for name, entry in entries.items():
            if isinstance(entry, dict):
                entry = View(entry)
            elif isinstance(entry, (list, tuple)):
                entry = [View(part) if isinstance(part, dict) else part for part in entry]
            setattr(self, name, entry)


class Weight:
    def __init__(self, copy, held):
        self.copy, self.held, self.here = copy, held, False

    def start(self):
        self.copy.start()

    def __call__(self):
        if not self.here:
            self.copy.wait()
            self.here = True
        return self.held


def fused_body(structures, *refs):
    entries = {}
    for structure in structures:
        count = structure.num_leaves
        entries.update(jax.tree.unflatten(structure, refs[:count]))
        refs = refs[count:]
    ref = View(entries)
    small = View(entries["held_blocks"])
    rows, width = ref.enc_in.shape
    hidden, channels, chips = ref.ff_bias.shape[1], ref.series.shape[1], HEADS
    packed_rows = rows // 2
    keys_total = chips * CORES * rows
    block_queries = chips * packed_rows
    column = width // (chips * CORES)
    depth = chips * CORES // QUAD

    place = lax.axis_index(SEQ)
    item = lax.axis_index(BATCH)
    core = lax.rem(place, 2)
    chip = place // 2
    x_place = lax.rem(chip, 2)
    z_place = chip // 2
    quad = lax.rem(place, QUAD)
    core_dev = (chip * 2 + (1 - core), item)
    x_dev = (z_place * QUAD + (1 - x_place) * 2 + core, item)
    diagonal_dev = (z_place * QUAD + (1 - x_place) * 2 + (1 - core), item)
    item_dev = (place, 1 - item)
    z_high, z_odd = z_place // 2, lax.rem(z_place, 2)
    near_dev = ((z_high * 2 + 1 - z_odd) * QUAD + quad, item)
    far_dev = (((1 - z_high) * 2 + z_odd) * QUAD + quad, item)
    x_quad = (1 - x_place) * 2 + core
    other_dev = (chip * 2 + (1 - core), 1 - item)
    item_quad = item * 2 + core
    next_quad = (1 - item) * 2 + core

    def same_core(step):
        peer = lax.rem(chip + step, chips)
        return peer, (peer * 2 + core, item)

    def z_peer(step):
        peer = lax.rem(z_place + step, depth)
        return peer, (peer * QUAD + quad, item)

    barrier = pltpu.get_barrier_semaphore()
    greeted = [core_dev, diagonal_dev, item_dev, other_dev] + [same_core(step)[1] for step in range(1, chips)]
    for device in greeted:
        pl.semaphore_signal(barrier, inc=1, device_id=device, device_id_type=MESH)

    blocks = []
    for index, (name, target) in enumerate(entries["held_blocks"].items()):
        blocks.append(pltpu.make_async_copy(entries[name], target, ref.block_sem.at[index]))
        blocks[-1].start()
    loaded = {}
    for index, name in enumerate(LOAD_ORDER):
        source, target = getattr(ref.weight, name), getattr(ref.held, name)
        copy = pltpu.make_async_copy(source, target, ref.load_sem.at[index])
        loaded[name] = Weight(copy, target)
    weight = View(loaded)
    for name in LOAD_ORDER[:LOAD_FIRST]:
        loaded[name].start()
    for copy in blocks:
        copy.wait()

    batches = []

    def ship(copies, meter=None):
        index = len(batches)
        made = []
        for source, target, device in copies:
            made.append(
                pltpu.make_async_remote_copy(
                    src_ref=source,
                    dst_ref=target,
                    send_sem=ref.send_sem.at[0],
                    recv_sem=ref.recv_sem.at[index],
                    device_id=device,
                    device_id_type=MESH,
                )
            )
            made[-1].start()
        batches.append((index, made, meter))
        return batches[-1]

    def send(source, target, device):
        return ship([(source, target, device)])

    def arrive(batch):
        index, made, meter = batch
        if meter is None:
            made[0].wait_recv()
        else:
            pltpu.make_async_copy(meter, meter, ref.recv_sem.at[index]).wait()

    def spread(source, target_at):
        copies = []
        for step in range(1, chips):
            peer, device = same_core(step)
            copies.append((source.at[peer], target_at(chip), device))
        return ship(copies, source.at[pl.ds(0, chips - 1)])

    def share(block):
        return [
            block,
            send(block.at[quad], block.at[quad], core_dev),
            send(block.at[quad], block.at[quad], x_dev),
        ]

    def relay(shared):
        block = shared[0]
        arrive(shared.pop())
        shared.append(send(block.at[x_quad], block.at[x_quad], core_dev))

    def settle(shared):
        while len(shared) > 1:
            arrive(shared.pop())

    def gathered(block, start, features):
        value = block[:, :, start : start + features]
        return value.reshape(value.shape[0] * value.shape[1], value.shape[2])

    def cut_columns(values, group, start):
        part = lane_index((rows, LANES)) // column
        for member in range(QUAD):
            total = None
            for level in range(depth):
                cut = values[:, level * LANES : (level + 1) * LANES]
                shift = (column * (level - member)) % LANES
                moved = pltpu.roll(cut, shift, axis=1) if shift else cut
                total = moved if total is None else jnp.where(part == level, moved, total)
            group.cut[member, :, start : start + LANES] = total.astype(BF16)

    def share_columns(group, start, stop):
        source, target = group.cut, group.met
        target[quad, :, start:stop] = source[quad, :, start:stop]
        copies = []
        for device, member in (
            (core_dev, x_place * 2 + 1 - core),
            (x_dev, x_quad),
            (diagonal_dev, (1 - x_place) * 2 + 1 - core),
        ):
            copies.append(
                (
                    source.at[member, :, pl.ds(start, stop - start)],
                    target.at[quad, :, pl.ds(start, stop - start)],
                    device,
                )
            )
        return ship(copies, target.at[pl.ds(0, QUAD - 1), :, pl.ds(start, stop - start)])

    def share_item(group):
        group.tokens[item_quad] = group.own[item]
        return [
            group.tokens,
            send(group.own.at[item], group.tokens.at[item_quad], core_dev),
            send(group.own.at[1 - item], group.tokens.at[item_quad], item_dev),
        ]

    def relay_item(shared):
        arrive(shared.pop())
        block = shared[0]
        shared.append(send(block.at[next_quad], block.at[next_quad], core_dev))

    def cut_cores(values, group, start):
        part = lane_index((rows, LANES)) // column
        for member in range(CORES):
            for pair in range(depth // 2):
                total = None
                for piece in range(QUAD):
                    level = pair * 2 + piece // 2
                    cut = values[:, level * LANES : (level + 1) * LANES]
                    place_in = 2 * (piece % 2) + member
                    shift = (column * (piece - place_in)) % LANES
                    moved = pltpu.roll(cut, shift, axis=1) if shift else cut
                    total = moved if total is None else jnp.where(part == piece, moved, total)
                at = start + pair * LANES
                group.cut[member, :, at : at + LANES] = total.astype(BF16)

    def share_cores(group):
        group.met[item_quad] = group.cut[core]
        return ship(
            [
                (group.cut.at[1 - core], group.met.at[item_quad], core_dev),
                (group.cut.at[core], group.met.at[item_quad], item_dev),
                (group.cut.at[1 - core], group.met.at[item_quad], other_dev),
            ],
            group.met.at[pl.ds(0, QUAD - 1)],
        )

    def build_cores(group):
        lanes = width // 2
        met = group.met[...].reshape(QUAD * rows, 2 * lanes)
        tokens = group.tokens[...]
        tokens = tokens.reshape(QUAD * rows, tokens.shape[2])
        for index, (start, stop) in enumerate(((0, hidden // 2), (hidden // 2, tokens.shape[1]))):
            gradient = mm_left_t(met[:, index * lanes : (index + 1) * lanes], tokens[:, start:stop])
            gradient = gradient.astype(BF16)
            for at in range(chips):
                group.part[at % 2, at // 4, at // 2 % 2, :, start:stop] = gradient[
                    at * column : (at + 1) * column
                ]

    def columns_of(group, start, stop):
        value = group.met[:, :, start:stop]
        return value.reshape(QUAD * rows, stop - start)

    def put_rows(target, level, start, values):
        half = target.shape[3]
        count = values.shape[0]
        done = 0
        while done < count:
            which, offset = divmod(start + done, half)
            take = min(count - done, half - offset)
            target[which, level // 2, level % 2, offset : offset + take, :] = values[
                done : done + take, :
            ]
            done += take

    def put_gradient(target, start, gradient):
        count = gradient.shape[0] // depth
        gradient = gradient.astype(BF16)
        short = -gradient.shape[1] % width
        pieces = gradient.shape[1] // width
        for level in range(depth):
            block = gradient[level * count : (level + 1) * count]
            for piece in range(pieces):
                put_rows(
                    target,
                    level,
                    start + piece * count,
                    block[:, piece * width : (piece + 1) * width],
                )
            if short:
                tail = jnp.concatenate(
                    [block[:, pieces * width :], jnp.zeros((count, short), BF16)], axis=1
                )
                put_rows(target, level, start + pieces * count, tail)

    def both_sums(left, right):
        return (left.astype(F32) + right.astype(F32)).astype(BF16)

    def steps_of(group, which, device):
        def near():
            group.half[...] = both_sums(group.part[which], group.item[...])
            return send(group.half.at[:, 1 - z_odd], group.near, near_dev)

        def far():
            group.pair[...] = both_sums(group.half[:, z_odd], group.near[...])
            return send(group.pair.at[1 - z_high], group.far, far_dev)

        def last():
            group.sum[item] = both_sums(group.pair[z_high], group.far[...])
            return send(group.sum.at[item], group.sum.at[item], item_dev)

        for level in range(2):
            group.pushes.append(
                partial(send, group.part.at[1 - which, level], group.item.at[level], device)
            )
        return [near, far, last]

    def advance(group):
        for batch in group.batches:
            arrive(batch)
        group.batches = [group.steps.pop(0)()]

    def push(group, count=1):
        for index in range(count):
            group.batches.append(group.pushes.pop(0)())

    def finish(group):
        for batch in group.batches:
            arrive(batch)

    def gather_depth(block, part, parts):
        count = rows // parts
        cut = pl.ds(part * count, count)
        here = block.at[z_place, x_place, cut]
        copies = [(here, here, z_peer(step)[1]) for step in range(1, depth)]
        return ship(copies, block.at[pl.ds(0, depth - 1), 0, cut])

    def gather_x(block, gathers):
        for batch in gathers:
            arrive(batch)
        return send(block.at[:, x_place], block.at[:, x_place], x_dev)

    def head_gradients(own, space, block):
        value = block[...]
        tokens = value.reshape((chips,) + value.shape[2:])
        tokens = jnp.concatenate([tokens, jnp.ones((chips, rows, LANES), BF16)], axis=2)
        features = tokens.shape[2]
        queries = own.t_query_grad[...].reshape(block_queries, LANES)
        total = None
        for half in range(HALVES):
            part = tokens[:, half * packed_rows : (half + 1) * packed_rows]
            part = mm_left_t(queries, part.reshape(block_queries, features))
            part = part[half * LANES // 2 : (half + 1) * LANES // 2]
            total = part if total is None else total + part
        pairs = own.t_pair_grad[...].reshape(chips * rows, LANES)
        both = mm_left_t(pairs, tokens.reshape(chips * rows, features))
        for index, gradient in enumerate((total, both[: LANES // 2], both[LANES // 2 :])):
            for which in range(CORES):
                space.mine[which, index * column : (index + 1) * column, :] = gradient[
                    which * column : (which + 1) * column
                ].astype(BF16)
        return send(space.mine.at[1 - core], space.core, core_dev)

    def heads_item(space, batch):
        arrive(batch)
        space.both[...] = both_sums(space.mine[core], space.core[...])
        return send(space.both, space.item, item_dev)

    def heads_done(space, batch, target):
        arrive(batch)
        target[...] = space.both[...].astype(F32) + space.item[...].astype(F32)

    def set_vector(row, value):
        ref.vec[row : row + 1, :] = value

    att_enc, att_self, att_cross = ref.attention
    dec_in_part, cross_part, enc_in_part, embed_part = ref.group
    dec_out_part, enc_out_part = ref.core_group
    for group in ref.group + ref.core_group:
        group.batches, group.pushes = [], []
    for group in ref.group:
        group.steps = steps_of(group, item, item_dev)
    for group in ref.core_group:
        group.steps = steps_of(group, x_place, x_dev)
    for group, result in zip(ref.group + ref.core_group, ref.sums):
        group.sum = result
    enc_ff = (weight.enc_ff_in, weight.enc_ff_out)
    dec_ff = (weight.dec_ff_in, weight.dec_ff_out)

    def build(group, row, start, features, tokens, wide=False):
        gradient = mm_left_t(columns_of(group, start, start + features), tokens)
        if wide:
            put_gradient(group.part, row, gradient)
            return
        for which in range(features // LANES):
            put_gradient(
                group.part,
                row + which * column,
                gradient[which * LANES : (which + 1) * LANES],
            )

    tau = ref.tau_scale[0]
    group_row = lax.broadcasted_iota(jnp.int32, small.channel_mask.shape, 0)
    chosen = jnp.where(
        group_row == ref.item_group[0], small.channel_mask[...].astype(F32), 0.0
    )
    channel_row = jnp.sum(chosen, axis=0, keepdims=True)
    masked = (small.series[...].astype(F32) * channel_row).astype(BF16)
    dec_hidden = small.dec_in[...]
    ref.g_dec_in[z_place, x_place] = dec_hidden
    ref.x_series[quad] = jnp.zeros(ref.x_series.shape[1:], BF16)
    ref.x_series[quad, :, 0:channels] = masked

    shift_row = small.delta_shift[...].astype(F32)
    ref.t_shift[...] = jnp.broadcast_to(
        jnp.concatenate([shift_row, shift_row], axis=1), ref.t_shift.shape
    )
    ref.shift[chip, core] = ref.t_shift[...]
    pl.semaphore_wait(barrier, len(greeted))
    go_shift = ship(
        [
            (ref.t_shift, ref.shift.at[chip, core], same_core(step)[1])
            for step in range(1, chips)
        ],
        ref.shift.at[pl.ds(0, chips - 1), 0],
    )

    embedded = small.enc_in[...].astype(F32) + mm(masked, weight.value_embed()[...])
    ref.embedded[...] = embedded
    enc_hidden = embedded.astype(BF16)
    ref.g_enc_hidden[z_place, x_place] = enc_hidden
    for name in LOAD_ORDER[LOAD_FIRST:]:
        loaded[name].start()

    def send_queries(own, query):
        for head, packed in enumerate(pack_rows(query)):
            own.t_query[head] = packed.astype(BF16)
        own.query[chip] = own.t_query[chip]
        return spread(own.t_query, lambda at: own.query.at[at])

    def send_pairs(own, keys, values):
        for head, packed in enumerate(pack_pairs(keys, values)):
            own.t_pair[head] = packed.astype(BF16)
        own.pair[chip, core] = own.t_pair[chip]
        return spread(own.t_pair, lambda at: own.pair.at[at, core])

    def pass_on(own):
        block = own.pair
        return send(block.at[:, core], block.at[:, core], core_dev)

    qkv = weight.enc_qkv()
    enc_query = mm(enc_hidden, qkv[0]) + small.enc_query_bias[...]
    enc_key = mm(enc_hidden, qkv[1])
    enc_value = mm(enc_hidden, qkv[2]) + small.enc_bias[0:1, :]
    go_enc_pair = send_pairs(att_enc, enc_key, enc_value)
    go_enc_query = send_queries(att_enc, enc_query)
    qkv = weight.dec_qkv()
    self_query = mm(dec_hidden, qkv[0]) + small.dec_bias[0:1, :]
    self_key = mm(dec_hidden, qkv[1])
    self_value = mm(dec_hidden, qkv[2]) + small.dec_bias[1:2, :]
    go_self_pair = send_pairs(att_self, self_key, self_value)
    go_self_query = send_queries(att_self, self_query)

    def attention(own, shifted, causal):
        pairs = own.pair[...].reshape(keys_total, LANES)
        pairs_t = pairs.T
        own.pair_t[...] = pairs_t
        query_t = own.query[...].reshape(block_queries, LANES).astype(F32).T
        zeros = jnp.zeros((LANES // 2, block_queries), F32)
        for half in range(HALVES):
            part = query_t[half * LANES // 2 : (half + 1) * LANES // 2]
            side = jnp.concatenate([part, zeros], axis=0).astype(BF16)
            scores = mm(pairs, side) * (tau * 0.125)
            if shifted:
                moved = ref.shift_columns[...]
                scores = scores + jnp.concatenate([moved] * (block_queries // LANES), axis=1)
            if causal:
                key_at = lax.broadcasted_iota(jnp.int32, scores.shape, 0)
                lane = lane_index(scores.shape)
                query_at = (
                    (lane // packed_rows * 2 + core) * rows
                    + half * packed_rows
                    + lane % packed_rows
                )
                scores = jnp.where(key_at > query_at, masked_score, scores)
            weights = jnp.exp(scores - jnp.max(scores, axis=0, keepdims=True))
            inverse = 1.0 / jnp.sum(weights, axis=0, keepdims=True)
            low_weights = weights.astype(BF16)
            own.weights[half] = low_weights
            own.inverse[half] = jnp.broadcast_to(inverse, (8, block_queries))
            mixed_t = mm(pairs_t, low_weights)[LANES // 2 :] * inverse
            own.mixed_t[half * LANES // 2 : (half + 1) * LANES // 2, :] = mixed_t
        mixed = own.mixed_t[...].T.astype(BF16)
        own.t_mixed[...] = mixed.reshape(chips, packed_rows, LANES)
        own.mixed[chip] = own.t_mixed[chip]
        return spread(own.t_mixed, lambda at: own.mixed.at[at])

    def mixed_rows(own):
        return unpack_rows(
            [own.mixed[head].astype(F32) for head in range(chips)]
        ).astype(BF16)

    arrive(go_shift)
    on_shift = send(ref.shift.at[:, core], ref.shift.at[:, core], core_dev)
    arrive(on_shift)
    for block in range(chips):
        line = low_lanes(ref.shift[block, 0], ref.shift[block, 1])[0:1, :] * 0.125
        ref.shift_columns[block * LANES : (block + 1) * LANES, :] = jnp.broadcast_to(
            line, (LANES, LANES)
        ).T
    arrive(go_enc_pair)
    on_enc = pass_on(att_enc)
    arrive(go_enc_query)
    arrive(on_enc)
    back_enc = attention(att_enc, True, False)
    go_dec_in = [gather_depth(ref.g_dec_in, 0, 2)]
    share_series = share(ref.x_series)
    arrive(go_self_pair)
    on_self = pass_on(att_self)
    arrive(go_self_query)
    arrive(on_self)
    back_self = attention(att_self, False, True)

    def feed_forward(values, weights, bias_row, out_bias, low_at, group, slope):
        low = values.astype(BF16)
        low_at[quad, :, 0:width] = low
        weight_in, weight_out = weights[0](), weights[1]()
        total = out_bias
        for piece in range(hidden // width):
            cut = slice(piece * width, (piece + 1) * width)
            pre = mm(low, weight_in[:, cut]) + small.ff_bias[bias_row : bias_row + 1, cut]
            normal = 0.5 * (1.0 + lax.erf(pre * 0.7071067811865476))
            act = (pre * normal).astype(BF16)
            slope[:, cut] = normal + pre * (
                jnp.exp(pre * pre * -0.5) * 0.3989422804014327
            )
            half, at = divmod(piece * width, hidden // 2)
            group.own[half, :, at : at + width] = act
            total = total + mm(act, weight_out[cut, :])
        return total

    def feed_forward_back(upstream, weights, slope, vector_row, group):
        low = upstream.astype(BF16)
        weight_in, weight_out = weights[0](), weights[1]()
        total = None
        for piece in range(hidden // width):
            cut = slice(piece * width, (piece + 1) * width)
            act_grad = mm_right_t(low, weight_out[cut, :])
            pre_grad = (act_grad * slope[:, cut]).astype(BF16)
            sums = jnp.sum(pre_grad.astype(F32), axis=0, keepdims=True)
            for member in range(QUAD):
                at = piece * LANES
                ref.vec[vector_row + member : vector_row + member + 1, at : at + LANES] = sums[
                    :, member * LANES : (member + 1) * LANES
                ]
                group.cut[member, :, at : at + LANES] = pre_grad[
                    :, member * LANES : (member + 1) * LANES
                ]
            more = mm_right_t(pre_grad, weight_in[:, cut])
            total = more if total is None else total + more
        return total

    def save_norm(index, unit, scale):
        ref.unit[index] = unit
        ref.scale[index] = jnp.broadcast_to(scale, (rows, LANES))

    def saved_norm(index):
        return ref.unit[index], ref.scale[index, :, 0:1]

    def keep_mixed(group, values):
        for half in range(HALVES):
            group.own[half, :, hidden // 2 :] = values[
                :, half * width // 2 : (half + 1) * width // 2
            ]

    arrive(back_enc)
    attended = mixed_rows(att_enc)
    keep_mixed(enc_out_part, attended)
    first, unit, scale = norm_forward(
        embedded + mm(attended, weight.enc_out()[...]) + small.enc_bias[1:2, :],
        small.enc_gain[0:1, :],
        small.enc_bias[3:4, :],
    )
    save_norm(0, unit, scale)
    second, unit, scale = norm_forward(
        first + feed_forward(
            first,
            enc_ff,
            0,
            small.enc_bias[2:3, :],
            ref.x_early,
            enc_out_part,
            ref.enc_slope,
        ),
        small.enc_gain[1:2, :],
        small.enc_bias[4:5, :],
    )
    save_norm(1, unit, scale)
    memory = second.astype(BF16)
    ref.x_early[quad, :, width : 2 * width] = memory
    share_enc_out = share_item(enc_out_part)
    qkv = weight.cross_qkv()
    cross_key = mm(memory, qkv[1])
    cross_value = mm(memory, qkv[2]) + small.dec_bias[4:5, :]
    go_cross_pair = send_pairs(att_cross, cross_key, cross_value)

    arrive(back_self)
    attended = mixed_rows(att_self)
    ref.x_early[quad, :, 2 * width : 3 * width] = attended
    first, unit, scale = norm_forward(
        small.dec_in[...].astype(F32)
        + mm(attended, weight.dec_out()[...])
        + small.dec_bias[2:3, :],
        small.dec_gain[0:1, :],
        small.dec_bias[7:8, :],
    )
    save_norm(2, unit, scale)
    ref.first_dec[...] = first
    low = first.astype(BF16)
    ref.x_early[quad, :, 3 * width : 4 * width] = low
    go_cross_query = send_queries(att_cross, mm(low, qkv[0]) + small.dec_bias[3:4, :])
    share_early = share(ref.x_early)
    go_dec_in.append(gather_depth(ref.g_dec_in, 1, 2))

    arrive(go_cross_pair)
    on_cross = pass_on(att_cross)
    arrive(go_cross_query)
    arrive(on_cross)
    back_cross = attention(att_cross, True, False)
    go_enc_hidden = [gather_depth(ref.g_enc_hidden, 0, 1)]
    on_dec_in = gather_x(ref.g_dec_in, go_dec_in)
    relay_item(share_enc_out)
    relay(share_series)
    arrive(back_cross)
    attended = mixed_rows(att_cross)
    keep_mixed(dec_out_part, attended)
    second, unit, scale = norm_forward(
        ref.first_dec[...]
        + mm(attended, weight.cross_out()[...])
        + small.dec_bias[5:6, :],
        small.dec_gain[1:2, :],
        small.dec_bias[8:9, :],
    )
    save_norm(3, unit, scale)

    forward = feed_forward(
        second,
        dec_ff,
        1,
        small.dec_bias[6:7, :],
        ref.x_late,
        dec_out_part,
        ref.dec_slope,
    )
    share_dec_out = share_item(dec_out_part)
    third, unit, scale = norm_forward(
        second + forward,
        small.dec_gain[2:3, :],
        small.dec_bias[9:10, :],
    )
    ref.dec_result[...] = third.astype(BF16)

    def norm_step(index, upstream, gain, gain_row, gain_vector, shift_vector):
        unit, scale = saved_norm(index)
        result, gain_grad, shift_grad = norm_back(
            upstream, unit, scale, gain[gain_row : gain_row + 1, :]
        )
        set_vector(gain_vector, gain_grad)
        set_vector(shift_vector, shift_grad)
        return result

    def column_sum(values):
        return jnp.sum(rounded(values), axis=0, keepdims=True)

    third_grad, gain_grad, shift_grad = norm_back(
        small.cotangent[...].astype(F32), unit, scale, small.dec_gain[2:3, :]
    )
    set_vector(20, gain_grad)
    set_vector(17, shift_grad)
    from_ff = feed_forward_back(third_grad, dec_ff, ref.dec_slope, 25, dec_in_part)
    second_grad = norm_step(3, third_grad + from_ff, small.dec_gain, 1, 19, 16)
    ref.second_grad[...] = second_grad

    def send_mixed_grad(own, branch_grad, out_weight):
        mixed_grad = mm_right_t(branch_grad.astype(BF16), out_weight[...])
        for head, packed in enumerate(pack_rows(mixed_grad)):
            own.t_grad[head] = packed.astype(BF16)
        own.grad[chip] = own.t_grad[chip]
        return spread(own.t_grad, lambda at: own.grad.at[at])

    go_cross_grad = send_mixed_grad(att_cross, second_grad, weight.cross_out())
    ff_width = hidden // QUAD

    def attention_back(own):
        pairs = own.pair[...].reshape(keys_total, LANES)
        pairs_t = own.pair_t[...]
        queries = own.query[...].reshape(block_queries, LANES).astype(F32)
        grads = own.grad[...].reshape(block_queries, LANES).astype(F32)
        grads_t = grads.T
        zeros = jnp.zeros((LANES // 2, block_queries), F32)
        blank = jnp.zeros_like(queries)
        query_grads = []
        key_total = value_total = None
        for half in range(HALVES):
            cut = slice(half * LANES // 2, (half + 1) * LANES // 2)
            grad_t = grads_t[cut]
            row_dot = jnp.sum(grad_t * own.mixed_t[cut, :], axis=0, keepdims=True)
            side = jnp.concatenate([zeros, grad_t], axis=0).astype(BF16)
            prob_grads = mm(pairs, side)
            probabilities = own.weights[half].astype(F32) * own.inverse[half, 0:1, :]
            score_grads = (probabilities * (prob_grads - row_dot)).astype(BF16)
            query_grads.append(mm(pairs_t, score_grads)[: LANES // 2])
            if half == 0:
                query_side = low_lanes(queries, blank)
                grad_side = low_lanes(blank, swap_halves(grads))
            else:
                query_side = low_lanes(swap_halves(queries), blank)
                grad_side = low_lanes(blank, grads)
            key_part = mm(score_grads, query_side.astype(BF16))
            value_part = mm(probabilities.astype(BF16), grad_side.astype(BF16))
            key_total = key_part if key_total is None else key_total + key_part
            value_total = value_part if value_total is None else value_total + value_part
        factor = tau * 0.125
        query_grad = (jnp.concatenate(query_grads, axis=0) * factor).T.astype(BF16)
        own.t_query_grad[...] = query_grad.reshape(chips, packed_rows, LANES)
        own.query_grad[chip] = own.t_query_grad[chip]
        go_query = spread(
            own.t_query_grad, lambda at: own.query_grad.at[at]
        )
        pair_grad = (key_total * factor + value_total).reshape(chips, CORES, rows, LANES)
        for which in range(CORES):
            own.pair_sum[which] = pair_grad[:, which]
            own.t_part[which] = pair_grad[:, which].astype(BF16)
        exchange = send(own.t_part.at[1 - core], own.part, core_dev)
        return go_query, exchange

    def attention_back_pairs(own, exchange):
        arrive(exchange)
        total = own.pair_sum[core] + own.part[...].astype(F32)
        own.t_pair_grad[...] = total.astype(BF16)
        own.pair_grad[chip] = own.t_pair_grad[chip]
        return spread(own.t_pair_grad, lambda at: own.pair_grad.at[at])

    def query_grad_rows(own):
        return unpack_rows(
            [own.query_grad[head].astype(F32) for head in range(chips)]
        )

    def pair_grad_rows(own):
        return unpack_pairs([own.pair_grad[head].astype(F32) for head in range(chips)])

    def input_grad(own, weights, first):
        query_grad = query_grad_rows(own)
        key_grad, value_grad = pair_grad_rows(own)
        return (
            first[...]
            + mm_right_t(query_grad.astype(BF16), weights[0])
            + mm_right_t(key_grad.astype(BF16), weights[1])
            + mm_right_t(value_grad.astype(BF16), weights[2])
        )

    now = SimpleNamespace()
    steps = []

    def step(body):
        steps.append(body)

    @step
    def late_rows():
        now.share_late = share(ref.x_late)

    @step
    def dec_in_columns():
        now.columns_dec_in = share_columns(dec_in_part, 0, ff_width)

    @step
    def dec_out_columns():
        cut_cores(third_grad, dec_out_part, 0)
        cut_cores(second_grad, dec_out_part, width // 2)
        now.columns_dec_out = share_cores(dec_out_part)
        set_vector(14, column_sum(third_grad))
        set_vector(13, column_sum(second_grad))

    @step
    def early_relay():
        relay(share_early)

    @step
    def cross_back():
        arrive(go_cross_grad)
        now.go_query, now.exchange = attention_back(att_cross)

    @step
    def late_relay():
        relay(now.share_late)

    @step
    def dec_out_relay():
        relay_item(share_dec_out)

    @step
    def cross_pairs():
        now.go_pair = attention_back_pairs(att_cross, now.exchange)

    @step
    def dec_in_build():
        settle(now.share_late)
        arrive(now.columns_dec_in)
        build(dec_in_part, 0, 0, ff_width, gathered(ref.x_late, 0, width), wide=True)
        push(dec_in_part, 2)

    @step
    def dec_out_build():
        settle(share_dec_out)
        arrive(now.columns_dec_out)
        build_cores(dec_out_part)

    @step
    def dec_out_push():
        push(dec_out_part)

    @step
    def dec_out_push_two():
        push(dec_out_part)

    @step
    def self_branch():
        arrive(now.go_query)
        now.cross_query_grad = query_grad_rows(att_cross)
        now.first_grad = norm_step(
            2,
            ref.second_grad[...]
            + mm_right_t(now.cross_query_grad.astype(BF16), weight.cross_qkv()[0]),
            small.dec_gain,
            0,
            18,
            15,
        )
        ref.first_grad[...] = now.first_grad
        now.go_self_grad = send_mixed_grad(att_self, now.first_grad, weight.dec_out())
        set_vector(10, column_sum(now.first_grad))

    @step
    def encoder_back():
        arrive(now.go_pair)
        qkv = weight.cross_qkv()
        now.cross_key_grad, now.cross_value_grad = pair_grad_rows(att_cross)
        memory_grad = mm_right_t(now.cross_key_grad.astype(BF16), qkv[1]) + mm_right_t(
            now.cross_value_grad.astype(BF16), qkv[2]
        )
        now.second = norm_step(1, memory_grad, small.enc_gain, 1, 7, 5)
        from_ff = feed_forward_back(now.second, enc_ff, ref.enc_slope, 21, enc_in_part)
        now.first = norm_step(0, now.second + from_ff, small.enc_gain, 0, 6, 4)
        ref.enc_first_grad[...] = now.first
        now.go_enc_grad = send_mixed_grad(att_enc, now.first, weight.enc_out())

    @step
    def vector_sums():
        set_vector(3, column_sum(now.second))
        set_vector(2, column_sum(now.first))
        set_vector(11, column_sum(now.cross_query_grad))
        set_vector(12, column_sum(now.cross_value_grad))
        for row in (0, 1, 8, 9, 29, 30, 31):
            set_vector(row, jnp.zeros((1, width), F32))
        now.vec_item = send(ref.vec, ref.vec_item, item_dev)

    @step
    def cross_columns():
        for index, values in enumerate(
            (now.cross_query_grad, now.cross_key_grad, now.cross_value_grad, now.first_grad)
        ):
            cut_columns(values, cross_part, index * LANES)
        now.columns_cross = share_columns(cross_part, 0, 4 * LANES)

    @step
    def enc_in_columns():
        now.columns_enc_in = share_columns(enc_in_part, 0, ff_width)

    @step
    def enc_out_columns():
        cut_cores(now.second, enc_out_part, 0)
        cut_cores(now.first, enc_out_part, width // 2)
        now.columns_enc_out = share_cores(enc_out_part)

    @step
    def self_back():
        arrive(now.go_self_grad)
        now.go_self_query_grad, now.exchange_self = attention_back(att_self)

    @step
    def enc_back():
        arrive(now.go_enc_grad)
        now.go_enc_query_grad, now.exchange_enc = attention_back(att_enc)

    @step
    def cross_build():
        settle(share_early)
        arrive(now.columns_cross)
        build(cross_part, 0, 0, LANES, gathered(ref.x_early, 3 * width, width))
        build(cross_part, column, LANES, 2 * LANES, gathered(ref.x_early, width, width))
        build(cross_part, 3 * column, 3 * LANES, LANES, gathered(ref.x_early, 2 * width, width))
        push(cross_part, 2)

    @step
    def enc_pairs():
        now.go_enc_pair_grad = attention_back_pairs(att_enc, now.exchange_enc)

    @step
    def self_pairs():
        now.go_self_pair_grad = attention_back_pairs(att_self, now.exchange_self)

    @step
    def enc_in_build():
        settle(share_early)
        arrive(now.columns_enc_in)
        build(enc_in_part, 0, 0, ff_width, gathered(ref.x_early, 0, width), wide=True)
        push(enc_in_part, 2)

    @step
    def enc_out_build():
        settle(share_enc_out)
        arrive(now.columns_enc_out)
        build_cores(enc_out_part)

    @step
    def enc_out_push():
        push(enc_out_part)

    @step
    def enc_out_push_two():
        push(enc_out_part)

    @step
    def self_heads():
        arrive(on_dec_in)
        now.core_self = head_gradients(att_self, ref.head_self, ref.g_dec_in)

    @step
    def self_heads_item():
        now.item_self = heads_item(ref.head_self, now.core_self)

    @step
    def self_heads_done():
        heads_done(ref.head_self, now.item_self, ref.heads[1])

    @step
    def enc_input():
        arrive(now.go_enc_query_grad)
        arrive(now.go_enc_pair_grad)
        total = input_grad(att_enc, weight.enc_qkv(), ref.enc_first_grad)
        ref.enc_grad[...] = total
        cut_columns(total, embed_part, 0)
        now.columns_embed = share_columns(embed_part, 0, LANES)

    @step
    def self_input():
        arrive(now.go_self_query_grad)
        arrive(now.go_self_pair_grad)
        ref.dec_grad[...] = input_grad(att_self, weight.dec_qkv(), ref.first_grad)

    @step
    def enc_hidden_hop():
        now.on_enc_hidden = gather_x(ref.g_enc_hidden, go_enc_hidden)

    @step
    def enc_heads():
        arrive(now.on_enc_hidden)
        now.core_enc = head_gradients(att_enc, ref.head_enc, ref.g_enc_hidden)

    @step
    def enc_heads_item():
        now.item_enc = heads_item(ref.head_enc, now.core_enc)

    @step
    def enc_heads_done():
        heads_done(ref.head_enc, now.item_enc, ref.heads[0])

    @step
    def embed_build():
        settle(share_series)
        arrive(now.columns_embed)
        build(embed_part, 0, 0, LANES, gathered(ref.x_series, 0, ref.x_series.shape[2]))
        push(embed_part, 2)

    @step
    def vector_core():
        arrive(now.vec_item)
        ref.vec_a[...] = ref.vec[...] + ref.vec_item[...]
        now.vec_core = send(ref.vec_a, ref.vec_core, core_dev)

    @step
    def vector_x():
        arrive(now.vec_core)
        ref.vec_b[...] = ref.vec_a[...] + ref.vec_core[...]
        now.vec_x = send(ref.vec_b, ref.vec_x, x_dev)

    @step
    def vector_depth():
        arrive(now.vec_x)
        ref.vec_c[...] = ref.vec_b[...] + ref.vec_x[...]
        copies = []
        for distance in range(1, depth):
            peer, device = z_peer(distance)
            lanes = pl.ds(pl.multiple_of(peer * LANES, LANES), LANES)
            copies.append((ref.vec_c.at[:, lanes], ref.vec_depth.at[distance - 1], device))
        now.vec_depth = ship(copies, ref.vec_depth)

    @step
    def vector_done():
        arrive(now.vec_depth)
        lanes = pl.ds(pl.multiple_of(z_place * LANES, LANES), LANES)
        total = ref.vec_c[:, lanes]
        for distance in range(1, depth):
            total = total + ref.vec_depth[distance - 1]
        ref.vectors[...] = total

    for group in (dec_in_part, dec_out_part, cross_part, enc_in_part, enc_out_part, embed_part):
        steps += [partial(advance, group)] * 3 + [partial(finish, group)]
    for index in ORDER:
        steps[index]()
    pltpu.make_async_copy(ref.sent, ref.sent, ref.send_sem.at[0]).wait()
    sent_rows = sum(
        math.prod(copy.src_ref.shape) * copy.src_ref.dtype.itemsize // (2 * LANES)
        for index, made, meter in batches
        for copy in made
    )
    if len(batches) != LINK_COUNT or sent_rows != SENT_ROWS:
        raise ValueError(len(batches), sent_rows)


def finish_body(*refs):
    (
        dec_in,
        enc_grad_in,
        dec_grad_in,
        ff_in_two,
        cross,
        ff_in_one,
        embed,
        ff_out_two,
        ff_out_one,
        head_enc,
        head_self,
        vectors,
        dec_out,
        enc_grad,
        dec_grad,
        g_embed,
        g_enc_qkv,
        g_enc_out,
        g_enc_ff_in,
        g_enc_ff_out,
        g_enc_query_bias,
        g_enc_bias,
        g_enc_gain,
        g_dec_qkv,
        g_dec_out,
        g_cross_qkv,
        g_cross_out,
        g_dec_ff_in,
        g_dec_ff_out,
        g_dec_bias,
        g_dec_gain,
        g_ff_bias,
    ) = refs
    place = lax.axis_index(SEQ)
    column, width = g_enc_out.shape
    channels = g_embed.shape[1]
    member = lax.rem(place, QUAD)
    dec_out[...] = dec_in[...]
    enc_grad[...] = enc_grad_in[...]
    dec_grad[...] = dec_grad_in[...]

    def whole(block):
        value = block[...]
        return value.reshape(value.shape[0] * value.shape[1], value.shape[2]).astype(F32)

    g_dec_ff_in[...] = whole(ff_in_two).T
    g_enc_ff_in[...] = whole(ff_in_one).T
    block = whole(cross)
    for index in range(3):
        g_cross_qkv[index] = block[index * column : (index + 1) * column]
    g_dec_out[...] = block[3 * column : 4 * column]
    for block, wide, narrow in (
        (ff_out_two, g_dec_ff_out, g_cross_out),
        (ff_out_one, g_enc_ff_out, g_enc_out),
    ):
        for half in range(HALVES):
            value = block[half].astype(F32)
            step = wide.shape[1] // 2
            wide[:, half * step : (half + 1) * step] = value[:, 0:step]
            rest = width // 2
            narrow[:, half * rest : (half + 1) * rest] = value[:, step : step + rest]
    late = []
    for block, target in ((head_enc, g_enc_qkv), (head_self, g_dec_qkv)):
        for index in range(3):
            target[index] = block[index * column : (index + 1) * column, 0:width]
        late.append(block[:, width : width + LANES].T[0:1])
    late_enc, late_self = late
    block = whole(embed)
    g_embed[:, 0:width] = block[0:column]
    g_embed[:, width:channels] = block[column : 2 * column, 0 : channels - width]

    values = vectors[...]
    moved = pltpu.roll(values, lax.rem(LANES - member * column, LANES), axis=1)
    rows = moved[:, 0:column]
    g_enc_query_bias[...] = late_enc[:, 0:column]
    g_enc_bias[...] = jnp.concatenate([late_enc[:, 2 * column : 3 * column], rows[2:6]], axis=0)
    g_enc_gain[...] = rows[6:8]
    g_dec_bias[...] = jnp.concatenate(
        [late_self[:, 0:column], late_self[:, 2 * column : 3 * column], rows[10:18]], axis=0
    )
    g_dec_gain[...] = rows[18:21]
    row_index = lax.broadcasted_iota(jnp.int32, values.shape, 0)
    for index in range(2):
        chosen = jnp.where(row_index == 21 + QUAD * index + member, values, 0.0)
        g_ff_bias[index : index + 1, :] = jnp.sum(chosen, axis=0, keepdims=True)


def fused_local(
    enc_in,
    series,
    channel_mask,
    item_group,
    tau_scale,
    delta_shift,
    dec_in,
    value_embed,
    enc_qkv,
    enc_out,
    enc_ff_in,
    enc_ff_out,
    enc_query_bias,
    enc_bias,
    enc_gain,
    dec_qkv,
    dec_out,
    cross_qkv,
    cross_out,
    dec_ff_in,
    dec_ff_out,
    dec_bias,
    dec_gain,
    ff_bias,
    cotangent,
):
    rows, width = enc_in.shape[1:]
    hidden = enc_ff_in.shape[1]
    channels = value_embed.shape[0]
    chips = HEADS
    column = width // (chips * CORES)
    depth = chips * CORES // QUAD
    padded = -(-channels // LANES) * LANES
    keys_total = chips * CORES * rows
    queries = chips * rows // 2
    in_smem = pl.BlockSpec(memory_space=pltpu.SMEM)
    in_vmem = pl.BlockSpec(memory_space=pltpu.VMEM)
    anywhere = pl.BlockSpec(memory_space=pl.ANY)

    weights = dict(
        value_embed=value_embed,
        enc_qkv=enc_qkv,
        enc_out=enc_out,
        enc_ff_in=enc_ff_in,
        enc_ff_out=enc_ff_out,
        dec_qkv=dec_qkv,
        dec_out=dec_out,
        cross_qkv=cross_qkv,
        cross_out=cross_out,
        dec_ff_in=dec_ff_in,
        dec_ff_out=dec_ff_out,
    )
    scalars = dict(item_group=item_group, tau_scale=tau_scale)
    blocks = dict(
        enc_in=enc_in[0],
        series=series[0],
        channel_mask=channel_mask,
        delta_shift=delta_shift,
        dec_in=dec_in[0],
        cotangent=cotangent[0],
        enc_query_bias=enc_query_bias[None],
        enc_bias=enc_bias,
        enc_gain=enc_gain,
        dec_bias=dec_bias,
        dec_gain=dec_gain,
        ff_bias=ff_bias,
    )
    inputs = (scalars, blocks, dict(weight=weights))
    in_specs = [in_smem] * len(scalars) + [anywhere] * (len(blocks) + len(weights))

    def low(*shape):
        return pltpu.VMEM(shape, BF16)

    def full(*shape):
        return pltpu.VMEM(shape, F32)

    def exchanged(features):
        return low(QUAD, rows, features)

    def attention_space():
        packed = low(chips, rows // 2, LANES)
        paired = low(chips, rows, LANES)
        both = low(chips, CORES, rows, LANES)
        return dict(
            query=packed,
            t_query=packed,
            mixed=packed,
            t_mixed=packed,
            grad=packed,
            t_grad=packed,
            query_grad=packed,
            t_query_grad=packed,
            t_pair=paired,
            pair=both,
            t_pair_grad=paired,
            pair_grad=paired,
            t_part=low(CORES, chips, rows, LANES),
            part=paired,
            pair_sum=full(CORES, chips, rows, LANES),
            pair_t=low(LANES, keys_total),
            weights=low(HALVES, keys_total, queries),
            inverse=full(HALVES, 8, queries),
            mixed_t=full(LANES, queries),
        )

    def sum_space(half, features):
        return dict(
            part=low(2, 2, 2, half, features),
            item=low(2, 2, half, features),
            half=low(2, 2, half, features),
            near=low(2, half, features),
            pair=low(2, half, features),
            far=low(half, features),
        )

    def group_space(count, features):
        return dict(
            cut=exchanged(features), met=exchanged(features), **sum_space(count // 2, width)
        )

    def core_group_space():
        features = (hidden + width) // 2
        return dict(
            own=low(HALVES, rows, features),
            tokens=exchanged(features),
            cut=low(CORES, rows, width),
            met=exchanged(width),
            **sum_space(column, features),
        )

    def head_space():
        shape = (3 * column, width + LANES)
        return dict(
            mine=low(CORES, *shape),
            core=low(*shape),
            both=low(*shape),
            item=low(*shape),
        )

    ff_width = hidden // QUAD
    group_rows = (LANES, 4 * column, LANES, 2 * column)
    group_features = (ff_width, 4 * LANES, ff_width, LANES)
    scratch = dict(
        held={name: low(*value.shape) for name, value in weights.items()},
        held_blocks={
            name: pltpu.VMEM(value.shape, value.dtype) for name, value in blocks.items()
        },
        block_sem=pltpu.SemaphoreType.DMA((len(blocks),)),
        g_dec_in=low(depth, 2, rows, width),
        g_enc_hidden=low(depth, 2, rows, width),
        x_series=exchanged(padded),
        x_early=exchanged(4 * width),
        x_late=exchanged(width),
        enc_slope=full(rows, hidden),
        dec_slope=full(rows, hidden),
        attention=[attention_space() for index in range(3)],
        group=[group_space(*sizes) for sizes in zip(group_rows, group_features)],
        core_group=[core_group_space() for index in range(2)],
        head_enc=head_space(),
        head_self=head_space(),
        t_shift=full(8, LANES),
        shift=full(chips, CORES, 8, LANES),
        shift_columns=full(keys_total, LANES),
        embedded=full(rows, width),
        first_dec=full(rows, width),
        second_grad=full(rows, width),
        first_grad=full(rows, width),
        enc_first_grad=full(rows, width),
        unit=full(4, rows, width),
        scale=full(4, rows, LANES),
        vec=full(32, width),
        vec_item=full(32, width),
        vec_a=full(32, width),
        vec_core=full(32, width),
        vec_b=full(32, width),
        vec_x=full(32, width),
        vec_c=full(32, width),
        vec_depth=full(depth - 1, 32, LANES),
        load_sem=pltpu.SemaphoreType.DMA((len(weights),)),
        send_sem=pltpu.SemaphoreType.DMA((1,)),
        sent=low(SENT_ROWS, LANES),
        recv_sem=pltpu.SemaphoreType.DMA((LINK_COUNT,)),
    )
    outputs = dict(
        dec_result=jax.ShapeDtypeStruct((rows, width), BF16),
        enc_grad=jax.ShapeDtypeStruct((rows, width), F32),
        dec_grad=jax.ShapeDtypeStruct((rows, width), F32),
        sums=[jax.ShapeDtypeStruct((2, count // 2, width), BF16) for count in group_rows]
        + [jax.ShapeDtypeStruct((2, column, (hidden + width) // 2), BF16)] * 2,
        heads=[jax.ShapeDtypeStruct((3 * column, width + LANES), F32)] * 2,
        vectors=jax.ShapeDtypeStruct((32, LANES), F32),
    )
    out_shapes, out_structure = jax.tree.flatten(outputs)
    scratch_shapes, scratch_structure = jax.tree.flatten(scratch)
    operands = jax.tree.leaves(inputs)
    structures = [jax.tree.structure(part) for part in inputs]
    results = pl.pallas_call(
        partial(fused_body, structures + [out_structure, scratch_structure]),
        out_shape=[pltpu.VMEM(leaf.shape, leaf.dtype) for leaf in out_shapes],
        in_specs=in_specs,
        out_specs=[in_vmem] * len(out_shapes),
        scratch_shapes=scratch_shapes,
        compiler_params=pltpu.CompilerParams(
            collective_id=1, has_side_effects=True, vmem_limit_bytes=VMEM_BYTES
        ),
        name="layers",
    )(*operands)
    results = jax.tree.unflatten(out_structure, results)
    results = [
        results[key] for key in ("dec_result", "enc_grad", "dec_grad")
    ] + results["sums"] + results["heads"] + [results["vectors"]]

    final = [
        (rows, width),
        (rows, width),
        (rows, width),
        (column, channels),
        (3, column, width),
        (column, width),
        (width, hidden // (chips * CORES)),
        (column, hidden),
        (1, column),
        (5, column),
        (2, column),
        (3, column, width),
        (column, width),
        (3, column, width),
        (column, width),
        (width, hidden // (chips * CORES)),
        (column, hidden),
        (10, column),
        (3, column),
        (2, hidden // (chips * CORES)),
    ]
    outputs = pl.pallas_call(
        finish_body,
        out_shape=[
            jax.ShapeDtypeStruct(shape, BF16 if index == 0 else F32)
            for index, shape in enumerate(final)
        ],
        in_specs=[in_vmem] * len(results),
        out_specs=[in_vmem] * len(final),
        compiler_params=pltpu.CompilerParams(vmem_limit_bytes=12 << 20),
        name="columns",
    )(*results)
    outputs = list(outputs)
    for index in range(3):
        outputs[index] = outputs[index][None]
    outputs[8] = outputs[8][0]
    for index in (3, 4, 5, 7, 11, 12, 13, 14, 16):
        outputs[index] = jnp.swapaxes(outputs[index], -1, -2)
    return tuple(outputs)


def solution(mesh):
    in_specs = (
        P(BATCH, SEQ, None),
        P(BATCH, SEQ, None),
        P(),
        P(BATCH),
        P(BATCH),
        P(BATCH, SEQ),
        P(BATCH, SEQ, None),
        P(),
        P(),
        P(),
        P(),
        P(),
        P(),
        P(),
        P(),
        P(),
        P(),
        P(),
        P(),
        P(),
        P(),
        P(),
        P(),
        P(),
        P(BATCH, SEQ, None),
    )
    out_specs = (
        P(BATCH, SEQ, None),
        P(BATCH, SEQ, None),
        P(BATCH, SEQ, None),
        P(None, SEQ),
        P(None, None, SEQ),
        P(None, SEQ),
        P(None, SEQ),
        P(None, SEQ),
        P(SEQ),
        P(None, SEQ),
        P(None, SEQ),
        P(None, None, SEQ),
        P(None, SEQ),
        P(None, None, SEQ),
        P(None, SEQ),
        P(None, SEQ),
        P(None, SEQ),
        P(None, SEQ),
        P(None, SEQ),
        P(None, SEQ),
    )
    fits = mesh.shape[SEQ] == HEADS * CORES and mesh.shape[BATCH] == 2
    return jax.shard_map(
        fused_local if fits else local, mesh=mesh, in_specs=in_specs, out_specs=out_specs, check_vma=False)
```
